32 devices in a mesh: blk: 8 (over z, y), rep: 4 (over x, core).
Axes of the slice: x: 2, y: 2, z: 4, core: 2. Of those that a mesh axis runs over, the one named last changes fastest.
Arguments:
- segment_ids: int32 [8192], P('rep'), parts along dimension 0, may hold values from 0 to 511, as said below
- block_mask: int32 [32, 8], P('rep'), parts along dimension 0, may hold values from 0 to 1, as said below
- queries: bfloat16 [8192, 640], P(('rep', 'blk')), parts along dimension 0, may hold values from -256 to 256
- keys: bfloat16 [8192, 640], P(('rep', 'blk')), parts along dimension 0, may hold values from -8 to 8
- values: bfloat16 [8192, 640], P(('rep', 'blk')), parts along dimension 0, may hold values from -6 to 6
- tokens: bfloat16 [8192, 1280], P(('rep', 'blk')), parts along dimension 0, may hold values from -6 to 6
- out_weight: bfloat16 [640, 1280], replicated, may hold values from -6 to 6
- owners: int32 [2048], P(('rep', 'blk')), parts along dimension 0, may hold values from 0 to 7, as said below
- offsets: int32 [2048], P(('rep', 'blk')), parts along dimension 0, may hold values from 0 to 127, as said below
Outputs:
- received: bfloat16 [4096, 5120], P(('rep', 'blk')), parts along dimension 0
The draws below stay inside these ranges and needn't reach their ends.
There are 4 independent parts, one for each index of `rep`. The reference program is written for one: setup_inputs(seed, part) draws one part's arguments, and reference() takes and returns one part's arrays. A program takes and returns all parts, laid end to end along the dimension named above; an argument that names none is the same for every part. Nothing has to cross between parts.
Inputs may be any that keep to these rules, and one draw needn't show every extreme that they name: `segment_ids`: never falls; every segment has a multiple of 4 patches and at most 768. `block_mask`: 1 exactly where the two blocks share a segment id. `owners`: the merged rows of one block name one owner at most 16 times; each owner is named by at most 128 rows. Rows that name the same owner have distinct offsets.
All inputs are finite; a program needn't handle non-finite values.
Results may differ from the reference program's by a relative error of at most 0.0065.
Values may be sent and summed in bfloat16 or wider, within the bound.
No kernel may reach another device: no remote copies, remote signals or barrier semaphores. Data moves between devices by JAX's collectives and lax.ppermute only.
A program may use at most 64 MiB of HBM per device.

```python
import jax
import jax.numpy as jnp
from jax import lax

D = 1280
HEADS = 8
HD = 80
TOK_DEV = 256
SPAN = 3
HF = 640
MERGED = 5120
NBLK = 8
TOKENS = 2048
SEGMAX = 768
MROWS = 64
CAP = 128
PAIR = 16


def segment_layout(key):
    quads = TOKENS // 4
    lengths = jax.random.randint(jax.random.fold_in(key, 11), (quads,), 1, SEGMAX // 4 + 1)
    lengths = lengths.at[0].set(1).at[1].set(SEGMAX // 4)
    bounds = jnp.cumsum(lengths)
    quad_seg = jnp.searchsorted(bounds, jnp.arange(quads), side='right').astype(jnp.int32)
    quad_seg = jnp.where(quad_seg == quad_seg[quads - 1], quads - 1, quad_seg).astype(jnp.int32)
    return jnp.repeat(quad_seg, 4)


def draw_segment_ids(key, part):
    return segment_layout(key)


def draw_block_mask(key, part):
    layout = segment_layout(key).reshape(NBLK, TOK_DEV)
    lowest = layout[:, 0]
    highest = layout[:, -1]
    joined = (lowest[:, None] <= highest[None, :]) & (lowest[None, :] <= highest[:, None])
    return joined.astype(jnp.int32)


def query_key_pair(key):
    query_draw = jax.random.truncated_normal(jax.random.fold_in(key, 21), -6.0, 6.0, (TOKENS, HEADS * HD), jnp.float32)
    key_draw = jax.random.truncated_normal(jax.random.fold_in(key, 22), -6.0, 6.0, (TOKENS, HEADS * HD), jnp.float32)
    return (query_draw, key_draw)


def draw_queries(key, part):
    return query_key_pair(key)[0].astype(jnp.bfloat16)


def draw_keys(key, part):
    return query_key_pair(key)[1].astype(jnp.bfloat16)


def owner_layout(key):
    total_rows = NBLK * MROWS
    entry = jnp.arange(total_rows)
    group = entry // (2 * CAP)
    within = entry % (2 * CAP)
    kind = (within >= CAP).astype(jnp.int32) + (within >= CAP + CAP // 2).astype(jnp.int32) + (within >= CAP + 3 * CAP // 4).astype(jnp.int32)
    starts = jnp.array([0, CAP, CAP + CAP // 2, CAP + 3 * CAP // 4], jnp.int32)
    slot = within - starts[kind]
    labels = jax.random.permutation(jax.random.fold_in(key, 31), NBLK).astype(jnp.int32)
    owner = labels[4 * group + kind]
    rotate = jax.random.randint(jax.random.fold_in(key, 32), (), 0, NBLK)
    unit = entry // PAIR
    sender = (unit + rotate) % NBLK
    local = unit // NBLK * PAIR + entry % PAIR
    orders = jax.vmap(lambda single: jax.random.permutation(single, MROWS))(jax.random.split(jax.random.fold_in(key, 33), NBLK))
    place = sender * MROWS + orders[sender, local]
    owners_out = jnp.zeros((total_rows,), jnp.int32).at[place].set(owner)
    offsets_out = jnp.zeros((total_rows,), jnp.int32).at[place].set(slot.astype(jnp.int32))
    return (owners_out, offsets_out)


def draw_owners(key, part):
    return owner_layout(key)[0]


def draw_offsets(key, part):
    return owner_layout(key)[1]


def levels(rng, extent, cuts, least, top_value):
    def one(axis_at, blocks):
        draws = jax.random.uniform(jax.random.fold_in(jax.random.fold_in(rng, 6), axis_at), (blocks,), jnp.float32, least / len(cuts), top_value / len(cuts))
        return jnp.repeat(jnp.exp(draws), extent[axis_at] // blocks).reshape((-1,) + (1,) * (len(extent) - axis_at - 1))

    gain = one(*cuts[0])
    for cut in cuts[1:]:
        gain = gain * one(*cut)
    return gain


def scatter_about(rng, shape, spread, reach, pieces=(), held_as=jnp.bfloat16):
    result = spread * jax.random.normal(rng, shape, jnp.float32)
    if pieces:
        result = result * levels(rng, shape, pieces, -0.22, 0.18)
    return jnp.clip(result, -reach, reach).astype(held_as)


def setup_inputs(seed: int = 0, part: int = 0) -> dict:
    key_of = jax.random.split(jax.random.key(seed), 10)
    own_keys = jax.random.split(jax.random.fold_in(key_of[9], part), 10)
    return {
        "segment_ids": draw_segment_ids(jax.random.fold_in(jax.random.fold_in(key_of[9], part), 71), part),
        "block_mask": draw_block_mask(jax.random.fold_in(jax.random.fold_in(key_of[9], part), 71), part),
        "queries": draw_queries(jax.random.fold_in(jax.random.fold_in(key_of[9], part), 71), part),
        "keys": draw_keys(jax.random.fold_in(jax.random.fold_in(key_of[9], part), 71), part),
        "values": scatter_about(own_keys[4], (TOKENS, HF), 1.0, 6.0, ((0, 8),)),
        "tokens": scatter_about(own_keys[5], (TOKENS, D), 0.5, 6.0, ((0, 8),)),
        "out_weight": scatter_about(key_of[6], (HF, D), 0.5, 6.0),
        "owners": draw_owners(jax.random.fold_in(jax.random.fold_in(key_of[9], part), 71), part),
        "offsets": draw_offsets(jax.random.fold_in(jax.random.fold_in(key_of[9], part), 71), part),
    }


NEG = -1e+30

def reference(segment_ids, block_mask, queries, keys, values, tokens, out_weight, owners, offsets):
    rows = TOK_DEV
    width = 2 * SPAN + 1
    hdim = queries.shape[1] // HEADS
    margin = SPAN * rows
    key_pad = jnp.pad(keys.astype(jnp.float32), ((margin, margin), (0, 0)))
    value_pad = jnp.pad(values.astype(jnp.float32), ((margin, margin), (0, 0)))
    seg_pad = jnp.pad(segment_ids, (margin, margin), constant_values=-1)
    mask_pad = jnp.pad(block_mask, ((0, 0), (SPAN, SPAN)))

    def one_block(index):
        start = index * rows
        query_block = lax.dynamic_slice_in_dim(queries, start, rows, 0).astype(jnp.float32).reshape(rows, HEADS, hdim)
        key_block = lax.dynamic_slice_in_dim(key_pad, start, width * rows, 0).reshape(width * rows, HEADS, hdim)
        value_block = lax.dynamic_slice_in_dim(value_pad, start, width * rows, 0).reshape(width * rows, HEADS, hdim)
        query_seg = lax.dynamic_slice_in_dim(segment_ids, start, rows, 0)
        key_seg = lax.dynamic_slice_in_dim(seg_pad, start, width * rows, 0)
        mask_row = lax.dynamic_index_in_dim(mask_pad, index, 0, keepdims=False)
        flags = jnp.repeat(lax.dynamic_slice_in_dim(mask_row, index, width, 0), rows)
        allowed = (query_seg[:, None] == key_seg[None, :]) & (flags[None, :] > 0)
        scores = jnp.einsum('rhd,khd->hrk', query_block, key_block) / jnp.sqrt(jnp.float32(hdim))
        scores = jnp.where(allowed[None], scores, NEG)
        peak = lax.optimization_barrier(jnp.max(scores, axis=2, keepdims=True))
        weights = jnp.where(allowed[None], jnp.exp(scores - peak), 0.0)
        total = lax.optimization_barrier(jnp.sum(weights, axis=2, keepdims=True))
        weights_low = lax.optimization_barrier(weights.astype(jnp.bfloat16)).astype(jnp.float32)
        mixed = jnp.einsum('hrk,khd->hrd', weights_low, value_block) / total
        return jnp.transpose(mixed, (1, 0, 2)).reshape(rows, HEADS * hdim).astype(jnp.bfloat16)
    attended = lax.map(one_block, jnp.arange(NBLK).astype(jnp.int32)).reshape(TOKENS, HEADS * hdim)
    hidden = (tokens.astype(jnp.float32) + jnp.dot(attended, out_weight, preferred_element_type=jnp.float32)).astype(jnp.bfloat16)
    merged = hidden.reshape(NBLK * MROWS, MERGED)
    target = (owners * CAP + offsets).astype(jnp.int32)
    return jnp.zeros((NBLK * CAP, MERGED), jnp.bfloat16).at[target].set(merged)
```

```python
import functools

import jax
import jax.numpy as jnp
from jax import lax
from jax.experimental import pallas as pl
from jax.experimental.pallas import tpu as pltpu
from jax.sharding import PartitionSpec as P

HEADS = 8
SPAN = 3
NEG = -1e30
LOG2E = 1.4426950408889634
VMEM_LIMIT = 40 * 1024 * 1024


def params():
    return pltpu.CompilerParams(vmem_limit_bytes=VMEM_LIMIT)


def vmem():
    return pl.BlockSpec(memory_space=pltpu.VMEM)


def smem():
    return pl.BlockSpec(memory_space=pltpu.SMEM)


def split_heads_kernel(q_ref, k_ref, v_ref, out_ref):
    hdim = q_ref.shape[1] // HEADS
    for part, ref in enumerate((q_ref, k_ref, v_ref)):
        turned = ref[...].T
        for head in range(HEADS):
            out_ref[head, part * hdim : (part + 1) * hdim, :] = turned[
                head * hdim : (head + 1) * hdim, :
            ]


def split_heads(queries, keys, values):
    rows, features = queries.shape
    hdim = features // HEADS
    return pl.pallas_call(
        split_heads_kernel,
        out_shape=jax.ShapeDtypeStruct((HEADS, 3 * hdim, rows), queries.dtype),
        in_specs=[vmem()] * 3,
        out_specs=vmem(),
        compiler_params=params(),
    )(queries, keys, values)


def attention_kernel(halo, low_ref, count_ref, x_ref, *refs):
    if halo:
        below_ref, above_ref, seg_ref, out_ref, key_s, value_s, seg_s = refs
    else:
        seg_ref, out_ref, key_s, seg_s = refs
    blocks, triple, rows = x_ref.shape
    hdim = triple // 3
    base = SPAN if halo else 0
    factor = LOG2E / (hdim**0.5)
    extended = blocks + 2 * base

    for b in range(extended):
        if b < base:
            key_s[b] = below_ref[b, :hdim, :].T
            value_s[b] = below_ref[b, hdim:, :]
        elif b >= base + blocks:
            key_s[b] = above_ref[b - base - blocks, :hdim, :].T
            value_s[b] = above_ref[b - base - blocks, hdim:, :]
        else:
            key_s[b] = x_ref[b - base, hdim : 2 * hdim, :].T
            if halo:
                value_s[b] = x_ref[b - base, 2 * hdim :, :]
        seg_s[b] = jnp.broadcast_to(seg_ref[b], (128, rows)).T

    def value_block(b):
        return value_s[b] if halo else x_ref[b, 2 * hdim :, :]

    def one_block(i, carry):
        low = low_ref[i]
        count = count_ref[i]
        query = x_ref[i, :hdim, :]
        query_seg = seg_ref[i + base]

        for size in range(1, 2 * SPAN + 2):

            @pl.when(count == size)
            def _():
                key = key_s[pl.ds(low, size)].reshape(size * rows, hdim)
                scores = jnp.dot(key, query, preferred_element_type=jnp.float32)
                key_seg = seg_s[pl.ds(low, size)].reshape(size * rows, 128)
                key_seg = jnp.concatenate([key_seg] * (rows // 128), axis=1)
                scores = jnp.where(key_seg == query_seg, scores, NEG)
                peak = jnp.max(scores, axis=0, keepdims=True)
                weights = jnp.exp2((scores - peak) * factor)
                total = jnp.sum(weights, axis=0, keepdims=True)
                weights = weights.astype(jnp.bfloat16)
                mixed = jnp.zeros((hdim, rows), jnp.float32)
                for b in range(size):
                    mixed += jnp.dot(
                        value_block(low + b),
                        weights[b * rows : (b + 1) * rows],
                        preferred_element_type=jnp.float32,
                    )
                out_ref[i] = (mixed / total).astype(out_ref.dtype)

        return carry

    lax.fori_loop(0, blocks, one_block, 0)


def attention(low, count, x, halos, segs):
    blocks, triple, rows = x.shape
    hdim = triple // 3
    extended = segs.shape[0]
    scratch = [pltpu.VMEM((extended, rows, hdim), jnp.bfloat16)]
    if halos:
        scratch.append(pltpu.VMEM((extended, hdim, rows), jnp.bfloat16))
    scratch.append(pltpu.VMEM((extended, rows, 128), jnp.float32))
    return pl.pallas_call(
        functools.partial(attention_kernel, bool(halos)),
        out_shape=jax.ShapeDtypeStruct((blocks, hdim, rows), jnp.bfloat16),
        in_specs=[smem(), smem()] + [vmem()] * (2 + len(halos)),
        out_specs=vmem(),
        scratch_shapes=scratch,
        compiler_params=params(),
    )(low, count, x, *halos, segs)


def project_kernel(slot_ref, attended_ref, weight_ref, tokens_ref, out_ref):
    slots = out_ref.shape[0]
    rows, width = tokens_ref.shape
    hidden = tokens_ref[...].astype(jnp.float32) + lax.dot_general(
        attended_ref[...],
        weight_ref[...],
        (((0,), (0,)), ((), ())),
        preferred_element_type=jnp.float32,
    )
    hidden = hidden.astype(jnp.bfloat16)
    slot = lax.broadcasted_iota(jnp.int32, (slots, rows), 0)
    place = lax.broadcasted_iota(jnp.int32, (slots, rows), 1) % 4
    mine = slot_ref[...] == slot
    for j in range(4):
        pick = jnp.where(mine & (place == j), 1.0, 0.0).astype(jnp.bfloat16)
        out_ref[:, j * width : (j + 1) * width] = jnp.dot(
            pick, hidden, preferred_element_type=jnp.float32
        ).astype(jnp.bfloat16)


def project(slot_of_patch, attended, out_weight, tokens, slots):
    rows, width = tokens.shape
    return pl.pallas_call(
        project_kernel,
        out_shape=jax.ShapeDtypeStruct((slots, 4 * width), jnp.bfloat16),
        in_specs=[vmem()] * 4,
        out_specs=vmem(),
        compiler_params=params(),
    )(slot_of_patch, attended, out_weight, tokens)


def place_kernel(offsets_ref, arrived_ref, out_ref):
    capacity = out_ref.shape[0]
    slots = arrived_ref.shape[0]
    row = lax.broadcasted_iota(jnp.int32, (capacity, slots), 0)
    pick = jnp.where(offsets_ref[...] == row, 1.0, 0.0).astype(jnp.bfloat16)
    out_ref[...] = jnp.dot(
        pick, arrived_ref[...], preferred_element_type=jnp.float32
    ).astype(jnp.bfloat16)


def place(offsets, arrived, capacity):
    slots, merged = arrived.shape
    step = merged // 4
    return pl.pallas_call(
        place_kernel,
        grid=(4,),
        out_shape=jax.ShapeDtypeStruct((capacity, merged), jnp.bfloat16),
        in_specs=[
            pl.BlockSpec((1, slots), lambda i: (0, 0)),
            pl.BlockSpec((slots, step), lambda i: (0, i)),
        ],
        out_specs=pl.BlockSpec((capacity, step), lambda i: (0, i)),
        compiler_params=params(),
    )(offsets, arrived)


def per_device(segment_ids, block_mask, queries, keys, values, tokens, out_weight, owners, offsets):
    rows, features = queries.shape
    hdim = features // HEADS
    nblocks = lax.axis_size("blk")
    block_index = lax.axis_index("blk")
    ngroups = nblocks // HEADS
    groups = None
    if ngroups > 1:
        groups = [[g * HEADS + h for h in range(HEADS)] for g in range(ngroups)]
    exchange = functools.partial(
        lax.all_to_all, axis_name="blk", split_axis=0, concat_axis=0, tiled=True
    )

    x = exchange(split_heads(queries, keys, values), axis_index_groups=groups)

    first = block_index // HEADS * HEADS
    segs = segment_ids.reshape(nblocks, 1, rows)
    base = 0
    halos = ()
    if ngroups > 1:
        base = SPAN
        up = [(i, i + HEADS) for i in range(nblocks - HEADS)]
        down = [(i + HEADS, i) for i in range(nblocks - HEADS)]
        halos = (
            lax.ppermute(x[HEADS - SPAN :, hdim:], "blk", up),
            lax.ppermute(x[:SPAN, hdim:], "blk", down),
        )
        segs = jnp.pad(segs, ((SPAN, SPAN), (0, 0), (0, 0)), constant_values=-1)
        segs = lax.dynamic_slice_in_dim(segs, first, HEADS + 2 * SPAN, 0)
    segs = segs.astype(jnp.float32)

    mask = lax.dynamic_slice_in_dim(block_mask, first, HEADS, 0)
    block = first + jnp.arange(HEADS)[:, None]
    other = jnp.arange(nblocks)[None, :]
    present = (mask > 0) & (jnp.abs(block - other) <= SPAN)
    low = jnp.min(jnp.where(present, other, nblocks), axis=1) - first + base
    count = jnp.sum(present.astype(jnp.int32), axis=1)

    attended = exchange(attention(low, count, x, halos, segs), axis_index_groups=groups)

    mrows = rows // 4
    capacity = 2 * mrows
    pair_rows = max(2, 2 * mrows // nblocks)
    slots = nblocks * pair_rows
    onehot = (owners[:, None] == jnp.arange(nblocks)[None, :]).astype(jnp.int32)
    ranks = jnp.sum((jnp.cumsum(onehot, axis=0) - 1) * onehot, axis=1)
    slot_index = owners * pair_rows + ranks
    match = slot_index[:, None] == jnp.arange(slots)[None, :]
    outgoing_offsets = capacity + jnp.sum(
        jnp.where(match, offsets[:, None] - capacity, 0), axis=0
    )
    arrived_offsets = exchange(outgoing_offsets)
    slot_of_patch = jnp.repeat(slot_index, 4)[None, :]

    outgoing = project(
        slot_of_patch, attended.reshape(features, rows), out_weight, tokens, slots
    )
    arrived = exchange(outgoing)
    return place(arrived_offsets[None, :], arrived, capacity)


def solution(mesh):
    placed = (
        P("rep"),
        P("rep", None),
        P(("rep", "blk"), None),
        P(("rep", "blk"), None),
        P(("rep", "blk"), None),
        P(("rep", "blk"), None),
        P(),
        P(("rep", "blk")),
        P(("rep", "blk")),
    )
    return jax.shard_map(
        per_device, mesh=mesh, in_specs=placed, out_specs=P(("rep", "blk"), None), check_vma=False
    )
```

```python
import functools

import jax
import jax.numpy as jnp
from jax import lax
from jax.experimental import pallas as pl
from jax.experimental.pallas import tpu as pltpu
from jax.sharding import PartitionSpec as P

HEADS = 8
SPAN = 3
NEG = -1e30
LOG2E = 1.4426950408889634
VMEM_LIMIT = 40 * 1024 * 1024


def params():
    return pltpu.CompilerParams(vmem_limit_bytes=VMEM_LIMIT)


def vmem():
    return pl.BlockSpec(memory_space=pltpu.VMEM)


def smem():
    return pl.BlockSpec(memory_space=pltpu.SMEM)


def split_heads_kernel(q_hbm, k_hbm, v_hbm, out_ref, held, sems):
    hdim = q_hbm.shape[1] // HEADS
    copies = [
        pltpu.make_async_copy(ref, held.at[part], sems.at[part])
        for part, ref in enumerate((q_hbm, k_hbm, v_hbm))
    ]
    for copy in copies:
        copy.start()
    for part, copy in enumerate(copies):
        copy.wait()
        turned = held[part].T
        for head in range(HEADS):
            out_ref[head, part * hdim : (part + 1) * hdim, :] = turned[
                head * hdim : (head + 1) * hdim, :
            ]


def split_heads(queries, keys, values):
    rows, features = queries.shape
    hdim = features // HEADS
    return pl.pallas_call(
        split_heads_kernel,
        out_shape=jax.ShapeDtypeStruct((HEADS, 3 * hdim, rows), queries.dtype),
        in_specs=[pl.BlockSpec(memory_space=pl.ANY)] * 3,
        out_specs=vmem(),
        scratch_shapes=[
            pltpu.VMEM((3, rows, features), queries.dtype),
            pltpu.SemaphoreType.DMA((3,)),
        ],
        compiler_params=pltpu.CompilerParams(vmem_limit_bytes=60 * 1024 * 1024),
    )(queries, keys, values)


def attention_kernel(halo, pair_rows, low_ref, count_ref, x_ref, slot_ref, *refs):
    if halo:
        below_ref, above_ref, seg_ref, out_ref, key_s, value_s, seg_s, picked_s = refs
    else:
        seg_ref, out_ref, key_s, seg_s, picked_s = refs
    blocks, triple, rows = x_ref.shape
    hdim = triple // 3
    slots = out_ref.shape[2]
    base = SPAN if halo else 0
    factor = LOG2E / (hdim**0.5)
    extended = blocks + 2 * base

    for b in range(extended):
        if b < base:
            key_s[b] = below_ref[b, :hdim, :].T
            value_s[b] = below_ref[b, hdim:, :]
        elif b >= base + blocks:
            key_s[b] = above_ref[b - base - blocks, :hdim, :].T
            value_s[b] = above_ref[b - base - blocks, hdim:, :]
        else:
            key_s[b] = x_ref[b - base, hdim : 2 * hdim, :].T
            if halo:
                value_s[b] = x_ref[b - base, 2 * hdim :, :]
        seg_s[b] = jnp.broadcast_to(seg_ref[b], (128, rows)).T

    def value_block(b):
        return value_s[b] if halo else x_ref[b, 2 * hdim :, :]

    slot = lax.broadcasted_iota(jnp.int32, (slots, rows), 0)
    quarter = lax.broadcasted_iota(jnp.int32, (slots, rows), 1) % 4

    def one_block(i, carry):
        low = low_ref[i]
        count = count_ref[i]
        query = x_ref[i, :hdim, :]
        query_seg = seg_ref[i + base]
        mine = slot_ref[i] == slot

        for size in range(1, 2 * SPAN + 2):

            @pl.when(count == size)
            def _():
                key = key_s[pl.ds(low, size)].reshape(size * rows, hdim)
                scores = jnp.dot(key, query, preferred_element_type=jnp.float32)
                key_seg = seg_s[pl.ds(low, size)].reshape(size * rows, 128)
                key_seg = jnp.concatenate([key_seg] * (rows // 128), axis=1)
                scores = jnp.where(key_seg == query_seg, scores, NEG)
                peak = jnp.max(scores, axis=0, keepdims=True)
                weights = jnp.exp2((scores - peak) * factor)
                total = jnp.sum(weights, axis=0, keepdims=True)
                weights = weights.astype(jnp.bfloat16)
                mixed = jnp.zeros((hdim, rows), jnp.float32)
                for b in range(size):
                    mixed += jnp.dot(
                        value_block(low + b),
                        weights[b * rows : (b + 1) * rows],
                        preferred_element_type=jnp.float32,
                    )
                attended = (mixed / total).astype(jnp.bfloat16)
                for j in range(4):
                    pick = jnp.where(mine & (quarter == j), 1.0, 0.0).astype(jnp.bfloat16)
                    picked_s[i, j * hdim : (j + 1) * hdim, :] = lax.dot_general(
                        attended,
                        pick,
                        (((1,), (1,)), ((), ())),
                        preferred_element_type=jnp.float32,
                    )

        return carry

    lax.fori_loop(0, blocks, one_block, 0)

    group = lax.broadcasted_iota(jnp.int32, (4 * hdim, slots), 1) // pair_rows % blocks
    for first in range(blocks):
        chosen = picked_s[0]
        for b in range(1, blocks):
            chosen = jnp.where(group == (first + b) % blocks, picked_s[b], chosen)
        out_ref[first] = chosen.astype(out_ref.dtype)


def attention(low, count, x, slot, halos, segs, slots, pair_rows):
    blocks, triple, rows = x.shape
    hdim = triple // 3
    extended = segs.shape[0]
    scratch = [pltpu.VMEM((extended, rows, hdim), jnp.bfloat16)]
    if halos:
        scratch.append(pltpu.VMEM((extended, hdim, rows), jnp.bfloat16))
    scratch.append(pltpu.VMEM((extended, rows, 128), jnp.float32))
    scratch.append(pltpu.VMEM((blocks, 4 * hdim, slots), jnp.float32))
    return pl.pallas_call(
        functools.partial(attention_kernel, bool(halos), pair_rows),
        out_shape=jax.ShapeDtypeStruct((blocks, 4 * hdim, slots), jnp.bfloat16),
        in_specs=[smem(), smem()] + [vmem()] * (3 + len(halos)),
        out_specs=vmem(),
        scratch_shapes=scratch,
        compiler_params=params(),
    )(low, count, x, slot, *halos, segs)


def arrange_kernel(slot_ref, tokens_ref, out_ref):
    slots = out_ref.shape[0]
    rows, width = tokens_ref.shape
    tokens = tokens_ref[...]
    slot = lax.broadcasted_iota(jnp.int32, (slots, rows), 0)
    quarter = lax.broadcasted_iota(jnp.int32, (slots, rows), 1) % 4
    mine = slot_ref[...] == slot
    for j in range(4):
        pick = jnp.where(mine & (quarter == j), 1.0, 0.0).astype(jnp.bfloat16)
        out_ref[:, j * width : (j + 1) * width] = jnp.dot(
            pick, tokens, preferred_element_type=jnp.float32
        ).astype(jnp.bfloat16)


def arrange(slot_of_patch, tokens, slots):
    rows, width = tokens.shape
    return pl.pallas_call(
        arrange_kernel,
        out_shape=jax.ShapeDtypeStruct((slots, 4 * width), jnp.bfloat16),
        in_specs=[vmem()] * 2,
        out_specs=vmem(),
        compiler_params=params(),
    )(slot_of_patch, tokens)


def finish_kernel(token_offsets_ref, offsets_ref, weight_ref, tokens_ref, attended_ref, out_hbm, held, sems):
    capacity, merged = out_hbm.shape
    groups, lanes = offsets_ref.shape
    width = merged // 4
    hdim = attended_ref.shape[1] // 4

    def pick(offsets):
        row = lax.broadcasted_iota(jnp.int32, (capacity, offsets.shape[1]), 0)
        return jnp.where(offsets == row, 1.0, 0.0).astype(jnp.bfloat16)

    token_pick = pick(token_offsets_ref[...])
    picks = [pick(offsets_ref[g : g + 1, :]) for g in range(groups)]
    copies = []
    for j in range(4):
        attended = jnp.zeros((capacity, HEADS * hdim), jnp.float32)
        for g in range(groups):
            turned = jnp.concatenate(
                [
                    attended_ref[g * HEADS + h, j * hdim : (j + 1) * hdim, :]
                    for h in range(HEADS)
                ],
                axis=0,
            )
            attended += lax.dot_general(
                picks[g], turned, (((1,), (1,)), ((), ())), preferred_element_type=jnp.float32
            )
        columns = slice(j * width, (j + 1) * width)
        hidden = jnp.dot(
            token_pick, tokens_ref[:, columns], preferred_element_type=jnp.float32
        ) + jnp.dot(
            attended.astype(jnp.bfloat16), weight_ref[...], preferred_element_type=jnp.float32
        )
        held[j] = hidden.astype(jnp.bfloat16)
        copy = pltpu.make_async_copy(held.at[j], out_hbm.at[:, columns], sems.at[j])
        copy.start()
        copies.append(copy)
    for copy in copies:
        copy.wait()


def finish(token_offsets, offsets, out_weight, tokens, attended, capacity):
    merged = tokens.shape[1]
    return pl.pallas_call(
        finish_kernel,
        out_shape=jax.ShapeDtypeStruct((capacity, merged), jnp.bfloat16),
        in_specs=[vmem()] * 5,
        out_specs=pl.BlockSpec(memory_space=pl.ANY),
        scratch_shapes=[
            pltpu.VMEM((4, capacity, merged // 4), jnp.bfloat16),
            pltpu.SemaphoreType.DMA((4,)),
        ],
        compiler_params=params(),
    )(token_offsets, offsets, out_weight, tokens, attended)


def per_device(segment_ids, block_mask, queries, keys, values, tokens, out_weight, owners, offsets):
    rows, features = queries.shape
    hdim = features // HEADS
    nblocks = lax.axis_size("blk")
    block_index = lax.axis_index("blk")
    ngroups = nblocks // HEADS
    groups = None
    if ngroups > 1:
        groups = [[g * HEADS + h for h in range(HEADS)] for g in range(ngroups)]
    exchange = functools.partial(
        lax.all_to_all, axis_name="blk", split_axis=0, concat_axis=0, tiled=True
    )

    x = exchange(split_heads(queries, keys, values), axis_index_groups=groups)

    mrows = rows // 4
    capacity = 2 * mrows
    pair_rows = max(2, 2 * mrows // nblocks)
    slots = nblocks * pair_rows
    onehot = (owners[:, None] == jnp.arange(nblocks)[None, :]).astype(jnp.int32)
    ranks = jnp.sum((jnp.cumsum(onehot, axis=0) - 1) * onehot, axis=1)
    slot_index = owners * pair_rows + ranks
    match = slot_index[:, None] == jnp.arange(slots)[None, :]
    outgoing_offsets = capacity + jnp.sum(
        jnp.where(match, offsets[:, None] - capacity, 0), axis=0
    )
    outgoing_offsets = outgoing_offsets.reshape(nblocks, pair_rows)
    outgoing_slots = jnp.broadcast_to(slot_index[None, :], (HEADS, mrows))
    if ngroups == 1:
        both = exchange(jnp.concatenate([outgoing_slots, outgoing_offsets], axis=1))
        slots_of, arrived_offsets = both[:, :mrows], both[:, mrows:]
    else:
        slots_of = exchange(outgoing_slots, axis_index_groups=groups)
        arrived_offsets = exchange(outgoing_offsets)

    outgoing = arrange(jnp.repeat(slot_index, 4)[None, :], tokens, slots)
    arrived_tokens = exchange(outgoing)

    first = block_index // HEADS * HEADS
    segs = segment_ids.reshape(nblocks, 1, rows)
    base = 0
    halos = ()
    if ngroups > 1:
        base = SPAN
        up = [(i, i + HEADS) for i in range(nblocks - HEADS)]
        down = [(i + HEADS, i) for i in range(nblocks - HEADS)]
        halos = (
            lax.ppermute(x[HEADS - SPAN :, hdim:], "blk", up),
            lax.ppermute(x[:SPAN, hdim:], "blk", down),
        )
        segs = jnp.pad(segs, ((SPAN, SPAN), (0, 0), (0, 0)), constant_values=-1)
        segs = lax.dynamic_slice_in_dim(segs, first, HEADS + 2 * SPAN, 0)
    segs = segs.astype(jnp.float32)

    mask = lax.dynamic_slice_in_dim(block_mask, first, HEADS, 0)
    block = first + jnp.arange(HEADS)[:, None]
    other = jnp.arange(nblocks)[None, :]
    present = (mask > 0) & (jnp.abs(block - other) <= SPAN)
    low = jnp.min(jnp.where(present, other, nblocks), axis=1) - first + base
    count = jnp.sum(present.astype(jnp.int32), axis=1)

    turn = jnp.arange(HEADS)[:, None] * pair_rows
    slots_of = jnp.repeat((slots_of + turn) % slots, 4, axis=1)[:, None, :]
    sent = attention(low, count, x, slots_of, halos, segs, slots, pair_rows)
    if ngroups > 1:
        sent = jnp.stack([jnp.roll(sent[o], -o * pair_rows, axis=1) for o in range(HEADS)])
        sent = sent.reshape(HEADS, 4 * hdim, ngroups, HEADS * pair_rows)
        sent = jnp.transpose(sent, (2, 0, 1, 3)).reshape(nblocks, 4 * hdim, HEADS * pair_rows)
        lane_offsets = arrived_offsets
    else:
        lane_offsets = jnp.roll(arrived_offsets, block_index, axis=0)
    arrived = exchange(sent)
    return finish(
        arrived_offsets.reshape(1, slots),
        lane_offsets.reshape(ngroups, HEADS * pair_rows),
        out_weight,
        arrived_tokens,
        arrived,
        capacity,
    )


def solution(mesh):
    placed = (
        P("rep"),
        P("rep", None),
        P(("rep", "blk"), None),
        P(("rep", "blk"), None),
        P(("rep", "blk"), None),
        P(("rep", "blk"), None),
        P(),
        P(("rep", "blk")),
        P(("rep", "blk")),
    )
    return jax.shard_map(
        per_device, mesh=mesh, in_specs=placed, out_specs=P(("rep", "blk"), None), check_vma=False
    )
```

```python
import functools

import jax
import jax.numpy as jnp
from jax import lax
from jax.experimental import pallas as pl
from jax.experimental.pallas import tpu as pltpu
from jax.sharding import PartitionSpec as P

HEADS = 8
SPAN = 3
NEG = -1e30
LOG2E = 1.4426950408889634
VMEM_LIMIT = 40 * 1024 * 1024


def params():
    return pltpu.CompilerParams(vmem_limit_bytes=VMEM_LIMIT)


def vmem():
    return pl.BlockSpec(memory_space=pltpu.VMEM)


def smem():
    return pl.BlockSpec(memory_space=pltpu.SMEM)


def split_heads_kernel(q_hbm, k_hbm, v_hbm, out_ref, held, sems):
    hdim = q_hbm.shape[1] // HEADS
    copies = [
        pltpu.make_async_copy(ref, held.at[part], sems.at[part])
        for part, ref in enumerate((q_hbm, k_hbm, v_hbm))
    ]
    for copy in copies:
        copy.start()
    for part, copy in enumerate(copies):
        copy.wait()
        turned = held[part].T
        for head in range(HEADS):
            out_ref[head, part * hdim : (part + 1) * hdim, :] = turned[
                head * hdim : (head + 1) * hdim, :
            ]


def split_heads(queries, keys, values):
    rows, features = queries.shape
    hdim = features // HEADS
    return pl.pallas_call(
        split_heads_kernel,
        out_shape=jax.ShapeDtypeStruct((HEADS, 3 * hdim, rows), queries.dtype),
        in_specs=[pl.BlockSpec(memory_space=pl.ANY)] * 3,
        out_specs=vmem(),
        scratch_shapes=[
            pltpu.VMEM((3, rows, features), queries.dtype),
            pltpu.SemaphoreType.DMA((3,)),
        ],
        compiler_params=pltpu.CompilerParams(vmem_limit_bytes=60 * 1024 * 1024),
    )(queries, keys, values)


def attention_kernel(halo, pair_rows, low_ref, count_ref, x_ref, slot_ref, *refs):
    if halo:
        below_ref, above_ref, seg_ref, out_ref, key_s, value_s, seg_s, picked_s = refs
    else:
        seg_ref, out_ref, key_s, seg_s, picked_s = refs
    blocks, triple, rows = x_ref.shape
    hdim = triple // 3
    slots = out_ref.shape[2]
    base = SPAN if halo else 0
    factor = LOG2E / (hdim**0.5)
    extended = blocks + 2 * base

    for b in range(extended):
        if b < base:
            key_s[b] = below_ref[b, :hdim, :].T
            value_s[b] = below_ref[b, hdim:, :]
        elif b >= base + blocks:
            key_s[b] = above_ref[b - base - blocks, :hdim, :].T
            value_s[b] = above_ref[b - base - blocks, hdim:, :]
        else:
            key_s[b] = x_ref[b - base, hdim : 2 * hdim, :].T
            if halo:
                value_s[b] = x_ref[b - base, 2 * hdim :, :]
        seg_s[b] = jnp.broadcast_to(seg_ref[b], (128, rows)).T

    def value_block(b):
        return value_s[b] if halo else x_ref[b, 2 * hdim :, :]

    slot = lax.broadcasted_iota(jnp.int32, (slots, rows), 0)
    quarter = lax.broadcasted_iota(jnp.int32, (slots, rows), 1) % 4

    def one_block(i, carry):
        low = low_ref[i]
        count = count_ref[i]
        query = x_ref[i, :hdim, :]
        query_seg = seg_ref[i + base]
        mine = slot_ref[i] == slot

        for size in range(1, 2 * SPAN + 2):

            @pl.when(count == size)
            def _():
                key = key_s[pl.ds(low, size)].reshape(size * rows, hdim)
                scores = jnp.dot(key, query, preferred_element_type=jnp.float32)
                key_seg = seg_s[pl.ds(low, size)].reshape(size * rows, 128)
                key_seg = jnp.concatenate([key_seg] * (rows // 128), axis=1)
                scores = jnp.where(key_seg == query_seg, scores, NEG)
                peak = jnp.max(scores, axis=0, keepdims=True)
                weights = jnp.exp2((scores - peak) * factor)
                total = jnp.sum(weights, axis=0, keepdims=True)
                weights = weights.astype(jnp.bfloat16)
                mixed = jnp.zeros((hdim, rows), jnp.float32)
                for b in range(size):
                    mixed += jnp.dot(
                        value_block(low + b),
                        weights[b * rows : (b + 1) * rows],
                        preferred_element_type=jnp.float32,
                    )
                attended = (mixed / total).astype(jnp.bfloat16)
                for j in range(4):
                    pick = jnp.where(mine & (quarter == j), 1.0, 0.0).astype(jnp.bfloat16)
                    picked_s[i, j * hdim : (j + 1) * hdim, :] = lax.dot_general(
                        attended,
                        pick,
                        (((1,), (1,)), ((), ())),
                        preferred_element_type=jnp.float32,
                    )

        return carry

    lax.fori_loop(0, blocks, one_block, 0)

    group = lax.broadcasted_iota(jnp.int32, (4 * hdim, slots), 1) // pair_rows % blocks
    for first in range(blocks):
        chosen = picked_s[0]
        for b in range(1, blocks):
            chosen = jnp.where(group == (first + b) % blocks, picked_s[b], chosen)
        out_ref[first] = chosen.astype(out_ref.dtype)


def attention(low, count, x, slot, halos, segs, slots, pair_rows):
    blocks, triple, rows = x.shape
    hdim = triple // 3
    extended = segs.shape[0]
    scratch = [pltpu.VMEM((extended, rows, hdim), jnp.bfloat16)]
    if halos:
        scratch.append(pltpu.VMEM((extended, hdim, rows), jnp.bfloat16))
    scratch.append(pltpu.VMEM((extended, rows, 128), jnp.float32))
    scratch.append(pltpu.VMEM((blocks, 4 * hdim, slots), jnp.float32))
    return pl.pallas_call(
        functools.partial(attention_kernel, bool(halos), pair_rows),
        out_shape=jax.ShapeDtypeStruct((blocks, 4 * hdim, slots), jnp.bfloat16),
        in_specs=[smem(), smem()] + [vmem()] * (3 + len(halos)),
        out_specs=vmem(),
        scratch_shapes=scratch,
        compiler_params=params(),
    )(low, count, x, slot, *halos, segs)


def arrange_kernel(slot_ref, tokens_ref, *out_refs):
    slots = out_refs[0].shape[0]
    rows, width = tokens_ref.shape
    tokens = tokens_ref[...]
    total = len(out_refs) * slots
    slot = lax.broadcasted_iota(jnp.int32, (total, rows), 0)
    quarter = lax.broadcasted_iota(jnp.int32, (total, rows), 1) % 4
    mine = slot_ref[...] == slot
    for j in range(4):
        pick = jnp.where(mine & (quarter == j), 1.0, 0.0).astype(jnp.bfloat16)
        picked = jnp.dot(pick, tokens, preferred_element_type=jnp.float32).astype(jnp.bfloat16)
        for d, out_ref in enumerate(out_refs):
            out_ref[:, j * width : (j + 1) * width] = picked[d * slots : (d + 1) * slots]


def arrange(slot_of_patch, tokens, pieces, slots):
    rows, width = tokens.shape
    return pl.pallas_call(
        arrange_kernel,
        out_shape=[jax.ShapeDtypeStruct((slots // pieces, 4 * width), jnp.bfloat16)] * pieces,
        in_specs=[vmem()] * 2,
        out_specs=[vmem()] * pieces,
        compiler_params=params(),
    )(slot_of_patch, tokens)


def finish_kernel(token_offsets_ref, offsets_ref, weight_hbm, attended_ref, *refs):
    *token_refs, out_hbm, weight, held, weight_sems, sems = refs
    capacity, merged = out_hbm.shape
    groups, lanes = offsets_ref.shape
    width = merged // 4
    hdim = attended_ref.shape[1] // 4
    part = weight.shape[0] // 4
    loads = []
    for j in range(4):
        piece = pl.ds(j * part, part)
        loads.append(
            pltpu.make_async_copy(weight_hbm.at[piece], weight.at[piece], weight_sems.at[j])
        )
        loads[j].start()

    def pick(offsets):
        row = lax.broadcasted_iota(jnp.int32, (capacity, offsets.shape[1]), 0)
        return jnp.where(offsets == row, 1.0, 0.0).astype(jnp.bfloat16)

    token_pick = pick(token_offsets_ref[...])
    picks = [pick(offsets_ref[g : g + 1, :]) for g in range(groups)]
    placed = []
    for j in range(4):
        attended = jnp.zeros((capacity, HEADS * hdim), jnp.float32)
        for g in range(groups):
            turned = jnp.concatenate(
                [
                    attended_ref[g * HEADS + h, j * hdim : (j + 1) * hdim, :]
                    for h in range(HEADS)
                ],
                axis=0,
            )
            attended += lax.dot_general(
                picks[g], turned, (((1,), (1,)), ((), ())), preferred_element_type=jnp.float32
            )
        placed.append(attended.astype(jnp.bfloat16))
    for load in loads:
        load.wait()
    copies = []
    for j in range(4):
        columns = slice(j * width, (j + 1) * width)
        tokens = jnp.concatenate([ref[:, columns] for ref in token_refs], axis=0)
        hidden = jnp.dot(token_pick, tokens, preferred_element_type=jnp.float32) + jnp.dot(
            placed[j], weight[...], preferred_element_type=jnp.float32
        )
        held[j] = hidden.astype(jnp.bfloat16)
        copy = pltpu.make_async_copy(held.at[j], out_hbm.at[:, columns], sems.at[j])
        copy.start()
        copies.append(copy)
    for copy in copies:
        copy.wait()


def finish(token_offsets, offsets, out_weight, attended, tokens, capacity):
    merged = tokens[0].shape[1]
    return pl.pallas_call(
        finish_kernel,
        out_shape=jax.ShapeDtypeStruct((capacity, merged), jnp.bfloat16),
        in_specs=[vmem()] * 2
        + [pl.BlockSpec(memory_space=pl.ANY)]
        + [vmem()] * (1 + len(tokens)),
        out_specs=pl.BlockSpec(memory_space=pl.ANY),
        scratch_shapes=[
            pltpu.VMEM(out_weight.shape, out_weight.dtype),
            pltpu.VMEM((4, capacity, merged // 4), jnp.bfloat16),
            pltpu.SemaphoreType.DMA((4,)),
            pltpu.SemaphoreType.DMA((4,)),
        ],
        compiler_params=params(),
    )(token_offsets, offsets, out_weight, attended, *tokens)


def per_device(segment_ids, block_mask, queries, keys, values, tokens, out_weight, owners, offsets):
    rows, features = queries.shape
    hdim = features // HEADS
    nblocks = lax.axis_size("blk")
    block_index = lax.axis_index("blk")
    ngroups = nblocks // HEADS
    first = block_index // HEADS * HEADS
    groups = None
    if ngroups > 1:
        groups = [[g * HEADS + h for h in range(HEADS)] for g in range(ngroups)]
    exchange = functools.partial(
        lax.all_to_all, axis_name="blk", split_axis=0, concat_axis=0, tiled=True
    )

    split = split_heads(queries, keys, values)
    split, tokens = lax.optimization_barrier((split, tokens))
    x = exchange(split, axis_index_groups=groups)

    mrows = rows // 4
    capacity = 2 * mrows
    pair_rows = max(2, 2 * mrows // nblocks)
    slots = nblocks * pair_rows

    def ranks_of(owners):
        onehot = (owners[..., None] == jnp.arange(nblocks)).astype(jnp.int32)
        return jnp.sum((jnp.cumsum(onehot, axis=-2) - 1) * onehot, axis=-1)

    pieces = nblocks if ngroups == 1 else 1
    own_slots = owners * pair_rows + ranks_of(owners)
    if pieces > 1:
        own_slots = (own_slots - block_index * pair_rows) % slots
    outgoing = arrange(jnp.repeat(own_slots, 4)[None, :], tokens, pieces, slots)
    if pieces > 1:
        arrived_tokens = [outgoing[0]] + [
            lax.ppermute(outgoing[d], "blk", [(i, (i + d) % nblocks) for i in range(nblocks)])
            for d in range(1, nblocks)
        ]
    else:
        arrived_tokens = [exchange(outgoing[0])]

    meta = lax.all_gather(jnp.stack([owners, offsets]), "blk")
    all_owners, all_offsets = meta[:, 0], meta[:, 1]
    all_ranks = ranks_of(all_owners)
    here = (all_owners == block_index)[..., None] & (all_ranks[..., None] == jnp.arange(pair_rows))
    arrived_offsets = capacity + jnp.sum(
        jnp.where(here, all_offsets[..., None] - capacity, 0), axis=1
    )

    segs = segment_ids.reshape(nblocks, 1, rows)
    base = 0
    halos = ()
    if ngroups > 1:
        base = SPAN
        up = [(i, i + HEADS) for i in range(nblocks - HEADS)]
        down = [(i + HEADS, i) for i in range(nblocks - HEADS)]
        halos = (
            lax.ppermute(x[HEADS - SPAN :, hdim:], "blk", up),
            lax.ppermute(x[:SPAN, hdim:], "blk", down),
        )
        segs = jnp.pad(segs, ((SPAN, SPAN), (0, 0), (0, 0)), constant_values=-1)
        segs = lax.dynamic_slice_in_dim(segs, first, HEADS + 2 * SPAN, 0)
    segs = segs.astype(jnp.float32)

    mask = lax.dynamic_slice_in_dim(block_mask, first, HEADS, 0)
    block = first + jnp.arange(HEADS)[:, None]
    other = jnp.arange(nblocks)[None, :]
    present = (mask > 0) & (jnp.abs(block - other) <= SPAN)
    low = jnp.min(jnp.where(present, other, nblocks), axis=1) - first + base
    count = jnp.sum(present.astype(jnp.int32), axis=1)

    slots_of = lax.dynamic_slice_in_dim(all_owners * pair_rows + all_ranks, first, HEADS, 0)
    turn = jnp.arange(HEADS)[:, None] * pair_rows
    slots_of = jnp.repeat((slots_of + turn) % slots, 4, axis=1)[:, None, :]
    sent = attention(low, count, x, slots_of, halos, segs, slots, pair_rows)
    if ngroups > 1:
        sent = jnp.stack([jnp.roll(sent[o], -o * pair_rows, axis=1) for o in range(HEADS)])
        sent = sent.reshape(HEADS, 4 * hdim, ngroups, HEADS * pair_rows)
        sent = jnp.transpose(sent, (2, 0, 1, 3)).reshape(nblocks, 4 * hdim, HEADS * pair_rows)
        lane_offsets = token_offsets = arrived_offsets
    else:
        lane_offsets = jnp.roll(arrived_offsets, block_index, axis=0)
        token_offsets = jnp.roll(arrived_offsets[::-1], block_index + 1, axis=0)
    arrived = exchange(sent)
    return finish(
        token_offsets.reshape(1, slots),
        lane_offsets.reshape(ngroups, HEADS * pair_rows),
        out_weight,
        arrived,
        arrived_tokens,
        capacity,
    )


def solution(mesh):
    placed = (
        P("rep"),
        P("rep", None),
        P(("rep", "blk"), None),
        P(("rep", "blk"), None),
        P(("rep", "blk"), None),
        P(("rep", "blk"), None),
        P(),
        P(("rep", "blk")),
        P(("rep", "blk")),
    )
    return jax.shard_map(
        per_device, mesh=mesh, in_specs=placed, out_specs=P(("rep", "blk"), None), check_vma=False
    )
```

```python
import functools

import jax
import jax.numpy as jnp
from jax import lax
from jax.experimental import pallas as pl
from jax.experimental.pallas import tpu as pltpu
from jax.sharding import PartitionSpec as P

HEADS = 8
SPAN = 3
NEG = -1e30
LOG2E = 1.4426950408889634
VMEM_LIMIT = 40 * 1024 * 1024


def params():
    return pltpu.CompilerParams(vmem_limit_bytes=VMEM_LIMIT)


def vmem():
    return pl.BlockSpec(memory_space=pltpu.VMEM)


def smem():
    return pl.BlockSpec(memory_space=pltpu.SMEM)


def split_heads_kernel(pair_rows, owners_ref, offsets_ref, q_hbm, k_hbm, v_hbm, out_ref, slot_ref, held, sems):
    rows, features = q_hbm.shape
    hdim = features // HEADS
    mrows = rows // 4
    copies = [
        pltpu.make_async_copy(ref, held.at[part], sems.at[part])
        for part, ref in enumerate((q_hbm, k_hbm, v_hbm))
    ]
    for copy in copies:
        copy.start()

    owner = jnp.broadcast_to(owners_ref[...].astype(jnp.float32), (mrows, mrows))
    earlier = lax.broadcasted_iota(jnp.int32, (mrows, mrows), 0)
    later = lax.broadcasted_iota(jnp.int32, (mrows, mrows), 1)
    column = jnp.sum(jnp.where(earlier == later, owner, 0.0), axis=1, keepdims=True)
    ahead = jnp.where((owner == column) & (earlier < later), 1.0, 0.0)
    slot = owner[:1] * pair_rows + jnp.sum(ahead, axis=0, keepdims=True)
    line = lax.broadcasted_iota(jnp.int32, (16, mrows), 0)
    meta = jnp.where(line == 0, slot, jnp.where(line == 1, offsets_ref[...].astype(jnp.float32), 0.0))
    row = lax.broadcasted_iota(jnp.int32, (mrows, rows), 0)
    patch = lax.broadcasted_iota(jnp.int32, (mrows, rows), 1)
    spread = jnp.where(patch // 4 == row, 1.0, 0.0).astype(jnp.bfloat16)
    meta = jnp.dot(meta.astype(jnp.bfloat16), spread, preferred_element_type=jnp.float32)
    slot_ref[...] = meta[:1].astype(jnp.int32)
    for head in range(HEADS):
        out_ref[head, 3 * hdim :, :] = meta.astype(jnp.bfloat16)

    for part, copy in enumerate(copies):
        copy.wait()
        turned = held[part].T
        for head in range(HEADS):
            out_ref[head, part * hdim : (part + 1) * hdim, :] = turned[
                head * hdim : (head + 1) * hdim, :
            ]


def split_heads(owners, offsets, queries, keys, values, pair_rows):
    rows, features = queries.shape
    hdim = features // HEADS
    return pl.pallas_call(
        functools.partial(split_heads_kernel, pair_rows),
        out_shape=(
            jax.ShapeDtypeStruct((HEADS, 3 * hdim + 16, rows), queries.dtype),
            jax.ShapeDtypeStruct((1, rows), jnp.int32),
        ),
        in_specs=[vmem()] * 2 + [pl.BlockSpec(memory_space=pl.ANY)] * 3,
        out_specs=(vmem(), vmem()),
        scratch_shapes=[
            pltpu.VMEM((3, rows, features), queries.dtype),
            pltpu.SemaphoreType.DMA((3,)),
        ],
        compiler_params=pltpu.CompilerParams(vmem_limit_bytes=60 * 1024 * 1024),
    )(owners, offsets, queries, keys, values)


def attention_kernel(halo, pair_rows, low_ref, count_ref, x_ref, *refs):
    if halo:
        below_ref, above_ref, seg_ref, out_ref, key_s, value_s, seg_s, picked_s = refs
    else:
        seg_ref, out_ref, key_s, seg_s, picked_s = refs
    blocks, lines, rows = x_ref.shape
    triple = lines - 16
    hdim = triple // 3
    slots = out_ref.shape[2]
    base = SPAN if halo else 0
    factor = LOG2E / (hdim**0.5)
    extended = blocks + 2 * base

    for b in range(extended):
        if b < base:
            key_s[b] = below_ref[b, :hdim, :].T
            value_s[b] = below_ref[b, hdim:, :]
        elif b >= base + blocks:
            key_s[b] = above_ref[b - base - blocks, :hdim, :].T
            value_s[b] = above_ref[b - base - blocks, hdim:, :]
        else:
            key_s[b] = x_ref[b - base, hdim : 2 * hdim, :].T
            if halo:
                value_s[b] = x_ref[b - base, 2 * hdim : triple, :]
        seg_s[b] = jnp.broadcast_to(seg_ref[b], (128, rows)).T

    def value_block(b):
        return value_s[b] if halo else x_ref[b, 2 * hdim : triple, :]

    slot = lax.broadcasted_iota(jnp.int32, (slots, rows), 0)
    quarter = lax.broadcasted_iota(jnp.int32, (slots, rows), 1) % 4

    def one_block(i, carry):
        low = low_ref[i]
        count = count_ref[i]
        query = x_ref[i, :hdim, :]
        query_seg = seg_ref[i + base]
        place = x_ref[i, triple:, :].astype(jnp.float32)[:1].astype(jnp.int32) + i * pair_rows
        mine = jnp.where(place >= slots, place - slots, place) == slot

        for size in range(1, 2 * SPAN + 2):

            @pl.when(count == size)
            def _():
                key = key_s[pl.ds(low, size)].reshape(size * rows, hdim)
                scores = jnp.dot(key, query, preferred_element_type=jnp.float32)
                key_seg = seg_s[pl.ds(low, size)].reshape(size * rows, 128)
                key_seg = jnp.concatenate([key_seg] * (rows // 128), axis=1)
                scores = jnp.where(key_seg == query_seg, scores, NEG)
                peak = jnp.max(scores, axis=0, keepdims=True)
                weights = jnp.exp2((scores - peak) * factor)
                total = jnp.sum(weights, axis=0, keepdims=True)
                weights = weights.astype(jnp.bfloat16)
                mixed = jnp.zeros((hdim, rows), jnp.float32)
                for b in range(size):
                    mixed += jnp.dot(
                        value_block(low + b),
                        weights[b * rows : (b + 1) * rows],
                        preferred_element_type=jnp.float32,
                    )
                attended = (mixed / total).astype(jnp.bfloat16)
                for j in range(4):
                    pick = jnp.where(mine & (quarter == j), 1.0, 0.0).astype(jnp.bfloat16)
                    picked_s[i, j * hdim : (j + 1) * hdim, :] = lax.dot_general(
                        attended,
                        pick,
                        (((1,), (1,)), ((), ())),
                        preferred_element_type=jnp.float32,
                    )

        return carry

    lax.fori_loop(0, blocks, one_block, 0)

    group = lax.broadcasted_iota(jnp.int32, (4 * hdim, slots), 1) // pair_rows % blocks
    for first in range(blocks):
        chosen = picked_s[0]
        for b in range(1, blocks):
            chosen = jnp.where(group == (first + b) % blocks, picked_s[b], chosen)
        out_ref[first] = chosen.astype(out_ref.dtype)


def attention(low, count, x, halos, segs, slots, pair_rows):
    blocks, lines, rows = x.shape
    hdim = (lines - 16) // 3
    extended = segs.shape[0]
    scratch = [pltpu.VMEM((extended, rows, hdim), jnp.bfloat16)]
    if halos:
        scratch.append(pltpu.VMEM((extended, hdim, rows), jnp.bfloat16))
    scratch.append(pltpu.VMEM((extended, rows, 128), jnp.float32))
    scratch.append(pltpu.VMEM((blocks, 4 * hdim, slots), jnp.float32))
    return pl.pallas_call(
        functools.partial(attention_kernel, bool(halos), pair_rows),
        out_shape=jax.ShapeDtypeStruct((blocks, 4 * hdim, slots), jnp.bfloat16),
        in_specs=[smem(), smem()] + [vmem()] * (2 + len(halos)),
        out_specs=vmem(),
        scratch_shapes=scratch,
        compiler_params=params(),
        cost_estimate=pl.CostEstimate(
            flops=8_000_000_000, bytes_accessed=8_000_000, transcendentals=3_000_000
        ),
    )(low, count, x, *halos, segs)


def arrange_kernel(slot_ref, tokens_ref, *out_refs):
    slots = out_refs[0].shape[0]
    rows, width = tokens_ref.shape
    tokens = tokens_ref[...]
    total = len(out_refs) * slots
    slot = lax.broadcasted_iota(jnp.int32, (total, rows), 0)
    quarter = lax.broadcasted_iota(jnp.int32, (total, rows), 1) % 4
    mine = slot_ref[...] == slot
    for j in range(4):
        pick = jnp.where(mine & (quarter == j), 1.0, 0.0).astype(jnp.bfloat16)
        picked = jnp.dot(pick, tokens, preferred_element_type=jnp.float32).astype(jnp.bfloat16)
        for d, out_ref in enumerate(out_refs):
            out_ref[:, j * width : (j + 1) * width] = picked[d * slots : (d + 1) * slots]


def arrange(slot_of_patch, tokens, pieces, slots):
    rows, width = tokens.shape
    return pl.pallas_call(
        arrange_kernel,
        out_shape=[jax.ShapeDtypeStruct((slots // pieces, 4 * width), jnp.bfloat16)] * pieces,
        in_specs=[vmem()] * 2,
        out_specs=[vmem()] * pieces,
        compiler_params=params(),
    )(slot_of_patch, tokens)


def finish_kernel(token_offsets_ref, offsets_ref, weight_hbm, attended_ref, *refs):
    *token_refs, out_hbm, weight, held, weight_sems, sems = refs
    capacity, merged = out_hbm.shape
    groups, lanes = offsets_ref.shape
    width = merged // 4
    hdim = attended_ref.shape[1] // 4
    part = weight.shape[0] // 4
    loads = []
    for j in range(4):
        piece = pl.ds(j * part, part)
        loads.append(
            pltpu.make_async_copy(weight_hbm.at[piece], weight.at[piece], weight_sems.at[j])
        )
        loads[j].start()

    def pick(offsets):
        row = lax.broadcasted_iota(jnp.int32, (capacity, offsets.shape[1]), 0)
        return jnp.where(offsets == row, 1.0, 0.0).astype(jnp.bfloat16)

    token_pick = pick(token_offsets_ref[...])
    picks = [pick(offsets_ref[g : g + 1, :]) for g in range(groups)]
    placed = []
    for j in range(4):
        attended = jnp.zeros((capacity, HEADS * hdim), jnp.float32)
        for g in range(groups):
            turned = jnp.concatenate(
                [
                    attended_ref[g * HEADS + h, j * hdim : (j + 1) * hdim, :]
                    for h in range(HEADS)
                ],
                axis=0,
            )
            attended += lax.dot_general(
                picks[g], turned, (((1,), (1,)), ((), ())), preferred_element_type=jnp.float32
            )
        placed.append(attended.astype(jnp.bfloat16))
    for load in loads:
        load.wait()
    copies = []
    for j in range(4):
        columns = slice(j * width, (j + 1) * width)
        tokens = jnp.concatenate([ref[:, columns] for ref in token_refs], axis=0)
        hidden = jnp.dot(token_pick, tokens, preferred_element_type=jnp.float32) + jnp.dot(
            placed[j], weight[...], preferred_element_type=jnp.float32
        )
        held[j] = hidden.astype(jnp.bfloat16)
        copy = pltpu.make_async_copy(held.at[j], out_hbm.at[:, columns], sems.at[j])
        copy.start()
        copies.append(copy)
    for copy in copies:
        copy.wait()


def finish(token_offsets, offsets, out_weight, attended, tokens, capacity):
    merged = tokens[0].shape[1]
    return pl.pallas_call(
        finish_kernel,
        out_shape=jax.ShapeDtypeStruct((capacity, merged), jnp.bfloat16),
        in_specs=[vmem()] * 2
        + [pl.BlockSpec(memory_space=pl.ANY)]
        + [vmem()] * (1 + len(tokens)),
        out_specs=pl.BlockSpec(memory_space=pl.ANY),
        scratch_shapes=[
            pltpu.VMEM(out_weight.shape, out_weight.dtype),
            pltpu.VMEM((4, capacity, merged // 4), jnp.bfloat16),
            pltpu.SemaphoreType.DMA((4,)),
            pltpu.SemaphoreType.DMA((4,)),
        ],
        compiler_params=params(),
    )(token_offsets, offsets, out_weight, attended, *tokens)


def per_device(segment_ids, block_mask, queries, keys, values, tokens, out_weight, owners, offsets):
    rows, features = queries.shape
    hdim = features // HEADS
    nblocks = lax.axis_size("blk")
    block_index = lax.axis_index("blk")
    ngroups = nblocks // HEADS
    first = block_index // HEADS * HEADS
    groups = None
    if ngroups > 1:
        groups = [[g * HEADS + h for h in range(HEADS)] for g in range(ngroups)]
    exchange = functools.partial(
        lax.all_to_all, axis_name="blk", split_axis=0, concat_axis=0, tiled=True
    )

    mrows = rows // 4
    capacity = 2 * mrows
    pair_rows = max(2, 2 * mrows // nblocks)
    slots = nblocks * pair_rows
    assert slots <= 256

    split, own_slots = split_heads(
        owners[None, :], offsets[None, :], queries, keys, values, pair_rows
    )
    split, own_slots = lax.optimization_barrier((split, own_slots))
    x = exchange(split, axis_index_groups=groups)

    pieces = nblocks if ngroups == 1 else 1
    if pieces > 1:
        own_slots = (own_slots - block_index * pair_rows) % slots
    outgoing = arrange(own_slots, tokens, pieces, slots)
    if pieces > 1:
        arrived_tokens = {0: outgoing[0]}
        for d in (4, 3, 5, 2, 6, 1, 7):
            route = [(i, (i + d) % nblocks) for i in range(nblocks)]
            arrived_tokens[d] = lax.ppermute(outgoing[d], "blk", route)
        early = (4, 3, 5, 2)
        x, *done = lax.optimization_barrier((x, *[arrived_tokens[d] for d in early]))
        arrived_tokens.update(zip(early, done))
        arrived_tokens = [arrived_tokens[d] for d in range(nblocks)]
    else:
        arrived_tokens = [exchange(outgoing[0])]

    if pieces > 1:
        meta = x[:, 3 * hdim : 3 * hdim + 2, ::4].astype(jnp.int32)
        all_slots, all_offsets = meta[:, 0], meta[:, 1]
        wanted = block_index * pair_rows + jnp.arange(pair_rows)
        here = all_slots[..., None] == wanted
        arrived_offsets = capacity + jnp.sum(
            jnp.where(here, all_offsets[..., None] - capacity, 0), axis=1
        )
    else:
        match = own_slots[0, ::4, None] == jnp.arange(slots)
        outgoing_offsets = capacity + jnp.sum(
            jnp.where(match, offsets[:, None] - capacity, 0), axis=0
        )
        arrived_offsets = exchange(outgoing_offsets.reshape(nblocks, pair_rows))

    segs = segment_ids.reshape(nblocks, 1, rows)
    base = 0
    halos = ()
    if ngroups > 1:
        base = SPAN
        up = [(i, i + HEADS) for i in range(nblocks - HEADS)]
        down = [(i + HEADS, i) for i in range(nblocks - HEADS)]
        halos = (
            lax.ppermute(x[HEADS - SPAN :, hdim : 3 * hdim], "blk", up),
            lax.ppermute(x[:SPAN, hdim : 3 * hdim], "blk", down),
        )
        segs = jnp.pad(segs, ((SPAN, SPAN), (0, 0), (0, 0)), constant_values=-1)
        segs = lax.dynamic_slice_in_dim(segs, first, HEADS + 2 * SPAN, 0)
    segs = segs.astype(jnp.float32)

    mask = lax.dynamic_slice_in_dim(block_mask, first, HEADS, 0)
    block = first + jnp.arange(HEADS)[:, None]
    other = jnp.arange(nblocks)[None, :]
    present = (mask > 0) & (jnp.abs(block - other) <= SPAN)
    low = jnp.min(jnp.where(present, other, nblocks), axis=1) - first + base
    count = jnp.sum(present.astype(jnp.int32), axis=1)

    sent = attention(low, count, x, halos, segs, slots, pair_rows)
    if ngroups > 1:
        sent = jnp.stack([jnp.roll(sent[o], -o * pair_rows, axis=1) for o in range(HEADS)])
        sent = sent.reshape(HEADS, 4 * hdim, ngroups, HEADS * pair_rows)
        sent = jnp.transpose(sent, (2, 0, 1, 3)).reshape(nblocks, 4 * hdim, HEADS * pair_rows)
        lane_offsets = token_offsets = arrived_offsets
    else:
        lane_offsets = jnp.roll(arrived_offsets, block_index, axis=0)
        token_offsets = jnp.roll(arrived_offsets[::-1], block_index + 1, axis=0)
    arrived = exchange(sent)
    return finish(
        token_offsets.reshape(1, slots),
        lane_offsets.reshape(ngroups, HEADS * pair_rows),
        out_weight,
        arrived,
        arrived_tokens,
        capacity,
    )


def solution(mesh):
    placed = (
        P("rep"),
        P("rep", None),
        P(("rep", "blk"), None),
        P(("rep", "blk"), None),
        P(("rep", "blk"), None),
        P(("rep", "blk"), None),
        P(),
        P(("rep", "blk")),
        P(("rep", "blk")),
    )
    return jax.shard_map(
        per_device, mesh=mesh, in_specs=placed, out_specs=P(("rep", "blk"), None), check_vma=False
    )
```

```python
import functools

import jax
import jax.numpy as jnp
from jax import lax
from jax.experimental import pallas as pl
from jax.experimental.pallas import tpu as pltpu
from jax.sharding import PartitionSpec as P

HEADS = 8
SPAN = 3
NEG = -1e30
LOG2E = 1.4426950408889634
META = 16
MIB = 1024 * 1024


def vmem():
    return pl.BlockSpec(memory_space=pltpu.VMEM)


def smem():
    return pl.BlockSpec(memory_space=pltpu.SMEM)


def hbm():
    return pl.BlockSpec(memory_space=pltpu.HBM)


def limit(mib):
    return pltpu.CompilerParams(vmem_limit_bytes=mib * MIB)


def prepare_kernel(pair_rows, head_ref, owners_ref, offsets_ref, q_hbm, k_hbm, v_hbm, *refs):
    outs, (slot_ref, held, turned, pieces, load_sems, store_sems) = refs[:HEADS], refs[HEADS:]
    rows, features = q_hbm.shape
    hdim = features // HEADS
    mrows = rows // 4
    loads = [
        pltpu.make_async_copy(ref, held.at[part], load_sems.at[part])
        for part, ref in enumerate((q_hbm, k_hbm, v_hbm))
    ]
    for load in loads:
        load.start()

    owner = jnp.broadcast_to(owners_ref[...].astype(jnp.float32), (mrows, mrows))
    earlier = lax.broadcasted_iota(jnp.int32, (mrows, mrows), 0)
    later = lax.broadcasted_iota(jnp.int32, (mrows, mrows), 1)
    column = jnp.sum(jnp.where(earlier == later, owner, 0.0), axis=1, keepdims=True)
    ahead = jnp.where((owner == column) & (earlier < later), 1.0, 0.0)
    slot = owner[:1] * pair_rows + jnp.sum(ahead, axis=0, keepdims=True)
    line = lax.broadcasted_iota(jnp.int32, (META, mrows), 0)
    offset = offsets_ref[...].astype(jnp.float32)
    meta = jnp.where(line == 0, slot, jnp.where(line == 1, offset, 0.0))
    row = lax.broadcasted_iota(jnp.int32, (mrows, rows), 0)
    patch = lax.broadcasted_iota(jnp.int32, (mrows, rows), 1)
    spread = jnp.where(patch // 4 == row, 1.0, 0.0).astype(jnp.bfloat16)
    meta = jnp.dot(meta.astype(jnp.bfloat16), spread, preferred_element_type=jnp.float32)
    slot_ref[...] = meta[:1].astype(jnp.int32)
    meta = meta.astype(jnp.bfloat16)

    for part, load in enumerate(loads):
        load.wait()
        turned[part] = held[part].T
    stores = []
    for d in range(HEADS):
        start = pl.multiple_of(head_ref[d] * hdim, 16)
        for part in range(3):
            pieces[d, part * hdim : (part + 1) * hdim, :] = turned[part, pl.ds(start, hdim), :]
        pieces[d, 3 * hdim :, :] = meta
        stores.append(pltpu.make_async_copy(pieces.at[d], outs[d], store_sems.at[d]))
        stores[d].start()
    for store in stores:
        store.wait()


def prepare(head, owners, offsets, queries, keys, values, pair_rows):
    rows, features = queries.shape
    lines = 3 * features // HEADS + META
    piece = jax.ShapeDtypeStruct((lines, rows), queries.dtype)
    *pieces, slot = pl.pallas_call(
        functools.partial(prepare_kernel, pair_rows),
        out_shape=[piece] * HEADS + [jax.ShapeDtypeStruct((1, rows), jnp.int32)],
        in_specs=[smem()] + [vmem()] * 2 + [hbm()] * 3,
        out_specs=[hbm()] * HEADS + [vmem()],
        scratch_shapes=[
            pltpu.VMEM((3, rows, features), queries.dtype),
            pltpu.VMEM((3, features, rows), queries.dtype),
            pltpu.VMEM((HEADS, lines, rows), queries.dtype),
            pltpu.SemaphoreType.DMA((3,)),
            pltpu.SemaphoreType.DMA((HEADS,)),
        ],
        compiler_params=limit(16),
    )(head, owners, offsets, queries, keys, values)
    return pieces, slot


def arrange_kernel(slot_ref, tokens_ref, *refs):
    *outs, held, sems = refs
    slots = outs[0].shape[0]
    rows, width = tokens_ref.shape
    tokens = tokens_ref[...]
    total = len(outs) * slots
    slot = lax.broadcasted_iota(jnp.int32, (total, rows), 0)
    quarter = lax.broadcasted_iota(jnp.int32, (1, rows), 1) % 4
    for j in range(4):
        mine = jnp.where(quarter == j, slot_ref[...], -1) == slot
        pick = jnp.where(mine, 1.0, 0.0).astype(jnp.bfloat16)
        held[:, j * width : (j + 1) * width] = jnp.dot(
            pick, tokens, preferred_element_type=jnp.float32
        ).astype(jnp.bfloat16)
    stores = [
        pltpu.make_async_copy(held.at[pl.ds(d * slots, slots)], out, sems.at[d])
        for d, out in enumerate(outs)
    ]
    for store in stores:
        store.start()
    for store in stores:
        store.wait()


def arrange(slot_of_patch, tokens, pieces, slots):
    rows, width = tokens.shape
    return pl.pallas_call(
        arrange_kernel,
        out_shape=[jax.ShapeDtypeStruct((slots // pieces, 4 * width), jnp.bfloat16)] * pieces,
        in_specs=[vmem()] * 2,
        out_specs=[hbm()] * pieces,
        scratch_shapes=[
            pltpu.VMEM((slots, 4 * width), jnp.bfloat16),
            pltpu.SemaphoreType.DMA((pieces,)),
        ],
        compiler_params=limit(16),
    )(slot_of_patch, tokens)


def attention_kernel(halo, pair_rows, source_ref, turn_ref, low_ref, count_ref, seg_ref, *refs):
    pieces, refs = refs[:HEADS], refs[HEADS:]
    if halo:
        below_ref, above_ref, *refs = refs
    outs, (x_s, key_s, value_s, seg_s, picked_s, sent_s, load_sems, store_sems) = (
        refs[:HEADS],
        refs[HEADS:],
    )
    blocks, lines, rows = x_s.shape
    triple = lines - META
    hdim = triple // 3
    slots = outs[0].shape[1]
    base = SPAN if halo else 0
    factor = LOG2E / (hdim**0.5)
    loads = [
        pltpu.make_async_copy(pieces[d], x_s.at[source_ref[d]], load_sems.at[d])
        for d in range(HEADS)
    ]
    for load in loads:
        load.start()
    for b in range(blocks + 2 * base):
        seg_s[b] = jnp.broadcast_to(seg_ref[b], (128, rows)).T
    for load in loads:
        load.wait()

    for b in range(blocks + 2 * base):
        if b < base:
            key_s[b] = below_ref[b, :hdim, :].T
            value_s[b] = below_ref[b, hdim:, :]
        elif b >= base + blocks:
            key_s[b] = above_ref[b - base - blocks, :hdim, :].T
            value_s[b] = above_ref[b - base - blocks, hdim:, :]
        else:
            key_s[b] = x_s[b - base, hdim : 2 * hdim, :].T
            value_s[b] = x_s[b - base, 2 * hdim : triple, :]

    slot = lax.broadcasted_iota(jnp.int32, (slots, rows), 0)
    quarter = lax.broadcasted_iota(jnp.int32, (1, rows), 1) % 4

    def one_block(i, carry):
        low = low_ref[i]
        count = count_ref[i]
        query = x_s[i, :hdim, :]
        query_seg = seg_ref[i + base]
        place = x_s[i, triple:, :].astype(jnp.float32)[:1].astype(jnp.int32) + i * pair_rows
        place = jnp.where(place >= slots, place - slots, place)

        for size in range(1, 2 * SPAN + 2):

            @pl.when(count == size)
            def _():
                key = key_s[pl.ds(low, size)].reshape(size * rows, hdim)
                scores = jnp.dot(key, query, preferred_element_type=jnp.float32)
                key_seg = seg_s[pl.ds(low, size)].reshape(size * rows, 128)
                key_seg = jnp.concatenate([key_seg] * (rows // 128), axis=1)
                scores = jnp.where(key_seg == query_seg, scores, NEG)
                peak = jnp.max(scores, axis=0, keepdims=True)
                weights = jnp.exp2((scores - peak) * factor)
                total = jnp.sum(weights, axis=0, keepdims=True)
                weights = weights.astype(jnp.bfloat16)
                mixed = jnp.zeros((hdim, rows), jnp.float32)
                for b in range(size):
                    mixed += jnp.dot(
                        value_s[low + b],
                        weights[b * rows : (b + 1) * rows],
                        preferred_element_type=jnp.float32,
                    )
                attended = (mixed / total).astype(jnp.bfloat16)
                for j in range(4):
                    mine = jnp.where(quarter == j, place, -1) == slot
                    pick = jnp.where(mine, 1.0, 0.0).astype(jnp.bfloat16)
                    picked_s[i, j * hdim : (j + 1) * hdim, :] = lax.dot_general(
                        attended,
                        pick,
                        (((1,), (1,)), ((), ())),
                        preferred_element_type=jnp.float32,
                    )

        return carry

    lax.fori_loop(0, blocks, one_block, 0)

    step = 32
    group = lax.broadcasted_iota(jnp.int32, (step, slots), 1) // pair_rows
    group = (group - turn_ref[0] + slots) % blocks
    for line in range(0, 4 * hdim, step):
        chosen = [picked_s[b, line : line + step, :] for b in range(blocks)]
        shift = 1
        while shift < blocks:
            moved = (group & shift) > 0
            chosen = [
                jnp.where(moved, chosen[(b + shift) % blocks], chosen[b]) for b in range(blocks)
            ]
            shift *= 2
        for d in range(blocks):
            sent_s[d, line : line + step, :] = chosen[-d % blocks].astype(sent_s.dtype)
    stores = [
        pltpu.make_async_copy(sent_s.at[d], outs[d], store_sems.at[d]) for d in range(HEADS)
    ]
    for store in stores:
        store.start()
    for store in stores:
        store.wait()


def attention(source, turn, low, count, segs, pieces, halos, slots, pair_rows):
    lines, rows = pieces[0].shape
    hdim = (lines - META) // 3
    extended = segs.shape[0]
    out = jax.ShapeDtypeStruct((4 * hdim, slots), jnp.bfloat16)
    return pl.pallas_call(
        functools.partial(attention_kernel, bool(halos), pair_rows),
        out_shape=[out] * HEADS,
        in_specs=[smem()] * 4 + [vmem()] + [hbm()] * HEADS + [vmem()] * len(halos),
        out_specs=[hbm()] * HEADS,
        scratch_shapes=[
            pltpu.VMEM((HEADS, lines, rows), jnp.bfloat16),
            pltpu.VMEM((extended, rows, hdim), jnp.bfloat16),
            pltpu.VMEM((extended, hdim, rows), jnp.bfloat16),
            pltpu.VMEM((extended, rows, 128), jnp.float32),
            pltpu.VMEM((HEADS, 4 * hdim, slots), jnp.float32),
            pltpu.VMEM((HEADS, 4 * hdim, slots), jnp.bfloat16),
            pltpu.SemaphoreType.DMA((HEADS,)),
            pltpu.SemaphoreType.DMA((HEADS,)),
        ],
        compiler_params=limit(24),
        cost_estimate=pl.CostEstimate(
            flops=8_000_000_000, bytes_accessed=8_000_000, transcendentals=3_000_000
        ),
    )(source, turn, low, count, segs, *pieces, *halos)


def finish_kernel(ring, source_ref, token_offsets_ref, offsets_ref, weight_hbm, *refs):
    *refs, out_hbm, weight, attended_s, tokens_s, held, weight_sems, att_sems, token_sems, sems = refs
    if ring:
        attended_refs, token_refs = refs[:HEADS], refs[HEADS:]
    else:
        attended_refs, token_refs = refs[:1], refs[1:]
    capacity, merged = out_hbm.shape
    groups, lanes = offsets_ref.shape
    width = merged // 4
    hdim = attended_s.shape[1] // 4
    slots = tokens_s.shape[0] // len(token_refs)

    attended_loads, weight_loads, token_loads = [], [], []
    if ring:
        for d, ref in enumerate(attended_refs):
            attended_loads.append(pltpu.make_async_copy(ref, attended_s.at[d], att_sems.at[d]))
    else:
        attended_loads.append(
            pltpu.make_async_copy(attended_refs[0], attended_s, att_sems.at[0])
        )
    for h in range(HEADS):
        head = pl.multiple_of((source_ref[h] if ring else h) * hdim, 16)
        weight_loads.append(
            pltpu.make_async_copy(
                weight_hbm.at[pl.ds(head, hdim)],
                weight.at[pl.ds(h * hdim, hdim)],
                weight_sems.at[h],
            )
        )
    for d, ref in enumerate(token_refs):
        token_loads.append(
            pltpu.make_async_copy(ref, tokens_s.at[pl.ds(d * slots, slots)], token_sems.at[d])
        )
    for load in attended_loads + weight_loads + token_loads:
        load.start()

    def pick(offsets):
        row = lax.broadcasted_iota(jnp.int32, (capacity, offsets.shape[1]), 0)
        return jnp.where(offsets == row, 1.0, 0.0).astype(jnp.bfloat16)

    token_pick = pick(token_offsets_ref[...])
    picks = [pick(offsets_ref[g : g + 1, :]) for g in range(groups)]
    for load in attended_loads:
        load.wait()
    placed = []
    for j in range(4):
        attended = jnp.zeros((capacity, HEADS * hdim), jnp.float32)
        for g in range(groups):
            turned = jnp.concatenate(
                [
                    attended_s[g * HEADS + h, j * hdim : (j + 1) * hdim, :]
                    for h in range(HEADS)
                ],
                axis=0,
            )
            attended += lax.dot_general(
                picks[g], turned, (((1,), (1,)), ((), ())), preferred_element_type=jnp.float32
            )
        placed.append(attended.astype(jnp.bfloat16))
    for load in weight_loads + token_loads:
        load.wait()
    stores = []
    for j in range(4):
        columns = slice(j * width, (j + 1) * width)
        hidden = jnp.dot(
            token_pick, tokens_s[:, columns], preferred_element_type=jnp.float32
        ) + jnp.dot(placed[j], weight[...], preferred_element_type=jnp.float32)
        held[j] = hidden.astype(jnp.bfloat16)
        stores.append(pltpu.make_async_copy(held.at[j], out_hbm.at[:, columns], sems.at[j]))
        stores[j].start()
    for store in stores:
        store.wait()


def finish(source, token_offsets, offsets, out_weight, attended, tokens, capacity):
    ring = len(attended) == HEADS
    merged = tokens[0].shape[1]
    features, width = out_weight.shape
    shape = (HEADS, *attended[0].shape) if ring else attended[0].shape
    return pl.pallas_call(
        functools.partial(finish_kernel, ring),
        out_shape=jax.ShapeDtypeStruct((capacity, merged), jnp.bfloat16),
        in_specs=[smem()] + [vmem()] * 2 + [hbm()] * (1 + len(attended) + len(tokens)),
        out_specs=hbm(),
        scratch_shapes=[
            pltpu.VMEM((features, width), jnp.bfloat16),
            pltpu.VMEM(shape, jnp.bfloat16),
            pltpu.VMEM((len(tokens) * tokens[0].shape[0], merged), jnp.bfloat16),
            pltpu.VMEM((4, capacity, width), jnp.bfloat16),
            pltpu.SemaphoreType.DMA((HEADS,)),
            pltpu.SemaphoreType.DMA((len(attended),)),
            pltpu.SemaphoreType.DMA((len(tokens),)),
            pltpu.SemaphoreType.DMA((4,)),
        ],
        compiler_params=limit(40),
    )(source, token_offsets, offsets, out_weight, *attended, *tokens)


FAR_FIRST = (4, 5, 3, 2, 6, 1, 7)
BESIDE_INPUTS = (4, 5)
BESIDE_ATTENTION = (3, 2, 6)


def per_device(segment_ids, block_mask, queries, keys, values, tokens, out_weight, owners, offsets):
    rows, features = queries.shape
    hdim = features // HEADS
    nblocks = lax.axis_size("blk")
    block_index = lax.axis_index("blk")
    ngroups = nblocks // HEADS
    ring = ngroups == 1
    first = block_index // HEADS * HEADS
    groups = [[g * HEADS + h for h in range(HEADS)] for g in range(ngroups)]
    exchange = functools.partial(
        lax.all_to_all, axis_name="blk", split_axis=0, concat_axis=0, tiled=True
    )

    def send(block, distance):
        route = [(i, (i + distance) % nblocks) for i in range(nblocks)]
        return lax.ppermute(block, "blk", route)

    mrows = rows // 4
    capacity = 2 * mrows
    pair_rows = max(2, 2 * mrows // nblocks)
    slots = nblocks * pair_rows
    assert slots <= 256

    steps = jnp.arange(HEADS)
    turn = block_index if ring else 0
    head = (turn + steps) % HEADS
    source = (turn - steps) % HEADS if ring else steps

    split, own_slots = prepare(
        head, owners[None, :], offsets[None, :], queries, keys, values, pair_rows
    )
    if ring:
        pieces = [split[0]] + [None] * (HEADS - 1)
        for d in FAR_FIRST:
            pieces[d] = send(split[d], d)
        own_slots = (own_slots - block_index * pair_rows) % slots
        outgoing = arrange(own_slots, tokens, nblocks, slots)
        arrived_tokens = [outgoing[0]] + [None] * (nblocks - 1)
        for d in BESIDE_INPUTS:
            arrived_tokens[d] = send(outgoing[d], d)
        held = lax.optimization_barrier(
            (pieces, [arrived_tokens[d] for d in BESIDE_INPUTS], list(outgoing))
        )
        pieces, outgoing = held[0], held[2]
        for d, block in zip(BESIDE_INPUTS, held[1]):
            arrived_tokens[d] = block
        for d in BESIDE_ATTENTION:
            arrived_tokens[d] = send(outgoing[d], d)
        x = jnp.stack([piece[3 * hdim :, ::4] for piece in pieces])
        meta = x[:, :2].astype(jnp.int32)
        all_slots, all_offsets = meta[:, 0], meta[:, 1]
        wanted = block_index * pair_rows + jnp.arange(pair_rows)
        here = all_slots[..., None] == wanted
        token_offsets = capacity + jnp.sum(
            jnp.where(here, all_offsets[..., None] - capacity, 0), axis=1
        )
        lane_offsets = token_offsets[(2 * block_index - steps) % HEADS]
    else:
        x = exchange(jnp.stack(split), axis_index_groups=groups)
        pieces = list(x)
        outgoing = arrange(own_slots, tokens, 1, slots)
        arrived_tokens = [exchange(outgoing[0])]
        match = own_slots[0, ::4, None] == jnp.arange(slots)
        outgoing_offsets = capacity + jnp.sum(
            jnp.where(match, offsets[:, None] - capacity, 0), axis=0
        )
        lane_offsets = token_offsets = exchange(outgoing_offsets.reshape(nblocks, pair_rows))

    segs = segment_ids.reshape(nblocks, 1, rows)
    base = 0
    halos = ()
    if not ring:
        base = SPAN
        up = [(i, i + HEADS) for i in range(nblocks - HEADS)]
        down = [(i + HEADS, i) for i in range(nblocks - HEADS)]
        halos = (
            lax.ppermute(x[HEADS - SPAN :, hdim : 3 * hdim], "blk", up),
            lax.ppermute(x[:SPAN, hdim : 3 * hdim], "blk", down),
        )
        segs = jnp.pad(segs, ((SPAN, SPAN), (0, 0), (0, 0)), constant_values=-1)
        segs = lax.dynamic_slice_in_dim(segs, first, HEADS + 2 * SPAN, 0)
    segs = segs.astype(jnp.float32)

    mask = lax.dynamic_slice_in_dim(block_mask, first, HEADS, 0)
    block = first + jnp.arange(HEADS)[:, None]
    other = jnp.arange(nblocks)[None, :]
    present = (mask > 0) & (jnp.abs(block - other) <= SPAN)
    low = jnp.min(jnp.where(present, other, nblocks), axis=1) - first + base
    count = jnp.sum(present.astype(jnp.int32), axis=1)

    turn = jnp.reshape(turn, (1,)).astype(jnp.int32)
    sent = attention(source, turn, low, count, segs, pieces, halos, slots, pair_rows)
    if ring:
        held = lax.optimization_barrier((sent, [arrived_tokens[d] for d in BESIDE_ATTENTION]))
        sent = held[0]
        for d, block in zip(BESIDE_ATTENTION, held[1]):
            arrived_tokens[d] = block
        arrived = [sent[0]] + [None] * (HEADS - 1)
        for d in FAR_FIRST:
            arrived[d] = send(sent[d], d)
        for d in FAR_FIRST:
            if arrived_tokens[d] is None:
                arrived_tokens[d] = send(outgoing[d], d)
    else:
        sent = jnp.stack([jnp.roll(sent[o], -o * pair_rows, axis=1) for o in range(HEADS)])
        sent = sent.reshape(HEADS, 4 * hdim, ngroups, HEADS * pair_rows)
        sent = jnp.transpose(sent, (2, 0, 1, 3)).reshape(nblocks, 4 * hdim, HEADS * pair_rows)
        arrived = [exchange(sent)]
    return finish(
        source,
        token_offsets.reshape(1, slots),
        lane_offsets.reshape(ngroups, HEADS * pair_rows),
        out_weight,
        arrived,
        arrived_tokens,
        capacity,
    )


def solution(mesh):
    placed = (
        P("rep"),
        P("rep", None),
        P(("rep", "blk"), None),
        P(("rep", "blk"), None),
        P(("rep", "blk"), None),
        P(("rep", "blk"), None),
        P(),
        P(("rep", "blk")),
        P(("rep", "blk")),
    )
    return jax.shard_map(
        per_device, mesh=mesh, in_specs=placed, out_specs=P(("rep", "blk"), None), check_vma=False
    )
```

```python
import functools

import jax
import jax.numpy as jnp
from jax import lax
from jax.experimental import pallas as pl
from jax.experimental.pallas import tpu as pltpu
from jax.sharding import PartitionSpec as P

HEADS = 8
HALF = HEADS // 2
SPAN = 3
WINDOW = 2 * SPAN + 2
NEG = -1e30
LOG2E = 1.4426950408889634
MIB = 1024 * 1024


def vmem():
    return pl.BlockSpec(memory_space=pltpu.VMEM)


def smem():
    return pl.BlockSpec(memory_space=pltpu.SMEM)


def anywhere():
    return pl.BlockSpec(memory_space=pl.ANY)


def limit(mib):
    return pltpu.CompilerParams(vmem_limit_bytes=mib * MIB)


def prepare_kernel(
    pair_rows, half_ref, owners_ref, offsets_ref, q_hbm, k_hbm, v_hbm,
    own_q, own_kv, swap_q, swap_kv, meta_ref, held, turned, sems,
):
    rows, features = q_hbm.shape
    part = features // 2
    mrows = rows // 4
    loads = [
        pltpu.make_async_copy(ref, held.at[i], sems.at[i])
        for i, ref in enumerate((k_hbm, v_hbm, q_hbm))
    ]
    for load in loads:
        load.start()

    owner = jnp.broadcast_to(owners_ref[...].astype(jnp.float32), (mrows, mrows))
    earlier = lax.broadcasted_iota(jnp.int32, (mrows, mrows), 0)
    later = lax.broadcasted_iota(jnp.int32, (mrows, mrows), 1)
    column = jnp.sum(jnp.where(earlier == later, owner, 0.0), axis=1, keepdims=True)
    ahead = jnp.where((owner == column) & (earlier < later), 1.0, 0.0)
    slot = owner[:1] * pair_rows + jnp.sum(ahead, axis=0, keepdims=True)
    line = lax.broadcasted_iota(jnp.int32, (8, mrows), 0)
    offset = offsets_ref[...].astype(jnp.float32)
    meta = jnp.where(line == 0, slot, jnp.where(line == 1, offset, 0.0))
    row = lax.broadcasted_iota(jnp.int32, (mrows, rows), 0)
    patch = lax.broadcasted_iota(jnp.int32, (mrows, rows), 1)
    spread = jnp.where(patch // 4 == row, 1.0, 0.0).astype(jnp.bfloat16)
    meta_ref[...] = jnp.dot(
        meta.astype(jnp.bfloat16), spread, preferred_element_type=jnp.float32
    )

    mine = pl.multiple_of(half_ref[0] * part, 16)
    other = pl.multiple_of((1 - half_ref[0]) * part, 16)
    for i in range(3):
        loads[i].wait()
        turned[i] = held[i].T
        if i < 2:
            own_kv[i * part : (i + 1) * part, :] = turned[i, pl.ds(mine, part), :]
            swap_kv[i * part : (i + 1) * part, :] = turned[i, pl.ds(other, part), :]
        else:
            own_q[...] = turned[i, pl.ds(mine, part), :]
            swap_q[...] = turned[i, pl.ds(other, part), :]


def prepare(half, owners, offsets, queries, keys, values, pair_rows):
    rows, features = queries.shape
    part = features // 2
    single = jax.ShapeDtypeStruct((part, rows), queries.dtype)
    double = jax.ShapeDtypeStruct((2 * part, rows), queries.dtype)
    return pl.pallas_call(
        functools.partial(prepare_kernel, pair_rows),
        out_shape=[single, double, single, double, jax.ShapeDtypeStruct((8, rows), jnp.float32)],
        in_specs=[smem()] + [vmem()] * 2 + [anywhere()] * 3,
        out_specs=[vmem()] * 5,
        scratch_shapes=[
            pltpu.VMEM((3, rows, features), queries.dtype),
            pltpu.VMEM((3, features, rows), queries.dtype),
            pltpu.SemaphoreType.DMA((3,)),
        ],
        compiler_params=limit(60),
    )(half, owners, offsets, queries, keys, values)


def attention_kernel(place_ref, half_ref, low_ref, count_ref, seg_ref, own_q, other_q, *refs):
    blocks, refs = refs[:WINDOW], refs[WINDOW:]
    own_out, other_out, query_s, key_s, value_s, seg_s, out_s = refs
    half = half_ref[0]
    part, rows = own_q.shape
    hdim = part // HALF
    factor = LOG2E / (hdim**0.5)
    query_s[half] = own_q[...]
    query_s[1 - half] = other_q[...]
    first = jnp.minimum(low_ref[0], low_ref[1])
    last = jnp.maximum(low_ref[0] + count_ref[0], low_ref[1] + count_ref[1])
    for b in range(WINDOW):
        seg_s[b] = jnp.broadcast_to(seg_ref[b], (128, rows)).T
    for i, block in enumerate(blocks):
        place = place_ref[i]

        @pl.when((place >= first) & (place < last))
        def _(block=block, place=place):
            for h in range(HALF):
                key_s[h, place] = block[h * hdim : (h + 1) * hdim, :].T
            value_s[place] = block[part:, :]

    def one_head(i, carry):
        which = i // HALF
        h = i % HALF
        low = low_ref[which]
        count = count_ref[which]
        lines = pl.ds(pl.multiple_of(h * hdim, 16), hdim)
        query = query_s[which, lines, :]
        query_seg = seg_ref[SPAN + which]

        for size in range(1, 2 * SPAN + 2):

            @pl.when(count == size)
            def _():
                key = key_s[h, pl.ds(low, size)].reshape(size * rows, hdim)
                scores = jnp.dot(key, query, preferred_element_type=jnp.float32)
                key_seg = seg_s[pl.ds(low, size)].reshape(size * rows, 128)
                key_seg = jnp.concatenate([key_seg] * (rows // 128), axis=1)
                scores = jnp.where(key_seg == query_seg, scores, NEG)
                peak = jnp.max(scores, axis=0, keepdims=True)
                weights = jnp.exp2((scores - peak) * factor)
                total = jnp.sum(weights, axis=0, keepdims=True)
                weights = weights.astype(jnp.bfloat16)
                mixed = jnp.zeros((hdim, rows), jnp.float32)
                for b in range(size):
                    mixed += jnp.dot(
                        value_s[low + b, lines, :],
                        weights[b * rows : (b + 1) * rows],
                        preferred_element_type=jnp.float32,
                    )
                out_s[which, lines, :] = (mixed / total).astype(out_s.dtype)

        return carry

    lax.fori_loop(0, 2 * HALF, one_head, 0)
    own_out[...] = out_s[half]
    other_out[...] = out_s[1 - half]


def attention(place, half, low, count, segs, own_q, other_q, blocks):
    part, rows = own_q.shape
    hdim = part // HALF
    return pl.pallas_call(
        attention_kernel,
        out_shape=[jax.ShapeDtypeStruct((part, rows), jnp.bfloat16)] * 2,
        in_specs=[smem()] * 4 + [vmem()] * (3 + WINDOW),
        out_specs=[vmem()] * 2,
        scratch_shapes=[
            pltpu.VMEM((2, part, rows), jnp.bfloat16),
            pltpu.VMEM((HALF, WINDOW, rows, hdim), jnp.bfloat16),
            pltpu.VMEM((WINDOW, part, rows), jnp.bfloat16),
            pltpu.VMEM((WINDOW, rows, 128), jnp.float32),
            pltpu.VMEM((2, part, rows), jnp.bfloat16),
        ],
        compiler_params=limit(24),
    )(place, half, low, count, segs, own_q, other_q, *blocks)


def project_kernel(
    capacity, half_ref, meta_ref, own_ref, other_ref, weight_ref, tokens_ref, out_ref
):
    slots = out_ref.shape[0]
    rows, width = tokens_ref.shape
    part = own_ref.shape[0]
    half = half_ref[0]
    hidden = tokens_ref[...].astype(jnp.float32)
    for ref, which in ((own_ref, half), (other_ref, 1 - half)):
        hidden += lax.dot_general(
            ref[...],
            weight_ref[pl.ds(pl.multiple_of(which * part, 16), part), :],
            (((0,), (0,)), ((), ())),
            preferred_element_type=jnp.float32,
        )
    hidden = hidden.astype(jnp.bfloat16)
    slot = lax.broadcasted_iota(jnp.int32, (slots, rows), 0).astype(jnp.float32)
    quarter = lax.broadcasted_iota(jnp.int32, (1, rows), 1) % 4
    for j in range(4):
        mine = jnp.where(quarter == j, meta_ref[:1], -1.0) == slot
        if j == 0:
            offset = jnp.where(mine, meta_ref[1:2] - capacity, 0.0)
            offset = capacity + jnp.sum(offset, axis=1, keepdims=True)
            out_ref[:, 4 * width :] = jnp.broadcast_to(offset, (slots, 128)).astype(jnp.bfloat16)
        pick = jnp.where(mine, 1.0, 0.0).astype(jnp.bfloat16)
        out_ref[:, j * width : (j + 1) * width] = jnp.dot(
            pick, hidden, preferred_element_type=jnp.float32
        ).astype(jnp.bfloat16)


def project(half, meta, own, other, out_weight, tokens, slots, capacity):
    rows, width = tokens.shape
    return pl.pallas_call(
        functools.partial(project_kernel, float(capacity)),
        out_shape=jax.ShapeDtypeStruct((slots, 4 * width + 128), jnp.bfloat16),
        in_specs=[smem()] + [vmem()] * 5,
        out_specs=vmem(),
        compiler_params=limit(24),
    )(half, meta, own, other, out_weight, tokens)


def place_kernel(arrived_ref, out_hbm, held, sems):
    capacity, merged = out_hbm.shape
    slots = arrived_ref.shape[0]
    step = merged // 4
    row = lax.broadcasted_iota(jnp.int32, (slots, capacity), 1).astype(jnp.float32)
    offset = arrived_ref[:, merged : merged + 128].astype(jnp.float32)[:, :1]
    pick = jnp.where(offset == row, 1.0, 0.0).astype(jnp.bfloat16)
    stores = []
    for j in range(4):
        columns = slice(j * step, (j + 1) * step)
        held[j] = lax.dot_general(
            pick,
            arrived_ref[:, columns],
            (((0,), (0,)), ((), ())),
            preferred_element_type=jnp.float32,
        ).astype(jnp.bfloat16)
        stores.append(pltpu.make_async_copy(held.at[j], out_hbm.at[:, columns], sems.at[j]))
        stores[j].start()
    for store in stores:
        store.wait()


def place(arrived, capacity, merged):
    return pl.pallas_call(
        place_kernel,
        out_shape=jax.ShapeDtypeStruct((capacity, merged), jnp.bfloat16),
        in_specs=[vmem()],
        out_specs=anywhere(),
        scratch_shapes=[
            pltpu.VMEM((4, capacity, merged // 4), jnp.bfloat16),
            pltpu.SemaphoreType.DMA((4,)),
        ],
        compiler_params=limit(24),
    )(arrived)


def per_device(segment_ids, block_mask, queries, keys, values, tokens, out_weight, owners, offsets):
    rows = queries.shape[0]
    width = tokens.shape[1]
    nblocks = lax.axis_size("blk")
    block_index = lax.axis_index("blk")
    half = block_index % 2
    pair = block_index - half
    mrows = rows // 4
    capacity = 2 * mrows
    pair_rows = max(2, 2 * mrows // nblocks)
    slots = nblocks * pair_rows
    assert slots <= 256

    def route(step):
        return [(i, i + step(i)) for i in range(nblocks) if 0 <= i + step(i) < nblocks]

    swap = functools.partial(
        lax.ppermute, axis_name="blk", perm=route(lambda i: 1 - 2 * (i % 2))
    )
    ahead = functools.partial(
        lax.ppermute, axis_name="blk", perm=route(lambda i: 2 if i % 2 else -2)
    )
    back = functools.partial(
        lax.ppermute, axis_name="blk", perm=route(lambda i: -2 if i % 2 else 2)
    )

    halves = half[None].astype(jnp.int32)
    own_q, own_kv, swap_q, swap_kv, meta = prepare(
        halves, owners[None, :], offsets[None, :], queries, keys, values, pair_rows
    )
    other_kv = swap(swap_kv)
    ahead_own = ahead(own_kv)
    back_own = back(own_kv)
    other_q = swap(swap_q)
    back_other = back(other_kv)
    ahead_other = ahead(other_kv)
    ahead_far = ahead(ahead_own)
    back_far = back(back_other)
    blocks = (own_kv, other_kv, ahead_own, ahead_other, back_own, back_other, ahead_far, back_far)
    places = jnp.where(
        half == 0,
        jnp.array([3, 4, 5, 6, 1, 2, 7, 0], jnp.int32),
        jnp.array([4, 3, 2, 1, 6, 5, 0, 7], jnp.int32),
    )

    segs = jnp.pad(segment_ids.reshape(nblocks, 1, rows), ((SPAN, SPAN), (0, 0), (0, 0)))
    segs = lax.dynamic_slice_in_dim(segs, pair, WINDOW, 0).astype(jnp.float32)
    mask = lax.dynamic_slice_in_dim(block_mask, pair, 2, 0)
    block = pair + jnp.arange(2)[:, None]
    other = jnp.arange(nblocks)[None, :]
    present = (mask > 0) & (jnp.abs(block - other) <= SPAN)
    low = jnp.min(jnp.where(present, other, nblocks), axis=1) - pair + SPAN
    count = jnp.sum(present.astype(jnp.int32), axis=1)

    own, other = attention(places, halves, low, count, segs, own_q, other_q, blocks)
    other = swap(other)
    outgoing = project(halves, meta, own, other, out_weight, tokens, slots, capacity)
    arrived = lax.all_to_all(outgoing, "blk", split_axis=0, concat_axis=0, tiled=True)
    return place(arrived, capacity, 4 * width)


def solution(mesh):
    placed = (
        P("rep"),
        P("rep", None),
        P(("rep", "blk"), None),
        P(("rep", "blk"), None),
        P(("rep", "blk"), None),
        P(("rep", "blk"), None),
        P(),
        P(("rep", "blk")),
        P(("rep", "blk")),
    )
    return jax.shard_map(
        per_device, mesh=mesh, in_specs=placed, out_specs=P(("rep", "blk"), None), check_vma=False
    )
```

```python
import functools

import jax
import jax.numpy as jnp
from jax import lax
from jax.experimental import pallas as pl
from jax.experimental.pallas import tpu as pltpu
from jax.sharding import PartitionSpec as P

HEADS = 8
HALF = HEADS // 2
SPAN = 3
WINDOW = 2 * SPAN + 2
NEAR = WINDOW // 2
NEG = -1e30
LOG2E = 1.4426950408889634
MIB = 1024 * 1024


def vmem():
    return pl.BlockSpec(memory_space=pltpu.VMEM)


def smem():
    return pl.BlockSpec(memory_space=pltpu.SMEM)


def anywhere():
    return pl.BlockSpec(memory_space=pl.ANY)


def limit(mib):
    return pltpu.CompilerParams(vmem_limit_bytes=mib * MIB)


def prepare_kernel(
    pair_rows, half_ref, owners_ref, offsets_ref, q_hbm, k_hbm, v_hbm,
    own_q, own_kv, swap_q, swap_kv, meta_ref, held, turned, sems,
):
    rows, features = q_hbm.shape
    part = features // 2
    mrows = rows // 4
    loads = [
        pltpu.make_async_copy(ref, held.at[i], sems.at[i])
        for i, ref in enumerate((k_hbm, v_hbm, q_hbm))
    ]
    for load in loads:
        load.start()

    owner = jnp.broadcast_to(owners_ref[...].astype(jnp.float32), (mrows, mrows))
    earlier = lax.broadcasted_iota(jnp.int32, (mrows, mrows), 0)
    later = lax.broadcasted_iota(jnp.int32, (mrows, mrows), 1)
    column = jnp.sum(jnp.where(earlier == later, owner, 0.0), axis=1, keepdims=True)
    ahead = jnp.where((owner == column) & (earlier < later), 1.0, 0.0)
    slot = owner[:1] * pair_rows + jnp.sum(ahead, axis=0, keepdims=True)
    line = lax.broadcasted_iota(jnp.int32, (8, mrows), 0)
    offset = offsets_ref[...].astype(jnp.float32)
    meta = jnp.where(line == 0, slot, jnp.where(line == 1, offset, 0.0))
    row = lax.broadcasted_iota(jnp.int32, (mrows, rows), 0)
    patch = lax.broadcasted_iota(jnp.int32, (mrows, rows), 1)
    spread = jnp.where(patch // 4 == row, 1.0, 0.0).astype(jnp.bfloat16)
    meta_ref[...] = jnp.dot(
        meta.astype(jnp.bfloat16), spread, preferred_element_type=jnp.float32
    )

    mine = pl.multiple_of(half_ref[0] * part, 16)
    other = pl.multiple_of((1 - half_ref[0]) * part, 16)
    for i in range(3):
        loads[i].wait()
        turned[i] = held[i].T
        if i < 2:
            own_kv[i * part : (i + 1) * part, :] = turned[i, pl.ds(mine, part), :]
            swap_kv[i * part : (i + 1) * part, :] = turned[i, pl.ds(other, part), :]
        else:
            own_q[...] = turned[i, pl.ds(mine, part), :]
            swap_q[...] = turned[i, pl.ds(other, part), :]


def prepare(half, owners, offsets, queries, keys, values, pair_rows):
    rows, features = queries.shape
    part = features // 2
    single = jax.ShapeDtypeStruct((part, rows), queries.dtype)
    double = jax.ShapeDtypeStruct((2 * part, rows), queries.dtype)
    return pl.pallas_call(
        functools.partial(prepare_kernel, pair_rows),
        out_shape=[single, double, single, double, jax.ShapeDtypeStruct((8, rows), jnp.float32)],
        in_specs=[smem()] + [vmem()] * 2 + [anywhere()] * 3,
        out_specs=[vmem()] * 5,
        scratch_shapes=[
            pltpu.VMEM((3, rows, features), queries.dtype),
            pltpu.VMEM((3, features, rows), queries.dtype),
            pltpu.SemaphoreType.DMA((3,)),
        ],
        compiler_params=limit(60),
    )(half, owners, offsets, queries, keys, values)


def attention_kernel(number, which, ends, need_ref, place_ref, seg_ref, query_seg_ref, *refs):
    queries, refs = refs[:number], refs[number:]
    blocks, refs = refs[:NEAR], refs[NEAR:]
    follows = which is not None
    if follows:
        (accum_b, peak_b, total_b), refs = refs[:3], refs[3:]
    if ends:
        out_ref, key_s, value_s, seg_s, chosen_s = refs
    else:
        accum_ref, peak_ref, total_ref, key_s, value_s, seg_s, chosen_s = refs
    part, rows = queries[0].shape
    hdim = part // HALF
    factor = LOG2E / (hdim**0.5)
    for b in range(NEAR):
        wanted = need_ref[0, b]
        for n in range(1, number):
            wanted = wanted + need_ref[n, b]

        @pl.when(wanted > 0)
        def _(b=b):
            seg_s[b] = jnp.broadcast_to(seg_ref[place_ref[b]], (128, rows)).T
            for h in range(HALF):
                key_s[h, b] = blocks[b][h * hdim : (h + 1) * hdim, :].T
            value_s[b] = blocks[b][part:, :]

    for n in range(number):
        size = 0
        for b in range(NEAR):
            chosen_s[size] = b
            size = size + need_ref[n, b]
        query_seg = query_seg_ref[n]

        def one_head(h, carry, n=n, size=size, query_seg=query_seg):
            lines = pl.ds(pl.multiple_of(h * hdim, 16), hdim)
            query = queries[n][lines, :]

            def finish(peak, total, accum):
                if ends:
                    out_ref[lines, :] = (accum / total).astype(out_ref.dtype)
                else:
                    peak_ref[n, h] = peak
                    total_ref[n, h] = total
                    accum_ref[n, lines, :] = accum

            if follows:

                @pl.when(size == 0)
                def _():
                    finish(peak_b[which, h], total_b[which, h], accum_b[which, lines, :])

            for fixed in range(1, NEAR + 1):

                @pl.when(size == fixed)
                def _():
                    picked = [chosen_s[b] for b in range(fixed)]
                    scores = []
                    for b in picked:
                        score = jnp.dot(key_s[h, b], query, preferred_element_type=jnp.float32)
                        key_seg = jnp.concatenate([seg_s[b]] * (rows // 128), axis=1)
                        scores.append(jnp.where(key_seg == query_seg, score, NEG))
                    peak = jnp.max(scores[0], axis=0, keepdims=True)
                    for score in scores[1:]:
                        peak = jnp.maximum(peak, jnp.max(score, axis=0, keepdims=True))
                    if follows:
                        peak = jnp.maximum(peak, peak_b[which, h])
                        scaled = jnp.exp2((peak_b[which, h] - peak) * factor)
                        total = total_b[which, h] * scaled
                        accum = accum_b[which, lines, :] * scaled
                    else:
                        total = jnp.zeros((1, rows), jnp.float32)
                        accum = jnp.zeros((hdim, rows), jnp.float32)
                    for b, score in zip(picked, scores):
                        weights = jnp.exp2((score - peak) * factor)
                        total += jnp.sum(weights, axis=0, keepdims=True)
                        accum += jnp.dot(
                            value_s[b, lines, :],
                            weights.astype(jnp.bfloat16),
                            preferred_element_type=jnp.float32,
                        )
                    finish(peak, total, accum)

            return carry

        lax.fori_loop(0, HALF, one_head, 0)


def attention(need, places, segs, query_segs, queries, blocks, before, which, ends):
    number = len(queries)
    part, rows = queries[0].shape
    hdim = part // HALF
    if ends:
        outs = jax.ShapeDtypeStruct((part, rows), jnp.bfloat16)
    else:
        row = jax.ShapeDtypeStruct((number, HALF, 1, rows), jnp.float32)
        outs = [jax.ShapeDtypeStruct((number, part, rows), jnp.float32), row, row]
    return pl.pallas_call(
        functools.partial(attention_kernel, number, which, ends),
        out_shape=outs,
        in_specs=[smem()] * 2 + [vmem()] * (2 + number + NEAR + (3 if before is not None else 0)),
        out_specs=vmem() if ends else [vmem()] * 3,
        scratch_shapes=[
            pltpu.VMEM((HALF, NEAR, rows, hdim), jnp.bfloat16),
            pltpu.VMEM((NEAR, part, rows), jnp.bfloat16),
            pltpu.VMEM((NEAR, rows, 128), jnp.float32),
            pltpu.SMEM((NEAR + 1,), jnp.int32),
        ],
        compiler_params=limit(16),
        cost_estimate=pl.CostEstimate(
            flops=2_000_000_000 * number, bytes_accessed=2_000_000, transcendentals=1_000_000
        ),
    )(need, places, segs, query_segs, *queries, *blocks, *(before or ()))


def project_kernel(
    capacity, half_ref, meta_ref, own_ref, other_ref, weight_ref, tokens_ref, out_ref
):
    slots = out_ref.shape[0]
    rows, width = tokens_ref.shape
    part = own_ref.shape[0]
    half = half_ref[0]
    hidden = tokens_ref[...].astype(jnp.float32)
    for ref, which in ((own_ref, half), (other_ref, 1 - half)):
        hidden += lax.dot_general(
            ref[...],
            weight_ref[pl.ds(pl.multiple_of(which * part, 16), part), :],
            (((0,), (0,)), ((), ())),
            preferred_element_type=jnp.float32,
        )
    hidden = hidden.astype(jnp.bfloat16)
    slot = lax.broadcasted_iota(jnp.int32, (slots, rows), 0).astype(jnp.float32)
    quarter = lax.broadcasted_iota(jnp.int32, (1, rows), 1) % 4
    for j in range(4):
        mine = jnp.where(quarter == j, meta_ref[:1], -1.0) == slot
        if j == 0:
            offset = jnp.where(mine, meta_ref[1:2] - capacity, 0.0)
            offset = capacity + jnp.sum(offset, axis=1, keepdims=True)
            out_ref[:, 4 * width :] = jnp.broadcast_to(offset, (slots, 128)).astype(jnp.bfloat16)
        pick = jnp.where(mine, 1.0, 0.0).astype(jnp.bfloat16)
        out_ref[:, j * width : (j + 1) * width] = jnp.dot(
            pick, hidden, preferred_element_type=jnp.float32
        ).astype(jnp.bfloat16)


def project(half, meta, own, other, out_weight, tokens, slots, capacity):
    rows, width = tokens.shape
    return pl.pallas_call(
        functools.partial(project_kernel, float(capacity)),
        out_shape=jax.ShapeDtypeStruct((slots, 4 * width + 128), jnp.bfloat16),
        in_specs=[smem()] + [vmem()] * 5,
        out_specs=vmem(),
        compiler_params=limit(24),
    )(half, meta, own, other, out_weight, tokens)


def place_kernel(arrived_ref, out_hbm, held, sems):
    capacity, merged = out_hbm.shape
    slots = arrived_ref.shape[0]
    step = merged // 4
    row = lax.broadcasted_iota(jnp.int32, (slots, capacity), 1).astype(jnp.float32)
    offset = arrived_ref[:, merged : merged + 128].astype(jnp.float32)[:, :1]
    pick = jnp.where(offset == row, 1.0, 0.0).astype(jnp.bfloat16)
    stores = []
    for j in range(4):
        columns = slice(j * step, (j + 1) * step)
        held[j] = lax.dot_general(
            pick,
            arrived_ref[:, columns],
            (((0,), (0,)), ((), ())),
            preferred_element_type=jnp.float32,
        ).astype(jnp.bfloat16)
        stores.append(pltpu.make_async_copy(held.at[j], out_hbm.at[:, columns], sems.at[j]))
        stores[j].start()
    for store in stores:
        store.wait()


def place(arrived, capacity, merged):
    return pl.pallas_call(
        place_kernel,
        out_shape=jax.ShapeDtypeStruct((capacity, merged), jnp.bfloat16),
        in_specs=[vmem()],
        out_specs=anywhere(),
        scratch_shapes=[
            pltpu.VMEM((4, capacity, merged // 4), jnp.bfloat16),
            pltpu.SemaphoreType.DMA((4,)),
        ],
        compiler_params=limit(24),
    )(arrived)


def per_device(segment_ids, block_mask, queries, keys, values, tokens, out_weight, owners, offsets):
    rows = queries.shape[0]
    width = tokens.shape[1]
    nblocks = lax.axis_size("blk")
    block_index = lax.axis_index("blk")
    half = block_index % 2
    pair = block_index - half
    mrows = rows // 4
    capacity = 2 * mrows
    pair_rows = max(2, 2 * mrows // nblocks)
    slots = nblocks * pair_rows
    assert slots <= 256

    def route(step):
        return [(i, i + step(i)) for i in range(nblocks) if 0 <= i + step(i) < nblocks]

    swap = functools.partial(
        lax.ppermute, axis_name="blk", perm=route(lambda i: 1 - 2 * (i % 2))
    )
    across = functools.partial(
        lax.ppermute, axis_name="blk", perm=route(lambda i: 1 if i % 2 else -1)
    )
    ahead = functools.partial(
        lax.ppermute, axis_name="blk", perm=route(lambda i: 2 if i % 2 else -2)
    )
    back = functools.partial(
        lax.ppermute, axis_name="blk", perm=route(lambda i: -2 if i % 2 else 2)
    )

    own_q, own_kv, swap_q, swap_kv, meta = prepare(
        half[None].astype(jnp.int32), owners[None, :], offsets[None, :],
        queries, keys, values, pair_rows,
    )
    other_kv = swap(swap_kv)
    back_other = across(swap_kv)
    ahead_own = ahead(own_kv)
    back_own = back(own_kv)
    other_q = swap(swap_q)
    ahead_other = ahead(other_kv)
    ahead_far = ahead(ahead_own)
    back_far = back(back_other)
    near = (own_kv, other_kv, ahead_own, back_own)
    far = (ahead_other, back_other, ahead_far, back_far)
    places = jnp.where(
        half == 0,
        jnp.array([3, 4, 5, 1, 6, 2, 7, 0], jnp.int32),
        jnp.array([4, 3, 2, 6, 1, 5, 0, 7], jnp.int32),
    )

    segs = jnp.pad(segment_ids.reshape(nblocks, 1, rows), ((SPAN, SPAN), (0, 0), (0, 0)))
    segs = lax.dynamic_slice_in_dim(segs, pair, WINDOW, 0).astype(jnp.float32)
    query_segs = segs[places[:2]]
    pair_mask = lax.dynamic_slice_in_dim(block_mask, pair, 2, 0)
    pair_mask = jnp.pad(pair_mask, ((0, 0), (SPAN, SPAN)))
    pair_mask = lax.dynamic_slice_in_dim(pair_mask, pair, WINDOW, 1)
    apart = jnp.arange(WINDOW)[None, :] - SPAN - jnp.arange(2)[:, None]
    need = ((pair_mask > 0) & (jnp.abs(apart) <= SPAN)).astype(jnp.int32)
    need = need[places[:2] - SPAN][:, places]

    state = attention(
        need[:, :NEAR], places[:NEAR], segs, query_segs, (own_q, other_q), near, None, None, False
    )
    far_need, far_places = need[:, NEAR:], places[NEAR:]
    other = attention(
        far_need[1:], far_places, segs, query_segs[1:], (other_q,), far, state, 1, True
    )
    other = swap(other)
    own = attention(
        far_need[:1], far_places, segs, query_segs[:1], (own_q,), far, state, 0, True
    )
    halves = half[None].astype(jnp.int32)
    outgoing = project(halves, meta, own, other, out_weight, tokens, slots, capacity)
    arrived = lax.all_to_all(outgoing, "blk", split_axis=0, concat_axis=0, tiled=True)
    return place(arrived, capacity, 4 * width)


def solution(mesh):
    placed = (
        P("rep"),
        P("rep", None),
        P(("rep", "blk"), None),
        P(("rep", "blk"), None),
        P(("rep", "blk"), None),
        P(("rep", "blk"), None),
        P(),
        P(("rep", "blk")),
        P(("rep", "blk")),
    )
    return jax.shard_map(
        per_device, mesh=mesh, in_specs=placed, out_specs=P(("rep", "blk"), None), check_vma=False
    )
```

```python
import functools

import jax
import jax.numpy as jnp
from jax import lax
from jax.experimental import pallas as pl
from jax.experimental.pallas import tpu as pltpu
from jax.sharding import PartitionSpec as P

HEADS = 8
HALF = HEADS // 2
SPAN = 3
NEG = -1e30
LOG2E = 1.4426950408889634
MIB = 1024 * 1024


def vmem():
    return pl.BlockSpec(memory_space=pltpu.VMEM)


def smem():
    return pl.BlockSpec(memory_space=pltpu.SMEM)


def anywhere():
    return pl.BlockSpec(memory_space=pl.ANY)


def limit(mib):
    return pltpu.CompilerParams(vmem_limit_bytes=mib * MIB)


def prepare_kernel(
    pair_rows, where_ref, owners_ref, offsets_ref, q_hbm, k_hbm, v_hbm,
    own_q, own_kv, swap_q, swap_kv, meta_ref, held, turned, sems,
):
    rows, features = q_hbm.shape
    part = features // 2
    mrows = rows // 4
    loads = [
        pltpu.make_async_copy(ref, held.at[i], sems.at[i])
        for i, ref in enumerate((k_hbm, v_hbm, q_hbm))
    ]
    for load in loads:
        load.start()

    owner = jnp.broadcast_to(owners_ref[...].astype(jnp.float32), (mrows, mrows))
    earlier = lax.broadcasted_iota(jnp.int32, (mrows, mrows), 0)
    later = lax.broadcasted_iota(jnp.int32, (mrows, mrows), 1)
    column = jnp.sum(jnp.where(earlier == later, owner, 0.0), axis=1, keepdims=True)
    ahead = jnp.where((owner == column) & (earlier < later), 1.0, 0.0)
    slot = owner[:1] * pair_rows + jnp.sum(ahead, axis=0, keepdims=True)
    line = lax.broadcasted_iota(jnp.int32, (8, mrows), 0)
    offset = offsets_ref[...].astype(jnp.float32)
    meta = jnp.where(line == 0, slot, jnp.where(line == 1, offset, 0.0))
    row = lax.broadcasted_iota(jnp.int32, (mrows, rows), 0)
    patch = lax.broadcasted_iota(jnp.int32, (mrows, rows), 1)
    spread = jnp.where(patch // 4 == row, 1.0, 0.0).astype(jnp.bfloat16)
    meta_ref[...] = jnp.dot(
        meta.astype(jnp.bfloat16), spread, preferred_element_type=jnp.float32
    )

    half = where_ref[0] % 2
    mine = pl.multiple_of(half * part, 16)
    other = pl.multiple_of((1 - half) * part, 16)
    for i in range(3):
        loads[i].wait()
        turned[i] = held[i].T
        if i < 2:
            own_kv[i * part : (i + 1) * part, :] = turned[i, pl.ds(mine, part), :]
            swap_kv[i * part : (i + 1) * part, :] = turned[i, pl.ds(other, part), :]
        else:
            own_q[...] = turned[i, pl.ds(mine, part), :]
            swap_q[...] = turned[i, pl.ds(other, part), :]


def prepare(where, owners, offsets, queries, keys, values, pair_rows):
    rows, features = queries.shape
    part = features // 2
    single = jax.ShapeDtypeStruct((part, rows), queries.dtype)
    double = jax.ShapeDtypeStruct((2 * part, rows), queries.dtype)
    return pl.pallas_call(
        functools.partial(prepare_kernel, pair_rows),
        out_shape=[single, double, single, double, jax.ShapeDtypeStruct((8, rows), jnp.float32)],
        in_specs=[smem()] + [vmem()] * 2 + [anywhere()] * 3,
        out_specs=[vmem()] * 5,
        scratch_shapes=[
            pltpu.VMEM((3, rows, features), queries.dtype),
            pltpu.VMEM((3, features, rows), queries.dtype),
            pltpu.SemaphoreType.DMA((3,)),
        ],
        compiler_params=limit(60),
    )(where, owners, offsets, queries, keys, values)


PLACES = ((3, 1), (4, -1), (5, -3), (1, 5), (6, -5), (2, 3), (7, -7), (0, 7))


def attention_kernel(kinds, numbers, which, ends, where_ref, mask_ref, seg_ref, *refs):
    queries, refs = refs[: len(kinds)], refs[len(kinds) :]
    blocks, refs = refs[: len(numbers)], refs[len(numbers) :]
    follows = which is not None
    if follows:
        before, refs = refs[0], refs[1:]
    out_ref, query_s, key_s, value_s, chosen_s = refs
    part, rows = queries[0].shape
    hdim = part // HALF
    wide = value_s.shape[2]
    nblocks = mask_ref.shape[0]
    factor = LOG2E / (hdim**0.5)
    me = where_ref[0]
    half = me % 2
    column = [me - half - SPAN + PLACES[b][0] + PLACES[b][1] * half for b in numbers]
    asker = [me if kind == 0 else me + 1 - 2 * half for kind in kinds]

    def needed(n, b):
        inside = (column[b] >= 0) & (column[b] < nblocks)
        inside &= jnp.abs(column[b] - asker[n]) <= SPAN
        allowed = mask_ref[asker[n], jnp.clip(column[b], 0, nblocks - 1)] > 0
        return (inside & allowed).astype(jnp.int32)

    need = [[needed(n, b) for b in range(len(numbers))] for n in range(len(kinds))]

    def segment(block):
        start = pl.multiple_of(jnp.clip(block, 0, nblocks - 1) * rows, 128)
        return seg_ref[:, pl.ds(start, rows)].astype(jnp.float32)

    for b in range(len(numbers)):
        wanted = need[0][b]
        for n in range(1, len(kinds)):
            wanted = wanted + need[n][b]

        @pl.when(wanted > 0)
        def _(b=b):
            key_s[b] = blocks[b][:part, :]
            for h in range(HALF):
                lines = slice(part + h * hdim, part + (h + 1) * hdim)
                value_s[b, h, :hdim, :] = blocks[b][lines, :]
                value_s[b, h, hdim:, :] = jnp.ones((wide - hdim, rows), jnp.bfloat16)

    for n in range(len(kinds)):
        size = 0
        for b in range(len(numbers)):
            chosen_s[size] = b
            size = size + need[n][b]
        for h in range(HALF):
            query_s[h] = queries[n][h * hdim : (h + 1) * hdim, :].T
        query_seg = jnp.broadcast_to(segment(asker[n]), (128, rows)).T
        query_seg = jnp.concatenate([query_seg] * (rows // 128), axis=1)

        def finish(h, peak, accum, n=n):
            if ends:
                turned = accum.T
                lines = pl.ds(pl.multiple_of(h * hdim, 16), hdim)
                out_ref[lines, :] = (turned[:hdim] / turned[hdim : hdim + 1]).astype(out_ref.dtype)
            else:
                peak = jnp.broadcast_to(peak, (rows, 128 - wide))
                out_ref[n, h] = jnp.concatenate([accum, peak], axis=1)

        if follows:

            @pl.when(size == 0)
            def _():
                def one_head(h, carry):
                    state = before[which, h]
                    finish(h, state[:, wide : wide + 1], state[:, :wide])
                    return carry

                lax.fori_loop(0, HALF, one_head, 0)

        for fixed in range(1, len(numbers) + 1):

            @pl.when(size == fixed)
            def _():
                picked = [chosen_s[b] for b in range(fixed)]
                key_segs = [
                    segment(sum(jnp.where(b == i, column[i], 0) for i in range(len(numbers))))
                    for b in picked
                ]

                def one_head(h):
                    lines = pl.ds(pl.multiple_of(h * hdim, 16), hdim)
                    query = query_s[h]
                    scores = []
                    for b, key_seg in zip(picked, key_segs):
                        score = jnp.dot(
                            query, key_s[b, lines, :], preferred_element_type=jnp.float32
                        )
                        scores.append(jnp.where(query_seg == key_seg, score, NEG))
                    peak = functools.reduce(jnp.maximum, scores)
                    peak = jnp.max(peak, axis=1, keepdims=True)
                    accum = jnp.zeros((rows, wide), jnp.float32)
                    if follows:
                        state = before[which, h]
                        old = state[:, wide : wide + 1]
                        peak = jnp.maximum(peak, old)
                        accum = state[:, :wide] * jnp.exp2((old - peak) * factor)
                    for b, score in zip(picked, scores):
                        weights = jnp.exp2((score - peak) * factor).astype(jnp.bfloat16)
                        accum += lax.dot_general(
                            weights,
                            value_s[b, h],
                            (((1,), (1,)), ((), ())),
                            preferred_element_type=jnp.float32,
                        )
                    finish(h, peak, accum)

                def two_heads(i, carry):
                    one_head(2 * i)
                    one_head(2 * i + 1)
                    return carry

                lax.fori_loop(0, HALF // 2, two_heads, 0)


def attention(where, mask, segs, queries, kinds, blocks, numbers, before, which, ends):
    part, rows = queries[0].shape
    hdim = part // HALF
    wide = hdim + 16
    if ends:
        out = jax.ShapeDtypeStruct((part, rows), jnp.bfloat16)
    else:
        out = jax.ShapeDtypeStruct((len(kinds), HALF, rows, 128), jnp.float32)
    return pl.pallas_call(
        functools.partial(attention_kernel, kinds, numbers, which, ends),
        out_shape=out,
        in_specs=[smem()] * 2
        + [vmem()] * (1 + len(kinds) + len(numbers) + (which is not None)),
        out_specs=vmem(),
        scratch_shapes=[
            pltpu.VMEM((HALF, rows, hdim), jnp.bfloat16),
            pltpu.VMEM((len(numbers), part, rows), jnp.bfloat16),
            pltpu.VMEM((len(numbers), HALF, wide, rows), jnp.bfloat16),
            pltpu.SMEM((len(numbers) + 1,), jnp.int32),
        ],
        compiler_params=limit(16),
        cost_estimate=pl.CostEstimate(
            flops=2_000_000_000 * len(kinds), bytes_accessed=2_000_000, transcendentals=1_000_000
        ),
    )(where, mask, segs, *queries, *blocks, *(() if which is None else (before,)))


def project_kernel(
    capacity, where_ref, meta_ref, own_ref, other_ref, weight_ref, tokens_ref, out_ref
):
    slots = out_ref.shape[0]
    rows, width = tokens_ref.shape
    part = own_ref.shape[0]
    half = where_ref[0] % 2
    hidden = tokens_ref[...].astype(jnp.float32)
    for ref, which in ((own_ref, half), (other_ref, 1 - half)):
        hidden += lax.dot_general(
            ref[...],
            weight_ref[pl.ds(pl.multiple_of(which * part, 16), part), :],
            (((0,), (0,)), ((), ())),
            preferred_element_type=jnp.float32,
        )
    hidden = hidden.astype(jnp.bfloat16)
    slot = lax.broadcasted_iota(jnp.int32, (slots, rows), 0).astype(jnp.float32)
    quarter = lax.broadcasted_iota(jnp.int32, (1, rows), 1) % 4
    for j in range(4):
        mine = jnp.where(quarter == j, meta_ref[:1], -1.0) == slot
        if j == 0:
            offset = jnp.where(mine, meta_ref[1:2] - capacity, 0.0)
            offset = capacity + jnp.sum(offset, axis=1, keepdims=True)
            out_ref[:, 4 * width :] = jnp.broadcast_to(offset, (slots, 128)).astype(jnp.bfloat16)
        pick = jnp.where(mine, 1.0, 0.0).astype(jnp.bfloat16)
        out_ref[:, j * width : (j + 1) * width] = jnp.dot(
            pick, hidden, preferred_element_type=jnp.float32
        ).astype(jnp.bfloat16)


def project(where, meta, own, other, out_weight, tokens, slots, capacity):
    rows, width = tokens.shape
    return pl.pallas_call(
        functools.partial(project_kernel, float(capacity)),
        out_shape=jax.ShapeDtypeStruct((slots, 4 * width + 128), jnp.bfloat16),
        in_specs=[smem()] + [vmem()] * 5,
        out_specs=vmem(),
        compiler_params=limit(24),
    )(where, meta, own, other, out_weight, tokens)


def place_kernel(arrived_ref, out_hbm, held, sems):
    capacity, merged = out_hbm.shape
    slots = arrived_ref.shape[0]
    step = merged // 4
    row = lax.broadcasted_iota(jnp.int32, (slots, capacity), 1).astype(jnp.float32)
    offset = arrived_ref[:, merged : merged + 128].astype(jnp.float32)[:, :1]
    pick = jnp.where(offset == row, 1.0, 0.0).astype(jnp.bfloat16)
    stores = []
    for j in range(4):
        columns = slice(j * step, (j + 1) * step)
        held[j] = lax.dot_general(
            pick,
            arrived_ref[:, columns],
            (((0,), (0,)), ((), ())),
            preferred_element_type=jnp.float32,
        ).astype(jnp.bfloat16)
        stores.append(pltpu.make_async_copy(held.at[j], out_hbm.at[:, columns], sems.at[j]))
        stores[j].start()
    for store in stores:
        store.wait()


def place(arrived, capacity, merged):
    return pl.pallas_call(
        place_kernel,
        out_shape=jax.ShapeDtypeStruct((capacity, merged), jnp.bfloat16),
        in_specs=[vmem()],
        out_specs=anywhere(),
        scratch_shapes=[
            pltpu.VMEM((4, capacity, merged // 4), jnp.bfloat16),
            pltpu.SemaphoreType.DMA((4,)),
        ],
        compiler_params=limit(24),
    )(arrived)


def per_device(segment_ids, block_mask, queries, keys, values, tokens, out_weight, owners, offsets):
    rows = queries.shape[0]
    width = tokens.shape[1]
    nblocks = lax.axis_size("blk")
    block_index = lax.axis_index("blk")
    mrows = rows // 4
    capacity = 2 * mrows
    pair_rows = max(2, 2 * mrows // nblocks)
    slots = nblocks * pair_rows
    assert slots <= 256

    def route(step):
        return [(i, i + step(i)) for i in range(nblocks) if 0 <= i + step(i) < nblocks]

    swap = functools.partial(
        lax.ppermute, axis_name="blk", perm=route(lambda i: 1 - 2 * (i % 2))
    )
    ahead = functools.partial(
        lax.ppermute, axis_name="blk", perm=route(lambda i: 2 if i % 2 else -2)
    )
    back = functools.partial(
        lax.ppermute, axis_name="blk", perm=route(lambda i: -2 if i % 2 else 2)
    )

    where = block_index[None].astype(jnp.int32)
    own_q, own_kv, swap_q, swap_kv, meta = prepare(
        where, owners[None, :], offsets[None, :], queries, keys, values, pair_rows
    )
    other_kv = swap(swap_kv)
    ahead_own = ahead(own_kv)
    back_own = back(own_kv)
    other_q = swap(swap_q)
    back_other = back(other_kv)
    ahead_other = ahead(other_kv)
    ahead_far = ahead(ahead_own)
    back_far = back(back_other)
    near = (own_kv, other_kv, ahead_own, back_own)
    far = (ahead_other, back_other, ahead_far, back_far)

    fixed = (where, block_mask, segment_ids[None, :])
    state = attention(*fixed, (own_q, other_q), (0, 1), near, (0, 1, 2, 3), None, None, False)
    other = attention(*fixed, (other_q,), (1,), far, (4, 5, 6, 7), state, 1, True)
    other = swap(other)
    own = attention(*fixed, (own_q,), (0,), far, (4, 5, 6, 7), state, 0, True)
    outgoing = project(where, meta, own, other, out_weight, tokens, slots, capacity)
    arrived = lax.all_to_all(outgoing, "blk", split_axis=0, concat_axis=0, tiled=True)
    return place(arrived, capacity, 4 * width)


def solution(mesh):
    placed = (
        P("rep"),
        P("rep", None),
        P(("rep", "blk"), None),
        P(("rep", "blk"), None),
        P(("rep", "blk"), None),
        P(("rep", "blk"), None),
        P(),
        P(("rep", "blk")),
        P(("rep", "blk")),
    )
    return jax.shard_map(
        per_device, mesh=mesh, in_specs=placed, out_specs=P(("rep", "blk"), None), check_vma=False
    )
```

```python
import functools

import jax
import jax.numpy as jnp
from jax import lax
from jax.experimental import pallas as pl
from jax.experimental.pallas import tpu as pltpu
from jax.sharding import PartitionSpec as P

HEADS = 8
HALF = HEADS // 2
SPAN = 3
NEG = -1e30
LOG2E = 1.4426950408889634
MIB = 1024 * 1024


def vmem():
    return pl.BlockSpec(memory_space=pltpu.VMEM)


def smem():
    return pl.BlockSpec(memory_space=pltpu.SMEM)


def anywhere():
    return pl.BlockSpec(memory_space=pl.ANY)


def limit(mib):
    return pltpu.CompilerParams(vmem_limit_bytes=mib * MIB)


def prepare_kernel(where_ref, q_hbm, k_hbm, v_hbm, own_q, own_kv, swap_q, swap_kv, held, turned, sems):
    part = q_hbm.shape[1] // 2
    loads = [
        pltpu.make_async_copy(ref, held.at[i], sems.at[i])
        for i, ref in enumerate((k_hbm, v_hbm, q_hbm))
    ]
    for load in loads:
        load.start()
    half = where_ref[0] % 2
    mine = pl.multiple_of(half * part, 16)
    other = pl.multiple_of((1 - half) * part, 16)
    for i in range(3):
        loads[i].wait()
        turned[i] = held[i].T
        if i < 2:
            own_kv[i * part : (i + 1) * part, :] = turned[i, pl.ds(mine, part), :]
            swap_kv[i * part : (i + 1) * part, :] = turned[i, pl.ds(other, part), :]
        else:
            own_q[...] = turned[i, pl.ds(mine, part), :]
            swap_q[...] = turned[i, pl.ds(other, part), :]


def prepare(where, queries, keys, values):
    rows, features = queries.shape
    part = features // 2
    single = jax.ShapeDtypeStruct((part, rows), queries.dtype)
    double = jax.ShapeDtypeStruct((2 * part, rows), queries.dtype)
    return pl.pallas_call(
        prepare_kernel,
        out_shape=[single, double, single, double],
        in_specs=[smem()] + [anywhere()] * 3,
        out_specs=[vmem()] * 4,
        scratch_shapes=[
            pltpu.VMEM((3, rows, features), queries.dtype),
            pltpu.VMEM((3, features, rows), queries.dtype),
            pltpu.SemaphoreType.DMA((3,)),
        ],
        compiler_params=limit(53),
    )(where, queries, keys, values)


PLACES = ((3, 1), (4, -1), (5, -3), (1, 5), (6, -5), (2, 3), (7, -7), (0, 7))


def attention_kernel(kinds, numbers, which, ends, where_ref, mask_ref, seg_ref, *refs):
    queries, refs = refs[: len(kinds)], refs[len(kinds) :]
    blocks, refs = refs[: len(numbers)], refs[len(numbers) :]
    follows = which is not None
    if follows:
        before, refs = refs[0], refs[1:]
    out_ref, query_s, key_s, value_s, chosen_s = refs
    part, rows = queries[0].shape
    hdim = part // HALF
    wide = value_s.shape[2]
    nblocks = mask_ref.shape[0]
    factor = LOG2E / (hdim**0.5)
    me = where_ref[0]
    half = me % 2
    column = [me - half - SPAN + PLACES[b][0] + PLACES[b][1] * half for b in numbers]
    asker = [me if kind == 0 else me + 1 - 2 * half for kind in kinds]

    def needed(n, b):
        inside = (column[b] >= 0) & (column[b] < nblocks)
        inside &= jnp.abs(column[b] - asker[n]) <= SPAN
        allowed = mask_ref[asker[n], jnp.clip(column[b], 0, nblocks - 1)] > 0
        return (inside & allowed).astype(jnp.int32)

    need = [[needed(n, b) for b in range(len(numbers))] for n in range(len(kinds))]

    def segment(block):
        start = pl.multiple_of(jnp.clip(block, 0, nblocks - 1) * rows, 128)
        return seg_ref[:, pl.ds(start, rows)].astype(jnp.float32)

    for b in range(len(numbers)):
        wanted = need[0][b]
        for n in range(1, len(kinds)):
            wanted = wanted + need[n][b]

        @pl.when(wanted > 0)
        def _(b=b):
            key_s[b] = blocks[b][:part, :]
            for h in range(HALF):
                lines = slice(part + h * hdim, part + (h + 1) * hdim)
                value_s[b, h, :hdim, :] = blocks[b][lines, :]
                value_s[b, h, hdim:, :] = jnp.ones((wide - hdim, rows), jnp.bfloat16)

    for n in range(len(kinds)):
        size = 0
        for b in range(len(numbers)):
            chosen_s[size] = b
            size = size + need[n][b]
        for h in range(HALF):
            query_s[h] = queries[n][h * hdim : (h + 1) * hdim, :].T
        query_seg = jnp.broadcast_to(segment(asker[n]), (128, rows)).T
        query_seg = jnp.concatenate([query_seg] * (rows // 128), axis=1)

        def finish(h, peak, accum, n=n):
            if ends:
                turned = accum.T
                lines = pl.ds(pl.multiple_of(h * hdim, 16), hdim)
                out_ref[lines, :] = (turned[:hdim] / turned[hdim : hdim + 1]).astype(out_ref.dtype)
            else:
                peak = jnp.broadcast_to(peak, (rows, 128 - wide))
                out_ref[n, h] = jnp.concatenate([accum, peak], axis=1)

        if follows:

            @pl.when(size == 0)
            def _():
                def one_head(h, carry):
                    state = before[which, h]
                    finish(h, state[:, wide : wide + 1], state[:, :wide])
                    return carry

                lax.fori_loop(0, HALF, one_head, 0)

        for fixed in range(1, len(numbers) + 1):

            @pl.when(size == fixed)
            def _():
                picked = [chosen_s[b] for b in range(fixed)]
                key_segs = [
                    segment(sum(jnp.where(b == i, column[i], 0) for i in range(len(numbers))))
                    for b in picked
                ]

                def one_head(h):
                    lines = pl.ds(pl.multiple_of(h * hdim, 16), hdim)
                    query = query_s[h]
                    scores = []
                    for b, key_seg in zip(picked, key_segs):
                        score = jnp.dot(
                            query, key_s[b, lines, :], preferred_element_type=jnp.float32
                        )
                        scores.append(jnp.where(query_seg == key_seg, score, NEG))
                    peak = functools.reduce(jnp.maximum, scores)
                    peak = jnp.max(peak, axis=1, keepdims=True)
                    accum = jnp.zeros((rows, wide), jnp.float32)
                    if follows:
                        state = before[which, h]
                        old = state[:, wide : wide + 1]
                        peak = jnp.maximum(peak, old)
                        accum = state[:, :wide] * jnp.exp2((old - peak) * factor)
                    for b, score in zip(picked, scores):
                        weights = jnp.exp2((score - peak) * factor).astype(jnp.bfloat16)
                        accum += lax.dot_general(
                            weights,
                            value_s[b, h],
                            (((1,), (1,)), ((), ())),
                            preferred_element_type=jnp.float32,
                        )
                    finish(h, peak, accum)

                def two_heads(i, carry):
                    one_head(2 * i)
                    one_head(2 * i + 1)
                    return carry

                lax.fori_loop(0, HALF // 2, two_heads, 0)


def attention(where, mask, segs, queries, kinds, blocks, numbers, before, which, ends):
    part, rows = queries[0].shape
    hdim = part // HALF
    wide = hdim + 16
    if ends:
        out = jax.ShapeDtypeStruct((part, rows), jnp.bfloat16)
    else:
        out = jax.ShapeDtypeStruct((len(kinds), HALF, rows, 128), jnp.float32)
    return pl.pallas_call(
        functools.partial(attention_kernel, kinds, numbers, which, ends),
        out_shape=out,
        in_specs=[smem()] * 2
        + [vmem()] * (1 + len(kinds) + len(numbers) + (which is not None)),
        out_specs=vmem(),
        scratch_shapes=[
            pltpu.VMEM((HALF, rows, hdim), jnp.bfloat16),
            pltpu.VMEM((len(numbers), part, rows), jnp.bfloat16),
            pltpu.VMEM((len(numbers), HALF, wide, rows), jnp.bfloat16),
            pltpu.SMEM((len(numbers) + 1,), jnp.int32),
        ],
        compiler_params=limit(16),
        cost_estimate=pl.CostEstimate(
            flops=2_000_000_000 * len(kinds), bytes_accessed=2_000_000, transcendentals=1_000_000
        ),
    )(where, mask, segs, *queries, *blocks, *(() if which is None else (before,)))


def project_kernel(
    pair_rows, where_ref, owners_ref, offsets_ref, own_ref, other_ref, weight_ref, tokens_ref, out_ref
):
    slots = out_ref.shape[0]
    rows, width = tokens_ref.shape
    mrows = rows // 4
    capacity = 2 * mrows
    owner = jnp.broadcast_to(owners_ref[...].astype(jnp.float32), (mrows, mrows))
    earlier = lax.broadcasted_iota(jnp.int32, (mrows, mrows), 0)
    later = lax.broadcasted_iota(jnp.int32, (mrows, mrows), 1)
    column = jnp.sum(jnp.where(earlier == later, owner, 0.0), axis=1, keepdims=True)
    ahead = jnp.where((owner == column) & (earlier < later), 1.0, 0.0)
    slot = owner[:1] * pair_rows + jnp.sum(ahead, axis=0, keepdims=True)
    line = lax.broadcasted_iota(jnp.int32, (16, mrows), 0)
    meta = jnp.where(line == 0, slot, jnp.where(line == 1, offsets_ref[...].astype(jnp.float32), 0.0))
    row = lax.broadcasted_iota(jnp.int32, (mrows, rows), 0)
    patch = lax.broadcasted_iota(jnp.int32, (mrows, rows), 1)
    spread = jnp.where(patch // 4 == row, 1.0, 0.0).astype(jnp.bfloat16)
    meta = jnp.dot(meta.astype(jnp.bfloat16), spread, preferred_element_type=jnp.float32)
    part = own_ref.shape[0]
    half = where_ref[0] % 2
    hidden = tokens_ref[...].astype(jnp.float32)
    for ref, which in ((own_ref, half), (other_ref, 1 - half)):
        hidden += lax.dot_general(
            ref[...],
            weight_ref[pl.ds(pl.multiple_of(which * part, 16), part), :],
            (((0,), (0,)), ((), ())),
            preferred_element_type=jnp.float32,
        )
    hidden = hidden.astype(jnp.bfloat16)
    slot = lax.broadcasted_iota(jnp.int32, (slots, rows), 0).astype(jnp.float32)
    quarter = lax.broadcasted_iota(jnp.int32, (1, rows), 1) % 4
    for j in range(4):
        mine = jnp.where(quarter == j, meta[:1], -1.0) == slot
        if j == 0:
            offset = jnp.where(mine, meta[1:2] - capacity, 0.0)
            offset = capacity + jnp.sum(offset, axis=1, keepdims=True)
            out_ref[:, 4 * width :] = jnp.broadcast_to(offset, (slots, 128)).astype(jnp.bfloat16)
        pick = jnp.where(mine, 1.0, 0.0).astype(jnp.bfloat16)
        out_ref[:, j * width : (j + 1) * width] = jnp.dot(
            pick, hidden, preferred_element_type=jnp.float32
        ).astype(jnp.bfloat16)


def project(where, owners, offsets, own, other, out_weight, tokens, slots, pair_rows):
    rows, width = tokens.shape
    return pl.pallas_call(
        functools.partial(project_kernel, pair_rows),
        out_shape=jax.ShapeDtypeStruct((slots, 4 * width + 128), jnp.bfloat16),
        in_specs=[smem()] + [vmem()] * 6,
        out_specs=vmem(),
        compiler_params=limit(24),
    )(where, owners, offsets, own, other, out_weight, tokens)


def place_kernel(arrived_ref, out_hbm, held, sems):
    capacity, merged = out_hbm.shape
    slots = arrived_ref.shape[0]
    step = merged // 4
    row = lax.broadcasted_iota(jnp.int32, (slots, capacity), 1).astype(jnp.float32)
    offset = arrived_ref[:, merged : merged + 128].astype(jnp.float32)[:, :1]
    pick = jnp.where(offset == row, 1.0, 0.0).astype(jnp.bfloat16)
    stores = []
    for j in range(4):
        columns = slice(j * step, (j + 1) * step)
        held[j] = lax.dot_general(
            pick,
            arrived_ref[:, columns],
            (((0,), (0,)), ((), ())),
            preferred_element_type=jnp.float32,
        ).astype(jnp.bfloat16)
        stores.append(pltpu.make_async_copy(held.at[j], out_hbm.at[:, columns], sems.at[j]))
        stores[j].start()
    for store in stores:
        store.wait()


def place(arrived, capacity, merged):
    return pl.pallas_call(
        place_kernel,
        out_shape=jax.ShapeDtypeStruct((capacity, merged), jnp.bfloat16),
        in_specs=[vmem()],
        out_specs=anywhere(),
        scratch_shapes=[
            pltpu.VMEM((4, capacity, merged // 4), jnp.bfloat16),
            pltpu.SemaphoreType.DMA((4,)),
        ],
        compiler_params=limit(24),
    )(arrived)


def per_device(segment_ids, block_mask, queries, keys, values, tokens, out_weight, owners, offsets):
    rows = queries.shape[0]
    width = tokens.shape[1]
    nblocks = lax.axis_size("blk")
    block_index = lax.axis_index("blk")
    mrows = rows // 4
    capacity = 2 * mrows
    pair_rows = max(2, 2 * mrows // nblocks)
    slots = nblocks * pair_rows
    assert slots <= 256

    def route(step):
        return [(i, i + step(i)) for i in range(nblocks) if 0 <= i + step(i) < nblocks]

    swap = functools.partial(
        lax.ppermute, axis_name="blk", perm=route(lambda i: 1 - 2 * (i % 2))
    )
    ahead = functools.partial(
        lax.ppermute, axis_name="blk", perm=route(lambda i: 2 if i % 2 else -2)
    )
    back = functools.partial(
        lax.ppermute, axis_name="blk", perm=route(lambda i: -2 if i % 2 else 2)
    )

    where = block_index[None].astype(jnp.int32)
    own_q, own_kv, swap_q, swap_kv = prepare(where, queries, keys, values)
    other_kv = swap(swap_kv)
    ahead_own = ahead(own_kv)
    back_own = back(own_kv)
    other_q = swap(swap_q)
    ready, back_own = lax.optimization_barrier((other_kv, back_own))
    back_other = back(ready)
    ahead_other = ahead(other_kv)
    ahead_far = ahead(ahead_own)
    back_far = back(back_other)
    near = (own_kv, other_kv, ahead_own, back_own)
    far = (ahead_other, back_other, ahead_far, back_far)

    fixed = (where, block_mask, segment_ids[None, :])
    state = attention(*fixed, (own_q, other_q), (0, 1), near, (0, 1, 2, 3), None, None, False)
    other = attention(*fixed, (other_q,), (1,), far, (4, 5, 6, 7), state, 1, True)
    other = swap(other)
    own = attention(*fixed, (own_q,), (0,), far, (4, 5, 6, 7), state, 0, True)
    outgoing = project(
        where, owners[None, :], offsets[None, :], own, other, out_weight, tokens, slots, pair_rows
    )
    arrived = lax.all_to_all(outgoing, "blk", split_axis=0, concat_axis=0, tiled=True)
    return place(arrived, capacity, 4 * width)


def solution(mesh):
    placed = (
        P("rep"),
        P("rep", None),
        P(("rep", "blk"), None),
        P(("rep", "blk"), None),
        P(("rep", "blk"), None),
        P(("rep", "blk"), None),
        P(),
        P(("rep", "blk")),
        P(("rep", "blk")),
    )
    return jax.shard_map(
        per_device, mesh=mesh, in_specs=placed, out_specs=P(("rep", "blk"), None), check_vma=False
    )
```

```python
import functools

import jax
import jax.numpy as jnp
from jax import lax
from jax.experimental import pallas as pl
from jax.experimental.pallas import tpu as pltpu
from jax.sharding import PartitionSpec as P

HEADS = 8
HALF = HEADS // 2
SPAN = 3
NEG = -1e30
LOG2E = 1.4426950408889634
MIB = 1024 * 1024


def vmem():
    return pl.BlockSpec(memory_space=pltpu.VMEM)


def smem():
    return pl.BlockSpec(memory_space=pltpu.SMEM)


def anywhere():
    return pl.BlockSpec(memory_space=pl.ANY)


def limit(mib):
    return pltpu.CompilerParams(vmem_limit_bytes=mib * MIB)


PLACES = ((3, 1), (4, -1), (5, -3), (1, 5), (6, -5), (2, 3), (7, -7), (0, 7))


def asking(me, kind):
    return me if kind == 0 else me + 1 - 2 * (me % 2)


def key_block(me, number):
    half = me % 2
    return me - half - SPAN + PLACES[number][0] + PLACES[number][1] * half


def prepare_kernel(where_ref, q_hbm, k_hbm, v_hbm, own_q, own_kv, swap_q, swap_kv, held, turned, sems):
    part = q_hbm.shape[1] // 2
    loads = [
        pltpu.make_async_copy(ref, held.at[i], sems.at[i])
        for i, ref in enumerate((k_hbm, v_hbm, q_hbm))
    ]
    for load in loads:
        load.start()
    me = where_ref[0]
    half = me % 2
    mine = pl.multiple_of(half * part, 16)
    other = pl.multiple_of((1 - half) * part, 16)
    for i in range(3):
        loads[i].wait()
        turned[i] = held[i].T
        if i < 2:
            own_kv[i * part : (i + 1) * part, :] = turned[i, pl.ds(mine, part), :]
            swap_kv[i * part : (i + 1) * part, :] = turned[i, pl.ds(other, part), :]
        else:
            own_q[...] = turned[i, pl.ds(mine, part), :]
            swap_q[...] = turned[i, pl.ds(other, part), :]


def prepare(where, queries, keys, values):
    rows, features = queries.shape
    part = features // 2
    single = jax.ShapeDtypeStruct((part, rows), queries.dtype)
    double = jax.ShapeDtypeStruct((2 * part, rows), queries.dtype)
    return pl.pallas_call(
        prepare_kernel,
        out_shape=[single, double, single, double],
        in_specs=[smem()] + [anywhere()] * 3,
        out_specs=[vmem()] * 4,
        scratch_shapes=[
            pltpu.VMEM((3, rows, features), queries.dtype),
            pltpu.VMEM((3, features, rows), queries.dtype),
            pltpu.SemaphoreType.DMA((3,)),
        ],
        compiler_params=limit(53),
    )(where, queries, keys, values)


def survey_kernel(where_ref, mask_ref, segs_ref, seg_out, need_out):
    seg_out[...] = segs_ref[...].astype(jnp.float32)
    me = where_ref[0]
    nblocks = mask_ref.shape[0]
    bits = jnp.int32(0)
    for kind in range(2):
        asker = asking(me, kind)
        for number in range(len(PLACES)):
            block = key_block(me, number)
            inside = (block >= 0) & (block < nblocks) & (jnp.abs(block - asker) <= SPAN)
            allowed = mask_ref[asker, jnp.clip(block, 0, nblocks - 1)] > 0
            bits += (inside & allowed).astype(jnp.int32) << (kind * len(PLACES) + number)
    need_out[...] = jnp.full(need_out.shape, bits, jnp.int32)


def survey(where, mask, segs):
    return pl.pallas_call(
        survey_kernel,
        out_shape=[
            jax.ShapeDtypeStruct(segs.shape, jnp.float32),
            jax.ShapeDtypeStruct((8, 128), jnp.int32),
        ],
        in_specs=[smem()] * 2 + [vmem()],
        out_specs=[vmem()] * 2,
        compiler_params=limit(16),
    )(where, mask, segs)


def attention_kernel(kinds, numbers, follows, ends, where_ref, need_ref, seg_ref, *refs):
    queries, refs = refs[: len(kinds)], refs[len(kinds) :]
    blocks, refs = refs[: len(numbers)], refs[len(numbers) :]
    if follows:
        before, refs = refs[0], refs[1:]
    out_ref, query_s, key_s, value_s, chosen_s = refs
    part, rows = queries[0].shape
    hdim = part // HALF
    wide = value_s.shape[2]
    nblocks = seg_ref.shape[1] // rows
    factor = LOG2E / (hdim**0.5)
    me = where_ref[0]
    column = [key_block(me, b) for b in numbers]
    asker = [asking(me, kind) for kind in kinds]
    bits = jnp.max(need_ref[...])
    need = [[(bits >> (kind * len(PLACES) + b)) & 1 for b in numbers] for kind in kinds]

    def segment(block):
        start = pl.multiple_of(jnp.clip(block, 0, nblocks - 1) * rows, 128)
        return seg_ref[:, pl.ds(start, rows)]

    for b in range(len(numbers)):
        wanted = need[0][b]
        for n in range(1, len(kinds)):
            wanted = wanted + need[n][b]

        @pl.when(wanted > 0)
        def _(b=b):
            key_s[b] = blocks[b][:part, :]
            for h in range(HALF):
                lines = slice(part + h * hdim, part + (h + 1) * hdim)
                value_s[b, h, :hdim, :] = blocks[b][lines, :]
                value_s[b, h, hdim:, :] = jnp.ones((wide - hdim, rows), jnp.bfloat16)

    for n in range(len(kinds)):
        size = 0
        for b in range(len(numbers)):
            chosen_s[size] = b
            size = size + need[n][b]
        for h in range(HALF):
            query_s[h] = queries[n][h * hdim : (h + 1) * hdim, :].T
        query_seg = jnp.broadcast_to(segment(asker[n]), (128, rows)).T
        query_seg = jnp.concatenate([query_seg] * (rows // 128), axis=1)

        def finish(h, peak, accum, n=n):
            if ends:
                turned = accum.T
                lines = pl.ds(pl.multiple_of(h * hdim, 16), hdim)
                out_ref[lines, :] = (turned[:hdim] / turned[hdim : hdim + 1]).astype(out_ref.dtype)
            else:
                peak = jnp.broadcast_to(peak, (rows, 128 - wide))
                out_ref[n, h] = jnp.concatenate([accum, peak], axis=1)

        if follows:

            @pl.when(size == 0)
            def _():
                def one_head(h, carry):
                    state = before[0, h]
                    finish(h, state[:, wide : wide + 1], state[:, :wide])
                    return carry

                lax.fori_loop(0, HALF, one_head, 0)

        for fixed in range(1, len(numbers) + 1):

            @pl.when(size == fixed)
            def _():
                picked = [chosen_s[b] for b in range(fixed)]
                key_segs = [
                    segment(sum(jnp.where(b == i, column[i], 0) for i in range(len(numbers))))
                    for b in picked
                ]

                def one_head(h):
                    lines = pl.ds(pl.multiple_of(h * hdim, 16), hdim)
                    query = query_s[h]
                    scores = []
                    for b, key_seg in zip(picked, key_segs):
                        score = jnp.dot(
                            query, key_s[b, lines, :], preferred_element_type=jnp.float32
                        )
                        scores.append(jnp.where(query_seg == key_seg, score, NEG))
                    peak = functools.reduce(jnp.maximum, scores)
                    peak = jnp.max(peak, axis=1, keepdims=True)
                    accum = jnp.zeros((rows, wide), jnp.float32)
                    if follows:
                        state = before[0, h]
                        old = state[:, wide : wide + 1]
                        peak = jnp.maximum(peak, old)
                        accum = state[:, :wide] * jnp.exp2((old - peak) * factor)
                    for b, score in zip(picked, scores):
                        weights = jnp.exp2((score - peak) * factor).astype(jnp.bfloat16)
                        accum += lax.dot_general(
                            weights,
                            value_s[b, h],
                            (((1,), (1,)), ((), ())),
                            preferred_element_type=jnp.float32,
                        )
                    finish(h, peak, accum)

                def two_heads(i, carry):
                    one_head(2 * i)
                    one_head(2 * i + 1)
                    return carry

                lax.fori_loop(0, HALF // 2, two_heads, 0)


def attention(where, need, segs, queries, kinds, blocks, numbers, before, ends):
    part, rows = queries[0].shape
    hdim = part // HALF
    wide = hdim + 16
    follows = before is not None
    if ends:
        out = jax.ShapeDtypeStruct((part, rows), jnp.bfloat16)
    else:
        out = jax.ShapeDtypeStruct((len(kinds), HALF, rows, 128), jnp.float32)
    return pl.pallas_call(
        functools.partial(attention_kernel, kinds, numbers, follows, ends),
        out_shape=out,
        in_specs=[smem()] + [vmem()] * (2 + len(kinds) + len(numbers) + follows),
        out_specs=vmem(),
        scratch_shapes=[
            pltpu.VMEM((HALF, rows, hdim), jnp.bfloat16),
            pltpu.VMEM((len(numbers), part, rows), jnp.bfloat16),
            pltpu.VMEM((len(numbers), HALF, wide, rows), jnp.bfloat16),
            pltpu.SMEM((len(numbers) + 1,), jnp.int32),
        ],
        compiler_params=limit(16),
        cost_estimate=pl.CostEstimate(
            flops=2_000_000_000 * len(kinds), bytes_accessed=2_000_000, transcendentals=1_000_000
        ),
    )(where, need, segs, *queries, *blocks, *((before,) if follows else ()))


def project_kernel(
    pair_rows, where_ref, owners_ref, offsets_ref, own_ref, other_ref, weight_ref, tokens_ref, *outs
):
    piece = outs[0].shape[0]
    slots = piece * len(outs)
    rows, width = tokens_ref.shape
    mrows = rows // 4
    capacity = 2 * mrows
    owner = jnp.broadcast_to(owners_ref[...].astype(jnp.float32), (mrows, mrows))
    earlier = lax.broadcasted_iota(jnp.int32, (mrows, mrows), 0)
    later = lax.broadcasted_iota(jnp.int32, (mrows, mrows), 1)
    column = jnp.sum(jnp.where(earlier == later, owner, 0.0), axis=1, keepdims=True)
    ahead = jnp.where((owner == column) & (earlier < later), 1.0, 0.0)
    slot = owner[:1] * pair_rows + jnp.sum(ahead, axis=0, keepdims=True)
    line = lax.broadcasted_iota(jnp.int32, (16, mrows), 0)
    meta = jnp.where(line == 0, slot, jnp.where(line == 1, offsets_ref[...].astype(jnp.float32), 0.0))
    row = lax.broadcasted_iota(jnp.int32, (mrows, rows), 0)
    patch = lax.broadcasted_iota(jnp.int32, (mrows, rows), 1)
    spread = jnp.where(patch // 4 == row, 1.0, 0.0).astype(jnp.bfloat16)
    meta = jnp.dot(meta.astype(jnp.bfloat16), spread, preferred_element_type=jnp.float32)
    part = own_ref.shape[0]
    half = where_ref[0] % 2
    hidden = tokens_ref[...].astype(jnp.float32)
    for ref, which in ((own_ref, half), (other_ref, 1 - half)):
        hidden += lax.dot_general(
            ref[...],
            weight_ref[pl.ds(pl.multiple_of(which * part, 16), part), :],
            (((0,), (0,)), ((), ())),
            preferred_element_type=jnp.float32,
        )
    hidden = hidden.astype(jnp.bfloat16)
    place = meta[:1]
    if len(outs) > 1:
        place = place - (where_ref[0] * pair_rows).astype(jnp.float32)
        place = jnp.where(place < 0, place + slots, place)
    slot = lax.broadcasted_iota(jnp.int32, (slots, rows), 0).astype(jnp.float32)
    quarter = lax.broadcasted_iota(jnp.int32, (1, rows), 1) % 4
    for j in range(4):
        mine = jnp.where(quarter == j, place, -1.0) == slot
        if j == 0:
            offset = jnp.where(mine, meta[1:2] - capacity, 0.0)
            offset = capacity + jnp.sum(offset, axis=1, keepdims=True)
            offset = jnp.broadcast_to(offset, (slots, 128)).astype(jnp.bfloat16)
            for d, out in enumerate(outs):
                out[:, 4 * width :] = offset[d * piece : (d + 1) * piece]
        pick = jnp.where(mine, 1.0, 0.0).astype(jnp.bfloat16)
        picked = jnp.dot(pick, hidden, preferred_element_type=jnp.float32).astype(jnp.bfloat16)
        for d, out in enumerate(outs):
            out[:, j * width : (j + 1) * width] = picked[d * piece : (d + 1) * piece]


def project(where, owners, offsets, own, other, out_weight, tokens, pieces, slots, pair_rows):
    rows, width = tokens.shape
    return pl.pallas_call(
        functools.partial(project_kernel, pair_rows),
        out_shape=[jax.ShapeDtypeStruct((slots // pieces, 4 * width + 128), jnp.bfloat16)] * pieces,
        in_specs=[smem()] + [vmem()] * 6,
        out_specs=[vmem()] * pieces,
        compiler_params=limit(24),
    )(where, owners, offsets, own, other, out_weight, tokens)


def place_kernel(*refs):
    *arrived, out_hbm, held, sems = refs
    capacity, merged = out_hbm.shape
    step = merged // 4

    def columns_of(start, size):
        return jnp.concatenate([ref[:, start : start + size] for ref in arrived], axis=0)

    offset = columns_of(merged, 128).astype(jnp.float32)[:, :1]
    row = lax.broadcasted_iota(jnp.int32, (offset.shape[0], capacity), 1).astype(jnp.float32)
    pick = jnp.where(offset == row, 1.0, 0.0).astype(jnp.bfloat16)
    stores = []
    for j in range(4):
        held[j] = lax.dot_general(
            pick,
            columns_of(j * step, step),
            (((0,), (0,)), ((), ())),
            preferred_element_type=jnp.float32,
        ).astype(jnp.bfloat16)
        columns = out_hbm.at[:, pl.ds(j * step, step)]
        stores.append(pltpu.make_async_copy(held.at[j], columns, sems.at[j]))
        stores[j].start()
    for store in stores:
        store.wait()


def place(arrived, capacity, merged):
    return pl.pallas_call(
        place_kernel,
        out_shape=jax.ShapeDtypeStruct((capacity, merged), jnp.bfloat16),
        in_specs=[vmem()] * len(arrived),
        out_specs=anywhere(),
        scratch_shapes=[
            pltpu.VMEM((4, capacity, merged // 4), jnp.bfloat16),
            pltpu.SemaphoreType.DMA((4,)),
        ],
        compiler_params=limit(24),
    )(*arrived)


def per_device(segment_ids, block_mask, queries, keys, values, tokens, out_weight, owners, offsets):
    rows = queries.shape[0]
    width = tokens.shape[1]
    nblocks = lax.axis_size("blk")
    block_index = lax.axis_index("blk")
    mrows = rows // 4
    capacity = 2 * mrows
    pair_rows = max(2, 2 * mrows // nblocks)
    slots = nblocks * pair_rows
    assert slots <= 256

    def route(step):
        return [(i, i + step(i)) for i in range(nblocks) if 0 <= i + step(i) < nblocks]

    swap = functools.partial(
        lax.ppermute, axis_name="blk", perm=route(lambda i: 1 - 2 * (i % 2))
    )
    ahead = functools.partial(
        lax.ppermute, axis_name="blk", perm=route(lambda i: 2 if i % 2 else -2)
    )
    back = functools.partial(
        lax.ppermute, axis_name="blk", perm=route(lambda i: -2 if i % 2 else 2)
    )

    where = block_index[None].astype(jnp.int32)
    own_q, own_kv, swap_q, swap_kv = prepare(where, queries, keys, values)
    segs, need = survey(where, block_mask, segment_ids[None, :])
    other_kv = swap(swap_kv)
    ahead_own = ahead(own_kv)
    back_own = back(own_kv)
    other_q = swap(swap_q)
    ready, back_own, segs, need = lax.optimization_barrier((other_kv, back_own, segs, need))
    back_other = back(ready)
    ahead_other = ahead(other_kv)
    ahead_far = ahead(ahead_own)
    near = (own_kv, other_kv, ahead_own, back_own)
    near_numbers, far_numbers = (0, 1, 2, 3), (4, 5, 6, 7)
    fixed = (where, need, segs)
    own = attention(*fixed, (own_q,), (0,), near, near_numbers, None, False)
    back_other, own = lax.optimization_barrier((back_other, own))
    back_far = back(back_other)
    other = attention(*fixed, (other_q,), (1,), near, near_numbers, None, False)
    far = (ahead_other, back_other, ahead_far, back_far)
    other = attention(*fixed, (other_q,), (1,), far, far_numbers, other, True)
    other = swap(other)
    own = attention(*fixed, (own_q,), (0,), far, far_numbers, own, True)

    pieces = nblocks if nblocks <= 8 else 1
    outgoing = project(
        where, owners[None, :], offsets[None, :], own, other, out_weight, tokens,
        pieces, slots, pair_rows,
    )
    if pieces > 1:
        arrived = [outgoing[0]] + [None] * (nblocks - 1)
        order = sorted(range(1, nblocks), key=lambda d: (min(d, nblocks - d) == 2, d))
        for d in order:
            arrived[d] = lax.ppermute(
                outgoing[d], "blk", [(i, (i + d) % nblocks) for i in range(nblocks)]
            )
    else:
        arrived = [lax.all_to_all(outgoing[0], "blk", split_axis=0, concat_axis=0, tiled=True)]
    return place(arrived, capacity, 4 * width)


def solution(mesh):
    placed = (
        P("rep"),
        P("rep", None),
        P(("rep", "blk"), None),
        P(("rep", "blk"), None),
        P(("rep", "blk"), None),
        P(("rep", "blk"), None),
        P(),
        P(("rep", "blk")),
        P(("rep", "blk")),
    )
    return jax.shard_map(
        per_device, mesh=mesh, in_specs=placed, out_specs=P(("rep", "blk"), None), check_vma=False
    )
```

```python
import functools

import jax
import jax.numpy as jnp
from jax import lax
from jax.experimental import pallas as pl
from jax.experimental.pallas import tpu as pltpu
from jax.sharding import PartitionSpec as P

HEADS = 8
HALF = HEADS // 2
SPAN = 3
NEG = -1e30
LOG2E = 1.4426950408889634
MIB = 1024 * 1024


def vmem():
    return pl.BlockSpec(memory_space=pltpu.VMEM)


def smem():
    return pl.BlockSpec(memory_space=pltpu.SMEM)


def anywhere():
    return pl.BlockSpec(memory_space=pl.ANY)


def limit(mib):
    return pltpu.CompilerParams(vmem_limit_bytes=mib * MIB)


PLACES = ((3, 1), (4, -1), (5, -3), (1, 5), (6, -5), (2, 3), (7, -7), (0, 7))


def asking(me, kind):
    return me if kind == 0 else me + 1 - 2 * (me % 2)


def key_block(me, number):
    half = me % 2
    return me - half - SPAN + PLACES[number][0] + PLACES[number][1] * half


def prepare_kernel(where_ref, q_hbm, k_hbm, v_hbm, own_q, own_kv, swap_q, swap_kv, held, turned, sems):
    part = q_hbm.shape[1] // 2
    loads = [
        pltpu.make_async_copy(ref, held.at[i], sems.at[i])
        for i, ref in enumerate((k_hbm, v_hbm, q_hbm))
    ]
    for load in loads:
        load.start()
    me = where_ref[0]
    half = me % 2
    mine = pl.multiple_of(half * part, 16)
    other = pl.multiple_of((1 - half) * part, 16)
    for i in range(3):
        loads[i].wait()
        turned[i] = held[i].T
        if i < 2:
            own_kv[i * part : (i + 1) * part, :] = turned[i, pl.ds(mine, part), :]
            swap_kv[i * part : (i + 1) * part, :] = turned[i, pl.ds(other, part), :]
        else:
            own_q[...] = turned[i, pl.ds(mine, part), :]
            swap_q[...] = turned[i, pl.ds(other, part), :]


def prepare(where, queries, keys, values):
    rows, features = queries.shape
    part = features // 2
    single = jax.ShapeDtypeStruct((part, rows), queries.dtype)
    double = jax.ShapeDtypeStruct((2 * part, rows), queries.dtype)
    return pl.pallas_call(
        prepare_kernel,
        out_shape=[single, double, single, double],
        in_specs=[smem()] + [anywhere()] * 3,
        out_specs=[vmem()] * 4,
        scratch_shapes=[
            pltpu.VMEM((3, rows, features), queries.dtype),
            pltpu.VMEM((3, features, rows), queries.dtype),
            pltpu.SemaphoreType.DMA((3,)),
        ],
        compiler_params=limit(53),
    )(where, queries, keys, values)


def survey_kernel(where_ref, mask_ref, segs_ref, seg_out, need_out):
    seg_out[...] = segs_ref[...].astype(jnp.float32)
    me = where_ref[0]
    nblocks = mask_ref.shape[0]
    bits = jnp.int32(0)
    for kind in range(2):
        asker = asking(me, kind)
        for number in range(len(PLACES)):
            block = key_block(me, number)
            inside = (block >= 0) & (block < nblocks) & (jnp.abs(block - asker) <= SPAN)
            allowed = mask_ref[asker, jnp.clip(block, 0, nblocks - 1)] > 0
            bits += (inside & allowed).astype(jnp.int32) << (kind * len(PLACES) + number)
    need_out[...] = jnp.full(need_out.shape, bits, jnp.int32)


def survey(where, mask, segs):
    return pl.pallas_call(
        survey_kernel,
        out_shape=[
            jax.ShapeDtypeStruct(segs.shape, jnp.float32),
            jax.ShapeDtypeStruct((8, 128), jnp.int32),
        ],
        in_specs=[smem()] * 2 + [vmem()],
        out_specs=[vmem()] * 2,
        compiler_params=limit(16),
    )(where, mask, segs)


def attention_kernel(kinds, numbers, follows, ends, where_ref, need_ref, seg_ref, *refs):
    queries, refs = refs[: len(kinds)], refs[len(kinds) :]
    blocks, refs = refs[: len(numbers)], refs[len(numbers) :]
    if follows:
        before, refs = refs[0], refs[1:]
    out_ref, query_s, key_s, value_s, chosen_s = refs
    part, rows = queries[0].shape
    hdim = part // HALF
    wide = value_s.shape[2]
    nblocks = seg_ref.shape[1] // rows
    factor = LOG2E / (hdim**0.5)
    me = where_ref[0]
    column = [key_block(me, b) for b in numbers]
    asker = [asking(me, kind) for kind in kinds]
    bits = jnp.max(need_ref[...])
    need = [[(bits >> (kind * len(PLACES) + b)) & 1 for b in numbers] for kind in kinds]

    def segment(block):
        start = pl.multiple_of(jnp.clip(block, 0, nblocks - 1) * rows, 128)
        return seg_ref[:, pl.ds(start, rows)]

    for b in range(len(numbers)):
        wanted = need[0][b]
        for n in range(1, len(kinds)):
            wanted = wanted + need[n][b]

        @pl.when(wanted > 0)
        def _(b=b):
            key_s[b] = blocks[b][:part, :]
            for h in range(HALF):
                lines = slice(part + h * hdim, part + (h + 1) * hdim)
                value_s[b, h, :hdim, :] = blocks[b][lines, :]
                value_s[b, h, hdim:, :] = jnp.ones((wide - hdim, rows), jnp.bfloat16)

    for n in range(len(kinds)):
        size = 0
        for b in range(len(numbers)):
            chosen_s[size] = b
            size = size + need[n][b]
        for h in range(HALF):
            query_s[h] = queries[n][h * hdim : (h + 1) * hdim, :].T
        query_seg = jnp.broadcast_to(segment(asker[n]), (128, rows)).T
        query_seg = jnp.concatenate([query_seg] * (rows // 128), axis=1)

        def finish(h, peak, accum, n=n):
            if ends:
                turned = accum.T
                lines = pl.ds(pl.multiple_of(h * hdim, 16), hdim)
                out_ref[lines, :] = (turned[:hdim] / turned[hdim : hdim + 1]).astype(out_ref.dtype)
            else:
                peak = jnp.broadcast_to(peak, (rows, 128 - wide))
                out_ref[n, h] = jnp.concatenate([accum, peak], axis=1)

        if follows:

            @pl.when(size == 0)
            def _():
                def one_head(h, carry):
                    state = before[0, h]
                    finish(h, state[:, wide : wide + 1], state[:, :wide])
                    return carry

                lax.fori_loop(0, HALF, one_head, 0)

        for fixed in range(1, len(numbers) + 1):

            @pl.when(size == fixed)
            def _():
                picked = [chosen_s[b] for b in range(fixed)]
                key_segs = [
                    segment(sum(jnp.where(b == i, column[i], 0) for i in range(len(numbers))))
                    for b in picked
                ]

                def one_head(h):
                    lines = pl.ds(pl.multiple_of(h * hdim, 16), hdim)
                    query = query_s[h]
                    scores = []
                    for b, key_seg in zip(picked, key_segs):
                        score = jnp.dot(
                            query, key_s[b, lines, :], preferred_element_type=jnp.float32
                        )
                        scores.append(jnp.where(query_seg == key_seg, score, NEG))
                    peak = functools.reduce(jnp.maximum, scores)
                    peak = jnp.max(peak, axis=1, keepdims=True)
                    accum = jnp.zeros((rows, wide), jnp.float32)
                    if follows:
                        state = before[0, h]
                        old = state[:, wide : wide + 1]
                        peak = jnp.maximum(peak, old)
                        accum = state[:, :wide] * jnp.exp2((old - peak) * factor)
                    for b, score in zip(picked, scores):
                        weights = jnp.exp2((score - peak) * factor).astype(jnp.bfloat16)
                        accum += lax.dot_general(
                            weights,
                            value_s[b, h],
                            (((1,), (1,)), ((), ())),
                            preferred_element_type=jnp.float32,
                        )
                    finish(h, peak, accum)

                def two_heads(i, carry):
                    one_head(2 * i)
                    one_head(2 * i + 1)
                    return carry

                lax.fori_loop(0, HALF // 2, two_heads, 0)


def attention(where, need, segs, queries, kinds, blocks, numbers, before, ends):
    part, rows = queries[0].shape
    hdim = part // HALF
    wide = hdim + 16
    follows = before is not None
    if ends:
        out = jax.ShapeDtypeStruct((part, rows), jnp.bfloat16)
    else:
        out = jax.ShapeDtypeStruct((len(kinds), HALF, rows, 128), jnp.float32)
    return pl.pallas_call(
        functools.partial(attention_kernel, kinds, numbers, follows, ends),
        out_shape=out,
        in_specs=[smem()] + [vmem()] * (2 + len(kinds) + len(numbers) + follows),
        out_specs=vmem(),
        scratch_shapes=[
            pltpu.VMEM((HALF, rows, hdim), jnp.bfloat16),
            pltpu.VMEM((len(numbers), part, rows), jnp.bfloat16),
            pltpu.VMEM((len(numbers), HALF, wide, rows), jnp.bfloat16),
            pltpu.SMEM((len(numbers) + 1,), jnp.int32),
        ],
        compiler_params=limit(16),
        cost_estimate=pl.CostEstimate(
            flops=2_000_000_000 * len(kinds), bytes_accessed=2_000_000, transcendentals=1_000_000
        ),
    )(where, need, segs, *queries, *blocks, *((before,) if follows else ()))


def project_kernel(
    pair_rows, where_ref, owners_ref, offsets_ref, own_ref, other_ref, weight_ref, tokens_ref, *outs
):
    piece = outs[0].shape[0]
    slots = piece * len(outs)
    rows, width = tokens_ref.shape
    mrows = rows // 4
    capacity = 2 * mrows
    owner = jnp.broadcast_to(owners_ref[...].astype(jnp.float32), (mrows, mrows))
    earlier = lax.broadcasted_iota(jnp.int32, (mrows, mrows), 0)
    later = lax.broadcasted_iota(jnp.int32, (mrows, mrows), 1)
    column = jnp.sum(jnp.where(earlier == later, owner, 0.0), axis=1, keepdims=True)
    ahead = jnp.where((owner == column) & (earlier < later), 1.0, 0.0)
    slot = owner[:1] * pair_rows + jnp.sum(ahead, axis=0, keepdims=True)
    line = lax.broadcasted_iota(jnp.int32, (16, mrows), 0)
    meta = jnp.where(line == 0, slot, jnp.where(line == 1, offsets_ref[...].astype(jnp.float32), 0.0))
    row = lax.broadcasted_iota(jnp.int32, (mrows, rows), 0)
    patch = lax.broadcasted_iota(jnp.int32, (mrows, rows), 1)
    spread = jnp.where(patch // 4 == row, 1.0, 0.0).astype(jnp.bfloat16)
    meta = jnp.dot(meta.astype(jnp.bfloat16), spread, preferred_element_type=jnp.float32)
    part = own_ref.shape[0]
    half = where_ref[0] % 2
    hidden = tokens_ref[...].astype(jnp.float32)
    for ref, which in ((own_ref, half), (other_ref, 1 - half)):
        hidden += lax.dot_general(
            ref[...],
            weight_ref[pl.ds(pl.multiple_of(which * part, 16), part), :],
            (((0,), (0,)), ((), ())),
            preferred_element_type=jnp.float32,
        )
    hidden = hidden.astype(jnp.bfloat16)
    place = meta[:1]
    if len(outs) > 1:
        place = place - (where_ref[0] * pair_rows).astype(jnp.float32)
        place = jnp.where(place < 0, place + slots, place)
    slot = lax.broadcasted_iota(jnp.int32, (slots, rows), 0).astype(jnp.float32)
    quarter = lax.broadcasted_iota(jnp.int32, (1, rows), 1) % 4
    for j in range(4):
        mine = jnp.where(quarter == j, place, -1.0) == slot
        if j == 0:
            offset = jnp.where(mine, meta[1:2] - capacity, 0.0)
            offset = capacity + jnp.sum(offset, axis=1, keepdims=True)
            offset = jnp.broadcast_to(offset, (slots, 128)).astype(jnp.bfloat16)
            for d, out in enumerate(outs):
                out[:, 4 * width :] = offset[d * piece : (d + 1) * piece]
        pick = jnp.where(mine, 1.0, 0.0).astype(jnp.bfloat16)
        picked = jnp.dot(pick, hidden, preferred_element_type=jnp.float32).astype(jnp.bfloat16)
        for d, out in enumerate(outs):
            out[:, j * width : (j + 1) * width] = picked[d * piece : (d + 1) * piece]


def project(where, owners, offsets, own, other, out_weight, tokens, pieces, slots, pair_rows):
    rows, width = tokens.shape
    return pl.pallas_call(
        functools.partial(project_kernel, pair_rows),
        out_shape=[jax.ShapeDtypeStruct((slots // pieces, 4 * width + 128), jnp.bfloat16)] * pieces,
        in_specs=[smem()] + [vmem()] * 6,
        out_specs=[vmem()] * pieces,
        compiler_params=limit(24),
    )(where, owners, offsets, own, other, out_weight, tokens)


def place_kernel(*refs):
    *arrived, out_hbm, held, sems = refs
    capacity, merged = out_hbm.shape
    step = merged // 4

    def columns_of(start, size):
        return jnp.concatenate([ref[:, start : start + size] for ref in arrived], axis=0)

    offset = columns_of(merged, 128).astype(jnp.float32)[:, :1]
    row = lax.broadcasted_iota(jnp.int32, (offset.shape[0], capacity), 1).astype(jnp.float32)
    pick = jnp.where(offset == row, 1.0, 0.0).astype(jnp.bfloat16)
    stores = []
    for j in range(4):
        held[j] = lax.dot_general(
            pick,
            columns_of(j * step, step),
            (((0,), (0,)), ((), ())),
            preferred_element_type=jnp.float32,
        ).astype(jnp.bfloat16)
        columns = out_hbm.at[:, pl.ds(j * step, step)]
        stores.append(pltpu.make_async_copy(held.at[j], columns, sems.at[j]))
        stores[j].start()
    for store in stores:
        store.wait()


def place(arrived, capacity, merged):
    return pl.pallas_call(
        place_kernel,
        out_shape=jax.ShapeDtypeStruct((capacity, merged), jnp.bfloat16),
        in_specs=[vmem()] * len(arrived),
        out_specs=anywhere(),
        scratch_shapes=[
            pltpu.VMEM((4, capacity, merged // 4), jnp.bfloat16),
            pltpu.SemaphoreType.DMA((4,)),
        ],
        compiler_params=limit(24),
    )(*arrived)


def per_device(segment_ids, block_mask, queries, keys, values, tokens, out_weight, owners, offsets):
    rows = queries.shape[0]
    width = tokens.shape[1]
    nblocks = lax.axis_size("blk")
    block_index = lax.axis_index("blk")
    mrows = rows // 4
    capacity = 2 * mrows
    pair_rows = max(2, 2 * mrows // nblocks)
    slots = nblocks * pair_rows
    assert slots <= 256

    def route(step):
        return [(i, i + step(i)) for i in range(nblocks) if 0 <= i + step(i) < nblocks]

    swap = functools.partial(
        lax.ppermute, axis_name="blk", perm=route(lambda i: 1 - 2 * (i % 2))
    )
    ahead = functools.partial(
        lax.ppermute, axis_name="blk", perm=route(lambda i: 2 if i % 2 else -2)
    )
    back = functools.partial(
        lax.ppermute, axis_name="blk", perm=route(lambda i: -2 if i % 2 else 2)
    )

    where = block_index[None].astype(jnp.int32)
    own_q, own_kv, swap_q, swap_kv = prepare(where, queries, keys, values)
    segs, need = survey(where, block_mask, segment_ids[None, :])
    other_kv = swap(swap_kv)
    ahead_own = ahead(own_kv)
    back_own = back(own_kv)
    ready, back_own, swap_q, segs, need = lax.optimization_barrier(
        (other_kv, back_own, swap_q, segs, need)
    )
    back_other = back(ready)
    other_q = swap(swap_q)
    back_far = back(back_other)
    ahead_other = ahead(other_kv)
    ahead_far = ahead(ahead_own)
    near = (own_kv, other_kv, ahead_own, back_own)
    near_numbers = (0, 1, 2, 3)
    fixed = (where, need, segs)
    own = attention(*fixed, (own_q,), (0,), near, near_numbers, None, False)
    other = attention(*fixed, (other_q,), (1,), near, near_numbers, None, False)
    far = (ahead_other, back_other, ahead_far)
    other = attention(*fixed, (other_q,), (1,), far, (4, 5, 6), other, True)
    other = swap(other)
    far = (ahead_other, back_other, back_far)
    own = attention(*fixed, (own_q,), (0,), far, (4, 5, 7), own, True)

    pieces = nblocks if nblocks <= 8 else 1
    outgoing = project(
        where, owners[None, :], offsets[None, :], own, other, out_weight, tokens,
        pieces, slots, pair_rows,
    )
    if pieces > 1:
        arrived = [outgoing[0]] + [None] * (nblocks - 1)
        order = sorted(range(1, nblocks), key=lambda d: (min(d, nblocks - d) == 2, d))
        for d in order:
            arrived[d] = lax.ppermute(
                outgoing[d], "blk", [(i, (i + d) % nblocks) for i in range(nblocks)]
            )
    else:
        arrived = [lax.all_to_all(outgoing[0], "blk", split_axis=0, concat_axis=0, tiled=True)]
    return place(arrived, capacity, 4 * width)


def solution(mesh):
    placed = (
        P("rep"),
        P("rep", None),
        P(("rep", "blk"), None),
        P(("rep", "blk"), None),
        P(("rep", "blk"), None),
        P(("rep", "blk"), None),
        P(),
        P(("rep", "blk")),
        P(("rep", "blk")),
    )
    return jax.shard_map(
        per_device, mesh=mesh, in_specs=placed, out_specs=P(("rep", "blk"), None), check_vma=False
    )
```

```python
import functools

import jax
import jax.numpy as jnp
from jax import lax
from jax.experimental import pallas as pl
from jax.experimental.pallas import tpu as pltpu
from jax.sharding import PartitionSpec as P

HEADS = 8
HALF = HEADS // 2
SPAN = 3
NEG = -1e30
LOG2E = 1.4426950408889634
MIB = 1024 * 1024


def vmem():
    return pl.BlockSpec(memory_space=pltpu.VMEM)


def smem():
    return pl.BlockSpec(memory_space=pltpu.SMEM)


def anywhere():
    return pl.BlockSpec(memory_space=pl.ANY)


def limit(mib):
    return pltpu.CompilerParams(vmem_limit_bytes=mib * MIB)


PLACES = ((3, 1), (4, -1), (5, -3), (1, 5), (6, -5), (2, 3), (7, -7), (0, 7))


def asking(me, kind):
    return me if kind == 0 else me + 1 - 2 * (me % 2)


def key_block(me, number):
    half = me % 2
    return me - half - SPAN + PLACES[number][0] + PLACES[number][1] * half


def prepare_kernel(where_ref, q_hbm, k_hbm, v_hbm, own_q, own_kv, swap_q, swap_kv, held, turned, sems):
    part = q_hbm.shape[1] // 2
    loads = [
        pltpu.make_async_copy(ref, held.at[i], sems.at[i])
        for i, ref in enumerate((k_hbm, v_hbm, q_hbm))
    ]
    for load in loads:
        load.start()
    me = where_ref[0]
    half = me % 2
    mine = pl.multiple_of(half * part, 16)
    other = pl.multiple_of((1 - half) * part, 16)
    for i in range(3):
        loads[i].wait()
        turned[i] = held[i].T
        if i < 2:
            own_kv[i * part : (i + 1) * part, :] = turned[i, pl.ds(mine, part), :]
            swap_kv[i * part : (i + 1) * part, :] = turned[i, pl.ds(other, part), :]
        else:
            own_q[...] = turned[i, pl.ds(mine, part), :]
            swap_q[...] = turned[i, pl.ds(other, part), :]


def prepare(where, queries, keys, values):
    rows, features = queries.shape
    part = features // 2
    single = jax.ShapeDtypeStruct((part, rows), queries.dtype)
    double = jax.ShapeDtypeStruct((2 * part, rows), queries.dtype)
    return pl.pallas_call(
        prepare_kernel,
        out_shape=[single, double, single, double],
        in_specs=[smem()] + [anywhere()] * 3,
        out_specs=[vmem()] * 4,
        scratch_shapes=[
            pltpu.VMEM((3, rows, features), queries.dtype),
            pltpu.VMEM((3, features, rows), queries.dtype),
            pltpu.SemaphoreType.DMA((3,)),
        ],
        compiler_params=limit(53),
    )(where, queries, keys, values)


def survey_kernel(where_ref, mask_ref, segs_ref, seg_out, need_out):
    seg_out[...] = segs_ref[...].astype(jnp.float32)
    me = where_ref[0]
    nblocks = mask_ref.shape[0]
    bits = jnp.int32(0)
    for kind in range(2):
        asker = asking(me, kind)
        for number in range(len(PLACES)):
            block = key_block(me, number)
            inside = (block >= 0) & (block < nblocks) & (jnp.abs(block - asker) <= SPAN)
            allowed = mask_ref[asker, jnp.clip(block, 0, nblocks - 1)] > 0
            bits += (inside & allowed).astype(jnp.int32) << (kind * len(PLACES) + number)
    need_out[...] = jnp.full(need_out.shape, bits, jnp.int32)


def survey(where, mask, segs):
    return pl.pallas_call(
        survey_kernel,
        out_shape=[
            jax.ShapeDtypeStruct(segs.shape, jnp.float32),
            jax.ShapeDtypeStruct((8, 128), jnp.int32),
        ],
        in_specs=[smem()] * 2 + [vmem()],
        out_specs=[vmem()] * 2,
        compiler_params=limit(16),
    )(where, mask, segs)


def attention_kernel(kinds, numbers, follows, ends, where_ref, need_ref, seg_ref, *refs):
    queries, refs = refs[: len(kinds)], refs[len(kinds) :]
    blocks, refs = refs[: len(numbers)], refs[len(numbers) :]
    if follows:
        before, refs = refs[0], refs[1:]
    out_ref, query_s, key_s, value_s, chosen_s = refs
    part, rows = queries[0].shape
    hdim = part // HALF
    wide = value_s.shape[2]
    nblocks = seg_ref.shape[1] // rows
    factor = LOG2E / (hdim**0.5)
    me = where_ref[0]
    column = [key_block(me, b) for b in numbers]
    asker = [asking(me, kind) for kind in kinds]
    bits = jnp.max(need_ref[...])
    need = [[(bits >> (kind * len(PLACES) + b)) & 1 for b in numbers] for kind in kinds]

    def segment(block):
        start = pl.multiple_of(jnp.clip(block, 0, nblocks - 1) * rows, 128)
        return seg_ref[:, pl.ds(start, rows)]

    for b in range(len(numbers)):
        wanted = need[0][b]
        for n in range(1, len(kinds)):
            wanted = wanted + need[n][b]

        @pl.when(wanted > 0)
        def _(b=b):
            key_s[b] = blocks[b][:part, :]
            for h in range(HALF):
                lines = slice(part + h * hdim, part + (h + 1) * hdim)
                value_s[b, h, :hdim, :] = blocks[b][lines, :]
                value_s[b, h, hdim:, :] = jnp.ones((wide - hdim, rows), jnp.bfloat16)

    for n in range(len(kinds)):
        size = 0
        for b in range(len(numbers)):
            chosen_s[size] = b
            size = size + need[n][b]
        for h in range(HALF):
            query_s[h] = queries[n][h * hdim : (h + 1) * hdim, :].T
        query_seg = jnp.broadcast_to(segment(asker[n]), (128, rows)).T
        query_seg = jnp.concatenate([query_seg] * (rows // 128), axis=1)

        def finish(h, peak, accum, n=n):
            if ends:
                turned = accum.T
                lines = pl.ds(pl.multiple_of(h * hdim, 16), hdim)
                out_ref[lines, :] = (turned[:hdim] / turned[hdim : hdim + 1]).astype(out_ref.dtype)
            else:
                peak = jnp.broadcast_to(peak, (rows, 128 - wide))
                out_ref[n, h] = jnp.concatenate([accum, peak], axis=1)

        if follows:

            @pl.when(size == 0)
            def _():
                def one_head(h, carry):
                    state = before[0, h]
                    finish(h, state[:, wide : wide + 1], state[:, :wide])
                    return carry

                lax.fori_loop(0, HALF, one_head, 0)

        for fixed in range(1, len(numbers) + 1):

            @pl.when(size == fixed)
            def _():
                picked = [chosen_s[b] for b in range(fixed)]
                key_segs = [
                    segment(sum(jnp.where(b == i, column[i], 0) for i in range(len(numbers))))
                    for b in picked
                ]

                def one_head(h):
                    lines = pl.ds(pl.multiple_of(h * hdim, 16), hdim)
                    query = query_s[h]
                    scores = []
                    for b, key_seg in zip(picked, key_segs):
                        score = jnp.dot(
                            query, key_s[b, lines, :], preferred_element_type=jnp.float32
                        )
                        scores.append(jnp.where(query_seg == key_seg, score, NEG))
                    peak = functools.reduce(jnp.maximum, scores)
                    peak = jnp.max(peak, axis=1, keepdims=True)
                    accum = jnp.zeros((rows, wide), jnp.float32)
                    if follows:
                        state = before[0, h]
                        old = state[:, wide : wide + 1]
                        peak = jnp.maximum(peak, old)
                        accum = state[:, :wide] * jnp.exp2((old - peak) * factor)
                    for b, score in zip(picked, scores):
                        weights = jnp.exp2((score - peak) * factor).astype(jnp.bfloat16)
                        accum += lax.dot_general(
                            weights,
                            value_s[b, h],
                            (((1,), (1,)), ((), ())),
                            preferred_element_type=jnp.float32,
                        )
                    finish(h, peak, accum)

                def two_heads(i, carry):
                    one_head(2 * i)
                    one_head(2 * i + 1)
                    return carry

                lax.fori_loop(0, HALF // 2, two_heads, 0)


def attention(where, need, segs, queries, kinds, blocks, numbers, before, ends):
    part, rows = queries[0].shape
    hdim = part // HALF
    wide = hdim + 16
    follows = before is not None
    if ends:
        out = jax.ShapeDtypeStruct((part, rows), jnp.bfloat16)
    else:
        out = jax.ShapeDtypeStruct((len(kinds), HALF, rows, 128), jnp.float32)
    return pl.pallas_call(
        functools.partial(attention_kernel, kinds, numbers, follows, ends),
        out_shape=out,
        in_specs=[smem()] + [vmem()] * (2 + len(kinds) + len(numbers) + follows),
        out_specs=vmem(),
        scratch_shapes=[
            pltpu.VMEM((HALF, rows, hdim), jnp.bfloat16),
            pltpu.VMEM((len(numbers), part, rows), jnp.bfloat16),
            pltpu.VMEM((len(numbers), HALF, wide, rows), jnp.bfloat16),
            pltpu.SMEM((len(numbers) + 1,), jnp.int32),
        ],
        compiler_params=limit(16),
        cost_estimate=pl.CostEstimate(
            flops=2_000_000_000 * len(kinds), bytes_accessed=2_000_000, transcendentals=1_000_000
        ),
    )(where, need, segs, *queries, *blocks, *((before,) if follows else ()))


def project_kernel(
    pair_rows, where_ref, owners_ref, offsets_ref, own_ref, other_ref, weight_ref, tokens_ref, *outs
):
    piece = outs[0].shape[0]
    slots = piece * len(outs)
    rows, width = tokens_ref.shape
    mrows = rows // 4
    capacity = 2 * mrows
    owner = jnp.broadcast_to(owners_ref[...].astype(jnp.float32), (mrows, mrows))
    earlier = lax.broadcasted_iota(jnp.int32, (mrows, mrows), 0)
    later = lax.broadcasted_iota(jnp.int32, (mrows, mrows), 1)
    column = jnp.sum(jnp.where(earlier == later, owner, 0.0), axis=1, keepdims=True)
    ahead = jnp.where((owner == column) & (earlier < later), 1.0, 0.0)
    slot = owner[:1] * pair_rows + jnp.sum(ahead, axis=0, keepdims=True)
    line = lax.broadcasted_iota(jnp.int32, (16, mrows), 0)
    meta = jnp.where(line == 0, slot, jnp.where(line == 1, offsets_ref[...].astype(jnp.float32), 0.0))
    row = lax.broadcasted_iota(jnp.int32, (mrows, rows), 0)
    patch = lax.broadcasted_iota(jnp.int32, (mrows, rows), 1)
    spread = jnp.where(patch // 4 == row, 1.0, 0.0).astype(jnp.bfloat16)
    meta = jnp.dot(meta.astype(jnp.bfloat16), spread, preferred_element_type=jnp.float32)
    part = own_ref.shape[0]
    half = where_ref[0] % 2
    hidden = tokens_ref[...].astype(jnp.float32)
    for ref, which in ((own_ref, half), (other_ref, 1 - half)):
        hidden += lax.dot_general(
            ref[...],
            weight_ref[pl.ds(pl.multiple_of(which * part, 16), part), :],
            (((0,), (0,)), ((), ())),
            preferred_element_type=jnp.float32,
        )
    hidden = hidden.astype(jnp.bfloat16)
    place = meta[:1]
    if len(outs) > 1:
        place = place - (where_ref[0] * pair_rows).astype(jnp.float32)
        place = jnp.where(place < 0, place + slots, place)
    slot = lax.broadcasted_iota(jnp.int32, (slots, rows), 0).astype(jnp.float32)
    quarter = lax.broadcasted_iota(jnp.int32, (1, rows), 1) % 4
    for j in range(4):
        mine = jnp.where(quarter == j, place, -1.0) == slot
        if j == 0:
            offset = jnp.where(mine, meta[1:2] - capacity, 0.0)
            offset = capacity + jnp.sum(offset, axis=1, keepdims=True)
            offset = jnp.broadcast_to(offset, (slots, 128)).astype(jnp.bfloat16)
            for d, out in enumerate(outs):
                out[:, 4 * width :] = offset[d * piece : (d + 1) * piece]
        pick = jnp.where(mine, 1.0, 0.0).astype(jnp.bfloat16)
        picked = jnp.dot(pick, hidden, preferred_element_type=jnp.float32).astype(jnp.bfloat16)
        for d, out in enumerate(outs):
            out[:, j * width : (j + 1) * width] = picked[d * piece : (d + 1) * piece]


def project(where, owners, offsets, own, other, out_weight, tokens, pieces, slots, pair_rows):
    rows, width = tokens.shape
    return pl.pallas_call(
        functools.partial(project_kernel, pair_rows),
        out_shape=[jax.ShapeDtypeStruct((slots // pieces, 4 * width + 128), jnp.bfloat16)] * pieces,
        in_specs=[smem()] + [vmem()] * 6,
        out_specs=[vmem()] * pieces,
        compiler_params=limit(24),
    )(where, owners, offsets, own, other, out_weight, tokens)


def place_kernel(*refs):
    *arrived, out_hbm, held, sems = refs
    capacity, merged = out_hbm.shape
    step = merged // 4

    def columns_of(start, size):
        return jnp.concatenate([ref[:, start : start + size] for ref in arrived], axis=0)

    offset = columns_of(merged, 128).astype(jnp.float32)[:, :1]
    row = lax.broadcasted_iota(jnp.int32, (offset.shape[0], capacity), 1).astype(jnp.float32)
    pick = jnp.where(offset == row, 1.0, 0.0).astype(jnp.bfloat16)
    stores = []
    for j in range(4):
        held[j] = lax.dot_general(
            pick,
            columns_of(j * step, step),
            (((0,), (0,)), ((), ())),
            preferred_element_type=jnp.float32,
        ).astype(jnp.bfloat16)
        columns = out_hbm.at[:, pl.ds(j * step, step)]
        stores.append(pltpu.make_async_copy(held.at[j], columns, sems.at[j]))
        stores[j].start()
    for store in stores:
        store.wait()


def place(arrived, capacity, merged):
    return pl.pallas_call(
        place_kernel,
        out_shape=jax.ShapeDtypeStruct((capacity, merged), jnp.bfloat16),
        in_specs=[vmem()] * len(arrived),
        out_specs=anywhere(),
        scratch_shapes=[
            pltpu.VMEM((4, capacity, merged // 4), jnp.bfloat16),
            pltpu.SemaphoreType.DMA((4,)),
        ],
        compiler_params=limit(24),
    )(*arrived)


def per_device(segment_ids, block_mask, queries, keys, values, tokens, out_weight, owners, offsets):
    rows = queries.shape[0]
    width = tokens.shape[1]
    nblocks = lax.axis_size("blk")
    block_index = lax.axis_index("blk")
    mrows = rows // 4
    capacity = 2 * mrows
    pair_rows = max(2, 2 * mrows // nblocks)
    slots = nblocks * pair_rows
    assert slots <= 256

    def route(step):
        return [(i, i + step(i)) for i in range(nblocks) if 0 <= i + step(i) < nblocks]

    swap = functools.partial(
        lax.ppermute, axis_name="blk", perm=route(lambda i: 1 - 2 * (i % 2))
    )
    ahead = functools.partial(
        lax.ppermute, axis_name="blk", perm=route(lambda i: 2 if i % 2 else -2)
    )
    back = functools.partial(
        lax.ppermute, axis_name="blk", perm=route(lambda i: -2 if i % 2 else 2)
    )

    where = block_index[None].astype(jnp.int32)
    own_q, own_kv, swap_q, swap_kv = prepare(where, queries, keys, values)
    segs, need = survey(where, block_mask, segment_ids[None, :])
    other_kv = swap(swap_kv)
    ahead_own = ahead(own_kv)
    back_own = back(own_kv)
    ready, ahead_own, segs, need = lax.optimization_barrier((other_kv, ahead_own, segs, need))
    ahead_far = ahead(ahead_own)
    back_other = back(ready)
    ready, back_own, swap_q = lax.optimization_barrier((ready, back_own, swap_q))
    other_q = swap(swap_q)
    ahead_other = ahead(ready)
    back_far = back(back_other)
    near = (own_kv, other_kv, ahead_own, back_own)
    near_numbers = (0, 1, 2, 3)
    fixed = (where, need, segs)
    own = attention(*fixed, (own_q,), (0,), near, near_numbers, None, False)
    other = attention(*fixed, (other_q,), (1,), near, near_numbers, None, False)
    far = (ahead_other, back_other, ahead_far)
    other = attention(*fixed, (other_q,), (1,), far, (4, 5, 6), other, True)
    other = swap(other)
    far = (ahead_other, back_other, back_far)
    own = attention(*fixed, (own_q,), (0,), far, (4, 5, 7), own, True)

    pieces = nblocks if nblocks <= 8 else 1
    outgoing = project(
        where, owners[None, :], offsets[None, :], own, other, out_weight, tokens,
        pieces, slots, pair_rows,
    )
    if pieces > 1:
        arrived = [outgoing[0]] + [None] * (nblocks - 1)
        order = sorted(range(1, nblocks), key=lambda d: (min(d, nblocks - d) == 2, d))
        for d in order:
            arrived[d] = lax.ppermute(
                outgoing[d], "blk", [(i, (i + d) % nblocks) for i in range(nblocks)]
            )
    else:
        arrived = [lax.all_to_all(outgoing[0], "blk", split_axis=0, concat_axis=0, tiled=True)]
    return place(arrived, capacity, 4 * width)


def solution(mesh):
    placed = (
        P("rep"),
        P("rep", None),
        P(("rep", "blk"), None),
        P(("rep", "blk"), None),
        P(("rep", "blk"), None),
        P(("rep", "blk"), None),
        P(),
        P(("rep", "blk")),
        P(("rep", "blk")),
    )
    return jax.shard_map(
        per_device, mesh=mesh, in_specs=placed, out_specs=P(("rep", "blk"), None), check_vma=False
    )
```

```python
import functools

import jax
import jax.numpy as jnp
from jax import lax
from jax.experimental import pallas as pl
from jax.experimental.pallas import tpu as pltpu
from jax.sharding import PartitionSpec as P

HEADS = 8
HALF = HEADS // 2
SPAN = 3
NEG = -1e30
LOG2E = 1.4426950408889634
MIB = 1024 * 1024


def vmem():
    return pl.BlockSpec(memory_space=pltpu.VMEM)


def smem():
    return pl.BlockSpec(memory_space=pltpu.SMEM)


def anywhere():
    return pl.BlockSpec(memory_space=pl.ANY)


def limit(mib):
    return pltpu.CompilerParams(vmem_limit_bytes=mib * MIB)


PLACES = ((3, 1), (4, -1), (5, -3), (1, 5), (6, -5), (2, 3), (7, -7), (0, 7))


def asking(me, kind):
    return me if kind == 0 else me + 1 - 2 * (me % 2)


def key_block(me, number):
    half = me % 2
    return me - half - SPAN + PLACES[number][0] + PLACES[number][1] * half


def prepare_kernel(where_ref, q_hbm, k_hbm, v_hbm, own_q, own_kv, swap_q, swap_kv, held, turned, sems):
    part = q_hbm.shape[1] // 2
    loads = [
        pltpu.make_async_copy(ref, held.at[i], sems.at[i])
        for i, ref in enumerate((k_hbm, v_hbm, q_hbm))
    ]
    for load in loads:
        load.start()
    me = where_ref[0]
    half = me % 2
    mine = pl.multiple_of(half * part, 16)
    other = pl.multiple_of((1 - half) * part, 16)
    for i in range(3):
        loads[i].wait()
        turned[i] = held[i].T
        if i < 2:
            own_kv[i * part : (i + 1) * part, :] = turned[i, pl.ds(mine, part), :]
            swap_kv[i * part : (i + 1) * part, :] = turned[i, pl.ds(other, part), :]
        else:
            own_q[...] = turned[i, pl.ds(mine, part), :]
            swap_q[...] = turned[i, pl.ds(other, part), :]


def prepare(where, queries, keys, values):
    rows, features = queries.shape
    part = features // 2
    single = jax.ShapeDtypeStruct((part, rows), queries.dtype)
    double = jax.ShapeDtypeStruct((2 * part, rows), queries.dtype)
    return pl.pallas_call(
        prepare_kernel,
        out_shape=[single, double, single, double],
        in_specs=[smem()] + [anywhere()] * 3,
        out_specs=[vmem()] * 4,
        scratch_shapes=[
            pltpu.VMEM((3, rows, features), queries.dtype),
            pltpu.VMEM((3, features, rows), queries.dtype),
            pltpu.SemaphoreType.DMA((3,)),
        ],
        compiler_params=limit(53),
    )(where, queries, keys, values)


def survey_kernel(where_ref, mask_ref, segs_ref, seg_out, need_out):
    seg_out[...] = segs_ref[...].astype(jnp.float32)
    me = where_ref[0]
    nblocks = mask_ref.shape[0]
    bits = jnp.int32(0)
    for kind in range(2):
        asker = asking(me, kind)
        for number in range(len(PLACES)):
            block = key_block(me, number)
            inside = (block >= 0) & (block < nblocks) & (jnp.abs(block - asker) <= SPAN)
            allowed = mask_ref[asker, jnp.clip(block, 0, nblocks - 1)] > 0
            bits += (inside & allowed).astype(jnp.int32) << (kind * len(PLACES) + number)
    need_out[...] = jnp.full(need_out.shape, bits, jnp.int32)


def survey(where, mask, segs):
    return pl.pallas_call(
        survey_kernel,
        out_shape=[
            jax.ShapeDtypeStruct(segs.shape, jnp.float32),
            jax.ShapeDtypeStruct((8, 128), jnp.int32),
        ],
        in_specs=[smem()] * 2 + [vmem()],
        out_specs=[vmem()] * 2,
        compiler_params=limit(16),
    )(where, mask, segs)


def attention_kernel(kinds, numbers, follows, ends, where_ref, need_ref, seg_ref, *refs):
    queries, refs = refs[: len(kinds)], refs[len(kinds) :]
    blocks, refs = refs[: len(numbers)], refs[len(numbers) :]
    if follows:
        before, refs = refs[0], refs[1:]
    out_ref, query_s, key_s, value_s, chosen_s = refs
    part, rows = queries[0].shape
    hdim = part // HALF
    wide = value_s.shape[2]
    nblocks = seg_ref.shape[1] // rows
    factor = LOG2E / (hdim**0.5)
    me = where_ref[0]
    column = [key_block(me, b) for b in numbers]
    asker = [asking(me, kind) for kind in kinds]
    bits = jnp.max(need_ref[...])
    need = [[(bits >> (kind * len(PLACES) + b)) & 1 for b in numbers] for kind in kinds]

    def segment(block):
        start = pl.multiple_of(jnp.clip(block, 0, nblocks - 1) * rows, 128)
        return seg_ref[:, pl.ds(start, rows)]

    for b in range(len(numbers)):
        wanted = need[0][b]
        for n in range(1, len(kinds)):
            wanted = wanted + need[n][b]

        @pl.when(wanted > 0)
        def _(b=b):
            key_s[b] = blocks[b][:part, :]
            for h in range(HALF):
                lines = slice(part + h * hdim, part + (h + 1) * hdim)
                value_s[b, h, :hdim, :] = blocks[b][lines, :]
                value_s[b, h, hdim:, :] = jnp.ones((wide - hdim, rows), jnp.bfloat16)

    for n in range(len(kinds)):
        size = 0
        for b in range(len(numbers)):
            chosen_s[size] = b
            size = size + need[n][b]
        for h in range(HALF):
            query_s[h] = queries[n][h * hdim : (h + 1) * hdim, :].T
        query_seg = jnp.broadcast_to(segment(asker[n]), (128, rows)).T
        query_seg = jnp.concatenate([query_seg] * (rows // 128), axis=1)

        def finish(h, peak, accum, n=n):
            if ends:
                turned = accum.T
                lines = slice(h * hdim, (h + 1) * hdim)
                out_ref[lines, :] = (turned[:hdim] / turned[hdim : hdim + 1]).astype(out_ref.dtype)
            else:
                peak = jnp.broadcast_to(peak, (rows, 128 - wide))
                out_ref[n, h] = jnp.concatenate([accum, peak], axis=1)

        if follows:

            @pl.when(size == 0)
            def _():
                for h in range(HALF):
                    state = before[0, h]
                    finish(h, state[:, wide : wide + 1], state[:, :wide])

        for fixed in range(1, len(numbers) + 1):

            @pl.when(size == fixed)
            def _():
                picked = [chosen_s[b] for b in range(fixed)]
                key_segs = [
                    segment(sum(jnp.where(b == i, column[i], 0) for i in range(len(numbers))))
                    for b in picked
                ]

                def one_head(h):
                    lines = slice(h * hdim, (h + 1) * hdim)
                    query = query_s[h]
                    scores = []
                    for b, key_seg in zip(picked, key_segs):
                        score = jnp.dot(
                            query, key_s[b, lines, :], preferred_element_type=jnp.float32
                        )
                        scores.append(jnp.where(query_seg == key_seg, score, NEG))
                    peak = functools.reduce(jnp.maximum, scores)
                    peak = jnp.max(peak, axis=1, keepdims=True)
                    accum = jnp.zeros((rows, wide), jnp.float32)
                    if follows:
                        state = before[0, h]
                        old = state[:, wide : wide + 1]
                        peak = jnp.maximum(peak, old)
                        accum = state[:, :wide] * jnp.exp2((old - peak) * factor)
                    for b, score in zip(picked, scores):
                        weights = jnp.exp2((score - peak) * factor).astype(jnp.bfloat16)
                        accum += lax.dot_general(
                            weights,
                            value_s[b, h],
                            (((1,), (1,)), ((), ())),
                            preferred_element_type=jnp.float32,
                        )
                    finish(h, peak, accum)

                for h in range(HALF):
                    one_head(h)


def attention(where, need, segs, queries, kinds, blocks, numbers, before, ends):
    part, rows = queries[0].shape
    hdim = part // HALF
    wide = hdim + 16
    follows = before is not None
    if ends:
        out = jax.ShapeDtypeStruct((part, rows), jnp.bfloat16)
    else:
        out = jax.ShapeDtypeStruct((len(kinds), HALF, rows, 128), jnp.float32)
    return pl.pallas_call(
        functools.partial(attention_kernel, kinds, numbers, follows, ends),
        out_shape=out,
        in_specs=[smem()] + [vmem()] * (2 + len(kinds) + len(numbers) + follows),
        out_specs=vmem(),
        scratch_shapes=[
            pltpu.VMEM((HALF, rows, hdim), jnp.bfloat16),
            pltpu.VMEM((len(numbers), part, rows), jnp.bfloat16),
            pltpu.VMEM((len(numbers), HALF, wide, rows), jnp.bfloat16),
            pltpu.SMEM((len(numbers) + 1,), jnp.int32),
        ],
        compiler_params=limit(16),
        cost_estimate=pl.CostEstimate(
            flops=2_000_000_000 * len(kinds), bytes_accessed=2_000_000, transcendentals=1_000_000
        ),
    )(where, need, segs, *queries, *blocks, *((before,) if follows else ()))


def project_kernel(
    pair_rows, where_ref, owners_ref, offsets_ref, own_ref, other_ref, weight_ref, tokens_ref, *outs
):
    piece = outs[0].shape[0]
    slots = piece * len(outs)
    rows, width = tokens_ref.shape
    mrows = rows // 4
    capacity = 2 * mrows
    owner = jnp.broadcast_to(owners_ref[...].astype(jnp.float32), (mrows, mrows))
    earlier = lax.broadcasted_iota(jnp.int32, (mrows, mrows), 0)
    later = lax.broadcasted_iota(jnp.int32, (mrows, mrows), 1)
    column = jnp.sum(jnp.where(earlier == later, owner, 0.0), axis=1, keepdims=True)
    ahead = jnp.where((owner == column) & (earlier < later), 1.0, 0.0)
    slot = owner[:1] * pair_rows + jnp.sum(ahead, axis=0, keepdims=True)
    line = lax.broadcasted_iota(jnp.int32, (16, mrows), 0)
    meta = jnp.where(line == 0, slot, jnp.where(line == 1, offsets_ref[...].astype(jnp.float32), 0.0))
    row = lax.broadcasted_iota(jnp.int32, (mrows, rows), 0)
    patch = lax.broadcasted_iota(jnp.int32, (mrows, rows), 1)
    spread = jnp.where(patch // 4 == row, 1.0, 0.0).astype(jnp.bfloat16)
    meta = jnp.dot(meta.astype(jnp.bfloat16), spread, preferred_element_type=jnp.float32)
    part = own_ref.shape[0]
    half = where_ref[0] % 2
    hidden = tokens_ref[...].astype(jnp.float32)
    for ref, which in ((own_ref, half), (other_ref, 1 - half)):
        hidden += lax.dot_general(
            ref[...],
            weight_ref[pl.ds(pl.multiple_of(which * part, 16), part), :],
            (((0,), (0,)), ((), ())),
            preferred_element_type=jnp.float32,
        )
    hidden = hidden.astype(jnp.bfloat16)
    place = meta[:1]
    if len(outs) > 1:
        place = place - (where_ref[0] * pair_rows).astype(jnp.float32)
        place = jnp.where(place < 0, place + slots, place)
    slot = lax.broadcasted_iota(jnp.int32, (slots, rows), 0).astype(jnp.float32)
    quarter = lax.broadcasted_iota(jnp.int32, (1, rows), 1) % 4
    for j in range(4):
        mine = jnp.where(quarter == j, place, -1.0) == slot
        if j == 0:
            offset = jnp.where(mine, meta[1:2] - capacity, 0.0)
            offset = capacity + jnp.sum(offset, axis=1, keepdims=True)
            offset = jnp.broadcast_to(offset, (slots, 128)).astype(jnp.bfloat16)
            for d, out in enumerate(outs):
                out[:, 4 * width :] = offset[d * piece : (d + 1) * piece]
        pick = jnp.where(mine, 1.0, 0.0).astype(jnp.bfloat16)
        picked = jnp.dot(pick, hidden, preferred_element_type=jnp.float32).astype(jnp.bfloat16)
        for d, out in enumerate(outs):
            out[:, j * width : (j + 1) * width] = picked[d * piece : (d + 1) * piece]


def project(where, owners, offsets, own, other, out_weight, tokens, pieces, slots, pair_rows):
    rows, width = tokens.shape
    return pl.pallas_call(
        functools.partial(project_kernel, pair_rows),
        out_shape=[jax.ShapeDtypeStruct((slots // pieces, 4 * width + 128), jnp.bfloat16)] * pieces,
        in_specs=[smem()] + [vmem()] * 6,
        out_specs=[vmem()] * pieces,
        compiler_params=limit(24),
    )(where, owners, offsets, own, other, out_weight, tokens)


def place_kernel(*refs):
    *arrived, out_hbm, held, sems = refs
    capacity, merged = out_hbm.shape
    step = merged // 4

    def columns_of(start, size):
        return jnp.concatenate([ref[:, start : start + size] for ref in arrived], axis=0)

    offset = columns_of(merged, 128).astype(jnp.float32)[:, :1]
    row = lax.broadcasted_iota(jnp.int32, (offset.shape[0], capacity), 1).astype(jnp.float32)
    pick = jnp.where(offset == row, 1.0, 0.0).astype(jnp.bfloat16)
    stores = []
    for j in range(4):
        held[j] = lax.dot_general(
            pick,
            columns_of(j * step, step),
            (((0,), (0,)), ((), ())),
            preferred_element_type=jnp.float32,
        ).astype(jnp.bfloat16)
        columns = out_hbm.at[:, pl.ds(j * step, step)]
        stores.append(pltpu.make_async_copy(held.at[j], columns, sems.at[j]))
        stores[j].start()
    for store in stores:
        store.wait()


def place(arrived, capacity, merged):
    return pl.pallas_call(
        place_kernel,
        out_shape=jax.ShapeDtypeStruct((capacity, merged), jnp.bfloat16),
        in_specs=[vmem()] * len(arrived),
        out_specs=anywhere(),
        scratch_shapes=[
            pltpu.VMEM((4, capacity, merged // 4), jnp.bfloat16),
            pltpu.SemaphoreType.DMA((4,)),
        ],
        compiler_params=limit(24),
    )(*arrived)


def per_device(segment_ids, block_mask, queries, keys, values, tokens, out_weight, owners, offsets):
    rows = queries.shape[0]
    width = tokens.shape[1]
    nblocks = lax.axis_size("blk")
    block_index = lax.axis_index("blk")
    mrows = rows // 4
    capacity = 2 * mrows
    pair_rows = max(2, 2 * mrows // nblocks)
    slots = nblocks * pair_rows
    assert slots <= 256

    def route(step):
        return [(i, i + step(i)) for i in range(nblocks) if 0 <= i + step(i) < nblocks]

    swap = functools.partial(
        lax.ppermute, axis_name="blk", perm=route(lambda i: 1 - 2 * (i % 2))
    )
    ahead = functools.partial(
        lax.ppermute, axis_name="blk", perm=route(lambda i: 2 if i % 2 else -2)
    )
    back = functools.partial(
        lax.ppermute, axis_name="blk", perm=route(lambda i: -2 if i % 2 else 2)
    )

    where = block_index[None].astype(jnp.int32)
    own_q, own_kv, swap_q, swap_kv = prepare(where, queries, keys, values)
    segs, need = survey(where, block_mask, segment_ids[None, :])
    other_kv = swap(swap_kv)
    ahead_own = ahead(own_kv)
    back_own = back(own_kv)
    ready, back_own, swap_q, segs, need = lax.optimization_barrier(
        (other_kv, back_own, swap_q, segs, need)
    )
    back_other = back(ready)
    other_q = swap(swap_q)
    back_far = back(back_other)
    ahead_other = ahead(other_kv)
    ahead_far = ahead(ahead_own)
    near = (own_kv, other_kv, ahead_own, back_own)
    near_numbers = (0, 1, 2, 3)
    fixed = (where, need, segs)
    own = attention(*fixed, (own_q,), (0,), near, near_numbers, None, False)
    other = attention(*fixed, (other_q,), (1,), near, near_numbers, None, False)
    far = (ahead_other, back_other, ahead_far)
    other = attention(*fixed, (other_q,), (1,), far, (4, 5, 6), other, True)
    other = swap(other)
    far = (ahead_other, back_other, back_far)
    own = attention(*fixed, (own_q,), (0,), far, (4, 5, 7), own, True)

    pieces = nblocks if nblocks <= 8 else 1
    outgoing = project(
        where, owners[None, :], offsets[None, :], own, other, out_weight, tokens,
        pieces, slots, pair_rows,
    )
    if pieces > 1:
        arrived = [outgoing[0]] + [None] * (nblocks - 1)
        order = sorted(range(1, nblocks), key=lambda d: (min(d, nblocks - d) == 2, d))
        for d in order:
            arrived[d] = lax.ppermute(
                outgoing[d], "blk", [(i, (i + d) % nblocks) for i in range(nblocks)]
            )
    else:
        arrived = [lax.all_to_all(outgoing[0], "blk", split_axis=0, concat_axis=0, tiled=True)]
    return place(arrived, capacity, 4 * width)


def solution(mesh):
    placed = (
        P("rep"),
        P("rep", None),
        P(("rep", "blk"), None),
        P(("rep", "blk"), None),
        P(("rep", "blk"), None),
        P(("rep", "blk"), None),
        P(),
        P(("rep", "blk")),
        P(("rep", "blk")),
    )
    return jax.shard_map(
        per_device, mesh=mesh, in_specs=placed, out_specs=P(("rep", "blk"), None), check_vma=False
    )
```

```python
import functools

import jax
import jax.numpy as jnp
from jax import lax
from jax.experimental import pallas as pl
from jax.experimental.pallas import tpu as pltpu
from jax.sharding import PartitionSpec as P

HEADS = 8
HALF = HEADS // 2
SPAN = 3
NEG = -1e30
LOG2E = 1.4426950408889634
MIB = 1024 * 1024


def vmem():
    return pl.BlockSpec(memory_space=pltpu.VMEM)


def smem():
    return pl.BlockSpec(memory_space=pltpu.SMEM)


def anywhere():
    return pl.BlockSpec(memory_space=pl.ANY)


def limit(mib):
    return pltpu.CompilerParams(vmem_limit_bytes=mib * MIB)


PLACES = ((3, 1), (4, -1), (5, -3), (1, 5), (6, -5), (2, 3), (7, -7), (0, 7))


def asking(me, kind):
    return me if kind == 0 else me + 1 - 2 * (me % 2)


def key_block(me, number):
    half = me % 2
    return me - half - SPAN + PLACES[number][0] + PLACES[number][1] * half


def prepare_kernel(where_ref, q_hbm, k_hbm, v_hbm, own_q, own_kv, swap_q, swap_kv, held, turned, sems):
    part = q_hbm.shape[1] // 2
    loads = [
        pltpu.make_async_copy(ref, held.at[i], sems.at[i])
        for i, ref in enumerate((k_hbm, v_hbm, q_hbm))
    ]
    for load in loads:
        load.start()
    me = where_ref[0]
    half = me % 2
    mine = pl.multiple_of(half * part, 16)
    other = pl.multiple_of((1 - half) * part, 16)
    for i in range(3):
        loads[i].wait()
        turned[i] = held[i].T
        if i < 2:
            own_kv[i * part : (i + 1) * part, :] = turned[i, pl.ds(mine, part), :]
            swap_kv[i * part : (i + 1) * part, :] = turned[i, pl.ds(other, part), :]
        else:
            own_q[...] = turned[i, pl.ds(mine, part), :]
            swap_q[...] = turned[i, pl.ds(other, part), :]


def prepare(where, queries, keys, values):
    rows, features = queries.shape
    part = features // 2
    single = jax.ShapeDtypeStruct((part, rows), queries.dtype)
    double = jax.ShapeDtypeStruct((2 * part, rows), queries.dtype)
    return pl.pallas_call(
        prepare_kernel,
        out_shape=[single, double, single, double],
        in_specs=[smem()] + [anywhere()] * 3,
        out_specs=[vmem()] * 4,
        scratch_shapes=[
            pltpu.VMEM((3, rows, features), queries.dtype),
            pltpu.VMEM((3, features, rows), queries.dtype),
            pltpu.SemaphoreType.DMA((3,)),
        ],
        compiler_params=limit(53),
    )(where, queries, keys, values)


def survey_kernel(where_ref, mask_ref, segs_ref, seg_out, need_out):
    seg_out[...] = segs_ref[...].astype(jnp.float32)
    me = where_ref[0]
    nblocks = mask_ref.shape[0]
    bits = jnp.int32(0)
    for kind in range(2):
        asker = asking(me, kind)
        for number in range(len(PLACES)):
            block = key_block(me, number)
            inside = (block >= 0) & (block < nblocks) & (jnp.abs(block - asker) <= SPAN)
            allowed = mask_ref[asker, jnp.clip(block, 0, nblocks - 1)] > 0
            bits += (inside & allowed).astype(jnp.int32) << (kind * len(PLACES) + number)
    need_out[...] = jnp.full(need_out.shape, bits, jnp.int32)


def survey(where, mask, segs):
    return pl.pallas_call(
        survey_kernel,
        out_shape=[
            jax.ShapeDtypeStruct(segs.shape, jnp.float32),
            jax.ShapeDtypeStruct((8, 128), jnp.int32),
        ],
        in_specs=[smem()] * 2 + [vmem()],
        out_specs=[vmem()] * 2,
        compiler_params=limit(16),
    )(where, mask, segs)


def attention_kernel(kinds, numbers, rows_of, follows, ends, where_ref, need_ref, seg_ref, *refs):
    queries, refs = refs[: len(kinds)], refs[len(kinds) :]
    arrays = max(array for array, _ in rows_of) + 1
    blocks, refs = refs[:arrays], refs[arrays:]
    if follows:
        before, refs = refs[0], refs[1:]
    out_ref, query_s, key_s, value_s, chosen_s = refs
    part, rows = queries[0].shape
    hdim = part // HALF
    wide = value_s.shape[2]
    nblocks = seg_ref.shape[1] // rows
    factor = LOG2E / (hdim**0.5)
    me = where_ref[0]
    column = [key_block(me, b) for b in numbers]
    asker = [asking(me, kind) for kind in kinds]
    bits = jnp.max(need_ref[...])
    need = [[(bits >> (kind * len(PLACES) + b)) & 1 for b in numbers] for kind in kinds]

    def segment(block):
        start = pl.multiple_of(jnp.clip(block, 0, nblocks - 1) * rows, 128)
        return seg_ref[:, pl.ds(start, rows)]

    for b in range(len(numbers)):
        wanted = need[0][b]
        for n in range(1, len(kinds)):
            wanted = wanted + need[n][b]

        @pl.when(wanted > 0)
        def _(b=b):
            array, first = rows_of[b]
            key_s[b] = blocks[array][first : first + part, :]
            for h in range(HALF):
                start = first + part + h * hdim
                value_s[b, h, :hdim, :] = blocks[array][start : start + hdim, :]
                value_s[b, h, hdim:, :] = jnp.ones((wide - hdim, rows), jnp.bfloat16)

    for n in range(len(kinds)):
        size = 0
        for b in range(len(numbers)):
            chosen_s[size] = b
            size = size + need[n][b]
        for h in range(HALF):
            query_s[h] = queries[n][h * hdim : (h + 1) * hdim, :].T
        query_seg = jnp.broadcast_to(segment(asker[n]), (128, rows)).T
        query_seg = jnp.concatenate([query_seg] * (rows // 128), axis=1)

        def finish(h, peak, accum, n=n):
            if ends:
                turned = accum.T
                lines = slice(h * hdim, (h + 1) * hdim)
                out_ref[lines, :] = (turned[:hdim] / turned[hdim : hdim + 1]).astype(out_ref.dtype)
            else:
                peak = jnp.broadcast_to(peak, (rows, 128 - wide))
                out_ref[n, h] = jnp.concatenate([accum, peak], axis=1)

        if follows:

            @pl.when(size == 0)
            def _():
                for h in range(HALF):
                    state = before[0, h]
                    finish(h, state[:, wide : wide + 1], state[:, :wide])

        for fixed in range(1, len(numbers) + 1):

            @pl.when(size == fixed)
            def _():
                picked = [chosen_s[b] for b in range(fixed)]
                key_segs = [
                    segment(sum(jnp.where(b == i, column[i], 0) for i in range(len(numbers))))
                    for b in picked
                ]

                def one_head(h):
                    lines = slice(h * hdim, (h + 1) * hdim)
                    query = query_s[h]
                    scores = []
                    for b, key_seg in zip(picked, key_segs):
                        score = jnp.dot(
                            query, key_s[b, lines, :], preferred_element_type=jnp.float32
                        )
                        scores.append(jnp.where(query_seg == key_seg, score, NEG))
                    peak = functools.reduce(jnp.maximum, scores)
                    peak = jnp.max(peak, axis=1, keepdims=True)
                    accum = jnp.zeros((rows, wide), jnp.float32)
                    if follows:
                        state = before[0, h]
                        old = state[:, wide : wide + 1]
                        peak = jnp.maximum(peak, old)
                        accum = state[:, :wide] * jnp.exp2((old - peak) * factor)
                    for b, score in zip(picked, scores):
                        weights = jnp.exp2((score - peak) * factor).astype(jnp.bfloat16)
                        accum += lax.dot_general(
                            weights,
                            value_s[b, h],
                            (((1,), (1,)), ((), ())),
                            preferred_element_type=jnp.float32,
                        )
                    finish(h, peak, accum)

                for h in range(HALF):
                    one_head(h)


def attention(where, need, segs, queries, kinds, blocks, numbers, before, ends):
    part, rows = queries[0].shape
    hdim = part // HALF
    wide = hdim + 16
    follows = before is not None
    rows_of = [
        (array, first)
        for array, block in enumerate(blocks)
        for first in range(0, block.shape[0], 2 * part)
    ]
    if ends:
        out = jax.ShapeDtypeStruct((part, rows), jnp.bfloat16)
    else:
        out = jax.ShapeDtypeStruct((len(kinds), HALF, rows, 128), jnp.float32)
    return pl.pallas_call(
        functools.partial(attention_kernel, kinds, numbers, rows_of, follows, ends),
        out_shape=out,
        in_specs=[smem()] + [vmem()] * (2 + len(kinds) + len(blocks) + follows),
        out_specs=vmem(),
        scratch_shapes=[
            pltpu.VMEM((HALF, rows, hdim), jnp.bfloat16),
            pltpu.VMEM((len(numbers), part, rows), jnp.bfloat16),
            pltpu.VMEM((len(numbers), HALF, wide, rows), jnp.bfloat16),
            pltpu.SMEM((len(numbers) + 1,), jnp.int32),
        ],
        compiler_params=limit(16),
        cost_estimate=pl.CostEstimate(
            flops=2_000_000_000 * len(kinds), bytes_accessed=2_000_000, transcendentals=1_000_000
        ),
    )(where, need, segs, *queries, *blocks, *((before,) if follows else ()))


def stack_kernel(*refs):
    *parts, out_ref = refs
    first = 0
    for ref in parts:
        out_ref[first : first + ref.shape[0], :] = ref[...]
        first += ref.shape[0]


def stack(*parts):
    lines = sum(part.shape[0] for part in parts)
    return pl.pallas_call(
        stack_kernel,
        out_shape=jax.ShapeDtypeStruct((lines, parts[0].shape[1]), parts[0].dtype),
        in_specs=[vmem()] * len(parts),
        out_specs=vmem(),
        compiler_params=limit(16),
    )(*parts)


def project_kernel(
    pair_rows, where_ref, owners_ref, offsets_ref, own_ref, other_ref, weight_ref, tokens_ref, *outs
):
    piece = outs[0].shape[0]
    slots = piece * len(outs)
    rows, width = tokens_ref.shape
    mrows = rows // 4
    capacity = 2 * mrows
    owner = jnp.broadcast_to(owners_ref[...].astype(jnp.float32), (mrows, mrows))
    earlier = lax.broadcasted_iota(jnp.int32, (mrows, mrows), 0)
    later = lax.broadcasted_iota(jnp.int32, (mrows, mrows), 1)
    column = jnp.sum(jnp.where(earlier == later, owner, 0.0), axis=1, keepdims=True)
    ahead = jnp.where((owner == column) & (earlier < later), 1.0, 0.0)
    slot = owner[:1] * pair_rows + jnp.sum(ahead, axis=0, keepdims=True)
    line = lax.broadcasted_iota(jnp.int32, (16, mrows), 0)
    meta = jnp.where(line == 0, slot, jnp.where(line == 1, offsets_ref[...].astype(jnp.float32), 0.0))
    row = lax.broadcasted_iota(jnp.int32, (mrows, rows), 0)
    patch = lax.broadcasted_iota(jnp.int32, (mrows, rows), 1)
    spread = jnp.where(patch // 4 == row, 1.0, 0.0).astype(jnp.bfloat16)
    meta = jnp.dot(meta.astype(jnp.bfloat16), spread, preferred_element_type=jnp.float32)
    part = own_ref.shape[0]
    half = where_ref[0] % 2
    hidden = tokens_ref[...].astype(jnp.float32)
    for ref, which in ((own_ref, half), (other_ref, 1 - half)):
        hidden += lax.dot_general(
            ref[...],
            weight_ref[pl.ds(pl.multiple_of(which * part, 16), part), :],
            (((0,), (0,)), ((), ())),
            preferred_element_type=jnp.float32,
        )
    hidden = hidden.astype(jnp.bfloat16)
    place = meta[:1]
    if len(outs) > 1:
        place = place - (where_ref[0] * pair_rows).astype(jnp.float32)
        place = jnp.where(place < 0, place + slots, place)
    slot = lax.broadcasted_iota(jnp.int32, (slots, rows), 0).astype(jnp.float32)
    quarter = lax.broadcasted_iota(jnp.int32, (1, rows), 1) % 4
    for j in range(4):
        mine = jnp.where(quarter == j, place, -1.0) == slot
        if j == 0:
            offset = jnp.where(mine, meta[1:2] - capacity, 0.0)
            offset = capacity + jnp.sum(offset, axis=1, keepdims=True)
            offset = jnp.broadcast_to(offset, (slots, 128)).astype(jnp.bfloat16)
            for d, out in enumerate(outs):
                out[:, 4 * width :] = offset[d * piece : (d + 1) * piece]
        pick = jnp.where(mine, 1.0, 0.0).astype(jnp.bfloat16)
        picked = jnp.dot(pick, hidden, preferred_element_type=jnp.float32).astype(jnp.bfloat16)
        for d, out in enumerate(outs):
            out[:, j * width : (j + 1) * width] = picked[d * piece : (d + 1) * piece]


def project(where, owners, offsets, own, other, out_weight, tokens, pieces, slots, pair_rows):
    rows, width = tokens.shape
    return pl.pallas_call(
        functools.partial(project_kernel, pair_rows),
        out_shape=[jax.ShapeDtypeStruct((slots // pieces, 4 * width + 128), jnp.bfloat16)] * pieces,
        in_specs=[smem()] + [vmem()] * 6,
        out_specs=[vmem()] * pieces,
        compiler_params=limit(24),
    )(where, owners, offsets, own, other, out_weight, tokens)


def place_kernel(*refs):
    *arrived, out_hbm, held, sems = refs
    capacity, merged = out_hbm.shape
    step = merged // 4

    def columns_of(start, size):
        return jnp.concatenate([ref[:, start : start + size] for ref in arrived], axis=0)

    offset = columns_of(merged, 128).astype(jnp.float32)[:, :1]
    row = lax.broadcasted_iota(jnp.int32, (offset.shape[0], capacity), 1).astype(jnp.float32)
    pick = jnp.where(offset == row, 1.0, 0.0).astype(jnp.bfloat16)
    stores = []
    for j in range(4):
        held[j] = lax.dot_general(
            pick,
            columns_of(j * step, step),
            (((0,), (0,)), ((), ())),
            preferred_element_type=jnp.float32,
        ).astype(jnp.bfloat16)
        columns = out_hbm.at[:, pl.ds(j * step, step)]
        stores.append(pltpu.make_async_copy(held.at[j], columns, sems.at[j]))
        stores[j].start()
    for store in stores:
        store.wait()


def place(arrived, capacity, merged):
    return pl.pallas_call(
        place_kernel,
        out_shape=jax.ShapeDtypeStruct((capacity, merged), jnp.bfloat16),
        in_specs=[vmem()] * len(arrived),
        out_specs=anywhere(),
        scratch_shapes=[
            pltpu.VMEM((4, capacity, merged // 4), jnp.bfloat16),
            pltpu.SemaphoreType.DMA((4,)),
        ],
        compiler_params=limit(24),
    )(*arrived)


def per_device(segment_ids, block_mask, queries, keys, values, tokens, out_weight, owners, offsets):
    rows = queries.shape[0]
    width = tokens.shape[1]
    nblocks = lax.axis_size("blk")
    block_index = lax.axis_index("blk")
    mrows = rows // 4
    capacity = 2 * mrows
    pair_rows = max(2, 2 * mrows // nblocks)
    slots = nblocks * pair_rows
    assert slots <= 256

    def route(step):
        return [(i, i + step(i)) for i in range(nblocks) if 0 <= i + step(i) < nblocks]

    swap = functools.partial(
        lax.ppermute, axis_name="blk", perm=route(lambda i: 1 - 2 * (i % 2))
    )
    ahead = functools.partial(
        lax.ppermute, axis_name="blk", perm=route(lambda i: 2 if i % 2 else -2)
    )
    back = functools.partial(
        lax.ppermute, axis_name="blk", perm=route(lambda i: -2 if i % 2 else 2)
    )

    where = block_index[None].astype(jnp.int32)
    own_q, own_kv, swap_q, swap_kv = prepare(where, queries, keys, values)
    segs, need = survey(where, block_mask, segment_ids[None, :])
    other_kv = swap(swap_kv)
    ahead_own = ahead(own_kv)
    back_own = back(own_kv)
    ready, back_own, swap_q, segs, need = lax.optimization_barrier(
        (other_kv, back_own, swap_q, segs, need)
    )
    back_other = back(ready)
    ahead_both = ahead(stack(other_kv, ahead_own))
    other_q = swap(swap_q)
    back_far = back(back_other)
    near = (own_kv, other_kv, ahead_own, back_own)
    near_numbers = (0, 1, 2, 3)
    fixed = (where, need, segs)
    own = attention(*fixed, (own_q,), (0,), near, near_numbers, None, False)
    other = attention(*fixed, (other_q,), (1,), near, near_numbers, None, False)
    far = (ahead_both, back_other)
    other = attention(*fixed, (other_q,), (1,), far, (4, 6, 5), other, True)
    other = swap(other)
    far = (ahead_both, back_other, back_far)
    own = attention(*fixed, (own_q,), (0,), far, (4, 6, 5, 7), own, True)

    pieces = nblocks if nblocks <= 8 else 1
    outgoing = project(
        where, owners[None, :], offsets[None, :], own, other, out_weight, tokens,
        pieces, slots, pair_rows,
    )
    if pieces > 1:
        arrived = [outgoing[0]] + [None] * (nblocks - 1)
        order = sorted(range(1, nblocks), key=lambda d: (min(d, nblocks - d) == 2, d))
        for d in order:
            arrived[d] = lax.ppermute(
                outgoing[d], "blk", [(i, (i + d) % nblocks) for i in range(nblocks)]
            )
    else:
        arrived = [lax.all_to_all(outgoing[0], "blk", split_axis=0, concat_axis=0, tiled=True)]
    return place(arrived, capacity, 4 * width)


def solution(mesh):
    placed = (
        P("rep"),
        P("rep", None),
        P(("rep", "blk"), None),
        P(("rep", "blk"), None),
        P(("rep", "blk"), None),
        P(("rep", "blk"), None),
        P(),
        P(("rep", "blk")),
        P(("rep", "blk")),
    )
    return jax.shard_map(
        per_device, mesh=mesh, in_specs=placed, out_specs=P(("rep", "blk"), None), check_vma=False
    )
```

```python
import functools

import jax
import jax.numpy as jnp
from jax import lax
from jax.experimental import pallas as pl
from jax.experimental.pallas import tpu as pltpu
from jax.sharding import PartitionSpec as P

HEADS = 8
HALF = HEADS // 2
SPAN = 3
NEG = -1e30
LOG2E = 1.4426950408889634
MIB = 1024 * 1024


def vmem():
    return pl.BlockSpec(memory_space=pltpu.VMEM)


def smem():
    return pl.BlockSpec(memory_space=pltpu.SMEM)


def anywhere():
    return pl.BlockSpec(memory_space=pl.ANY)


def limit(mib):
    return pltpu.CompilerParams(vmem_limit_bytes=mib * MIB)


PLACES = ((3, 1), (4, -1), (5, -3), (1, 5), (6, -5), (2, 3), (7, -7), (0, 7))


def asking(me, kind):
    return me if kind == 0 else me + 1 - 2 * (me % 2)


def key_block(me, number):
    half = me % 2
    return me - half - SPAN + PLACES[number][0] + PLACES[number][1] * half


def prepare_kernel(where_ref, q_hbm, k_hbm, v_hbm, own_q, own_kv, swap_q, swap_kv, held, turned, sems):
    part = q_hbm.shape[1] // 2
    loads = [
        pltpu.make_async_copy(ref, held.at[i], sems.at[i])
        for i, ref in enumerate((k_hbm, v_hbm, q_hbm))
    ]
    for load in loads:
        load.start()
    me = where_ref[0]
    half = me % 2
    mine = pl.multiple_of(half * part, 16)
    other = pl.multiple_of((1 - half) * part, 16)
    for i in range(3):
        loads[i].wait()
        turned[i] = held[i].T
        if i < 2:
            own_kv[i * part : (i + 1) * part, :] = turned[i, pl.ds(mine, part), :]
            swap_kv[i * part : (i + 1) * part, :] = turned[i, pl.ds(other, part), :]
        else:
            own_q[...] = turned[i, pl.ds(mine, part), :]
            swap_q[...] = turned[i, pl.ds(other, part), :]


def prepare(where, queries, keys, values):
    rows, features = queries.shape
    part = features // 2
    single = jax.ShapeDtypeStruct((part, rows), queries.dtype)
    double = jax.ShapeDtypeStruct((2 * part, rows), queries.dtype)
    return pl.pallas_call(
        prepare_kernel,
        out_shape=[single, double, single, double],
        in_specs=[smem()] + [anywhere()] * 3,
        out_specs=[vmem()] * 4,
        scratch_shapes=[
            pltpu.VMEM((3, rows, features), queries.dtype),
            pltpu.VMEM((3, features, rows), queries.dtype),
            pltpu.SemaphoreType.DMA((3,)),
        ],
        compiler_params=limit(53),
    )(where, queries, keys, values)


def survey_kernel(where_ref, mask_ref, segs_ref, seg_out, need_out):
    seg_out[...] = segs_ref[...].astype(jnp.float32)
    me = where_ref[0]
    nblocks = mask_ref.shape[0]
    bits = jnp.int32(0)
    for kind in range(2):
        asker = asking(me, kind)
        for number in range(len(PLACES)):
            block = key_block(me, number)
            inside = (block >= 0) & (block < nblocks) & (jnp.abs(block - asker) <= SPAN)
            allowed = mask_ref[asker, jnp.clip(block, 0, nblocks - 1)] > 0
            bits += (inside & allowed).astype(jnp.int32) << (kind * len(PLACES) + number)
    need_out[...] = jnp.full(need_out.shape, bits, jnp.int32)


def survey(where, mask, segs):
    return pl.pallas_call(
        survey_kernel,
        out_shape=[
            jax.ShapeDtypeStruct(segs.shape, jnp.float32),
            jax.ShapeDtypeStruct((8, 128), jnp.int32),
        ],
        in_specs=[smem()] * 2 + [vmem()],
        out_specs=[vmem()] * 2,
        compiler_params=limit(16),
    )(where, mask, segs)


def attention_kernel(kinds, numbers, rows_of, follows, ends, where_ref, need_ref, seg_ref, *refs):
    queries, refs = refs[: len(kinds)], refs[len(kinds) :]
    arrays = max(array for array, _ in rows_of) + 1
    blocks, refs = refs[:arrays], refs[arrays:]
    if follows:
        before, refs = refs[0], refs[1:]
    out_ref, query_s, key_s, value_s, chosen_s = refs
    part, rows = queries[0].shape
    hdim = part // HALF
    wide = value_s.shape[2]
    nblocks = seg_ref.shape[1] // rows
    factor = LOG2E / (hdim**0.5)
    me = where_ref[0]
    column = [key_block(me, b) for b in numbers]
    asker = [asking(me, kind) for kind in kinds]
    bits = jnp.max(need_ref[...])
    need = [[(bits >> (kind * len(PLACES) + b)) & 1 for b in numbers] for kind in kinds]

    def segment(block):
        start = pl.multiple_of(jnp.clip(block, 0, nblocks - 1) * rows, 128)
        return seg_ref[:, pl.ds(start, rows)]

    for b in range(len(numbers)):
        wanted = need[0][b]
        for n in range(1, len(kinds)):
            wanted = wanted + need[n][b]

        @pl.when(wanted > 0)
        def _(b=b):
            array, first = rows_of[b]
            key_s[b] = blocks[array][first : first + part, :]
            for h in range(HALF):
                start = first + part + h * hdim
                value_s[b, h, :hdim, :] = blocks[array][start : start + hdim, :]
                value_s[b, h, hdim:, :] = jnp.ones((wide - hdim, rows), jnp.bfloat16)

    for n in range(len(kinds)):
        size = 0
        for b in range(len(numbers)):
            chosen_s[size] = b
            size = size + need[n][b]
        for h in range(HALF):
            query_s[h] = queries[n][h * hdim : (h + 1) * hdim, :].T
        query_seg = jnp.broadcast_to(segment(asker[n]), (128, rows)).T
        query_seg = jnp.concatenate([query_seg] * (rows // 128), axis=1)

        def finish(h, peak, accum, n=n):
            if ends:
                turned = accum.T
                lines = slice(h * hdim, (h + 1) * hdim)
                out_ref[lines, :] = (turned[:hdim] / turned[hdim : hdim + 1]).astype(out_ref.dtype)
            else:
                peak = jnp.broadcast_to(peak, (rows, 128 - wide))
                out_ref[n, h] = jnp.concatenate([accum, peak], axis=1)

        if follows:

            @pl.when(size == 0)
            def _():
                for h in range(HALF):
                    state = before[0, h]
                    finish(h, state[:, wide : wide + 1], state[:, :wide])

        for fixed in range(1, len(numbers) + 1):

            @pl.when(size == fixed)
            def _():
                picked = [chosen_s[b] for b in range(fixed)]
                key_segs = [
                    segment(sum(jnp.where(b == i, column[i], 0) for i in range(len(numbers))))
                    for b in picked
                ]

                def one_head(h):
                    lines = slice(h * hdim, (h + 1) * hdim)
                    query = query_s[h]
                    scores = []
                    for b, key_seg in zip(picked, key_segs):
                        score = jnp.dot(
                            query, key_s[b, lines, :], preferred_element_type=jnp.float32
                        )
                        scores.append(jnp.where(query_seg == key_seg, score, NEG))
                    peak = functools.reduce(jnp.maximum, scores)
                    peak = jnp.max(peak, axis=1, keepdims=True)
                    accum = jnp.zeros((rows, wide), jnp.float32)
                    if follows:
                        state = before[0, h]
                        old = state[:, wide : wide + 1]
                        peak = jnp.maximum(peak, old)
                        accum = state[:, :wide] * jnp.exp2((old - peak) * factor)
                    for b, score in zip(picked, scores):
                        weights = jnp.exp2((score - peak) * factor).astype(jnp.bfloat16)
                        accum += lax.dot_general(
                            weights,
                            value_s[b, h],
                            (((1,), (1,)), ((), ())),
                            preferred_element_type=jnp.float32,
                        )
                    finish(h, peak, accum)

                for h in range(HALF):
                    one_head(h)


def attention(where, need, segs, queries, kinds, blocks, numbers, before, ends):
    part, rows = queries[0].shape
    hdim = part // HALF
    wide = hdim + 16
    follows = before is not None
    rows_of = [
        (array, first)
        for array, block in enumerate(blocks)
        for first in range(0, block.shape[0], 2 * part)
    ]
    if ends:
        out = jax.ShapeDtypeStruct((part, rows), jnp.bfloat16)
    else:
        out = jax.ShapeDtypeStruct((len(kinds), HALF, rows, 128), jnp.float32)
    return pl.pallas_call(
        functools.partial(attention_kernel, kinds, numbers, rows_of, follows, ends),
        out_shape=out,
        in_specs=[smem()] + [vmem()] * (2 + len(kinds) + len(blocks) + follows),
        out_specs=vmem(),
        scratch_shapes=[
            pltpu.VMEM((HALF, rows, hdim), jnp.bfloat16),
            pltpu.VMEM((len(numbers), part, rows), jnp.bfloat16),
            pltpu.VMEM((len(numbers), HALF, wide, rows), jnp.bfloat16),
            pltpu.SMEM((len(numbers) + 1,), jnp.int32),
        ],
        compiler_params=limit(16),
        cost_estimate=pl.CostEstimate(
            flops=2_000_000_000 * len(kinds), bytes_accessed=2_000_000, transcendentals=1_000_000
        ),
    )(where, need, segs, *queries, *blocks, *((before,) if follows else ()))


def stack_kernel(*refs):
    *parts, out_ref = refs
    first = 0
    for ref in parts:
        out_ref[first : first + ref.shape[0], :] = ref[...]
        first += ref.shape[0]


def stack(*parts):
    lines = sum(part.shape[0] for part in parts)
    return pl.pallas_call(
        stack_kernel,
        out_shape=jax.ShapeDtypeStruct((lines, parts[0].shape[1]), parts[0].dtype),
        in_specs=[vmem()] * len(parts),
        out_specs=vmem(),
        compiler_params=limit(16),
    )(*parts)


def project_kernel(
    pair_rows, where_ref, owners_ref, offsets_ref, own_ref, other_ref, weight_ref, tokens_ref, *outs
):
    piece = outs[0].shape[0]
    slots = piece * len(outs)
    rows, width = tokens_ref.shape
    mrows = rows // 4
    capacity = 2 * mrows
    owner = jnp.broadcast_to(owners_ref[...].astype(jnp.float32), (mrows, mrows))
    earlier = lax.broadcasted_iota(jnp.int32, (mrows, mrows), 0)
    later = lax.broadcasted_iota(jnp.int32, (mrows, mrows), 1)
    column = jnp.sum(jnp.where(earlier == later, owner, 0.0), axis=1, keepdims=True)
    ahead = jnp.where((owner == column) & (earlier < later), 1.0, 0.0)
    slot = owner[:1] * pair_rows + jnp.sum(ahead, axis=0, keepdims=True)
    line = lax.broadcasted_iota(jnp.int32, (16, mrows), 0)
    meta = jnp.where(line == 0, slot, jnp.where(line == 1, offsets_ref[...].astype(jnp.float32), 0.0))
    row = lax.broadcasted_iota(jnp.int32, (mrows, rows), 0)
    patch = lax.broadcasted_iota(jnp.int32, (mrows, rows), 1)
    spread = jnp.where(patch // 4 == row, 1.0, 0.0).astype(jnp.bfloat16)
    meta = jnp.dot(meta.astype(jnp.bfloat16), spread, preferred_element_type=jnp.float32)
    part = own_ref.shape[0]
    half = where_ref[0] % 2
    hidden = tokens_ref[...].astype(jnp.float32)
    for ref, which in ((own_ref, half), (other_ref, 1 - half)):
        hidden += lax.dot_general(
            ref[...],
            weight_ref[pl.ds(pl.multiple_of(which * part, 16), part), :],
            (((0,), (0,)), ((), ())),
            preferred_element_type=jnp.float32,
        )
    hidden = hidden.astype(jnp.bfloat16)
    place = meta[:1]
    if len(outs) > 1:
        place = place - (where_ref[0] * pair_rows).astype(jnp.float32)
        place = jnp.where(place < 0, place + slots, place)
    slot = lax.broadcasted_iota(jnp.int32, (slots, rows), 0).astype(jnp.float32)
    quarter = lax.broadcasted_iota(jnp.int32, (1, rows), 1) % 4
    for j in range(4):
        mine = jnp.where(quarter == j, place, -1.0) == slot
        if j == 0:
            offset = jnp.where(mine, meta[1:2] - capacity, 0.0)
            offset = capacity + jnp.sum(offset, axis=1, keepdims=True)
            offset = jnp.broadcast_to(offset, (slots, 128)).astype(jnp.bfloat16)
            for d, out in enumerate(outs):
                out[:, 4 * width :] = offset[d * piece : (d + 1) * piece]
        pick = jnp.where(mine, 1.0, 0.0).astype(jnp.bfloat16)
        picked = jnp.dot(pick, hidden, preferred_element_type=jnp.float32).astype(jnp.bfloat16)
        for d, out in enumerate(outs):
            out[:, j * width : (j + 1) * width] = picked[d * piece : (d + 1) * piece]


def project(where, owners, offsets, own, other, out_weight, tokens, pieces, slots, pair_rows):
    rows, width = tokens.shape
    return pl.pallas_call(
        functools.partial(project_kernel, pair_rows),
        out_shape=[jax.ShapeDtypeStruct((slots // pieces, 4 * width + 128), jnp.bfloat16)] * pieces,
        in_specs=[smem()] + [vmem()] * 6,
        out_specs=[vmem()] * pieces,
        compiler_params=limit(24),
    )(where, owners, offsets, own, other, out_weight, tokens)


def place_kernel(*refs):
    *arrived, out_hbm, held, sems = refs
    capacity, merged = out_hbm.shape
    step = merged // 4

    def columns_of(start, size):
        return jnp.concatenate([ref[:, start : start + size] for ref in arrived], axis=0)

    offset = columns_of(merged, 128).astype(jnp.float32)[:, :1]
    row = lax.broadcasted_iota(jnp.int32, (offset.shape[0], capacity), 1).astype(jnp.float32)
    pick = jnp.where(offset == row, 1.0, 0.0).astype(jnp.bfloat16)
    stores = []
    for j in range(4):
        held[j] = lax.dot_general(
            pick,
            columns_of(j * step, step),
            (((0,), (0,)), ((), ())),
            preferred_element_type=jnp.float32,
        ).astype(jnp.bfloat16)
        columns = out_hbm.at[:, pl.ds(j * step, step)]
        stores.append(pltpu.make_async_copy(held.at[j], columns, sems.at[j]))
        stores[j].start()
    for store in stores:
        store.wait()


def place(arrived, capacity, merged):
    return pl.pallas_call(
        place_kernel,
        out_shape=jax.ShapeDtypeStruct((capacity, merged), jnp.bfloat16),
        in_specs=[vmem()] * len(arrived),
        out_specs=anywhere(),
        scratch_shapes=[
            pltpu.VMEM((4, capacity, merged // 4), jnp.bfloat16),
            pltpu.SemaphoreType.DMA((4,)),
        ],
        compiler_params=limit(24),
    )(*arrived)


def per_device(segment_ids, block_mask, queries, keys, values, tokens, out_weight, owners, offsets):
    rows = queries.shape[0]
    width = tokens.shape[1]
    nblocks = lax.axis_size("blk")
    block_index = lax.axis_index("blk")
    mrows = rows // 4
    capacity = 2 * mrows
    pair_rows = max(2, 2 * mrows // nblocks)
    slots = nblocks * pair_rows
    assert slots <= 256

    def route(step):
        return [(i, i + step(i)) for i in range(nblocks) if 0 <= i + step(i) < nblocks]

    swap = functools.partial(
        lax.ppermute, axis_name="blk", perm=route(lambda i: 1 - 2 * (i % 2))
    )
    ahead = functools.partial(
        lax.ppermute, axis_name="blk", perm=route(lambda i: 2 if i % 2 else -2)
    )
    back = functools.partial(
        lax.ppermute, axis_name="blk", perm=route(lambda i: -2 if i % 2 else 2)
    )

    relay = functools.partial(
        lax.ppermute,
        axis_name="blk",
        perm=route(lambda i: -1 if i == 1 else 1 if i == nblocks - 2 else -2 if i % 2 else 2),
    )

    where = block_index[None].astype(jnp.int32)
    own_q, own_kv, swap_q, swap_kv = prepare(where, queries, keys, values)
    segs, need = survey(where, block_mask, segment_ids[None, :])
    other_kv = swap(swap_kv)
    ahead_own = ahead(own_kv)
    back_own = back(own_kv)
    back_other = relay(other_kv)
    both = stack(other_kv, ahead_own)
    both, back_own, swap_q, segs, need = lax.optimization_barrier(
        (both, back_own, swap_q, segs, need)
    )
    other_q = swap(swap_q)
    ahead_both = ahead(both)
    near = (own_kv, other_kv, ahead_own, back_own)
    near_numbers = (0, 1, 2, 3)
    fixed = (where, need, segs)
    own = attention(*fixed, (own_q,), (0,), near, near_numbers, None, False)
    other = attention(*fixed, (other_q,), (1,), near, near_numbers, None, False)
    back_other, other, own = lax.optimization_barrier((back_other, other, own))
    back_far = relay(back_other)
    far = (ahead_both, back_other)
    other = attention(*fixed, (other_q,), (1,), far, (4, 6, 5), other, True)
    other = swap(other)
    far = (ahead_both, back_other, back_far)
    own = attention(*fixed, (own_q,), (0,), far, (4, 6, 5, 7), own, True)

    pieces = nblocks if nblocks <= 8 else 1
    outgoing = project(
        where, owners[None, :], offsets[None, :], own, other, out_weight, tokens,
        pieces, slots, pair_rows,
    )
    if pieces > 1:
        arrived = [outgoing[0]] + [None] * (nblocks - 1)
        order = sorted(range(1, nblocks), key=lambda d: (min(d, nblocks - d) == 2, d))
        for d in order:
            arrived[d] = lax.ppermute(
                outgoing[d], "blk", [(i, (i + d) % nblocks) for i in range(nblocks)]
            )
    else:
        arrived = [lax.all_to_all(outgoing[0], "blk", split_axis=0, concat_axis=0, tiled=True)]
    return place(arrived, capacity, 4 * width)


def solution(mesh):
    placed = (
        P("rep"),
        P("rep", None),
        P(("rep", "blk"), None),
        P(("rep", "blk"), None),
        P(("rep", "blk"), None),
        P(("rep", "blk"), None),
        P(),
        P(("rep", "blk")),
        P(("rep", "blk")),
    )
    return jax.shard_map(
        per_device, mesh=mesh, in_specs=placed, out_specs=P(("rep", "blk"), None), check_vma=False
    )
```

```python
import functools

import jax
import jax.numpy as jnp
from jax import lax
from jax.experimental import pallas as pl
from jax.experimental.pallas import tpu as pltpu
from jax.sharding import PartitionSpec as P

HEADS = 8
HALF = HEADS // 2
SPAN = 3
NEG = -1e30
LOG2E = 1.4426950408889634
MIB = 1024 * 1024


def vmem():
    return pl.BlockSpec(memory_space=pltpu.VMEM)


def smem():
    return pl.BlockSpec(memory_space=pltpu.SMEM)


def anywhere():
    return pl.BlockSpec(memory_space=pl.ANY)


def limit(mib):
    return pltpu.CompilerParams(vmem_limit_bytes=mib * MIB)


PLACES = ((3, 1), (4, -1), (5, -3), (1, 5), (6, -5), (2, 3), (7, -7), (0, 7))


def asking(me, kind):
    return me if kind == 0 else me + 1 - 2 * (me % 2)


def key_block(me, number):
    half = me % 2
    return me - half - SPAN + PLACES[number][0] + PLACES[number][1] * half


def prepare_kernel(where_ref, q_hbm, k_hbm, v_hbm, own_q, own_kv, swap_q, swap_kv, held, turned, sems):
    part = q_hbm.shape[1] // 2
    loads = [
        pltpu.make_async_copy(ref, held.at[i], sems.at[i])
        for i, ref in enumerate((k_hbm, v_hbm, q_hbm))
    ]
    for load in loads:
        load.start()
    me = where_ref[0]
    half = me % 2
    mine = pl.multiple_of(half * part, 16)
    other = pl.multiple_of((1 - half) * part, 16)
    for i in range(3):
        loads[i].wait()
        turned[i] = held[i].T
        if i < 2:
            own_kv[i * part : (i + 1) * part, :] = turned[i, pl.ds(mine, part), :]
            swap_kv[i * part : (i + 1) * part, :] = turned[i, pl.ds(other, part), :]
        else:
            own_q[...] = turned[i, pl.ds(mine, part), :]
            swap_q[...] = turned[i, pl.ds(other, part), :]


def prepare(where, queries, keys, values):
    rows, features = queries.shape
    part = features // 2
    single = jax.ShapeDtypeStruct((part, rows), queries.dtype)
    double = jax.ShapeDtypeStruct((2 * part, rows), queries.dtype)
    return pl.pallas_call(
        prepare_kernel,
        out_shape=[single, double, single, double],
        in_specs=[smem()] + [anywhere()] * 3,
        out_specs=[vmem()] * 4,
        scratch_shapes=[
            pltpu.VMEM((3, rows, features), queries.dtype),
            pltpu.VMEM((3, features, rows), queries.dtype),
            pltpu.SemaphoreType.DMA((3,)),
        ],
        compiler_params=limit(53),
    )(where, queries, keys, values)


def survey_kernel(where_ref, mask_ref, segs_ref, seg_out, need_out):
    seg_out[...] = segs_ref[...].astype(jnp.float32)
    me = where_ref[0]
    nblocks = mask_ref.shape[0]
    bits = jnp.int32(0)
    for kind in range(2):
        asker = asking(me, kind)
        for number in range(len(PLACES)):
            block = key_block(me, number)
            inside = (block >= 0) & (block < nblocks) & (jnp.abs(block - asker) <= SPAN)
            allowed = mask_ref[asker, jnp.clip(block, 0, nblocks - 1)] > 0
            bits += (inside & allowed).astype(jnp.int32) << (kind * len(PLACES) + number)
    need_out[...] = jnp.full(need_out.shape, bits, jnp.int32)


def survey(where, mask, segs):
    return pl.pallas_call(
        survey_kernel,
        out_shape=[
            jax.ShapeDtypeStruct(segs.shape, jnp.float32),
            jax.ShapeDtypeStruct((8, 128), jnp.int32),
        ],
        in_specs=[smem()] * 2 + [vmem()],
        out_specs=[vmem()] * 2,
        compiler_params=limit(16),
    )(where, mask, segs)


def attention_kernel(kinds, numbers, rows_of, follows, ends, where_ref, need_ref, seg_ref, *refs):
    queries, refs = refs[: len(kinds)], refs[len(kinds) :]
    arrays = max(array for array, _ in rows_of) + 1
    blocks, refs = refs[:arrays], refs[arrays:]
    if follows:
        before, refs = refs[0], refs[1:]
    out_ref, query_s, key_s, value_s, chosen_s = refs
    part, rows = queries[0].shape
    hdim = part // HALF
    wide = value_s.shape[2]
    nblocks = seg_ref.shape[1] // rows
    factor = LOG2E / (hdim**0.5)
    me = where_ref[0]
    column = [key_block(me, b) for b in numbers]
    asker = [asking(me, kind) for kind in kinds]
    bits = jnp.max(need_ref[...])
    need = [[(bits >> (kind * len(PLACES) + b)) & 1 for b in numbers] for kind in kinds]

    def segment(block):
        start = pl.multiple_of(jnp.clip(block, 0, nblocks - 1) * rows, 128)
        return seg_ref[:, pl.ds(start, rows)]

    for b in range(len(numbers)):
        wanted = need[0][b]
        for n in range(1, len(kinds)):
            wanted = wanted + need[n][b]

        @pl.when(wanted > 0)
        def _(b=b):
            array, first = rows_of[b]
            key_s[b] = blocks[array][first : first + part, :]
            for h in range(HALF):
                start = first + part + h * hdim
                value_s[b, h, :hdim, :] = blocks[array][start : start + hdim, :]
                value_s[b, h, hdim:, :] = jnp.ones((wide - hdim, rows), jnp.bfloat16)

    for n in range(len(kinds)):
        size = 0
        for b in range(len(numbers)):
            chosen_s[size] = b
            size = size + need[n][b]
        for h in range(HALF):
            query_s[h] = queries[n][h * hdim : (h + 1) * hdim, :].T
        query_seg = jnp.broadcast_to(segment(asker[n]), (128, rows)).T
        query_seg = jnp.concatenate([query_seg] * (rows // 128), axis=1)

        def finish(h, peak, accum, n=n):
            if ends:
                turned = accum.T
                lines = slice(h * hdim, (h + 1) * hdim)
                out_ref[lines, :] = (turned[:hdim] / turned[hdim : hdim + 1]).astype(out_ref.dtype)
            else:
                peak = jnp.broadcast_to(peak, (rows, 128 - wide))
                out_ref[n, h] = jnp.concatenate([accum, peak], axis=1)

        if follows:

            @pl.when(size == 0)
            def _():
                for h in range(HALF):
                    state = before[0, h]
                    finish(h, state[:, wide : wide + 1], state[:, :wide])

        for fixed in range(1, len(numbers) + 1):

            @pl.when(size == fixed)
            def _():
                picked = [chosen_s[b] for b in range(fixed)]
                key_segs = [
                    segment(sum(jnp.where(b == i, column[i], 0) for i in range(len(numbers))))
                    for b in picked
                ]

                def one_head(h):
                    lines = slice(h * hdim, (h + 1) * hdim)
                    query = query_s[h]
                    scores = []
                    for b, key_seg in zip(picked, key_segs):
                        score = jnp.dot(
                            query, key_s[b, lines, :], preferred_element_type=jnp.float32
                        )
                        scores.append(jnp.where(query_seg == key_seg, score, NEG))
                    peak = functools.reduce(jnp.maximum, scores)
                    peak = jnp.max(peak, axis=1, keepdims=True)
                    accum = jnp.zeros((rows, wide), jnp.float32)
                    if follows:
                        state = before[0, h]
                        old = state[:, wide : wide + 1]
                        peak = jnp.maximum(peak, old)
                        accum = state[:, :wide] * jnp.exp2((old - peak) * factor)
                    for b, score in zip(picked, scores):
                        weights = jnp.exp2((score - peak) * factor).astype(jnp.bfloat16)
                        accum += lax.dot_general(
                            weights,
                            value_s[b, h],
                            (((1,), (1,)), ((), ())),
                            preferred_element_type=jnp.float32,
                        )
                    finish(h, peak, accum)

                for h in range(HALF):
                    one_head(h)


def attention(where, need, segs, queries, kinds, blocks, numbers, before, ends):
    part, rows = queries[0].shape
    hdim = part // HALF
    wide = hdim + 16
    follows = before is not None
    rows_of = [
        (array, first)
        for array, block in enumerate(blocks)
        for first in range(0, block.shape[0], 2 * part)
    ]
    if ends:
        out = jax.ShapeDtypeStruct((part, rows), jnp.bfloat16)
    else:
        out = jax.ShapeDtypeStruct((len(kinds), HALF, rows, 128), jnp.float32)
    return pl.pallas_call(
        functools.partial(attention_kernel, kinds, numbers, rows_of, follows, ends),
        out_shape=out,
        in_specs=[smem()] + [vmem()] * (2 + len(kinds) + len(blocks) + follows),
        out_specs=vmem(),
        scratch_shapes=[
            pltpu.VMEM((HALF, rows, hdim), jnp.bfloat16),
            pltpu.VMEM((len(numbers), part, rows), jnp.bfloat16),
            pltpu.VMEM((len(numbers), HALF, wide, rows), jnp.bfloat16),
            pltpu.SMEM((len(numbers) + 1,), jnp.int32),
        ],
        compiler_params=limit(16),
        cost_estimate=pl.CostEstimate(
            flops=2_000_000_000 * len(kinds), bytes_accessed=2_000_000, transcendentals=1_000_000
        ),
    )(where, need, segs, *queries, *blocks, *((before,) if follows else ()))


def stack_kernel(*refs):
    *parts, out_ref = refs
    first = 0
    for ref in parts:
        out_ref[first : first + ref.shape[0], :] = ref[...]
        first += ref.shape[0]


def stack(*parts):
    lines = sum(part.shape[0] for part in parts)
    return pl.pallas_call(
        stack_kernel,
        out_shape=jax.ShapeDtypeStruct((lines, parts[0].shape[1]), parts[0].dtype),
        in_specs=[vmem()] * len(parts),
        out_specs=vmem(),
        compiler_params=limit(16),
    )(*parts)


def project_kernel(
    pair_rows, order, where_ref, owners_ref, offsets_ref, own_ref, other_ref, weight_ref, tokens_ref, *outs
):
    piece = outs[0].shape[0]
    slots = piece * len(outs)
    rows, width = tokens_ref.shape
    mrows = rows // 4
    capacity = 2 * mrows
    owner = owners_ref[...]
    if len(outs) > 1:
        owner = owner ^ where_ref[0]
    owner = jnp.broadcast_to(owner.astype(jnp.float32), (mrows, mrows))
    earlier = lax.broadcasted_iota(jnp.int32, (mrows, mrows), 0)
    later = lax.broadcasted_iota(jnp.int32, (mrows, mrows), 1)
    column = jnp.sum(jnp.where(earlier == later, owner, 0.0), axis=1, keepdims=True)
    ahead = jnp.where((owner == column) & (earlier < later), 1.0, 0.0)
    slot = owner[:1] * pair_rows + jnp.sum(ahead, axis=0, keepdims=True)
    line = lax.broadcasted_iota(jnp.int32, (16, mrows), 0)
    meta = jnp.where(line == 0, slot, jnp.where(line == 1, offsets_ref[...].astype(jnp.float32), 0.0))
    row = lax.broadcasted_iota(jnp.int32, (mrows, rows), 0)
    patch = lax.broadcasted_iota(jnp.int32, (mrows, rows), 1)
    spread = jnp.where(patch // 4 == row, 1.0, 0.0).astype(jnp.bfloat16)
    meta = jnp.dot(meta.astype(jnp.bfloat16), spread, preferred_element_type=jnp.float32)
    part = own_ref.shape[0]
    half = where_ref[0] % 2
    hidden = tokens_ref[...].astype(jnp.float32)
    for ref, which in ((own_ref, half), (other_ref, 1 - half)):
        hidden += lax.dot_general(
            ref[...],
            weight_ref[pl.ds(pl.multiple_of(which * part, 16), part), :],
            (((0,), (0,)), ((), ())),
            preferred_element_type=jnp.float32,
        )
    hidden = hidden.astype(jnp.bfloat16)
    slot = lax.broadcasted_iota(jnp.int32, (slots, rows), 0).astype(jnp.float32)
    quarter = lax.broadcasted_iota(jnp.int32, (1, rows), 1) % 4
    for j in range(4):
        mine = jnp.where(quarter == j, meta[:1], -1.0) == slot
        if j == 0:
            offset = jnp.where(mine, meta[1:2] - capacity, 0.0)
            offset = capacity + jnp.sum(offset, axis=1, keepdims=True)
            offset = jnp.broadcast_to(offset, (slots, 128)).astype(jnp.bfloat16)
            for d, out in zip(order, outs):
                out[:, 4 * width :] = offset[d * piece : (d + 1) * piece]
        pick = jnp.where(mine, 1.0, 0.0).astype(jnp.bfloat16)
        picked = jnp.dot(pick, hidden, preferred_element_type=jnp.float32).astype(jnp.bfloat16)
        for d, out in zip(order, outs):
            out[:, j * width : (j + 1) * width] = picked[d * piece : (d + 1) * piece]


def project(where, owners, offsets, own, other, out_weight, tokens, order, slots, pair_rows):
    rows, width = tokens.shape
    pieces = len(order)
    return pl.pallas_call(
        functools.partial(project_kernel, pair_rows, order),
        out_shape=[jax.ShapeDtypeStruct((slots // pieces, 4 * width + 128), jnp.bfloat16)] * pieces,
        in_specs=[smem()] + [vmem()] * 6,
        out_specs=[vmem()] * pieces,
        compiler_params=limit(24),
    )(where, owners, offsets, own, other, out_weight, tokens)


def place_kernel(*refs):
    *arrived, out_hbm, held, sems = refs
    capacity, merged = out_hbm.shape
    step = merged // 4

    def columns_of(start, size):
        return jnp.concatenate([ref[:, start : start + size] for ref in arrived], axis=0)

    offset = columns_of(merged, 128).astype(jnp.float32)[:, :1]
    row = lax.broadcasted_iota(jnp.int32, (offset.shape[0], capacity), 1).astype(jnp.float32)
    pick = jnp.where(offset == row, 1.0, 0.0).astype(jnp.bfloat16)
    stores = []
    for j in range(4):
        held[j] = lax.dot_general(
            pick,
            columns_of(j * step, step),
            (((0,), (0,)), ((), ())),
            preferred_element_type=jnp.float32,
        ).astype(jnp.bfloat16)
        columns = out_hbm.at[:, pl.ds(j * step, step)]
        stores.append(pltpu.make_async_copy(held.at[j], columns, sems.at[j]))
        stores[j].start()
    for store in stores:
        store.wait()


def place(arrived, capacity, merged):
    return pl.pallas_call(
        place_kernel,
        out_shape=jax.ShapeDtypeStruct((capacity, merged), jnp.bfloat16),
        in_specs=[vmem()] * len(arrived),
        out_specs=anywhere(),
        scratch_shapes=[
            pltpu.VMEM((4, capacity, merged // 4), jnp.bfloat16),
            pltpu.SemaphoreType.DMA((4,)),
        ],
        compiler_params=limit(24),
    )(*arrived)


def per_device(segment_ids, block_mask, queries, keys, values, tokens, out_weight, owners, offsets):
    rows = queries.shape[0]
    width = tokens.shape[1]
    nblocks = lax.axis_size("blk")
    block_index = lax.axis_index("blk")
    mrows = rows // 4
    capacity = 2 * mrows
    pair_rows = max(2, 2 * mrows // nblocks)
    slots = nblocks * pair_rows
    assert slots <= 256

    def route(step):
        return [(i, i + step(i)) for i in range(nblocks) if 0 <= i + step(i) < nblocks]

    swap = functools.partial(
        lax.ppermute, axis_name="blk", perm=route(lambda i: 1 - 2 * (i % 2))
    )
    ahead = functools.partial(
        lax.ppermute, axis_name="blk", perm=route(lambda i: 2 if i % 2 else -2)
    )
    back = functools.partial(
        lax.ppermute, axis_name="blk", perm=route(lambda i: -2 if i % 2 else 2)
    )

    relay = functools.partial(
        lax.ppermute,
        axis_name="blk",
        perm=route(lambda i: -1 if i == 1 else 1 if i == nblocks - 2 else -2 if i % 2 else 2),
    )

    where = block_index[None].astype(jnp.int32)
    own_q, own_kv, swap_q, swap_kv = prepare(where, queries, keys, values)
    segs, need = survey(where, block_mask, segment_ids[None, :])
    other_kv = swap(swap_kv)
    ahead_own = ahead(own_kv)
    back_own = back(own_kv)
    ready, back_own, swap_q, segs, need = lax.optimization_barrier(
        (other_kv, back_own, swap_q, segs, need)
    )
    back_other = relay(ready)
    ahead_both = ahead(stack(other_kv, ahead_own))
    other_q = swap(swap_q)
    near = (own_kv, other_kv, ahead_own, back_own)
    near_numbers = (0, 1, 2, 3)
    fixed = (where, need, segs)
    own = attention(*fixed, (own_q,), (0,), near, near_numbers, None, False)
    other = attention(*fixed, (other_q,), (1,), near, near_numbers, None, False)
    back_other, other = lax.optimization_barrier((back_other, other))
    back_far = relay(back_other)
    far = (ahead_both, back_other)
    other = attention(*fixed, (other_q,), (1,), far, (4, 6, 5), other, True)
    other = swap(other)
    far = (ahead_both, back_other, back_far)
    own = attention(*fixed, (own_q,), (0,), far, (4, 6, 5, 7), own, True)

    order = tuple(range(nblocks)) if nblocks in (4, 8) else (0,)
    outgoing = project(
        where, owners[None, :], offsets[None, :], own, other, out_weight, tokens,
        order, slots, pair_rows,
    )
    if len(order) > 1:
        arrived = list(outgoing)

        def cross(d):
            arrived[d] = lax.ppermute(arrived[d], "blk", [(i, i ^ d) for i in range(nblocks)])

        short, *late = range(nblocks // 2 - 1, 0, -1)
        for d in (*range(nblocks // 2, nblocks), short):
            cross(d)
        group = lax.optimization_barrier([arrived[d] for d in (short, *late)])
        for d, block in zip((short, *late), group):
            arrived[d] = block
        for d in late:
            cross(d)
    else:
        arrived = [lax.all_to_all(outgoing[0], "blk", split_axis=0, concat_axis=0, tiled=True)]
    return place(arrived, capacity, 4 * width)


def solution(mesh):
    placed = (
        P("rep"),
        P("rep", None),
        P(("rep", "blk"), None),
        P(("rep", "blk"), None),
        P(("rep", "blk"), None),
        P(("rep", "blk"), None),
        P(),
        P(("rep", "blk")),
        P(("rep", "blk")),
    )
    return jax.shard_map(
        per_device, mesh=mesh, in_specs=placed, out_specs=P(("rep", "blk"), None), check_vma=False
    )
```

```python
import functools

import jax
import jax.numpy as jnp
from jax import lax
from jax.experimental import pallas as pl
from jax.experimental.pallas import tpu as pltpu
from jax.sharding import PartitionSpec as P

HEADS = 8
HALF = HEADS // 2
SPAN = 3
NEG = -1e30
LOG2E = 1.4426950408889634
MIB = 1024 * 1024


def vmem():
    return pl.BlockSpec(memory_space=pltpu.VMEM)


def smem():
    return pl.BlockSpec(memory_space=pltpu.SMEM)


def anywhere():
    return pl.BlockSpec(memory_space=pl.ANY)


def limit(mib):
    return pltpu.CompilerParams(vmem_limit_bytes=mib * MIB)


PLACES = ((3, 1), (4, -1), (5, -3), (1, 5), (6, -5), (2, 3), (7, -7), (0, 7))


def asking(me, kind):
    return me if kind == 0 else me + 1 - 2 * (me % 2)


def key_block(me, number):
    half = me % 2
    return me - half - SPAN + PLACES[number][0] + PLACES[number][1] * half


def prepare_kernel(where_ref, q_hbm, k_hbm, v_hbm, own_q, own_kv, swap_q, swap_kv, held, turned, sems):
    part = q_hbm.shape[1] // 2
    loads = [
        pltpu.make_async_copy(ref, held.at[i], sems.at[i])
        for i, ref in enumerate((k_hbm, v_hbm, q_hbm))
    ]
    for load in loads:
        load.start()
    me = where_ref[0]
    half = me % 2
    mine = pl.multiple_of(half * part, 16)
    other = pl.multiple_of((1 - half) * part, 16)
    for i in range(3):
        loads[i].wait()
        turned[i] = held[i].T
        if i < 2:
            own_kv[i * part : (i + 1) * part, :] = turned[i, pl.ds(mine, part), :]
            swap_kv[i * part : (i + 1) * part, :] = turned[i, pl.ds(other, part), :]
        else:
            own_q[...] = turned[i, pl.ds(mine, part), :]
            swap_q[...] = turned[i, pl.ds(other, part), :]


def prepare(where, queries, keys, values):
    rows, features = queries.shape
    part = features // 2
    single = jax.ShapeDtypeStruct((part, rows), queries.dtype)
    double = jax.ShapeDtypeStruct((2 * part, rows), queries.dtype)
    return pl.pallas_call(
        prepare_kernel,
        out_shape=[single, double, single, double],
        in_specs=[smem()] + [anywhere()] * 3,
        out_specs=[vmem()] * 4,
        scratch_shapes=[
            pltpu.VMEM((3, rows, features), queries.dtype),
            pltpu.VMEM((3, features, rows), queries.dtype),
            pltpu.SemaphoreType.DMA((3,)),
        ],
        compiler_params=limit(53),
    )(where, queries, keys, values)


def survey_kernel(where_ref, mask_ref, segs_ref, seg_out, need_out):
    seg_out[...] = segs_ref[...].astype(jnp.float32)
    me = where_ref[0]
    nblocks = mask_ref.shape[0]
    bits = jnp.int32(0)
    for kind in range(2):
        asker = asking(me, kind)
        for number in range(len(PLACES)):
            block = key_block(me, number)
            inside = (block >= 0) & (block < nblocks) & (jnp.abs(block - asker) <= SPAN)
            allowed = mask_ref[asker, jnp.clip(block, 0, nblocks - 1)] > 0
            bits += (inside & allowed).astype(jnp.int32) << (kind * len(PLACES) + number)
    need_out[...] = jnp.full(need_out.shape, bits, jnp.int32)


def survey(where, mask, segs):
    return pl.pallas_call(
        survey_kernel,
        out_shape=[
            jax.ShapeDtypeStruct(segs.shape, jnp.float32),
            jax.ShapeDtypeStruct((8, 128), jnp.int32),
        ],
        in_specs=[smem()] * 2 + [vmem()],
        out_specs=[vmem()] * 2,
        compiler_params=limit(16),
    )(where, mask, segs)


def attention_kernel(kinds, numbers, rows_of, follows, ends, where_ref, need_ref, seg_ref, *refs):
    queries, refs = refs[: len(kinds)], refs[len(kinds) :]
    arrays = max(array for array, _ in rows_of) + 1
    blocks, refs = refs[:arrays], refs[arrays:]
    if follows:
        before, refs = refs[0], refs[1:]
    out_ref, query_s, key_s, value_s, chosen_s = refs
    part, rows = queries[0].shape
    hdim = part // HALF
    wide = value_s.shape[2]
    nblocks = seg_ref.shape[1] // rows
    factor = LOG2E / (hdim**0.5)
    me = where_ref[0]
    column = [key_block(me, b) for b in numbers]
    asker = [asking(me, kind) for kind in kinds]
    bits = jnp.max(need_ref[...])
    need = [[(bits >> (kind * len(PLACES) + b)) & 1 for b in numbers] for kind in kinds]

    def segment(block):
        start = pl.multiple_of(jnp.clip(block, 0, nblocks - 1) * rows, 128)
        return seg_ref[:, pl.ds(start, rows)]

    for b in range(len(numbers)):
        wanted = need[0][b]
        for n in range(1, len(kinds)):
            wanted = wanted + need[n][b]

        @pl.when(wanted > 0)
        def _(b=b):
            array, first = rows_of[b]
            key_s[b] = blocks[array][first : first + part, :]
            for h in range(HALF):
                start = first + part + h * hdim
                value_s[b, h, :hdim, :] = blocks[array][start : start + hdim, :]
                value_s[b, h, hdim:, :] = jnp.ones((wide - hdim, rows), jnp.bfloat16)

    for n in range(len(kinds)):
        size = 0
        for b in range(len(numbers)):
            chosen_s[size] = b
            size = size + need[n][b]
        for h in range(HALF):
            query_s[h] = queries[n][h * hdim : (h + 1) * hdim, :].T
        query_seg = jnp.broadcast_to(segment(asker[n]), (128, rows)).T
        query_seg = jnp.concatenate([query_seg] * (rows // 128), axis=1)

        def finish(h, peak, accum, n=n):
            if ends:
                turned = accum.T
                lines = slice(h * hdim, (h + 1) * hdim)
                out_ref[lines, :] = (turned[:hdim] / turned[hdim : hdim + 1]).astype(out_ref.dtype)
            else:
                peak = jnp.broadcast_to(peak, (rows, 128 - wide))
                out_ref[n, h] = jnp.concatenate([accum, peak], axis=1)

        if follows:

            @pl.when(size == 0)
            def _():
                for h in range(HALF):
                    state = before[0, h]
                    finish(h, state[:, wide : wide + 1], state[:, :wide])

        for fixed in range(1, len(numbers) + 1):

            @pl.when(size == fixed)
            def _():
                picked = [chosen_s[b] for b in range(fixed)]
                key_segs = [
                    segment(sum(jnp.where(b == i, column[i], 0) for i in range(len(numbers))))
                    for b in picked
                ]

                def one_head(h):
                    lines = slice(h * hdim, (h + 1) * hdim)
                    query = query_s[h]
                    scores = []
                    for b, key_seg in zip(picked, key_segs):
                        score = jnp.dot(
                            query, key_s[b, lines, :], preferred_element_type=jnp.float32
                        )
                        scores.append(jnp.where(query_seg == key_seg, score, NEG))
                    peak = functools.reduce(jnp.maximum, scores)
                    peak = jnp.max(peak, axis=1, keepdims=True)
                    accum = jnp.zeros((rows, wide), jnp.float32)
                    if follows:
                        state = before[0, h]
                        old = state[:, wide : wide + 1]
                        peak = jnp.maximum(peak, old)
                        accum = state[:, :wide] * jnp.exp2((old - peak) * factor)
                    for b, score in zip(picked, scores):
                        weights = jnp.exp2((score - peak) * factor).astype(jnp.bfloat16)
                        accum += lax.dot_general(
                            weights,
                            value_s[b, h],
                            (((1,), (1,)), ((), ())),
                            preferred_element_type=jnp.float32,
                        )
                    finish(h, peak, accum)

                for h in range(HALF):
                    one_head(h)


def attention(where, need, segs, queries, kinds, blocks, numbers, before, ends):
    part, rows = queries[0].shape
    hdim = part // HALF
    wide = hdim + 16
    follows = before is not None
    rows_of = [
        (array, first)
        for array, block in enumerate(blocks)
        for first in range(0, block.shape[0], 2 * part)
    ]
    if ends:
        out = jax.ShapeDtypeStruct((part, rows), jnp.bfloat16)
    else:
        out = jax.ShapeDtypeStruct((len(kinds), HALF, rows, 128), jnp.float32)
    return pl.pallas_call(
        functools.partial(attention_kernel, kinds, numbers, rows_of, follows, ends),
        out_shape=out,
        in_specs=[smem()] + [vmem()] * (2 + len(kinds) + len(blocks) + follows),
        out_specs=vmem(),
        scratch_shapes=[
            pltpu.VMEM((HALF, rows, hdim), jnp.bfloat16),
            pltpu.VMEM((len(numbers), part, rows), jnp.bfloat16),
            pltpu.VMEM((len(numbers), HALF, wide, rows), jnp.bfloat16),
            pltpu.SMEM((len(numbers) + 1,), jnp.int32),
        ],
        compiler_params=limit(16),
        cost_estimate=pl.CostEstimate(
            flops=2_000_000_000 * len(kinds), bytes_accessed=2_000_000, transcendentals=1_000_000
        ),
    )(where, need, segs, *queries, *blocks, *((before,) if follows else ()))


def stack_kernel(*refs):
    *parts, out_ref = refs
    first = 0
    for ref in parts:
        out_ref[first : first + ref.shape[0], :] = ref[...]
        first += ref.shape[0]


def stack(*parts):
    lines = sum(part.shape[0] for part in parts)
    return pl.pallas_call(
        stack_kernel,
        out_shape=jax.ShapeDtypeStruct((lines, parts[0].shape[1]), parts[0].dtype),
        in_specs=[vmem()] * len(parts),
        out_specs=vmem(),
        compiler_params=limit(16),
    )(*parts)


def project_kernel(
    pair_rows, order, where_ref, owners_ref, offsets_ref, own_ref, other_ref, weight_ref, tokens_ref, *outs
):
    piece = outs[0].shape[0]
    slots = piece * len(outs)
    rows, width = tokens_ref.shape
    mrows = rows // 4
    capacity = 2 * mrows
    owner = owners_ref[...]
    if len(outs) > 1:
        owner = owner ^ where_ref[0]
    owner = jnp.broadcast_to(owner.astype(jnp.float32), (mrows, mrows))
    earlier = lax.broadcasted_iota(jnp.int32, (mrows, mrows), 0)
    later = lax.broadcasted_iota(jnp.int32, (mrows, mrows), 1)
    column = jnp.sum(jnp.where(earlier == later, owner, 0.0), axis=1, keepdims=True)
    ahead = jnp.where((owner == column) & (earlier < later), 1.0, 0.0)
    slot = owner[:1] * pair_rows + jnp.sum(ahead, axis=0, keepdims=True)
    line = lax.broadcasted_iota(jnp.int32, (16, mrows), 0)
    meta = jnp.where(line == 0, slot, jnp.where(line == 1, offsets_ref[...].astype(jnp.float32), 0.0))
    row = lax.broadcasted_iota(jnp.int32, (mrows, rows), 0)
    patch = lax.broadcasted_iota(jnp.int32, (mrows, rows), 1)
    spread = jnp.where(patch // 4 == row, 1.0, 0.0).astype(jnp.bfloat16)
    meta = jnp.dot(meta.astype(jnp.bfloat16), spread, preferred_element_type=jnp.float32)
    part = own_ref.shape[0]
    half = where_ref[0] % 2
    hidden = tokens_ref[...].astype(jnp.float32)
    for ref, which in ((own_ref, half), (other_ref, 1 - half)):
        hidden += lax.dot_general(
            ref[...],
            weight_ref[pl.ds(pl.multiple_of(which * part, 16), part), :],
            (((0,), (0,)), ((), ())),
            preferred_element_type=jnp.float32,
        )
    hidden = hidden.astype(jnp.bfloat16)
    slot = lax.broadcasted_iota(jnp.int32, (slots, rows), 0).astype(jnp.float32)
    quarter = lax.broadcasted_iota(jnp.int32, (1, rows), 1) % 4
    for j in range(4):
        mine = jnp.where(quarter == j, meta[:1], -1.0) == slot
        if j == 0:
            offset = jnp.where(mine, meta[1:2] - capacity, 0.0)
            offset = capacity + jnp.sum(offset, axis=1, keepdims=True)
            offset = jnp.broadcast_to(offset, (slots, 128)).astype(jnp.bfloat16)
            for d, out in zip(order, outs):
                out[:, 4 * width :] = offset[d * piece : (d + 1) * piece]
        pick = jnp.where(mine, 1.0, 0.0).astype(jnp.bfloat16)
        picked = jnp.dot(pick, hidden, preferred_element_type=jnp.float32).astype(jnp.bfloat16)
        for d, out in zip(order, outs):
            out[:, j * width : (j + 1) * width] = picked[d * piece : (d + 1) * piece]


def project(where, owners, offsets, own, other, out_weight, tokens, order, slots, pair_rows):
    rows, width = tokens.shape
    pieces = len(order)
    return pl.pallas_call(
        functools.partial(project_kernel, pair_rows, order),
        out_shape=[jax.ShapeDtypeStruct((slots // pieces, 4 * width + 128), jnp.bfloat16)] * pieces,
        in_specs=[smem()] + [vmem()] * 6,
        out_specs=[vmem()] * pieces,
        compiler_params=limit(24),
    )(where, owners, offsets, own, other, out_weight, tokens)


def place_kernel(*refs):
    *arrived, out_hbm, held, sems = refs
    capacity, merged = out_hbm.shape
    step = merged // 4

    def columns_of(start, size):
        return jnp.concatenate([ref[:, start : start + size] for ref in arrived], axis=0)

    offset = columns_of(merged, 128).astype(jnp.float32)[:, :1]
    row = lax.broadcasted_iota(jnp.int32, (offset.shape[0], capacity), 1).astype(jnp.float32)
    pick = jnp.where(offset == row, 1.0, 0.0).astype(jnp.bfloat16)
    stores = []
    for j in range(4):
        held[j] = lax.dot_general(
            pick,
            columns_of(j * step, step),
            (((0,), (0,)), ((), ())),
            preferred_element_type=jnp.float32,
        ).astype(jnp.bfloat16)
        columns = out_hbm.at[:, pl.ds(j * step, step)]
        stores.append(pltpu.make_async_copy(held.at[j], columns, sems.at[j]))
        stores[j].start()
    for store in stores:
        store.wait()


def place(arrived, capacity, merged):
    return pl.pallas_call(
        place_kernel,
        out_shape=jax.ShapeDtypeStruct((capacity, merged), jnp.bfloat16),
        in_specs=[vmem()] * len(arrived),
        out_specs=anywhere(),
        scratch_shapes=[
            pltpu.VMEM((4, capacity, merged // 4), jnp.bfloat16),
            pltpu.SemaphoreType.DMA((4,)),
        ],
        compiler_params=limit(24),
    )(*arrived)


def per_device(segment_ids, block_mask, queries, keys, values, tokens, out_weight, owners, offsets):
    rows = queries.shape[0]
    width = tokens.shape[1]
    nblocks = lax.axis_size("blk")
    block_index = lax.axis_index("blk")
    mrows = rows // 4
    capacity = 2 * mrows
    pair_rows = max(2, 2 * mrows // nblocks)
    slots = nblocks * pair_rows
    assert slots <= 256

    def route(step):
        return [(i, i + step(i)) for i in range(nblocks) if 0 <= i + step(i) < nblocks]

    swap = functools.partial(
        lax.ppermute, axis_name="blk", perm=route(lambda i: 1 - 2 * (i % 2))
    )
    ahead = functools.partial(
        lax.ppermute, axis_name="blk", perm=route(lambda i: 2 if i % 2 else -2)
    )
    back = functools.partial(
        lax.ppermute, axis_name="blk", perm=route(lambda i: -2 if i % 2 else 2)
    )

    relay = functools.partial(
        lax.ppermute,
        axis_name="blk",
        perm=route(lambda i: -1 if i == 1 else 1 if i == nblocks - 2 else -2 if i % 2 else 2),
    )

    where = block_index[None].astype(jnp.int32)
    own_q, own_kv, swap_q, swap_kv = prepare(where, queries, keys, values)
    segs, need = survey(where, block_mask, segment_ids[None, :])
    other_kv = swap(swap_kv)
    ahead_own = ahead(own_kv)
    back_own = back(own_kv)
    ready, back_own, segs, need = lax.optimization_barrier((other_kv, back_own, segs, need))
    back_other = relay(ready)
    ahead_both = ahead(stack(other_kv, ahead_own))
    near = (own_kv, other_kv, ahead_own, back_own)
    near_numbers = (0, 1, 2, 3)
    fixed = (where, need, segs)
    own = attention(*fixed, (own_q,), (0,), near, near_numbers, None, False)
    swap_q, own = lax.optimization_barrier((swap_q, own))
    other_q = swap(swap_q)
    other = attention(*fixed, (other_q,), (1,), near, near_numbers, None, False)
    back_other, other = lax.optimization_barrier((back_other, other))
    back_far = relay(back_other)
    far = (ahead_both, back_other)
    other = attention(*fixed, (other_q,), (1,), far, (4, 6, 5), other, True)
    other = swap(other)
    far = (ahead_both, back_other, back_far)
    own = attention(*fixed, (own_q,), (0,), far, (4, 6, 5, 7), own, True)

    order = tuple(range(nblocks)) if nblocks in (4, 8) else (0,)
    outgoing = project(
        where, owners[None, :], offsets[None, :], own, other, out_weight, tokens,
        order, slots, pair_rows,
    )
    if len(order) > 1:
        arrived = list(outgoing)

        def cross(d):
            arrived[d] = lax.ppermute(arrived[d], "blk", [(i, i ^ d) for i in range(nblocks)])

        short, *late = range(nblocks // 2 - 1, 0, -1)
        for d in (*range(nblocks // 2, nblocks), short):
            cross(d)
        group = lax.optimization_barrier([arrived[d] for d in (short, *late)])
        for d, block in zip((short, *late), group):
            arrived[d] = block
        for d in late:
            cross(d)
    else:
        arrived = [lax.all_to_all(outgoing[0], "blk", split_axis=0, concat_axis=0, tiled=True)]
    return place(arrived, capacity, 4 * width)


def solution(mesh):
    placed = (
        P("rep"),
        P("rep", None),
        P(("rep", "blk"), None),
        P(("rep", "blk"), None),
        P(("rep", "blk"), None),
        P(("rep", "blk"), None),
        P(),
        P(("rep", "blk")),
        P(("rep", "blk")),
    )
    return jax.shard_map(
        per_device, mesh=mesh, in_specs=placed, out_specs=P(("rep", "blk"), None), check_vma=False
    )
```

```python
import functools

import jax
import jax.numpy as jnp
from jax import lax
from jax.experimental import pallas as pl
from jax.experimental.pallas import tpu as pltpu
from jax.sharding import PartitionSpec as P

HEADS = 8
HALF = HEADS // 2
SPAN = 3
NEG = -1e30
LOG2E = 1.4426950408889634
MIB = 1024 * 1024


def vmem():
    return pl.BlockSpec(memory_space=pltpu.VMEM)


def smem():
    return pl.BlockSpec(memory_space=pltpu.SMEM)


def anywhere():
    return pl.BlockSpec(memory_space=pl.ANY)


def limit(mib):
    return pltpu.CompilerParams(vmem_limit_bytes=mib * MIB)


PLACES = ((3, 1), (4, -1), (5, -3), (1, 5), (6, -5), (2, 3), (7, -7), (0, 7))


def asking(me, kind):
    return me if kind == 0 else me + 1 - 2 * (me % 2)


def key_block(me, number):
    half = me % 2
    return me - half - SPAN + PLACES[number][0] + PLACES[number][1] * half


def prepare_kernel(where_ref, q_hbm, k_hbm, v_hbm, own_q, own_kv, swap_q, swap_kv, held, turned, sems):
    part = q_hbm.shape[1] // 2
    loads = [
        pltpu.make_async_copy(ref, held.at[i], sems.at[i])
        for i, ref in enumerate((k_hbm, v_hbm, q_hbm))
    ]
    for load in loads:
        load.start()
    me = where_ref[0]
    half = me % 2
    mine = pl.multiple_of(half * part, 16)
    other = pl.multiple_of((1 - half) * part, 16)
    for i in range(3):
        loads[i].wait()
        turned[i] = held[i].T
        if i < 2:
            own_kv[i * part : (i + 1) * part, :] = turned[i, pl.ds(mine, part), :]
            swap_kv[i * part : (i + 1) * part, :] = turned[i, pl.ds(other, part), :]
        else:
            own_q[...] = turned[i, pl.ds(mine, part), :]
            swap_q[...] = turned[i, pl.ds(other, part), :]


def prepare(where, queries, keys, values):
    rows, features = queries.shape
    part = features // 2
    single = jax.ShapeDtypeStruct((part, rows), queries.dtype)
    double = jax.ShapeDtypeStruct((2 * part, rows), queries.dtype)
    return pl.pallas_call(
        prepare_kernel,
        out_shape=[single, double, single, double],
        in_specs=[smem()] + [anywhere()] * 3,
        out_specs=[vmem()] * 4,
        scratch_shapes=[
            pltpu.VMEM((3, rows, features), queries.dtype),
            pltpu.VMEM((3, features, rows), queries.dtype),
            pltpu.SemaphoreType.DMA((3,)),
        ],
        compiler_params=limit(53),
    )(where, queries, keys, values)


def survey_kernel(where_ref, mask_ref, segs_ref, seg_out, need_out):
    seg_out[...] = segs_ref[...].astype(jnp.float32)
    me = where_ref[0]
    nblocks = mask_ref.shape[0]
    bits = jnp.int32(0)
    for kind in range(2):
        asker = asking(me, kind)
        for number in range(len(PLACES)):
            block = key_block(me, number)
            inside = (block >= 0) & (block < nblocks) & (jnp.abs(block - asker) <= SPAN)
            allowed = mask_ref[asker, jnp.clip(block, 0, nblocks - 1)] > 0
            bits += (inside & allowed).astype(jnp.int32) << (kind * len(PLACES) + number)
    need_out[...] = jnp.full(need_out.shape, bits, jnp.int32)


def survey(where, mask, segs):
    return pl.pallas_call(
        survey_kernel,
        out_shape=[
            jax.ShapeDtypeStruct(segs.shape, jnp.float32),
            jax.ShapeDtypeStruct((8, 128), jnp.int32),
        ],
        in_specs=[smem()] * 2 + [vmem()],
        out_specs=[vmem()] * 2,
        compiler_params=limit(16),
    )(where, mask, segs)


def attention_kernel(kinds, numbers, rows_of, follows, ends, where_ref, need_ref, seg_ref, *refs):
    queries, refs = refs[: len(kinds)], refs[len(kinds) :]
    arrays = max(array for array, _ in rows_of) + 1
    blocks, refs = refs[:arrays], refs[arrays:]
    if follows:
        before, refs = refs[0], refs[1:]
    out_ref, query_s, key_s, value_s, chosen_s = refs
    part, rows = queries[0].shape
    hdim = part // HALF
    wide = value_s.shape[2]
    nblocks = seg_ref.shape[1] // rows
    factor = LOG2E / (hdim**0.5)
    me = where_ref[0]
    column = [key_block(me, b) for b in numbers]
    asker = [asking(me, kind) for kind in kinds]
    bits = jnp.max(need_ref[...])
    need = [[(bits >> (kind * len(PLACES) + b)) & 1 for b in numbers] for kind in kinds]

    def segment(block):
        start = pl.multiple_of(jnp.clip(block, 0, nblocks - 1) * rows, 128)
        return seg_ref[:, pl.ds(start, rows)]

    for b in range(len(numbers)):
        wanted = need[0][b]
        for n in range(1, len(kinds)):
            wanted = wanted + need[n][b]

        @pl.when(wanted > 0)
        def _(b=b):
            array, first = rows_of[b]
            key_s[b] = blocks[array][first : first + part, :]
            for h in range(HALF):
                start = first + part + h * hdim
                value_s[b, h, :hdim, :] = blocks[array][start : start + hdim, :]
                value_s[b, h, hdim:, :] = jnp.ones((wide - hdim, rows), jnp.bfloat16)

    for n in range(len(kinds)):
        size = 0
        for b in range(len(numbers)):
            chosen_s[size] = b
            size = size + need[n][b]
        for h in range(HALF):
            query_s[h] = queries[n][h * hdim : (h + 1) * hdim, :].T
        query_seg = jnp.broadcast_to(segment(asker[n]), (128, rows)).T
        query_seg = jnp.concatenate([query_seg] * (rows // 128), axis=1)

        def finish(h, peak, accum, n=n):
            if ends:
                turned = accum.T
                lines = slice(h * hdim, (h + 1) * hdim)
                out_ref[lines, :] = (turned[:hdim] / turned[hdim : hdim + 1]).astype(out_ref.dtype)
            else:
                peak = jnp.broadcast_to(peak, (rows, 128 - wide))
                out_ref[n, h] = jnp.concatenate([accum, peak], axis=1)

        if follows:

            @pl.when(size == 0)
            def _():
                for h in range(HALF):
                    state = before[0, h]
                    finish(h, state[:, wide : wide + 1], state[:, :wide])

        for fixed in range(1, len(numbers) + 1):

            @pl.when(size == fixed)
            def _():
                picked = [chosen_s[b] for b in range(fixed)]
                key_segs = [
                    segment(sum(jnp.where(b == i, column[i], 0) for i in range(len(numbers))))
                    for b in picked
                ]

                def one_head(h):
                    lines = slice(h * hdim, (h + 1) * hdim)
                    query = query_s[h]
                    scores = []
                    for b, key_seg in zip(picked, key_segs):
                        score = jnp.dot(
                            query, key_s[b, lines, :], preferred_element_type=jnp.float32
                        )
                        scores.append(jnp.where(query_seg == key_seg, score, NEG))
                    peak = functools.reduce(jnp.maximum, scores)
                    peak = jnp.max(peak, axis=1, keepdims=True)
                    accum = jnp.zeros((rows, wide), jnp.float32)
                    if follows:
                        state = before[0, h]
                        old = state[:, wide : wide + 1]
                        peak = jnp.maximum(peak, old)
                        accum = state[:, :wide] * jnp.exp2((old - peak) * factor)
                    for b, score in zip(picked, scores):
                        weights = jnp.exp2((score - peak) * factor).astype(jnp.bfloat16)
                        accum += lax.dot_general(
                            weights,
                            value_s[b, h],
                            (((1,), (1,)), ((), ())),
                            preferred_element_type=jnp.float32,
                        )
                    finish(h, peak, accum)

                for h in range(HALF):
                    one_head(h)


def attention(where, need, segs, queries, kinds, blocks, numbers, before, ends):
    part, rows = queries[0].shape
    hdim = part // HALF
    wide = hdim + 16
    follows = before is not None
    rows_of = [
        (array, first)
        for array, block in enumerate(blocks)
        for first in range(0, block.shape[0], 2 * part)
    ]
    if ends:
        out = jax.ShapeDtypeStruct((part, rows), jnp.bfloat16)
    else:
        out = jax.ShapeDtypeStruct((len(kinds), HALF, rows, 128), jnp.float32)
    return pl.pallas_call(
        functools.partial(attention_kernel, kinds, numbers, rows_of, follows, ends),
        out_shape=out,
        in_specs=[smem()] + [vmem()] * (2 + len(kinds) + len(blocks) + follows),
        out_specs=vmem(),
        scratch_shapes=[
            pltpu.VMEM((HALF, rows, hdim), jnp.bfloat16),
            pltpu.VMEM((len(numbers), part, rows), jnp.bfloat16),
            pltpu.VMEM((len(numbers), HALF, wide, rows), jnp.bfloat16),
            pltpu.SMEM((len(numbers) + 1,), jnp.int32),
        ],
        compiler_params=limit(16),
        cost_estimate=pl.CostEstimate(flops=1000, bytes_accessed=1000, transcendentals=0),
    )(where, need, segs, *queries, *blocks, *((before,) if follows else ()))


def stack_kernel(*refs):
    *parts, out_ref = refs
    first = 0
    for ref in parts:
        out_ref[first : first + ref.shape[0], :] = ref[...]
        first += ref.shape[0]


def stack(*parts):
    lines = sum(part.shape[0] for part in parts)
    return pl.pallas_call(
        stack_kernel,
        out_shape=jax.ShapeDtypeStruct((lines, parts[0].shape[1]), parts[0].dtype),
        in_specs=[vmem()] * len(parts),
        out_specs=vmem(),
        compiler_params=limit(16),
    )(*parts)


def project_kernel(
    pair_rows, order, where_ref, owners_ref, offsets_ref, own_ref, other_ref, weight_ref, tokens_ref, *outs
):
    piece = outs[0].shape[0]
    slots = piece * len(outs)
    rows, width = tokens_ref.shape
    mrows = rows // 4
    capacity = 2 * mrows
    owner = owners_ref[...]
    if len(outs) > 1:
        owner = owner ^ where_ref[0]
    owner = jnp.broadcast_to(owner.astype(jnp.float32), (mrows, mrows))
    earlier = lax.broadcasted_iota(jnp.int32, (mrows, mrows), 0)
    later = lax.broadcasted_iota(jnp.int32, (mrows, mrows), 1)
    column = jnp.sum(jnp.where(earlier == later, owner, 0.0), axis=1, keepdims=True)
    ahead = jnp.where((owner == column) & (earlier < later), 1.0, 0.0)
    slot = owner[:1] * pair_rows + jnp.sum(ahead, axis=0, keepdims=True)
    line = lax.broadcasted_iota(jnp.int32, (16, mrows), 0)
    meta = jnp.where(line == 0, slot, jnp.where(line == 1, offsets_ref[...].astype(jnp.float32), 0.0))
    row = lax.broadcasted_iota(jnp.int32, (mrows, rows), 0)
    patch = lax.broadcasted_iota(jnp.int32, (mrows, rows), 1)
    spread = jnp.where(patch // 4 == row, 1.0, 0.0).astype(jnp.bfloat16)
    meta = jnp.dot(meta.astype(jnp.bfloat16), spread, preferred_element_type=jnp.float32)
    part = own_ref.shape[0]
    half = where_ref[0] % 2
    hidden = tokens_ref[...].astype(jnp.float32)
    for ref, which in ((own_ref, half), (other_ref, 1 - half)):
        hidden += lax.dot_general(
            ref[...],
            weight_ref[pl.ds(pl.multiple_of(which * part, 16), part), :],
            (((0,), (0,)), ((), ())),
            preferred_element_type=jnp.float32,
        )
    hidden = hidden.astype(jnp.bfloat16)
    slot = lax.broadcasted_iota(jnp.int32, (slots, rows), 0).astype(jnp.float32)
    quarter = lax.broadcasted_iota(jnp.int32, (1, rows), 1) % 4
    for j in range(4):
        mine = jnp.where(quarter == j, meta[:1], -1.0) == slot
        if j == 0:
            offset = jnp.where(mine, meta[1:2] - capacity, 0.0)
            offset = capacity + jnp.sum(offset, axis=1, keepdims=True)
            offset = jnp.broadcast_to(offset, (slots, 128)).astype(jnp.bfloat16)
            for d, out in zip(order, outs):
                out[:, 4 * width :] = offset[d * piece : (d + 1) * piece]
        pick = jnp.where(mine, 1.0, 0.0).astype(jnp.bfloat16)
        picked = jnp.dot(pick, hidden, preferred_element_type=jnp.float32).astype(jnp.bfloat16)
        for d, out in zip(order, outs):
            out[:, j * width : (j + 1) * width] = picked[d * piece : (d + 1) * piece]


def project(where, owners, offsets, own, other, out_weight, tokens, order, slots, pair_rows):
    rows, width = tokens.shape
    pieces = len(order)
    return pl.pallas_call(
        functools.partial(project_kernel, pair_rows, order),
        out_shape=[jax.ShapeDtypeStruct((slots // pieces, 4 * width + 128), jnp.bfloat16)] * pieces,
        in_specs=[smem()] + [vmem()] * 6,
        out_specs=[vmem()] * pieces,
        compiler_params=limit(24),
    )(where, owners, offsets, own, other, out_weight, tokens)


def place_kernel(*refs):
    *arrived, out_hbm, held, sems = refs
    capacity, merged = out_hbm.shape
    step = merged // 4

    def columns_of(start, size):
        return jnp.concatenate([ref[:, start : start + size] for ref in arrived], axis=0)

    offset = columns_of(merged, 128).astype(jnp.float32)[:, :1]
    row = lax.broadcasted_iota(jnp.int32, (offset.shape[0], capacity), 1).astype(jnp.float32)
    pick = jnp.where(offset == row, 1.0, 0.0).astype(jnp.bfloat16)
    stores = []
    for j in range(4):
        held[j] = lax.dot_general(
            pick,
            columns_of(j * step, step),
            (((0,), (0,)), ((), ())),
            preferred_element_type=jnp.float32,
        ).astype(jnp.bfloat16)
        columns = out_hbm.at[:, pl.ds(j * step, step)]
        stores.append(pltpu.make_async_copy(held.at[j], columns, sems.at[j]))
        stores[j].start()
    for store in stores:
        store.wait()


def place(arrived, capacity, merged):
    return pl.pallas_call(
        place_kernel,
        out_shape=jax.ShapeDtypeStruct((capacity, merged), jnp.bfloat16),
        in_specs=[vmem()] * len(arrived),
        out_specs=anywhere(),
        scratch_shapes=[
            pltpu.VMEM((4, capacity, merged // 4), jnp.bfloat16),
            pltpu.SemaphoreType.DMA((4,)),
        ],
        compiler_params=limit(24),
    )(*arrived)


def per_device(segment_ids, block_mask, queries, keys, values, tokens, out_weight, owners, offsets):
    rows = queries.shape[0]
    width = tokens.shape[1]
    nblocks = lax.axis_size("blk")
    block_index = lax.axis_index("blk")
    mrows = rows // 4
    capacity = 2 * mrows
    pair_rows = max(2, 2 * mrows // nblocks)
    slots = nblocks * pair_rows
    assert slots <= 256

    def route(step):
        return [(i, i + step(i)) for i in range(nblocks) if 0 <= i + step(i) < nblocks]

    swap = functools.partial(
        lax.ppermute, axis_name="blk", perm=route(lambda i: 1 - 2 * (i % 2))
    )
    ahead = functools.partial(
        lax.ppermute, axis_name="blk", perm=route(lambda i: 2 if i % 2 else -2)
    )
    back = functools.partial(
        lax.ppermute, axis_name="blk", perm=route(lambda i: -2 if i % 2 else 2)
    )

    relay = functools.partial(
        lax.ppermute,
        axis_name="blk",
        perm=route(lambda i: -1 if i == 1 else 1 if i == nblocks - 2 else -2 if i % 2 else 2),
    )

    where = block_index[None].astype(jnp.int32)
    own_q, own_kv, swap_q, swap_kv = prepare(where, queries, keys, values)
    segs, need = survey(where, block_mask, segment_ids[None, :])
    other_kv = swap(swap_kv)
    ahead_own = ahead(own_kv)
    back_own = back(own_kv)
    ready, back_own, swap_q = lax.optimization_barrier((other_kv, back_own, swap_q))
    back_other = relay(ready)
    ahead_both = ahead(stack(other_kv, ahead_own))
    other_q = swap(swap_q)
    near = (own_kv, other_kv, ahead_own, back_own)
    near_numbers = (0, 1, 2, 3)
    fixed = (where, need, segs)
    own = attention(*fixed, (own_q,), (0,), near, near_numbers, None, False)
    other = attention(*fixed, (other_q,), (1,), near, near_numbers, None, False)
    back_other, other = lax.optimization_barrier((back_other, other))
    back_far = relay(back_other)
    far = (ahead_both, back_other)
    other = attention(*fixed, (other_q,), (1,), far, (4, 6, 5), other, True)
    other = swap(other)
    far = (ahead_both, back_other, back_far)
    own = attention(*fixed, (own_q,), (0,), far, (4, 6, 5, 7), own, True)

    order = tuple(range(nblocks)) if nblocks in (4, 8) else (0,)
    outgoing = project(
        where, owners[None, :], offsets[None, :], own, other, out_weight, tokens,
        order, slots, pair_rows,
    )
    if len(order) > 1:
        arrived = list(outgoing)

        def cross(d):
            arrived[d] = lax.ppermute(arrived[d], "blk", [(i, i ^ d) for i in range(nblocks)])

        short, *late = range(nblocks // 2 - 1, 0, -1)
        for d in (*range(nblocks // 2, nblocks), short):
            cross(d)
        group = lax.optimization_barrier([arrived[d] for d in (short, *late)])
        for d, block in zip((short, *late), group):
            arrived[d] = block
        for d in late:
            cross(d)
    else:
        arrived = [lax.all_to_all(outgoing[0], "blk", split_axis=0, concat_axis=0, tiled=True)]
    return place(arrived, capacity, 4 * width)


def solution(mesh):
    placed = (
        P("rep"),
        P("rep", None),
        P(("rep", "blk"), None),
        P(("rep", "blk"), None),
        P(("rep", "blk"), None),
        P(("rep", "blk"), None),
        P(),
        P(("rep", "blk")),
        P(("rep", "blk")),
    )
    return jax.shard_map(
        per_device, mesh=mesh, in_specs=placed, out_specs=P(("rep", "blk"), None), check_vma=False
    )
```

```python
import functools

import jax
import jax.numpy as jnp
from jax import lax
from jax.experimental import pallas as pl
from jax.experimental.pallas import tpu as pltpu
from jax.sharding import PartitionSpec as P

HEADS = 8
HALF = HEADS // 2
SPAN = 3
NEG = -1e30
LOG2E = 1.4426950408889634
MIB = 1024 * 1024


def vmem():
    return pl.BlockSpec(memory_space=pltpu.VMEM)


def smem():
    return pl.BlockSpec(memory_space=pltpu.SMEM)


def anywhere():
    return pl.BlockSpec(memory_space=pl.ANY)


def limit(mib):
    return pltpu.CompilerParams(vmem_limit_bytes=mib * MIB)


PLACES = ((3, 1), (4, -1), (5, -3), (1, 5), (6, -5), (2, 3), (7, -7), (0, 7))


def asking(me, kind):
    return me if kind == 0 else me + 1 - 2 * (me % 2)


def key_block(me, number):
    half = me % 2
    return me - half - SPAN + PLACES[number][0] + PLACES[number][1] * half


def prepare_kernel(where_ref, q_hbm, k_hbm, v_hbm, own_q, own_kv, swap_q, swap_kv, held, turned, sems):
    part = q_hbm.shape[1] // 2
    loads = [
        pltpu.make_async_copy(ref, held.at[i], sems.at[i])
        for i, ref in enumerate((k_hbm, v_hbm, q_hbm))
    ]
    for load in loads:
        load.start()
    me = where_ref[0]
    half = me % 2
    mine = pl.multiple_of(half * part, 16)
    other = pl.multiple_of((1 - half) * part, 16)
    for i in range(3):
        loads[i].wait()
        turned[i] = held[i].T
        if i < 2:
            own_kv[i * part : (i + 1) * part, :] = turned[i, pl.ds(mine, part), :]
            swap_kv[i * part : (i + 1) * part, :] = turned[i, pl.ds(other, part), :]
        else:
            own_q[...] = turned[i, pl.ds(mine, part), :]
            swap_q[...] = turned[i, pl.ds(other, part), :]


def prepare(where, queries, keys, values):
    rows, features = queries.shape
    part = features // 2
    single = jax.ShapeDtypeStruct((part, rows), queries.dtype)
    double = jax.ShapeDtypeStruct((2 * part, rows), queries.dtype)
    return pl.pallas_call(
        prepare_kernel,
        out_shape=[single, double, single, double],
        in_specs=[smem()] + [anywhere()] * 3,
        out_specs=[vmem()] * 4,
        scratch_shapes=[
            pltpu.VMEM((3, rows, features), queries.dtype),
            pltpu.VMEM((3, features, rows), queries.dtype),
            pltpu.SemaphoreType.DMA((3,)),
        ],
        compiler_params=limit(53),
    )(where, queries, keys, values)


def survey_kernel(where_ref, mask_ref, segs_ref, seg_out, need_out):
    seg_out[...] = segs_ref[...].astype(jnp.float32)
    me = where_ref[0]
    nblocks = mask_ref.shape[0]
    bits = jnp.int32(0)
    for kind in range(2):
        asker = asking(me, kind)
        for number in range(len(PLACES)):
            block = key_block(me, number)
            inside = (block >= 0) & (block < nblocks) & (jnp.abs(block - asker) <= SPAN)
            allowed = mask_ref[asker, jnp.clip(block, 0, nblocks - 1)] > 0
            bits += (inside & allowed).astype(jnp.int32) << (kind * len(PLACES) + number)
    need_out[...] = jnp.full(need_out.shape, bits, jnp.int32)


def survey(where, mask, segs):
    return pl.pallas_call(
        survey_kernel,
        out_shape=[
            jax.ShapeDtypeStruct(segs.shape, jnp.float32),
            jax.ShapeDtypeStruct((8, 128), jnp.int32),
        ],
        in_specs=[smem()] * 2 + [vmem()],
        out_specs=[vmem()] * 2,
        compiler_params=limit(16),
    )(where, mask, segs)


def attention_kernel(kinds, numbers, rows_of, follows, ends, where_ref, need_ref, seg_ref, *refs):
    queries, refs = refs[: len(kinds)], refs[len(kinds) :]
    arrays = max(array for array, _ in rows_of) + 1
    blocks, refs = refs[:arrays], refs[arrays:]
    if follows:
        before, refs = refs[0], refs[1:]
    out_ref, query_s, key_s, value_s, chosen_s = refs
    part, rows = queries[0].shape
    hdim = part // HALF
    wide = value_s.shape[2]
    nblocks = seg_ref.shape[1] // rows
    factor = LOG2E / (hdim**0.5)
    me = where_ref[0]
    column = [key_block(me, b) for b in numbers]
    asker = [asking(me, kind) for kind in kinds]
    bits = jnp.max(need_ref[...])
    need = [[(bits >> (kind * len(PLACES) + b)) & 1 for b in numbers] for kind in kinds]

    def segment(block):
        start = pl.multiple_of(jnp.clip(block, 0, nblocks - 1) * rows, 128)
        return seg_ref[:, pl.ds(start, rows)]

    for b in range(len(numbers)):
        wanted = need[0][b]
        for n in range(1, len(kinds)):
            wanted = wanted + need[n][b]

        @pl.when(wanted > 0)
        def _(b=b):
            array, first = rows_of[b]
            key_s[b] = blocks[array][first : first + part, :]
            for h in range(HALF):
                start = first + part + h * hdim
                value_s[b, h, :hdim, :] = blocks[array][start : start + hdim, :]
                value_s[b, h, hdim:, :] = jnp.ones((wide - hdim, rows), jnp.bfloat16)

    for n in range(len(kinds)):
        size = 0
        for b in range(len(numbers)):
            chosen_s[size] = b
            size = size + need[n][b]
        for h in range(HALF):
            query_s[h] = queries[n][h * hdim : (h + 1) * hdim, :].T
        query_seg = jnp.broadcast_to(segment(asker[n]), (128, rows)).T
        query_seg = jnp.concatenate([query_seg] * (rows // 128), axis=1)

        def finish(h, peak, accum, n=n):
            if ends:
                turned = accum.T
                lines = slice(h * hdim, (h + 1) * hdim)
                out_ref[lines, :] = (turned[:hdim] / turned[hdim : hdim + 1]).astype(out_ref.dtype)
            else:
                peak = jnp.broadcast_to(peak, (rows, 128 - wide))
                out_ref[n, h] = jnp.concatenate([accum, peak], axis=1)

        if follows:

            @pl.when(size == 0)
            def _():
                for h in range(HALF):
                    state = before[0, h]
                    finish(h, state[:, wide : wide + 1], state[:, :wide])

        for fixed in range(1, len(numbers) + 1):

            @pl.when(size == fixed)
            def _():
                picked = [chosen_s[b] for b in range(fixed)]
                key_segs = [
                    segment(sum(jnp.where(b == i, column[i], 0) for i in range(len(numbers))))
                    for b in picked
                ]

                def one_head(h):
                    lines = slice(h * hdim, (h + 1) * hdim)
                    query = query_s[h]
                    scores = []
                    for b, key_seg in zip(picked, key_segs):
                        score = jnp.dot(
                            query, key_s[b, lines, :], preferred_element_type=jnp.float32
                        )
                        scores.append(jnp.where(query_seg == key_seg, score, NEG))
                    peak = functools.reduce(jnp.maximum, scores)
                    peak = jnp.max(peak, axis=1, keepdims=True)
                    accum = jnp.zeros((rows, wide), jnp.float32)
                    if follows:
                        state = before[0, h]
                        old = state[:, wide : wide + 1]
                        peak = jnp.maximum(peak, old)
                        accum = state[:, :wide] * jnp.exp2((old - peak) * factor)
                    for b, score in zip(picked, scores):
                        weights = jnp.exp2((score - peak) * factor).astype(jnp.bfloat16)
                        accum += lax.dot_general(
                            weights,
                            value_s[b, h],
                            (((1,), (1,)), ((), ())),
                            preferred_element_type=jnp.float32,
                        )
                    finish(h, peak, accum)

                for h in range(HALF):
                    one_head(h)


def attention(where, need, segs, queries, kinds, blocks, numbers, before, ends):
    part, rows = queries[0].shape
    hdim = part // HALF
    wide = hdim + 16
    follows = before is not None
    rows_of = [
        (array, first)
        for array, block in enumerate(blocks)
        for first in range(0, block.shape[0], 2 * part)
    ]
    if ends:
        out = jax.ShapeDtypeStruct((part, rows), jnp.bfloat16)
    else:
        out = jax.ShapeDtypeStruct((len(kinds), HALF, rows, 128), jnp.float32)
    return pl.pallas_call(
        functools.partial(attention_kernel, kinds, numbers, rows_of, follows, ends),
        out_shape=out,
        in_specs=[smem()] + [vmem()] * (2 + len(kinds) + len(blocks) + follows),
        out_specs=vmem(),
        scratch_shapes=[
            pltpu.VMEM((HALF, rows, hdim), jnp.bfloat16),
            pltpu.VMEM((len(numbers), part, rows), jnp.bfloat16),
            pltpu.VMEM((len(numbers), HALF, wide, rows), jnp.bfloat16),
            pltpu.SMEM((len(numbers) + 1,), jnp.int32),
        ],
        compiler_params=limit(16),
        cost_estimate=pl.CostEstimate(flops=1000, bytes_accessed=1000, transcendentals=0),
    )(where, need, segs, *queries, *blocks, *((before,) if follows else ()))


def stack_kernel(*refs):
    *parts, out_ref = refs
    first = 0
    for ref in parts:
        out_ref[first : first + ref.shape[0], :] = ref[...]
        first += ref.shape[0]


def stack(*parts):
    lines = sum(part.shape[0] for part in parts)
    return pl.pallas_call(
        stack_kernel,
        out_shape=jax.ShapeDtypeStruct((lines, parts[0].shape[1]), parts[0].dtype),
        in_specs=[vmem()] * len(parts),
        out_specs=vmem(),
        compiler_params=limit(16),
    )(*parts)


def project_kernel(
    pair_rows, order, where_ref, owners_ref, offsets_ref, own_ref, other_ref, weight_ref, tokens_ref, *outs
):
    piece = outs[0].shape[0]
    slots = piece * len(outs)
    rows, width = tokens_ref.shape
    mrows = rows // 4
    capacity = 2 * mrows
    owner = owners_ref[...]
    if len(outs) > 1:
        owner = owner ^ where_ref[0]
    owner = jnp.broadcast_to(owner.astype(jnp.float32), (mrows, mrows))
    earlier = lax.broadcasted_iota(jnp.int32, (mrows, mrows), 0)
    later = lax.broadcasted_iota(jnp.int32, (mrows, mrows), 1)
    column = jnp.sum(jnp.where(earlier == later, owner, 0.0), axis=1, keepdims=True)
    ahead = jnp.where((owner == column) & (earlier < later), 1.0, 0.0)
    slot = owner[:1] * pair_rows + jnp.sum(ahead, axis=0, keepdims=True)
    line = lax.broadcasted_iota(jnp.int32, (16, mrows), 0)
    meta = jnp.where(line == 0, slot, jnp.where(line == 1, offsets_ref[...].astype(jnp.float32), 0.0))
    row = lax.broadcasted_iota(jnp.int32, (mrows, rows), 0)
    patch = lax.broadcasted_iota(jnp.int32, (mrows, rows), 1)
    spread = jnp.where(patch // 4 == row, 1.0, 0.0).astype(jnp.bfloat16)
    meta = jnp.dot(meta.astype(jnp.bfloat16), spread, preferred_element_type=jnp.float32)
    part = own_ref.shape[0]
    half = where_ref[0] % 2
    hidden = tokens_ref[...].astype(jnp.float32)
    for ref, which in ((own_ref, half), (other_ref, 1 - half)):
        hidden += lax.dot_general(
            ref[...],
            weight_ref[pl.ds(pl.multiple_of(which * part, 16), part), :],
            (((0,), (0,)), ((), ())),
            preferred_element_type=jnp.float32,
        )
    hidden = hidden.astype(jnp.bfloat16)
    slot = lax.broadcasted_iota(jnp.int32, (slots, rows), 0).astype(jnp.float32)
    quarter = lax.broadcasted_iota(jnp.int32, (1, rows), 1) % 4
    for j in range(4):
        mine = jnp.where(quarter == j, meta[:1], -1.0) == slot
        if j == 0:
            offset = jnp.where(mine, meta[1:2] - capacity, 0.0)
            offset = capacity + jnp.sum(offset, axis=1, keepdims=True)
            offset = jnp.broadcast_to(offset, (slots, 128)).astype(jnp.bfloat16)
            for d, out in zip(order, outs):
                out[:, 4 * width :] = offset[d * piece : (d + 1) * piece]
        pick = jnp.where(mine, 1.0, 0.0).astype(jnp.bfloat16)
        picked = jnp.dot(pick, hidden, preferred_element_type=jnp.float32).astype(jnp.bfloat16)
        for d, out in zip(order, outs):
            out[:, j * width : (j + 1) * width] = picked[d * piece : (d + 1) * piece]


def project(where, owners, offsets, own, other, out_weight, tokens, order, slots, pair_rows):
    rows, width = tokens.shape
    pieces = len(order)
    return pl.pallas_call(
        functools.partial(project_kernel, pair_rows, order),
        out_shape=[jax.ShapeDtypeStruct((slots // pieces, 4 * width + 128), jnp.bfloat16)] * pieces,
        in_specs=[smem()] + [vmem()] * 6,
        out_specs=[vmem()] * pieces,
        compiler_params=limit(24),
    )(where, owners, offsets, own, other, out_weight, tokens)


def place_kernel(*refs):
    *arrived, out_hbm, held, sems = refs
    capacity, merged = out_hbm.shape
    step = merged // 4

    def columns_of(start, size):
        return jnp.concatenate([ref[:, start : start + size] for ref in arrived], axis=0)

    offset = columns_of(merged, 128).astype(jnp.float32)[:, :1]
    row = lax.broadcasted_iota(jnp.int32, (offset.shape[0], capacity), 1).astype(jnp.float32)
    pick = jnp.where(offset == row, 1.0, 0.0).astype(jnp.bfloat16)
    stores = []
    for j in range(4):
        held[j] = lax.dot_general(
            pick,
            columns_of(j * step, step),
            (((0,), (0,)), ((), ())),
            preferred_element_type=jnp.float32,
        ).astype(jnp.bfloat16)
        columns = out_hbm.at[:, pl.ds(j * step, step)]
        stores.append(pltpu.make_async_copy(held.at[j], columns, sems.at[j]))
        stores[j].start()
    for store in stores:
        store.wait()


def place(arrived, capacity, merged):
    return pl.pallas_call(
        place_kernel,
        out_shape=jax.ShapeDtypeStruct((capacity, merged), jnp.bfloat16),
        in_specs=[vmem()] * len(arrived),
        out_specs=anywhere(),
        scratch_shapes=[
            pltpu.VMEM((4, capacity, merged // 4), jnp.bfloat16),
            pltpu.SemaphoreType.DMA((4,)),
        ],
        compiler_params=limit(24),
    )(*arrived)


def per_device(segment_ids, block_mask, queries, keys, values, tokens, out_weight, owners, offsets):
    rows = queries.shape[0]
    width = tokens.shape[1]
    nblocks = lax.axis_size("blk")
    block_index = lax.axis_index("blk")
    mrows = rows // 4
    capacity = 2 * mrows
    pair_rows = max(2, 2 * mrows // nblocks)
    slots = nblocks * pair_rows
    assert slots <= 256

    def route(step):
        return [(i, i + step(i)) for i in range(nblocks) if 0 <= i + step(i) < nblocks]

    swap = functools.partial(
        lax.ppermute, axis_name="blk", perm=route(lambda i: 1 - 2 * (i % 2))
    )
    ahead = functools.partial(
        lax.ppermute, axis_name="blk", perm=route(lambda i: 2 if i % 2 else -2)
    )
    back = functools.partial(
        lax.ppermute, axis_name="blk", perm=route(lambda i: -2 if i % 2 else 2)
    )

    relay = functools.partial(
        lax.ppermute,
        axis_name="blk",
        perm=route(lambda i: -1 if i == 1 else 1 if i == nblocks - 2 else -2 if i % 2 else 2),
    )

    where = block_index[None].astype(jnp.int32)
    own_q, own_kv, swap_q, swap_kv = prepare(where, queries, keys, values)
    segs, need = survey(where, block_mask, segment_ids[None, :])
    other_kv = swap(swap_kv)
    ahead_own = ahead(own_kv)
    back_own = back(own_kv)
    ready, back_own, swap_q = lax.optimization_barrier((other_kv, back_own, swap_q))
    back_other = relay(ready)
    ahead_both = ahead(stack(other_kv, ahead_own))
    other_q = swap(swap_q)
    near = (own_kv, other_kv, ahead_own, back_own)
    near_numbers = (0, 1, 2, 3)
    fixed = (where, need, segs)
    own = attention(*fixed, (own_q,), (0,), near, near_numbers, None, False)
    back_other, own = lax.optimization_barrier((back_other, own))
    back_far = relay(back_other)
    other = attention(*fixed, (other_q,), (1,), near, near_numbers, None, False)
    far = (ahead_both, back_other)
    other = attention(*fixed, (other_q,), (1,), far, (4, 6, 5), other, True)
    other = swap(other)
    far = (ahead_both, back_other, back_far)
    own = attention(*fixed, (own_q,), (0,), far, (4, 6, 5, 7), own, True)

    order = tuple(range(nblocks)) if nblocks in (4, 8) else (0,)
    outgoing = project(
        where, owners[None, :], offsets[None, :], own, other, out_weight, tokens,
        order, slots, pair_rows,
    )
    if len(order) > 1:
        arrived = list(outgoing)

        def cross(d):
            arrived[d] = lax.ppermute(arrived[d], "blk", [(i, i ^ d) for i in range(nblocks)])

        short, *late = range(nblocks // 2 - 1, 0, -1)
        for d in (*range(nblocks // 2, nblocks), short):
            cross(d)
        group = lax.optimization_barrier([arrived[d] for d in (short, *late)])
        for d, block in zip((short, *late), group):
            arrived[d] = block
        for d in late:
            cross(d)
    else:
        arrived = [lax.all_to_all(outgoing[0], "blk", split_axis=0, concat_axis=0, tiled=True)]
    return place(arrived, capacity, 4 * width)


def solution(mesh):
    placed = (
        P("rep"),
        P("rep", None),
        P(("rep", "blk"), None),
        P(("rep", "blk"), None),
        P(("rep", "blk"), None),
        P(("rep", "blk"), None),
        P(),
        P(("rep", "blk")),
        P(("rep", "blk")),
    )
    return jax.shard_map(
        per_device, mesh=mesh, in_specs=placed, out_specs=P(("rep", "blk"), None), check_vma=False
    )
```

```python
import functools

import jax
import jax.numpy as jnp
from jax import lax
from jax.experimental import pallas as pl
from jax.experimental.pallas import tpu as pltpu
from jax.sharding import PartitionSpec as P

HEADS = 8
HALF = HEADS // 2
SPAN = 3
NEG = -1e30
LOG2E = 1.4426950408889634
MIB = 1024 * 1024


def vmem():
    return pl.BlockSpec(memory_space=pltpu.VMEM)


def smem():
    return pl.BlockSpec(memory_space=pltpu.SMEM)


def anywhere():
    return pl.BlockSpec(memory_space=pl.ANY)


def limit(mib):
    return pltpu.CompilerParams(vmem_limit_bytes=mib * MIB)


PLACES = ((3, 1), (4, -1), (5, -3), (1, 5), (6, -5), (2, 3), (7, -7), (0, 7))


def asking(me, kind):
    return me if kind == 0 else me + 1 - 2 * (me % 2)


def key_block(me, number):
    half = me % 2
    return me - half - SPAN + PLACES[number][0] + PLACES[number][1] * half


def prepare_kernel(where_ref, q_hbm, k_hbm, v_hbm, own_q, own_kv, swap_q, swap_kv, held, turned, sems):
    part = q_hbm.shape[1] // 2
    loads = [
        pltpu.make_async_copy(ref, held.at[i], sems.at[i])
        for i, ref in enumerate((k_hbm, v_hbm, q_hbm))
    ]
    for load in loads:
        load.start()
    me = where_ref[0]
    half = me % 2
    mine = pl.multiple_of(half * part, 16)
    other = pl.multiple_of((1 - half) * part, 16)
    for i in range(3):
        loads[i].wait()
        turned[i] = held[i].T
        if i < 2:
            own_kv[i * part : (i + 1) * part, :] = turned[i, pl.ds(mine, part), :]
            swap_kv[i * part : (i + 1) * part, :] = turned[i, pl.ds(other, part), :]
        else:
            own_q[...] = turned[i, pl.ds(mine, part), :]
            swap_q[...] = turned[i, pl.ds(other, part), :]


def prepare(where, queries, keys, values):
    rows, features = queries.shape
    part = features // 2
    single = jax.ShapeDtypeStruct((part, rows), queries.dtype)
    double = jax.ShapeDtypeStruct((2 * part, rows), queries.dtype)
    return pl.pallas_call(
        prepare_kernel,
        out_shape=[single, double, single, double],
        in_specs=[smem()] + [anywhere()] * 3,
        out_specs=[vmem()] * 4,
        scratch_shapes=[
            pltpu.VMEM((3, rows, features), queries.dtype),
            pltpu.VMEM((3, features, rows), queries.dtype),
            pltpu.SemaphoreType.DMA((3,)),
        ],
        compiler_params=limit(53),
    )(where, queries, keys, values)


def survey_kernel(where_ref, mask_ref, segs_ref, seg_out, need_out):
    seg_out[...] = segs_ref[...].astype(jnp.float32)
    me = where_ref[0]
    nblocks = mask_ref.shape[0]
    bits = jnp.int32(0)
    for kind in range(2):
        asker = asking(me, kind)
        for number in range(len(PLACES)):
            block = key_block(me, number)
            inside = (block >= 0) & (block < nblocks) & (jnp.abs(block - asker) <= SPAN)
            allowed = mask_ref[asker, jnp.clip(block, 0, nblocks - 1)] > 0
            bits += (inside & allowed).astype(jnp.int32) << (kind * len(PLACES) + number)
    need_out[...] = jnp.full(need_out.shape, bits, jnp.int32)


def survey(where, mask, segs):
    return pl.pallas_call(
        survey_kernel,
        out_shape=[
            jax.ShapeDtypeStruct(segs.shape, jnp.float32),
            jax.ShapeDtypeStruct((8, 128), jnp.int32),
        ],
        in_specs=[smem()] * 2 + [vmem()],
        out_specs=[vmem()] * 2,
        compiler_params=limit(16),
    )(where, mask, segs)


def attention_kernel(kinds, numbers, rows_of, follows, ends, where_ref, need_ref, seg_ref, *refs):
    queries, refs = refs[: len(kinds)], refs[len(kinds) :]
    arrays = max(array for array, _ in rows_of) + 1
    blocks, refs = refs[:arrays], refs[arrays:]
    if follows:
        before, refs = refs[0], refs[1:]
    out_ref, query_s, key_s, value_s, chosen_s = refs
    part, rows = queries[0].shape
    hdim = part // HALF
    wide = value_s.shape[2]
    nblocks = seg_ref.shape[1] // rows
    factor = LOG2E / (hdim**0.5)
    me = where_ref[0]
    column = [key_block(me, b) for b in numbers]
    asker = [asking(me, kind) for kind in kinds]
    bits = jnp.max(need_ref[...])
    need = [[(bits >> (kind * len(PLACES) + b)) & 1 for b in numbers] for kind in kinds]

    def segment(block):
        start = pl.multiple_of(jnp.clip(block, 0, nblocks - 1) * rows, 128)
        return seg_ref[:, pl.ds(start, rows)]

    for b in range(len(numbers)):
        wanted = need[0][b]
        for n in range(1, len(kinds)):
            wanted = wanted + need[n][b]

        @pl.when(wanted > 0)
        def _(b=b):
            array, first = rows_of[b]
            key_s[b] = blocks[array][first : first + part, :]
            for h in range(HALF):
                start = first + part + h * hdim
                value_s[b, h, :hdim, :] = blocks[array][start : start + hdim, :]
                value_s[b, h, hdim:, :] = jnp.ones((wide - hdim, rows), jnp.bfloat16)

    for n in range(len(kinds)):
        size = 0
        for b in range(len(numbers)):
            chosen_s[size] = b
            size = size + need[n][b]
        for h in range(HALF):
            query_s[h] = queries[n][h * hdim : (h + 1) * hdim, :].T
        query_seg = jnp.broadcast_to(segment(asker[n]), (128, rows)).T
        query_seg = jnp.concatenate([query_seg] * (rows // 128), axis=1)

        def finish(h, peak, accum, n=n):
            if ends:
                turned = accum.T
                lines = slice(h * hdim, (h + 1) * hdim)
                out_ref[lines, :] = (turned[:hdim] / turned[hdim : hdim + 1]).astype(out_ref.dtype)
            else:
                peak = jnp.broadcast_to(peak, (rows, 128 - wide))
                out_ref[n, h] = jnp.concatenate([accum, peak], axis=1)

        if follows:

            @pl.when(size == 0)
            def _():
                for h in range(HALF):
                    state = before[0, h]
                    finish(h, state[:, wide : wide + 1], state[:, :wide])

        for fixed in range(1, len(numbers) + 1):

            @pl.when(size == fixed)
            def _():
                picked = [chosen_s[b] for b in range(fixed)]
                key_segs = [
                    segment(sum(jnp.where(b == i, column[i], 0) for i in range(len(numbers))))
                    for b in picked
                ]

                def one_head(h):
                    lines = slice(h * hdim, (h + 1) * hdim)
                    query = query_s[h]
                    scores = []
                    for b, key_seg in zip(picked, key_segs):
                        score = jnp.dot(
                            query, key_s[b, lines, :], preferred_element_type=jnp.float32
                        )
                        scores.append(jnp.where(query_seg == key_seg, score, NEG))
                    peak = functools.reduce(jnp.maximum, scores)
                    peak = jnp.max(peak, axis=1, keepdims=True)
                    accum = jnp.zeros((rows, wide), jnp.float32)
                    if follows:
                        state = before[0, h]
                        old = state[:, wide : wide + 1]
                        peak = jnp.maximum(peak, old)
                        accum = state[:, :wide] * jnp.exp2((old - peak) * factor)
                    for b, score in zip(picked, scores):
                        weights = jnp.exp2((score - peak) * factor).astype(jnp.bfloat16)
                        accum += lax.dot_general(
                            weights,
                            value_s[b, h],
                            (((1,), (1,)), ((), ())),
                            preferred_element_type=jnp.float32,
                        )
                    finish(h, peak, accum)

                for h in range(HALF):
                    one_head(h)


def attention(where, need, segs, queries, kinds, blocks, numbers, before, ends):
    part, rows = queries[0].shape
    hdim = part // HALF
    wide = hdim + 16
    follows = before is not None
    rows_of = [
        (array, first)
        for array, block in enumerate(blocks)
        for first in range(0, block.shape[0], 2 * part)
    ]
    if ends:
        out = jax.ShapeDtypeStruct((part, rows), jnp.bfloat16)
    else:
        out = jax.ShapeDtypeStruct((len(kinds), HALF, rows, 128), jnp.float32)
    return pl.pallas_call(
        functools.partial(attention_kernel, kinds, numbers, rows_of, follows, ends),
        out_shape=out,
        in_specs=[smem()] + [vmem()] * (2 + len(kinds) + len(blocks) + follows),
        out_specs=vmem(),
        scratch_shapes=[
            pltpu.VMEM((HALF, rows, hdim), jnp.bfloat16),
            pltpu.VMEM((len(numbers), part, rows), jnp.bfloat16),
            pltpu.VMEM((len(numbers), HALF, wide, rows), jnp.bfloat16),
            pltpu.SMEM((len(numbers) + 1,), jnp.int32),
        ],
        compiler_params=limit(16),
        cost_estimate=pl.CostEstimate(flops=1000, bytes_accessed=1000, transcendentals=0),
    )(where, need, segs, *queries, *blocks, *((before,) if follows else ()))


def stack_kernel(*refs):
    *parts, out_ref = refs
    first = 0
    for ref in parts:
        out_ref[first : first + ref.shape[0], :] = ref[...]
        first += ref.shape[0]


def stack(*parts):
    lines = sum(part.shape[0] for part in parts)
    return pl.pallas_call(
        stack_kernel,
        out_shape=jax.ShapeDtypeStruct((lines, parts[0].shape[1]), parts[0].dtype),
        in_specs=[vmem()] * len(parts),
        out_specs=vmem(),
        compiler_params=limit(16),
    )(*parts)


def project_kernel(
    pair_rows, order, where_ref, owners_ref, offsets_ref, own_ref, other_ref, weight_ref, tokens_ref, *outs
):
    piece = outs[0].shape[0]
    slots = piece * len(outs)
    rows, width = tokens_ref.shape
    mrows = rows // 4
    capacity = 2 * mrows
    owner = owners_ref[...]
    if len(outs) > 1:
        owner = owner ^ where_ref[0]
    owner = jnp.broadcast_to(owner.astype(jnp.float32), (mrows, mrows))
    earlier = lax.broadcasted_iota(jnp.int32, (mrows, mrows), 0)
    later = lax.broadcasted_iota(jnp.int32, (mrows, mrows), 1)
    column = jnp.sum(jnp.where(earlier == later, owner, 0.0), axis=1, keepdims=True)
    ahead = jnp.where((owner == column) & (earlier < later), 1.0, 0.0)
    slot = owner[:1] * pair_rows + jnp.sum(ahead, axis=0, keepdims=True)
    line = lax.broadcasted_iota(jnp.int32, (16, mrows), 0)
    meta = jnp.where(line == 0, slot, jnp.where(line == 1, offsets_ref[...].astype(jnp.float32), 0.0))
    row = lax.broadcasted_iota(jnp.int32, (mrows, rows), 0)
    patch = lax.broadcasted_iota(jnp.int32, (mrows, rows), 1)
    spread = jnp.where(patch // 4 == row, 1.0, 0.0).astype(jnp.bfloat16)
    meta = jnp.dot(meta.astype(jnp.bfloat16), spread, preferred_element_type=jnp.float32)
    part = own_ref.shape[0]
    half = where_ref[0] % 2
    hidden = tokens_ref[...].astype(jnp.float32)
    for ref, which in ((own_ref, half), (other_ref, 1 - half)):
        hidden += lax.dot_general(
            ref[...],
            weight_ref[pl.ds(pl.multiple_of(which * part, 16), part), :],
            (((0,), (0,)), ((), ())),
            preferred_element_type=jnp.float32,
        )
    hidden = hidden.astype(jnp.bfloat16)
    slot = lax.broadcasted_iota(jnp.int32, (slots, rows), 0).astype(jnp.float32)
    quarter = lax.broadcasted_iota(jnp.int32, (1, rows), 1) % 4
    for j in range(4):
        mine = jnp.where(quarter == j, meta[:1], -1.0) == slot
        if j == 0:
            offset = jnp.where(mine, meta[1:2] - capacity, 0.0)
            offset = capacity + jnp.sum(offset, axis=1, keepdims=True)
            offset = jnp.broadcast_to(offset, (slots, 128)).astype(jnp.bfloat16)
            for d, out in zip(order, outs):
                out[:, 4 * width :] = offset[d * piece : (d + 1) * piece]
        pick = jnp.where(mine, 1.0, 0.0).astype(jnp.bfloat16)
        picked = jnp.dot(pick, hidden, preferred_element_type=jnp.float32).astype(jnp.bfloat16)
        for d, out in zip(order, outs):
            out[:, j * width : (j + 1) * width] = picked[d * piece : (d + 1) * piece]


def project(where, owners, offsets, own, other, out_weight, tokens, order, slots, pair_rows):
    rows, width = tokens.shape
    pieces = len(order)
    return pl.pallas_call(
        functools.partial(project_kernel, pair_rows, order),
        out_shape=[jax.ShapeDtypeStruct((slots // pieces, 4 * width + 128), jnp.bfloat16)] * pieces,
        in_specs=[smem()] + [vmem()] * 6,
        out_specs=[vmem()] * pieces,
        compiler_params=limit(24),
    )(where, owners, offsets, own, other, out_weight, tokens)


def place_kernel(*refs):
    *arrived, out_hbm, held, sems = refs
    capacity, merged = out_hbm.shape
    step = merged // 4

    def columns_of(start, size):
        return jnp.concatenate([ref[:, start : start + size] for ref in arrived], axis=0)

    offset = columns_of(merged, 128).astype(jnp.float32)[:, :1]
    row = lax.broadcasted_iota(jnp.int32, (offset.shape[0], capacity), 1).astype(jnp.float32)
    pick = jnp.where(offset == row, 1.0, 0.0).astype(jnp.bfloat16)
    stores = []
    for j in range(4):
        held[j] = lax.dot_general(
            pick,
            columns_of(j * step, step),
            (((0,), (0,)), ((), ())),
            preferred_element_type=jnp.float32,
        ).astype(jnp.bfloat16)
        columns = out_hbm.at[:, pl.ds(j * step, step)]
        stores.append(pltpu.make_async_copy(held.at[j], columns, sems.at[j]))
        stores[j].start()
    for store in stores:
        store.wait()


def place(arrived, capacity, merged):
    return pl.pallas_call(
        place_kernel,
        out_shape=jax.ShapeDtypeStruct((capacity, merged), jnp.bfloat16),
        in_specs=[vmem()] * len(arrived),
        out_specs=anywhere(),
        scratch_shapes=[
            pltpu.VMEM((4, capacity, merged // 4), jnp.bfloat16),
            pltpu.SemaphoreType.DMA((4,)),
        ],
        compiler_params=limit(24),
    )(*arrived)


def per_device(segment_ids, block_mask, queries, keys, values, tokens, out_weight, owners, offsets):
    rows = queries.shape[0]
    width = tokens.shape[1]
    nblocks = lax.axis_size("blk")
    block_index = lax.axis_index("blk")
    mrows = rows // 4
    capacity = 2 * mrows
    pair_rows = max(2, 2 * mrows // nblocks)
    slots = nblocks * pair_rows
    assert slots <= 256

    def route(step):
        return [(i, i + step(i)) for i in range(nblocks) if 0 <= i + step(i) < nblocks]

    swap = functools.partial(
        lax.ppermute, axis_name="blk", perm=route(lambda i: 1 - 2 * (i % 2))
    )
    ahead = functools.partial(
        lax.ppermute, axis_name="blk", perm=route(lambda i: 2 if i % 2 else -2)
    )
    back = functools.partial(
        lax.ppermute, axis_name="blk", perm=route(lambda i: -2 if i % 2 else 2)
    )

    relay = functools.partial(
        lax.ppermute,
        axis_name="blk",
        perm=route(lambda i: -1 if i == 1 else 1 if i == nblocks - 2 else -2 if i % 2 else 2),
    )

    where = block_index[None].astype(jnp.int32)
    own_q, own_kv, swap_q, swap_kv = prepare(where, queries, keys, values)
    segs, need = survey(where, block_mask, segment_ids[None, :])
    other_kv = swap(swap_kv)
    ahead_own = ahead(own_kv)
    back_own = back(own_kv)
    ready, back_own, swap_q, segs, need = lax.optimization_barrier(
        (other_kv, back_own, swap_q, segs, need)
    )
    back_other = back(ready)
    ahead_other = ahead(other_kv)
    ahead_far = ahead(ahead_own)
    other_q = swap(swap_q)
    near = (own_kv, other_kv, ahead_own, back_own)
    near_numbers = (0, 1, 2, 3)
    fixed = (where, need, segs)
    own = attention(*fixed, (own_q,), (0,), near, near_numbers, None, False)
    back_other, own = lax.optimization_barrier((back_other, own))
    back_far = relay(back_other)
    other = attention(*fixed, (other_q,), (1,), near, near_numbers, None, False)
    middle = (ahead_other, back_other)
    other = attention(*fixed, (other_q,), (1,), middle, (4, 5), other, False)
    other = attention(*fixed, (other_q,), (1,), (ahead_far,), (6,), other, True)
    other = swap(other)
    own = attention(*fixed, (own_q,), (0,), (*middle, back_far), (4, 5, 7), own, True)

    order = tuple(range(nblocks)) if nblocks in (4, 8) else (0,)
    outgoing = project(
        where, owners[None, :], offsets[None, :], own, other, out_weight, tokens,
        order, slots, pair_rows,
    )
    if len(order) > 1:
        arrived = list(outgoing)

        def cross(d):
            arrived[d] = lax.ppermute(arrived[d], "blk", [(i, i ^ d) for i in range(nblocks)])

        short, *late = range(nblocks // 2 - 1, 0, -1)
        for d in (*range(nblocks // 2, nblocks), short):
            cross(d)
        group = lax.optimization_barrier([arrived[d] for d in (short, *late)])
        for d, block in zip((short, *late), group):
            arrived[d] = block
        for d in late:
            cross(d)
    else:
        arrived = [lax.all_to_all(outgoing[0], "blk", split_axis=0, concat_axis=0, tiled=True)]
    return place(arrived, capacity, 4 * width)


def solution(mesh):
    placed = (
        P("rep"),
        P("rep", None),
        P(("rep", "blk"), None),
        P(("rep", "blk"), None),
        P(("rep", "blk"), None),
        P(("rep", "blk"), None),
        P(),
        P(("rep", "blk")),
        P(("rep", "blk")),
    )
    return jax.shard_map(
        per_device, mesh=mesh, in_specs=placed, out_specs=P(("rep", "blk"), None), check_vma=False
    )
```

```python
import functools

import jax
import jax.numpy as jnp
from jax import lax
from jax.experimental import pallas as pl
from jax.experimental.pallas import tpu as pltpu
from jax.sharding import PartitionSpec as P

HEADS = 8
HALF = HEADS // 2
SPAN = 3
NEG = -1e30
LOG2E = 1.4426950408889634
MIB = 1024 * 1024


def vmem():
    return pl.BlockSpec(memory_space=pltpu.VMEM)


def smem():
    return pl.BlockSpec(memory_space=pltpu.SMEM)


def anywhere():
    return pl.BlockSpec(memory_space=pl.ANY)


def limit(mib):
    return pltpu.CompilerParams(vmem_limit_bytes=mib * MIB)


PLACES = ((3, 1), (4, -1), (5, -3), (1, 5), (6, -5), (2, 3), (7, -7), (0, 7))


def asking(me, kind):
    return me if kind == 0 else me + 1 - 2 * (me % 2)


def key_block(me, number):
    half = me % 2
    return me - half - SPAN + PLACES[number][0] + PLACES[number][1] * half


def prepare_kernel(where_ref, q_hbm, k_hbm, v_hbm, own_q, own_kv, swap_q, swap_kv, held, turned, sems):
    part = q_hbm.shape[1] // 2
    loads = [
        pltpu.make_async_copy(ref, held.at[i], sems.at[i])
        for i, ref in enumerate((k_hbm, v_hbm, q_hbm))
    ]
    for load in loads:
        load.start()
    me = where_ref[0]
    half = me % 2
    mine = pl.multiple_of(half * part, 16)
    other = pl.multiple_of((1 - half) * part, 16)
    for i in range(3):
        loads[i].wait()
        turned[i] = held[i].T
        if i < 2:
            own_kv[i * part : (i + 1) * part, :] = turned[i, pl.ds(mine, part), :]
            swap_kv[i * part : (i + 1) * part, :] = turned[i, pl.ds(other, part), :]
        else:
            own_q[...] = turned[i, pl.ds(mine, part), :]
            swap_q[...] = turned[i, pl.ds(other, part), :]


def prepare(where, queries, keys, values):
    rows, features = queries.shape
    part = features // 2
    single = jax.ShapeDtypeStruct((part, rows), queries.dtype)
    double = jax.ShapeDtypeStruct((2 * part, rows), queries.dtype)
    return pl.pallas_call(
        prepare_kernel,
        out_shape=[single, double, single, double],
        in_specs=[smem()] + [anywhere()] * 3,
        out_specs=[vmem()] * 4,
        scratch_shapes=[
            pltpu.VMEM((3, rows, features), queries.dtype),
            pltpu.VMEM((3, features, rows), queries.dtype),
            pltpu.SemaphoreType.DMA((3,)),
        ],
        compiler_params=limit(53),
    )(where, queries, keys, values)


def survey_kernel(where_ref, mask_ref, segs_ref, seg_out, need_out):
    seg_out[...] = segs_ref[...].astype(jnp.float32)
    me = where_ref[0]
    nblocks = mask_ref.shape[0]
    bits = jnp.int32(0)
    for kind in range(2):
        asker = asking(me, kind)
        for number in range(len(PLACES)):
            block = key_block(me, number)
            inside = (block >= 0) & (block < nblocks) & (jnp.abs(block - asker) <= SPAN)
            allowed = mask_ref[asker, jnp.clip(block, 0, nblocks - 1)] > 0
            bits += (inside & allowed).astype(jnp.int32) << (kind * len(PLACES) + number)
    need_out[...] = jnp.full(need_out.shape, bits, jnp.int32)


def survey(where, mask, segs):
    return pl.pallas_call(
        survey_kernel,
        out_shape=[
            jax.ShapeDtypeStruct(segs.shape, jnp.float32),
            jax.ShapeDtypeStruct((8, 128), jnp.int32),
        ],
        in_specs=[smem()] * 2 + [vmem()],
        out_specs=[vmem()] * 2,
        compiler_params=limit(16),
    )(where, mask, segs)


def attention_kernel(kinds, numbers, rows_of, follows, ends, where_ref, need_ref, seg_ref, *refs):
    queries, refs = refs[: len(kinds)], refs[len(kinds) :]
    arrays = max(array for array, _ in rows_of) + 1
    blocks, refs = refs[:arrays], refs[arrays:]
    if follows:
        before, refs = refs[0], refs[1:]
    out_ref, query_s, key_s, value_s, chosen_s = refs
    part, rows = queries[0].shape
    hdim = part // HALF
    wide = value_s.shape[2]
    nblocks = seg_ref.shape[1] // rows
    factor = LOG2E / (hdim**0.5)
    me = where_ref[0]
    column = [key_block(me, b) for b in numbers]
    asker = [asking(me, kind) for kind in kinds]
    bits = jnp.max(need_ref[...])
    need = [[(bits >> (kind * len(PLACES) + b)) & 1 for b in numbers] for kind in kinds]

    def segment(block):
        start = pl.multiple_of(jnp.clip(block, 0, nblocks - 1) * rows, 128)
        return seg_ref[:, pl.ds(start, rows)]

    for b in range(len(numbers)):
        wanted = need[0][b]
        for n in range(1, len(kinds)):
            wanted = wanted + need[n][b]

        @pl.when(wanted > 0)
        def _(b=b):
            array, first = rows_of[b]
            key_s[b] = blocks[array][first : first + part, :]
            for h in range(HALF):
                start = first + part + h * hdim
                value_s[b, h, :hdim, :] = blocks[array][start : start + hdim, :]
                value_s[b, h, hdim:, :] = jnp.ones((wide - hdim, rows), jnp.bfloat16)

    for n in range(len(kinds)):
        size = 0
        for b in range(len(numbers)):
            chosen_s[size] = b
            size = size + need[n][b]
        for h in range(HALF):
            query_s[h] = queries[n][h * hdim : (h + 1) * hdim, :].T
        query_seg = jnp.broadcast_to(segment(asker[n]), (128, rows)).T
        query_seg = jnp.concatenate([query_seg] * (rows // 128), axis=1)

        def finish(h, peak, accum, n=n):
            if ends:
                turned = accum.T
                lines = slice(h * hdim, (h + 1) * hdim)
                out_ref[lines, :] = (turned[:hdim] / turned[hdim : hdim + 1]).astype(out_ref.dtype)
            else:
                peak = jnp.broadcast_to(peak, (rows, 128 - wide))
                out_ref[n, h] = jnp.concatenate([accum, peak], axis=1)

        if follows:

            @pl.when(size == 0)
            def _():
                for h in range(HALF):
                    state = before[0, h]
                    finish(h, state[:, wide : wide + 1], state[:, :wide])

        for fixed in range(1, len(numbers) + 1):

            @pl.when(size == fixed)
            def _():
                picked = [chosen_s[b] for b in range(fixed)]
                key_segs = [
                    segment(sum(jnp.where(b == i, column[i], 0) for i in range(len(numbers))))
                    for b in picked
                ]

                def one_head(h):
                    lines = slice(h * hdim, (h + 1) * hdim)
                    query = query_s[h]
                    scores = []
                    for b, key_seg in zip(picked, key_segs):
                        score = jnp.dot(
                            query, key_s[b, lines, :], preferred_element_type=jnp.float32
                        )
                        scores.append(jnp.where(query_seg == key_seg, score, NEG))
                    peak = functools.reduce(jnp.maximum, scores)
                    peak = jnp.max(peak, axis=1, keepdims=True)
                    accum = jnp.zeros((rows, wide), jnp.float32)
                    if follows:
                        state = before[0, h]
                        old = state[:, wide : wide + 1]
                        peak = jnp.maximum(peak, old)
                        accum = state[:, :wide] * jnp.exp2((old - peak) * factor)
                    for b, score in zip(picked, scores):
                        weights = jnp.exp2((score - peak) * factor).astype(jnp.bfloat16)
                        accum += lax.dot_general(
                            weights,
                            value_s[b, h],
                            (((1,), (1,)), ((), ())),
                            preferred_element_type=jnp.float32,
                        )
                    finish(h, peak, accum)

                for h in range(HALF):
                    one_head(h)


def attention(where, need, segs, queries, kinds, blocks, numbers, before, ends):
    part, rows = queries[0].shape
    hdim = part // HALF
    wide = hdim + 16
    follows = before is not None
    rows_of = [
        (array, first)
        for array, block in enumerate(blocks)
        for first in range(0, block.shape[0], 2 * part)
    ]
    if ends:
        out = jax.ShapeDtypeStruct((part, rows), jnp.bfloat16)
    else:
        out = jax.ShapeDtypeStruct((len(kinds), HALF, rows, 128), jnp.float32)
    return pl.pallas_call(
        functools.partial(attention_kernel, kinds, numbers, rows_of, follows, ends),
        out_shape=out,
        in_specs=[smem()] + [vmem()] * (2 + len(kinds) + len(blocks) + follows),
        out_specs=vmem(),
        scratch_shapes=[
            pltpu.VMEM((HALF, rows, hdim), jnp.bfloat16),
            pltpu.VMEM((len(numbers), part, rows), jnp.bfloat16),
            pltpu.VMEM((len(numbers), HALF, wide, rows), jnp.bfloat16),
            pltpu.SMEM((len(numbers) + 1,), jnp.int32),
        ],
        compiler_params=limit(16),
        cost_estimate=pl.CostEstimate(flops=1000, bytes_accessed=1000, transcendentals=0),
    )(where, need, segs, *queries, *blocks, *((before,) if follows else ()))


def stack_kernel(*refs):
    *parts, out_ref = refs
    first = 0
    for ref in parts:
        out_ref[first : first + ref.shape[0], :] = ref[...]
        first += ref.shape[0]


def stack(*parts):
    lines = sum(part.shape[0] for part in parts)
    return pl.pallas_call(
        stack_kernel,
        out_shape=jax.ShapeDtypeStruct((lines, parts[0].shape[1]), parts[0].dtype),
        in_specs=[vmem()] * len(parts),
        out_specs=vmem(),
        compiler_params=limit(16),
    )(*parts)


def project_kernel(
    pair_rows, order, where_ref, owners_ref, offsets_ref, own_ref, other_ref, weight_ref, tokens_ref, *outs
):
    piece = outs[0].shape[0]
    slots = piece * len(outs)
    rows, width = tokens_ref.shape
    mrows = rows // 4
    capacity = 2 * mrows
    owner = owners_ref[...]
    if len(outs) > 1:
        owner = owner ^ where_ref[0]
    owner = jnp.broadcast_to(owner.astype(jnp.float32), (mrows, mrows))
    earlier = lax.broadcasted_iota(jnp.int32, (mrows, mrows), 0)
    later = lax.broadcasted_iota(jnp.int32, (mrows, mrows), 1)
    column = jnp.sum(jnp.where(earlier == later, owner, 0.0), axis=1, keepdims=True)
    ahead = jnp.where((owner == column) & (earlier < later), 1.0, 0.0)
    slot = owner[:1] * pair_rows + jnp.sum(ahead, axis=0, keepdims=True)
    line = lax.broadcasted_iota(jnp.int32, (16, mrows), 0)
    meta = jnp.where(line == 0, slot, jnp.where(line == 1, offsets_ref[...].astype(jnp.float32), 0.0))
    row = lax.broadcasted_iota(jnp.int32, (mrows, rows), 0)
    patch = lax.broadcasted_iota(jnp.int32, (mrows, rows), 1)
    spread = jnp.where(patch // 4 == row, 1.0, 0.0).astype(jnp.bfloat16)
    meta = jnp.dot(meta.astype(jnp.bfloat16), spread, preferred_element_type=jnp.float32)
    part = own_ref.shape[0]
    half = where_ref[0] % 2
    hidden = tokens_ref[...].astype(jnp.float32)
    for ref, which in ((own_ref, half), (other_ref, 1 - half)):
        hidden += lax.dot_general(
            ref[...],
            weight_ref[pl.ds(pl.multiple_of(which * part, 16), part), :],
            (((0,), (0,)), ((), ())),
            preferred_element_type=jnp.float32,
        )
    hidden = hidden.astype(jnp.bfloat16)
    slot = lax.broadcasted_iota(jnp.int32, (slots, rows), 0).astype(jnp.float32)
    quarter = lax.broadcasted_iota(jnp.int32, (1, rows), 1) % 4
    for j in range(4):
        mine = jnp.where(quarter == j, meta[:1], -1.0) == slot
        if j == 0:
            offset = jnp.where(mine, meta[1:2] - capacity, 0.0)
            offset = capacity + jnp.sum(offset, axis=1, keepdims=True)
            offset = jnp.broadcast_to(offset, (slots, 128)).astype(jnp.bfloat16)
            for d, out in zip(order, outs):
                out[:, 4 * width :] = offset[d * piece : (d + 1) * piece]
        pick = jnp.where(mine, 1.0, 0.0).astype(jnp.bfloat16)
        picked = jnp.dot(pick, hidden, preferred_element_type=jnp.float32).astype(jnp.bfloat16)
        for d, out in zip(order, outs):
            out[:, j * width : (j + 1) * width] = picked[d * piece : (d + 1) * piece]


def project(where, owners, offsets, own, other, out_weight, tokens, order, slots, pair_rows):
    rows, width = tokens.shape
    pieces = len(order)
    return pl.pallas_call(
        functools.partial(project_kernel, pair_rows, order),
        out_shape=[jax.ShapeDtypeStruct((slots // pieces, 4 * width + 128), jnp.bfloat16)] * pieces,
        in_specs=[smem()] + [vmem()] * 6,
        out_specs=[vmem()] * pieces,
        compiler_params=limit(24),
    )(where, owners, offsets, own, other, out_weight, tokens)


def place_kernel(*refs):
    *arrived, out_hbm, held, sems = refs
    capacity, merged = out_hbm.shape
    step = merged // 4

    def columns_of(start, size):
        return jnp.concatenate([ref[:, start : start + size] for ref in arrived], axis=0)

    offset = columns_of(merged, 128).astype(jnp.float32)[:, :1]
    row = lax.broadcasted_iota(jnp.int32, (offset.shape[0], capacity), 1).astype(jnp.float32)
    pick = jnp.where(offset == row, 1.0, 0.0).astype(jnp.bfloat16)
    stores = []
    for j in range(4):
        held[j] = lax.dot_general(
            pick,
            columns_of(j * step, step),
            (((0,), (0,)), ((), ())),
            preferred_element_type=jnp.float32,
        ).astype(jnp.bfloat16)
        columns = out_hbm.at[:, pl.ds(j * step, step)]
        stores.append(pltpu.make_async_copy(held.at[j], columns, sems.at[j]))
        stores[j].start()
    for store in stores:
        store.wait()


def place(arrived, capacity, merged):
    return pl.pallas_call(
        place_kernel,
        out_shape=jax.ShapeDtypeStruct((capacity, merged), jnp.bfloat16),
        in_specs=[vmem()] * len(arrived),
        out_specs=anywhere(),
        scratch_shapes=[
            pltpu.VMEM((4, capacity, merged // 4), jnp.bfloat16),
            pltpu.SemaphoreType.DMA((4,)),
        ],
        compiler_params=limit(24),
    )(*arrived)


def per_device(segment_ids, block_mask, queries, keys, values, tokens, out_weight, owners, offsets):
    rows = queries.shape[0]
    width = tokens.shape[1]
    nblocks = lax.axis_size("blk")
    block_index = lax.axis_index("blk")
    mrows = rows // 4
    capacity = 2 * mrows
    pair_rows = max(2, 2 * mrows // nblocks)
    slots = nblocks * pair_rows
    assert slots <= 256

    def route(step):
        return [(i, i + step(i)) for i in range(nblocks) if 0 <= i + step(i) < nblocks]

    swap = functools.partial(
        lax.ppermute, axis_name="blk", perm=route(lambda i: 1 - 2 * (i % 2))
    )
    ahead = functools.partial(
        lax.ppermute, axis_name="blk", perm=route(lambda i: 2 if i % 2 else -2)
    )
    back = functools.partial(
        lax.ppermute, axis_name="blk", perm=route(lambda i: -2 if i % 2 else 2)
    )

    relay = functools.partial(
        lax.ppermute,
        axis_name="blk",
        perm=route(lambda i: -1 if i == 1 else 1 if i == nblocks - 2 else -2 if i % 2 else 2),
    )

    where = block_index[None].astype(jnp.int32)
    own_q, own_kv, swap_q, swap_kv = prepare(where, queries, keys, values)
    segs, need = survey(where, block_mask, segment_ids[None, :])
    other_kv = swap(swap_kv)
    ahead_own = ahead(own_kv)
    back_own = back(own_kv)
    other_q = swap(swap_q)
    ready, back_own, other_q = lax.optimization_barrier((other_kv, back_own, other_q))
    back_other = relay(ready)
    ahead_both = ahead(stack(other_kv, ahead_own))
    near = (own_kv, other_kv, ahead_own, back_own)
    near_numbers = (0, 1, 2, 3)
    fixed = (where, need, segs)
    own = attention(*fixed, (own_q,), (0,), near, near_numbers, None, False)
    back_other, own = lax.optimization_barrier((back_other, own))
    back_far = relay(back_other)
    other = attention(*fixed, (other_q,), (1,), near, near_numbers, None, False)
    far = (ahead_both, back_other)
    other = attention(*fixed, (other_q,), (1,), far, (4, 6, 5), other, True)
    other = swap(other)
    far = (ahead_both, back_other, back_far)
    own = attention(*fixed, (own_q,), (0,), far, (4, 6, 5, 7), own, True)

    order = tuple(range(nblocks)) if nblocks in (4, 8) else (0,)
    outgoing = project(
        where, owners[None, :], offsets[None, :], own, other, out_weight, tokens,
        order, slots, pair_rows,
    )
    if len(order) > 1:
        arrived = list(outgoing)

        def cross(d):
            arrived[d] = lax.ppermute(arrived[d], "blk", [(i, i ^ d) for i in range(nblocks)])

        short, *late = range(nblocks // 2 - 1, 0, -1)
        for d in (*range(nblocks // 2, nblocks), short):
            cross(d)
        group = lax.optimization_barrier([arrived[d] for d in (short, *late)])
        for d, block in zip((short, *late), group):
            arrived[d] = block
        for d in late:
            cross(d)
    else:
        arrived = [lax.all_to_all(outgoing[0], "blk", split_axis=0, concat_axis=0, tiled=True)]
    return place(arrived, capacity, 4 * width)


def solution(mesh):
    placed = (
        P("rep"),
        P("rep", None),
        P(("rep", "blk"), None),
        P(("rep", "blk"), None),
        P(("rep", "blk"), None),
        P(("rep", "blk"), None),
        P(),
        P(("rep", "blk")),
        P(("rep", "blk")),
    )
    return jax.shard_map(
        per_device, mesh=mesh, in_specs=placed, out_specs=P(("rep", "blk"), None), check_vma=False
    )
```

```python
import functools

import jax
import jax.numpy as jnp
from jax import lax
from jax.experimental import pallas as pl
from jax.experimental.pallas import tpu as pltpu
from jax.sharding import PartitionSpec as P

HEADS = 8
HALF = HEADS // 2
SPAN = 3
NEG = -1e30
LOG2E = 1.4426950408889634
MIB = 1024 * 1024


def vmem():
    return pl.BlockSpec(memory_space=pltpu.VMEM)


def smem():
    return pl.BlockSpec(memory_space=pltpu.SMEM)


def anywhere():
    return pl.BlockSpec(memory_space=pl.ANY)


def limit(mib):
    return pltpu.CompilerParams(vmem_limit_bytes=mib * MIB)


PLACES = ((3, 1), (4, -1), (5, -3), (1, 5), (6, -5), (2, 3), (7, -7), (0, 7))


def asking(me, kind):
    return me if kind == 0 else me + 1 - 2 * (me % 2)


def key_block(me, number):
    half = me % 2
    return me - half - SPAN + PLACES[number][0] + PLACES[number][1] * half


def prepare_kernel(where_ref, q_hbm, k_hbm, v_hbm, own_q, own_kv, swap_q, swap_kv, held, turned, sems):
    part = q_hbm.shape[1] // 2
    loads = [
        pltpu.make_async_copy(ref, held.at[i], sems.at[i])
        for i, ref in enumerate((k_hbm, v_hbm, q_hbm))
    ]
    for load in loads:
        load.start()
    me = where_ref[0]
    half = me % 2
    mine = pl.multiple_of(half * part, 16)
    other = pl.multiple_of((1 - half) * part, 16)
    for i in range(3):
        loads[i].wait()
        turned[i] = held[i].T
        if i < 2:
            own_kv[i * part : (i + 1) * part, :] = turned[i, pl.ds(mine, part), :]
            swap_kv[i * part : (i + 1) * part, :] = turned[i, pl.ds(other, part), :]
        else:
            own_q[...] = turned[i, pl.ds(mine, part), :]
            swap_q[...] = turned[i, pl.ds(other, part), :]


def prepare(where, queries, keys, values):
    rows, features = queries.shape
    part = features // 2
    single = jax.ShapeDtypeStruct((part, rows), queries.dtype)
    double = jax.ShapeDtypeStruct((2 * part, rows), queries.dtype)
    return pl.pallas_call(
        prepare_kernel,
        out_shape=[single, double, single, double],
        in_specs=[smem()] + [anywhere()] * 3,
        out_specs=[vmem()] * 4,
        scratch_shapes=[
            pltpu.VMEM((3, rows, features), queries.dtype),
            pltpu.VMEM((3, features, rows), queries.dtype),
            pltpu.SemaphoreType.DMA((3,)),
        ],
        compiler_params=limit(53),
    )(where, queries, keys, values)


def survey_kernel(where_ref, mask_ref, segs_ref, seg_out, need_out):
    seg_out[...] = segs_ref[...].astype(jnp.float32)
    me = where_ref[0]
    nblocks = mask_ref.shape[0]
    bits = jnp.int32(0)
    for kind in range(2):
        asker = asking(me, kind)
        for number in range(len(PLACES)):
            block = key_block(me, number)
            inside = (block >= 0) & (block < nblocks) & (jnp.abs(block - asker) <= SPAN)
            allowed = mask_ref[asker, jnp.clip(block, 0, nblocks - 1)] > 0
            bits += (inside & allowed).astype(jnp.int32) << (kind * len(PLACES) + number)
    need_out[...] = jnp.full(need_out.shape, bits, jnp.int32)


def survey(where, mask, segs):
    return pl.pallas_call(
        survey_kernel,
        out_shape=[
            jax.ShapeDtypeStruct(segs.shape, jnp.float32),
            jax.ShapeDtypeStruct((8, 128), jnp.int32),
        ],
        in_specs=[smem()] * 2 + [vmem()],
        out_specs=[vmem()] * 2,
        compiler_params=limit(16),
    )(where, mask, segs)


def attention_kernel(kinds, numbers, rows_of, follows, ends, where_ref, need_ref, seg_ref, *refs):
    queries, refs = refs[: len(kinds)], refs[len(kinds) :]
    arrays = max(array for array, _ in rows_of) + 1
    blocks, refs = refs[:arrays], refs[arrays:]
    if follows:
        before, refs = refs[0], refs[1:]
    out_ref, query_s, key_s, value_s, chosen_s = refs
    part, rows = queries[0].shape
    hdim = part // HALF
    wide = value_s.shape[2]
    nblocks = seg_ref.shape[1] // rows
    factor = LOG2E / (hdim**0.5)
    me = where_ref[0]
    column = [key_block(me, b) for b in numbers]
    asker = [asking(me, kind) for kind in kinds]
    bits = jnp.max(need_ref[...])
    need = [[(bits >> (kind * len(PLACES) + b)) & 1 for b in numbers] for kind in kinds]

    def segment(block):
        start = pl.multiple_of(jnp.clip(block, 0, nblocks - 1) * rows, 128)
        return seg_ref[:, pl.ds(start, rows)]

    for b in range(len(numbers)):
        wanted = need[0][b]
        for n in range(1, len(kinds)):
            wanted = wanted + need[n][b]

        @pl.when(wanted > 0)
        def _(b=b):
            array, first = rows_of[b]
            key_s[b] = blocks[array][first : first + part, :]
            for h in range(HALF):
                start = first + part + h * hdim
                value_s[b, h, :hdim, :] = blocks[array][start : start + hdim, :]
                value_s[b, h, hdim:, :] = jnp.ones((wide - hdim, rows), jnp.bfloat16)

    for n in range(len(kinds)):
        size = 0
        for b in range(len(numbers)):
            chosen_s[size] = b
            size = size + need[n][b]
        for h in range(HALF):
            query_s[h] = queries[n][h * hdim : (h + 1) * hdim, :].T
        query_seg = jnp.broadcast_to(segment(asker[n]), (128, rows)).T
        query_seg = jnp.concatenate([query_seg] * (rows // 128), axis=1)

        def finish(h, peak, accum, n=n):
            if ends:
                turned = accum.T
                lines = slice(h * hdim, (h + 1) * hdim)
                out_ref[lines, :] = (turned[:hdim] / turned[hdim : hdim + 1]).astype(out_ref.dtype)
            else:
                peak = jnp.broadcast_to(peak, (rows, 128 - wide))
                out_ref[n, h] = jnp.concatenate([accum, peak], axis=1)

        if follows:

            @pl.when(size == 0)
            def _():
                for h in range(HALF):
                    state = before[0, h]
                    finish(h, state[:, wide : wide + 1], state[:, :wide])

        for fixed in range(1, len(numbers) + 1):

            @pl.when(size == fixed)
            def _():
                picked = [chosen_s[b] for b in range(fixed)]
                key_segs = [
                    segment(sum(jnp.where(b == i, column[i], 0) for i in range(len(numbers))))
                    for b in picked
                ]

                def one_head(h):
                    lines = slice(h * hdim, (h + 1) * hdim)
                    query = query_s[h]
                    scores = []
                    for b, key_seg in zip(picked, key_segs):
                        score = jnp.dot(
                            query, key_s[b, lines, :], preferred_element_type=jnp.float32
                        )
                        scores.append(jnp.where(query_seg == key_seg, score, NEG))
                    peak = functools.reduce(jnp.maximum, scores)
                    peak = jnp.max(peak, axis=1, keepdims=True)
                    accum = jnp.zeros((rows, wide), jnp.float32)
                    if follows:
                        state = before[0, h]
                        old = state[:, wide : wide + 1]
                        peak = jnp.maximum(peak, old)
                        accum = state[:, :wide] * jnp.exp2((old - peak) * factor)
                    for b, score in zip(picked, scores):
                        weights = jnp.exp2((score - peak) * factor).astype(jnp.bfloat16)
                        accum += lax.dot_general(
                            weights,
                            value_s[b, h],
                            (((1,), (1,)), ((), ())),
                            preferred_element_type=jnp.float32,
                        )
                    finish(h, peak, accum)

                for h in range(HALF):
                    one_head(h)


def attention(where, need, segs, queries, kinds, blocks, numbers, before, ends):
    part, rows = queries[0].shape
    hdim = part // HALF
    wide = hdim + 16
    follows = before is not None
    rows_of = [
        (array, first)
        for array, block in enumerate(blocks)
        for first in range(0, block.shape[0], 2 * part)
    ]
    if ends:
        out = jax.ShapeDtypeStruct((part, rows), jnp.bfloat16)
    else:
        out = jax.ShapeDtypeStruct((len(kinds), HALF, rows, 128), jnp.float32)
    return pl.pallas_call(
        functools.partial(attention_kernel, kinds, numbers, rows_of, follows, ends),
        out_shape=out,
        in_specs=[smem()] + [vmem()] * (2 + len(kinds) + len(blocks) + follows),
        out_specs=vmem(),
        scratch_shapes=[
            pltpu.VMEM((HALF, rows, hdim), jnp.bfloat16),
            pltpu.VMEM((len(numbers), part, rows), jnp.bfloat16),
            pltpu.VMEM((len(numbers), HALF, wide, rows), jnp.bfloat16),
            pltpu.SMEM((len(numbers) + 1,), jnp.int32),
        ],
        compiler_params=limit(16),
        cost_estimate=pl.CostEstimate(flops=1000, bytes_accessed=1000, transcendentals=0),
    )(where, need, segs, *queries, *blocks, *((before,) if follows else ()))


def stack_kernel(*refs):
    *parts, out_ref = refs
    first = 0
    for ref in parts:
        out_ref[first : first + ref.shape[0], :] = ref[...]
        first += ref.shape[0]


def stack(*parts):
    lines = sum(part.shape[0] for part in parts)
    return pl.pallas_call(
        stack_kernel,
        out_shape=jax.ShapeDtypeStruct((lines, parts[0].shape[1]), parts[0].dtype),
        in_specs=[vmem()] * len(parts),
        out_specs=vmem(),
        compiler_params=limit(16),
    )(*parts)


def half_of(where_ref, weight_ref, part, own):
    half = where_ref[0] % 2 if own else 1 - where_ref[0] % 2
    return weight_ref[pl.ds(pl.multiple_of(half * part, 16), part), :]


def begin_kernel(
    pair_rows, pieces, where_ref, owners_ref, offsets_ref, own_ref, weight_ref, tokens_ref,
    hidden_ref, meta_ref,
):
    rows = tokens_ref.shape[0]
    mrows = rows // 4
    owner = owners_ref[...]
    if pieces > 1:
        owner = owner ^ where_ref[0]
    owner = jnp.broadcast_to(owner.astype(jnp.float32), (mrows, mrows))
    earlier = lax.broadcasted_iota(jnp.int32, (mrows, mrows), 0)
    later = lax.broadcasted_iota(jnp.int32, (mrows, mrows), 1)
    column = jnp.sum(jnp.where(earlier == later, owner, 0.0), axis=1, keepdims=True)
    ahead = jnp.where((owner == column) & (earlier < later), 1.0, 0.0)
    slot = owner[:1] * pair_rows + jnp.sum(ahead, axis=0, keepdims=True)
    line = lax.broadcasted_iota(jnp.int32, (16, mrows), 0)
    meta = jnp.where(line == 0, slot, jnp.where(line == 1, offsets_ref[...].astype(jnp.float32), 0.0))
    row = lax.broadcasted_iota(jnp.int32, (mrows, rows), 0)
    patch = lax.broadcasted_iota(jnp.int32, (mrows, rows), 1)
    spread = jnp.where(patch // 4 == row, 1.0, 0.0).astype(jnp.bfloat16)
    meta_ref[...] = jnp.dot(
        meta.astype(jnp.bfloat16), spread, preferred_element_type=jnp.float32
    )
    hidden_ref[...] = tokens_ref[...].astype(jnp.float32) + lax.dot_general(
        own_ref[...],
        half_of(where_ref, weight_ref, own_ref.shape[0], True),
        (((0,), (0,)), ((), ())),
        preferred_element_type=jnp.float32,
    )


def begin(where, owners, offsets, own, out_weight, tokens, pieces, pair_rows):
    return pl.pallas_call(
        functools.partial(begin_kernel, pair_rows, pieces),
        out_shape=[
            jax.ShapeDtypeStruct(tokens.shape, jnp.float32),
            jax.ShapeDtypeStruct((16, tokens.shape[0]), jnp.float32),
        ],
        in_specs=[smem()] + [vmem()] * 5,
        out_specs=[vmem()] * 2,
        compiler_params=limit(24),
    )(where, owners, offsets, own, out_weight, tokens)


def project_kernel(order, where_ref, hidden_ref, meta_ref, other_ref, weight_ref, *outs):
    piece = outs[0].shape[0]
    slots = piece * len(outs)
    rows, width = hidden_ref.shape
    capacity = rows // 2
    meta = meta_ref[...]
    hidden = hidden_ref[...] + lax.dot_general(
        other_ref[...],
        half_of(where_ref, weight_ref, other_ref.shape[0], False),
        (((0,), (0,)), ((), ())),
        preferred_element_type=jnp.float32,
    )
    hidden = hidden.astype(jnp.bfloat16)
    slot = lax.broadcasted_iota(jnp.int32, (slots, rows), 0).astype(jnp.float32)
    quarter = lax.broadcasted_iota(jnp.int32, (1, rows), 1) % 4
    for j in range(4):
        mine = jnp.where(quarter == j, meta[:1], -1.0) == slot
        if j == 0:
            offset = jnp.where(mine, meta[1:2] - capacity, 0.0)
            offset = capacity + jnp.sum(offset, axis=1, keepdims=True)
            offset = jnp.broadcast_to(offset, (slots, 128)).astype(jnp.bfloat16)
            for d, out in zip(order, outs):
                out[:, 4 * width :] = offset[d * piece : (d + 1) * piece]
        pick = jnp.where(mine, 1.0, 0.0).astype(jnp.bfloat16)
        picked = jnp.dot(pick, hidden, preferred_element_type=jnp.float32).astype(jnp.bfloat16)
        for d, out in zip(order, outs):
            out[:, j * width : (j + 1) * width] = picked[d * piece : (d + 1) * piece]


def project(where, hidden, meta, other, out_weight, order, slots):
    width = hidden.shape[1]
    pieces = len(order)
    return pl.pallas_call(
        functools.partial(project_kernel, order),
        out_shape=[jax.ShapeDtypeStruct((slots // pieces, 4 * width + 128), jnp.bfloat16)] * pieces,
        in_specs=[smem()] + [vmem()] * 4,
        out_specs=[vmem()] * pieces,
        compiler_params=limit(24),
    )(where, hidden, meta, other, out_weight)


def place_kernel(*refs):
    *arrived, out_hbm, held, sems = refs
    capacity, merged = out_hbm.shape
    step = merged // 4

    def columns_of(start, size):
        return jnp.concatenate([ref[:, start : start + size] for ref in arrived], axis=0)

    offset = columns_of(merged, 128).astype(jnp.float32)[:, :1]
    row = lax.broadcasted_iota(jnp.int32, (offset.shape[0], capacity), 1).astype(jnp.float32)
    pick = jnp.where(offset == row, 1.0, 0.0).astype(jnp.bfloat16)
    stores = []
    for j in range(4):
        held[j] = lax.dot_general(
            pick,
            columns_of(j * step, step),
            (((0,), (0,)), ((), ())),
            preferred_element_type=jnp.float32,
        ).astype(jnp.bfloat16)
        columns = out_hbm.at[:, pl.ds(j * step, step)]
        stores.append(pltpu.make_async_copy(held.at[j], columns, sems.at[j]))
        stores[j].start()
    for store in stores:
        store.wait()


def place(arrived, capacity, merged):
    return pl.pallas_call(
        place_kernel,
        out_shape=jax.ShapeDtypeStruct((capacity, merged), jnp.bfloat16),
        in_specs=[vmem()] * len(arrived),
        out_specs=anywhere(),
        scratch_shapes=[
            pltpu.VMEM((4, capacity, merged // 4), jnp.bfloat16),
            pltpu.SemaphoreType.DMA((4,)),
        ],
        compiler_params=limit(24),
    )(*arrived)


def per_device(segment_ids, block_mask, queries, keys, values, tokens, out_weight, owners, offsets):
    rows = queries.shape[0]
    width = tokens.shape[1]
    nblocks = lax.axis_size("blk")
    block_index = lax.axis_index("blk")
    mrows = rows // 4
    capacity = 2 * mrows
    pair_rows = max(2, 2 * mrows // nblocks)
    slots = nblocks * pair_rows
    assert slots <= 256

    def route(step):
        return [(i, i + step(i)) for i in range(nblocks) if 0 <= i + step(i) < nblocks]

    swap = functools.partial(
        lax.ppermute, axis_name="blk", perm=route(lambda i: 1 - 2 * (i % 2))
    )
    ahead = functools.partial(
        lax.ppermute, axis_name="blk", perm=route(lambda i: 2 if i % 2 else -2)
    )
    back = functools.partial(
        lax.ppermute, axis_name="blk", perm=route(lambda i: -2 if i % 2 else 2)
    )

    relay = functools.partial(
        lax.ppermute,
        axis_name="blk",
        perm=route(lambda i: -1 if i == 1 else 1 if i == nblocks - 2 else -2 if i % 2 else 2),
    )

    where = block_index[None].astype(jnp.int32)
    own_q, own_kv, swap_q, swap_kv = prepare(where, queries, keys, values)
    segs, need = survey(where, block_mask, segment_ids[None, :])
    other_kv = swap(swap_kv)
    ahead_own = ahead(own_kv)
    back_own = back(own_kv)
    other_q = swap(swap_q)
    ready, back_own, other_q = lax.optimization_barrier((other_kv, back_own, other_q))
    back_other = relay(ready)
    ahead_both = ahead(stack(other_kv, ahead_own))
    near = (own_kv, other_kv, ahead_own, back_own)
    near_numbers = (0, 1, 2, 3)
    fixed = (where, need, segs)
    own = attention(*fixed, (own_q,), (0,), near, near_numbers, None, False)
    back_other, own = lax.optimization_barrier((back_other, own))
    back_far = relay(back_other)
    other = attention(
        *fixed, (other_q,), (1,), (*near, back_other), (*near_numbers, 5), None, False
    )
    other = attention(*fixed, (other_q,), (1,), (ahead_both,), (4, 6), other, True)
    other = swap(other)
    far = (ahead_both, back_other, back_far)
    own = attention(*fixed, (own_q,), (0,), far, (4, 6, 5, 7), own, True)

    order = tuple(range(nblocks)) if nblocks in (4, 8) else (0,)
    hidden, meta = begin(
        where, owners[None, :], offsets[None, :], own, out_weight, tokens, len(order), pair_rows
    )
    outgoing = project(where, hidden, meta, other, out_weight, order, slots)
    if len(order) > 1:
        arrived = list(outgoing)

        def cross(d):
            arrived[d] = lax.ppermute(arrived[d], "blk", [(i, i ^ d) for i in range(nblocks)])

        short, *late = range(nblocks // 2 - 1, 0, -1)
        for d in (*range(nblocks // 2, nblocks), short):
            cross(d)
        group = lax.optimization_barrier([arrived[d] for d in (short, *late)])
        for d, block in zip((short, *late), group):
            arrived[d] = block
        for d in late:
            cross(d)
    else:
        arrived = [lax.all_to_all(outgoing[0], "blk", split_axis=0, concat_axis=0, tiled=True)]
    return place(arrived, capacity, 4 * width)


def solution(mesh):
    placed = (
        P("rep"),
        P("rep", None),
        P(("rep", "blk"), None),
        P(("rep", "blk"), None),
        P(("rep", "blk"), None),
        P(("rep", "blk"), None),
        P(),
        P(("rep", "blk")),
        P(("rep", "blk")),
    )
    return jax.shard_map(
        per_device, mesh=mesh, in_specs=placed, out_specs=P(("rep", "blk"), None), check_vma=False
    )
```

```python
import functools

import jax
import jax.numpy as jnp
from jax import lax
from jax.experimental import pallas as pl
from jax.experimental.pallas import tpu as pltpu
from jax.sharding import PartitionSpec as P

HEADS = 8
HALF = HEADS // 2
SPAN = 3
NEG = -1e30
LOG2E = 1.4426950408889634
MIB = 1024 * 1024


def vmem():
    return pl.BlockSpec(memory_space=pltpu.VMEM)


def smem():
    return pl.BlockSpec(memory_space=pltpu.SMEM)


def anywhere():
    return pl.BlockSpec(memory_space=pl.ANY)


def limit(mib):
    return pltpu.CompilerParams(vmem_limit_bytes=mib * MIB)


PLACES = ((3, 1), (4, -1), (5, -3), (1, 5), (6, -5), (2, 3), (7, -7), (0, 7))


def asking(me, kind):
    return me if kind == 0 else me + 1 - 2 * (me % 2)


def key_block(me, number):
    half = me % 2
    return me - half - SPAN + PLACES[number][0] + PLACES[number][1] * half


def prepare_kernel(number, where_ref, *refs):
    sources, (own, swap, held, turned, sems) = refs[:number], refs[number:]
    part = held.shape[2] // 2
    loads = [
        pltpu.make_async_copy(ref, held.at[i], sems.at[i]) for i, ref in enumerate(sources)
    ]
    for load in loads:
        load.start()
    half = where_ref[0] % 2
    mine = pl.multiple_of(half * part, 16)
    other = pl.multiple_of((1 - half) * part, 16)
    for i in range(number):
        loads[i].wait()
        turned[i] = held[i].T
        own[i * part : (i + 1) * part, :] = turned[i, pl.ds(mine, part), :]
        swap[i * part : (i + 1) * part, :] = turned[i, pl.ds(other, part), :]


def prepare(where, *arrays):
    number = len(arrays)
    rows, features = arrays[0].shape
    out = jax.ShapeDtypeStruct((number * features // 2, rows), arrays[0].dtype)
    return pl.pallas_call(
        functools.partial(prepare_kernel, number),
        out_shape=[out] * 2,
        in_specs=[smem()] + [anywhere()] * number,
        out_specs=[vmem()] * 2,
        scratch_shapes=[
            pltpu.VMEM((number, rows, features), arrays[0].dtype),
            pltpu.VMEM((number, features, rows), arrays[0].dtype),
            pltpu.SemaphoreType.DMA((number,)),
        ],
        compiler_params=limit(53),
    )(where, *arrays)


def survey_kernel(where_ref, mask_ref, segs_ref, seg_out, need_out):
    seg_out[...] = segs_ref[...].astype(jnp.float32)
    me = where_ref[0]
    nblocks = mask_ref.shape[0]
    bits = jnp.int32(0)
    for kind in range(2):
        asker = asking(me, kind)
        for number in range(len(PLACES)):
            block = key_block(me, number)
            inside = (block >= 0) & (block < nblocks) & (jnp.abs(block - asker) <= SPAN)
            allowed = mask_ref[asker, jnp.clip(block, 0, nblocks - 1)] > 0
            bits += (inside & allowed).astype(jnp.int32) << (kind * len(PLACES) + number)
    need_out[...] = jnp.full(need_out.shape, bits, jnp.int32)


def survey(where, mask, segs):
    return pl.pallas_call(
        survey_kernel,
        out_shape=[
            jax.ShapeDtypeStruct(segs.shape, jnp.float32),
            jax.ShapeDtypeStruct((8, 128), jnp.int32),
        ],
        in_specs=[smem()] * 2 + [vmem()],
        out_specs=[vmem()] * 2,
        compiler_params=limit(16),
    )(where, mask, segs)


def attention_kernel(kinds, numbers, rows_of, follows, ends, where_ref, need_ref, seg_ref, *refs):
    queries, refs = refs[: len(kinds)], refs[len(kinds) :]
    arrays = max(array for array, _ in rows_of) + 1
    blocks, refs = refs[:arrays], refs[arrays:]
    if follows:
        (accum_b, peak_b), refs = refs[:2], refs[2:]
    if ends:
        out_ref, query_s, key_s, value_s, chosen_s = refs
    else:
        accum_ref, peak_ref, query_s, key_s, value_s, chosen_s = refs
    part, rows = queries[0].shape
    hdim = part // HALF
    wide = value_s.shape[2]
    nblocks = seg_ref.shape[1] // rows
    factor = LOG2E / (hdim**0.5)
    me = where_ref[0]
    column = [key_block(me, b) for b in numbers]
    asker = [asking(me, kind) for kind in kinds]
    bits = jnp.max(need_ref[...])
    need = [[(bits >> (kind * len(PLACES) + b)) & 1 for b in numbers] for kind in kinds]

    def segment(block):
        start = pl.multiple_of(jnp.clip(block, 0, nblocks - 1) * rows, 128)
        return seg_ref[:, pl.ds(start, rows)]

    for b in range(len(numbers)):
        wanted = need[0][b]
        for n in range(1, len(kinds)):
            wanted = wanted + need[n][b]

        @pl.when(wanted > 0)
        def _(b=b):
            array, first = rows_of[b]
            key_s[b] = blocks[array][first : first + part, :]
            for h in range(HALF):
                start = first + part + h * hdim
                value_s[b, h, :hdim, :] = blocks[array][start : start + hdim, :]
                value_s[b, h, hdim:, :] = jnp.ones((wide - hdim, rows), jnp.bfloat16)

    for n in range(len(kinds)):
        size = 0
        for b in range(len(numbers)):
            chosen_s[size] = b
            size = size + need[n][b]
        for h in range(HALF):
            query_s[h] = queries[n][h * hdim : (h + 1) * hdim, :].T
        query_seg = jnp.broadcast_to(segment(asker[n]), (128, rows)).T
        query_seg = jnp.concatenate([query_seg] * (rows // 128), axis=1)

        def finish(h, peak, accum, n=n):
            if ends:
                turned = accum.T
                lines = slice(h * hdim, (h + 1) * hdim)
                out_ref[lines, :] = (turned[:hdim] / turned[hdim : hdim + 1]).astype(out_ref.dtype)
            else:
                accum_ref[n, h] = accum
                peak_ref[n, h] = peak

        if follows:

            @pl.when(size == 0)
            def _():
                for h in range(HALF):
                    finish(h, peak_b[0, h], accum_b[0, h])

        for fixed in range(1, len(numbers) + 1):

            @pl.when(size == fixed)
            def _():
                picked = [chosen_s[b] for b in range(fixed)]
                key_segs = [
                    segment(sum(jnp.where(b == i, column[i], 0) for i in range(len(numbers))))
                    for b in picked
                ]

                def one_head(h):
                    lines = slice(h * hdim, (h + 1) * hdim)
                    query = query_s[h]
                    scores = []
                    for b, key_seg in zip(picked, key_segs):
                        score = jnp.dot(
                            query, key_s[b, lines, :], preferred_element_type=jnp.float32
                        )
                        scores.append(jnp.where(query_seg == key_seg, score, NEG))
                    peak = functools.reduce(jnp.maximum, scores)
                    peak = jnp.max(peak, axis=1, keepdims=True)
                    peak = jnp.broadcast_to(peak, (rows, wide))
                    accum = jnp.zeros((rows, wide), jnp.float32)
                    if follows:
                        old = peak_b[0, h]
                        peak = jnp.maximum(peak, old)
                        accum = accum_b[0, h] * jnp.exp2((old - peak) * factor)
                    spread = jnp.concatenate([peak] * (rows // wide), axis=1)
                    for b, score in zip(picked, scores):
                        weights = jnp.exp2((score - spread) * factor).astype(jnp.bfloat16)
                        accum += lax.dot_general(
                            weights,
                            value_s[b, h],
                            (((1,), (1,)), ((), ())),
                            preferred_element_type=jnp.float32,
                        )
                    finish(h, peak, accum)

                for h in range(HALF):
                    one_head(h)


def attention(where, need, segs, queries, kinds, blocks, numbers, before, ends):
    part, rows = queries[0].shape
    hdim = part // HALF
    wide = 128
    follows = before is not None
    rows_of = [
        (array, first)
        for array, block in enumerate(blocks)
        for first in range(0, block.shape[0], 2 * part)
    ]
    if ends:
        out = jax.ShapeDtypeStruct((part, rows), jnp.bfloat16)
    else:
        out = [jax.ShapeDtypeStruct((len(kinds), HALF, rows, wide), jnp.float32)] * 2
    return pl.pallas_call(
        functools.partial(attention_kernel, kinds, numbers, rows_of, follows, ends),
        out_shape=out,
        in_specs=[smem()] + [vmem()] * (2 + len(kinds) + len(blocks) + 2 * follows),
        out_specs=vmem() if ends else [vmem()] * 2,
        scratch_shapes=[
            pltpu.VMEM((HALF, rows, hdim), jnp.bfloat16),
            pltpu.VMEM((len(numbers), part, rows), jnp.bfloat16),
            pltpu.VMEM((len(numbers), HALF, wide, rows), jnp.bfloat16),
            pltpu.SMEM((len(numbers) + 1,), jnp.int32),
        ],
        compiler_params=limit(16),
        cost_estimate=pl.CostEstimate(flops=1000, bytes_accessed=1000, transcendentals=0),
    )(where, need, segs, *queries, *blocks, *(before or ()))


def stack_kernel(*refs):
    *parts, out_ref = refs
    first = 0
    for ref in parts:
        out_ref[first : first + ref.shape[0], :] = ref[...]
        first += ref.shape[0]


def stack(*parts):
    lines = sum(part.shape[0] for part in parts)
    return pl.pallas_call(
        stack_kernel,
        out_shape=jax.ShapeDtypeStruct((lines, parts[0].shape[1]), parts[0].dtype),
        in_specs=[vmem()] * len(parts),
        out_specs=vmem(),
        compiler_params=limit(16),
    )(*parts)


def half_of(where_ref, weight_ref, part, own):
    half = where_ref[0] % 2 if own else 1 - where_ref[0] % 2
    return weight_ref[pl.ds(pl.multiple_of(half * part, 16), part), :]


def begin_kernel(
    pair_rows, pieces, where_ref, owners_ref, offsets_ref, own_ref, weight_ref, tokens_ref,
    hidden_ref, meta_ref,
):
    rows = tokens_ref.shape[0]
    mrows = rows // 4
    owner = owners_ref[...]
    if pieces > 1:
        owner = owner ^ where_ref[0]
    owner = jnp.broadcast_to(owner.astype(jnp.float32), (mrows, mrows))
    earlier = lax.broadcasted_iota(jnp.int32, (mrows, mrows), 0)
    later = lax.broadcasted_iota(jnp.int32, (mrows, mrows), 1)
    column = jnp.sum(jnp.where(earlier == later, owner, 0.0), axis=1, keepdims=True)
    ahead = jnp.where((owner == column) & (earlier < later), 1.0, 0.0)
    slot = owner[:1] * pair_rows + jnp.sum(ahead, axis=0, keepdims=True)
    line = lax.broadcasted_iota(jnp.int32, (16, mrows), 0)
    meta = jnp.where(line == 0, slot, jnp.where(line == 1, offsets_ref[...].astype(jnp.float32), 0.0))
    row = lax.broadcasted_iota(jnp.int32, (mrows, rows), 0)
    patch = lax.broadcasted_iota(jnp.int32, (mrows, rows), 1)
    spread = jnp.where(patch // 4 == row, 1.0, 0.0).astype(jnp.bfloat16)
    meta_ref[...] = jnp.dot(
        meta.astype(jnp.bfloat16), spread, preferred_element_type=jnp.float32
    )
    hidden_ref[...] = tokens_ref[...].astype(jnp.float32) + lax.dot_general(
        own_ref[...],
        half_of(where_ref, weight_ref, own_ref.shape[0], True),
        (((0,), (0,)), ((), ())),
        preferred_element_type=jnp.float32,
    )


def begin(where, owners, offsets, own, out_weight, tokens, pieces, pair_rows):
    return pl.pallas_call(
        functools.partial(begin_kernel, pair_rows, pieces),
        out_shape=[
            jax.ShapeDtypeStruct(tokens.shape, jnp.float32),
            jax.ShapeDtypeStruct((16, tokens.shape[0]), jnp.float32),
        ],
        in_specs=[smem()] + [vmem()] * 5,
        out_specs=[vmem()] * 2,
        compiler_params=limit(24),
    )(where, owners, offsets, own, out_weight, tokens)


def project_kernel(order, where_ref, hidden_ref, meta_ref, other_ref, weight_ref, *outs):
    piece = outs[0].shape[0]
    slots = piece * len(outs)
    rows, width = hidden_ref.shape
    capacity = rows // 2
    meta = meta_ref[...]
    hidden = hidden_ref[...] + lax.dot_general(
        other_ref[...],
        half_of(where_ref, weight_ref, other_ref.shape[0], False),
        (((0,), (0,)), ((), ())),
        preferred_element_type=jnp.float32,
    )
    hidden = hidden.astype(jnp.bfloat16)
    slot = lax.broadcasted_iota(jnp.int32, (slots, rows), 0).astype(jnp.float32)
    quarter = lax.broadcasted_iota(jnp.int32, (1, rows), 1) % 4
    for j in range(4):
        mine = jnp.where(quarter == j, meta[:1], -1.0) == slot
        if j == 0:
            offset = jnp.where(mine, meta[1:2] - capacity, 0.0)
            offset = capacity + jnp.sum(offset, axis=1, keepdims=True)
            offset = jnp.broadcast_to(offset, (slots, 128)).astype(jnp.bfloat16)
            for d, out in zip(order, outs):
                out[:, 4 * width :] = offset[d * piece : (d + 1) * piece]
        pick = jnp.where(mine, 1.0, 0.0).astype(jnp.bfloat16)
        picked = jnp.dot(pick, hidden, preferred_element_type=jnp.float32).astype(jnp.bfloat16)
        for d, out in zip(order, outs):
            out[:, j * width : (j + 1) * width] = picked[d * piece : (d + 1) * piece]


def project(where, hidden, meta, other, out_weight, order, slots):
    width = hidden.shape[1]
    pieces = len(order)
    return pl.pallas_call(
        functools.partial(project_kernel, order),
        out_shape=[jax.ShapeDtypeStruct((slots // pieces, 4 * width + 128), jnp.bfloat16)] * pieces,
        in_specs=[smem()] + [vmem()] * 4,
        out_specs=[vmem()] * pieces,
        compiler_params=limit(24),
    )(where, hidden, meta, other, out_weight)


def place_kernel(*refs):
    *arrived, out_hbm, held, sems = refs
    capacity, merged = out_hbm.shape
    step = merged // 4

    def columns_of(start, size):
        return jnp.concatenate([ref[:, start : start + size] for ref in arrived], axis=0)

    offset = columns_of(merged, 128).astype(jnp.float32)[:, :1]
    row = lax.broadcasted_iota(jnp.int32, (offset.shape[0], capacity), 1).astype(jnp.float32)
    pick = jnp.where(offset == row, 1.0, 0.0).astype(jnp.bfloat16)
    stores = []
    for j in range(4):
        held[j] = lax.dot_general(
            pick,
            columns_of(j * step, step),
            (((0,), (0,)), ((), ())),
            preferred_element_type=jnp.float32,
        ).astype(jnp.bfloat16)
        columns = out_hbm.at[:, pl.ds(j * step, step)]
        stores.append(pltpu.make_async_copy(held.at[j], columns, sems.at[j]))
        stores[j].start()
    for store in stores:
        store.wait()


def place(arrived, capacity, merged):
    return pl.pallas_call(
        place_kernel,
        out_shape=jax.ShapeDtypeStruct((capacity, merged), jnp.bfloat16),
        in_specs=[vmem()] * len(arrived),
        out_specs=anywhere(),
        scratch_shapes=[
            pltpu.VMEM((4, capacity, merged // 4), jnp.bfloat16),
            pltpu.SemaphoreType.DMA((4,)),
        ],
        compiler_params=limit(24),
    )(*arrived)


def per_device(segment_ids, block_mask, queries, keys, values, tokens, out_weight, owners, offsets):
    rows = queries.shape[0]
    width = tokens.shape[1]
    nblocks = lax.axis_size("blk")
    block_index = lax.axis_index("blk")
    mrows = rows // 4
    capacity = 2 * mrows
    pair_rows = max(2, 2 * mrows // nblocks)
    slots = nblocks * pair_rows
    assert slots <= 256

    def route(step):
        return [(i, i + step(i)) for i in range(nblocks) if 0 <= i + step(i) < nblocks]

    swap = functools.partial(
        lax.ppermute, axis_name="blk", perm=route(lambda i: 1 - 2 * (i % 2))
    )
    ahead = functools.partial(
        lax.ppermute, axis_name="blk", perm=route(lambda i: 2 if i % 2 else -2)
    )
    back = functools.partial(
        lax.ppermute, axis_name="blk", perm=route(lambda i: -2 if i % 2 else 2)
    )

    relay = functools.partial(
        lax.ppermute,
        axis_name="blk",
        perm=route(lambda i: -1 if i == 1 else 1 if i == nblocks - 2 else -2 if i % 2 else 2),
    )

    where = block_index[None].astype(jnp.int32)
    own_kv, swap_kv = prepare(where, keys, values)
    queries, own_kv, swap_kv = lax.optimization_barrier((queries, own_kv, swap_kv))
    own_q, swap_q = prepare(where, queries)
    segs, need = survey(where, block_mask, segment_ids[None, :])
    other_kv = swap(swap_kv)
    ahead_own = ahead(own_kv)
    back_own = back(own_kv)
    other_q = swap(swap_q)
    ready, back_own, other_q = lax.optimization_barrier((other_kv, back_own, other_q))
    back_other = relay(ready)
    ahead_both = ahead(stack(other_kv, ahead_own))
    near = (own_kv, other_kv, ahead_own, back_own)
    near_numbers = (0, 1, 2, 3)
    fixed = (where, need, segs)
    own = attention(*fixed, (own_q,), (0,), near, near_numbers, None, False)
    back_other, own = lax.optimization_barrier((back_other, own))
    back_far = relay(back_other)
    other = attention(
        *fixed, (other_q,), (1,), (*near, back_other), (*near_numbers, 5), None, False
    )
    other = attention(*fixed, (other_q,), (1,), (ahead_both,), (4, 6), other, True)
    other = swap(other)
    far = (ahead_both, back_other, back_far)
    own = attention(*fixed, (own_q,), (0,), far, (4, 6, 5, 7), own, True)

    order = tuple(range(nblocks)) if nblocks in (4, 8) else (0,)
    hidden, meta = begin(
        where, owners[None, :], offsets[None, :], own, out_weight, tokens, len(order), pair_rows
    )
    outgoing = project(where, hidden, meta, other, out_weight, order, slots)
    if len(order) > 1:
        arrived = list(outgoing)

        def cross(d):
            arrived[d] = lax.ppermute(arrived[d], "blk", [(i, i ^ d) for i in range(nblocks)])

        short, *late = range(nblocks // 2 - 1, 0, -1)
        for d in (*range(nblocks // 2, nblocks), short):
            cross(d)
        group = lax.optimization_barrier([arrived[d] for d in (short, *late)])
        for d, block in zip((short, *late), group):
            arrived[d] = block
        for d in late:
            cross(d)
    else:
        arrived = [lax.all_to_all(outgoing[0], "blk", split_axis=0, concat_axis=0, tiled=True)]
    return place(arrived, capacity, 4 * width)


def solution(mesh):
    placed = (
        P("rep"),
        P("rep", None),
        P(("rep", "blk"), None),
        P(("rep", "blk"), None),
        P(("rep", "blk"), None),
        P(("rep", "blk"), None),
        P(),
        P(("rep", "blk")),
        P(("rep", "blk")),
    )
    return jax.shard_map(
        per_device, mesh=mesh, in_specs=placed, out_specs=P(("rep", "blk"), None), check_vma=False
    )
```

```python
import functools

import jax
import jax.numpy as jnp
from jax import lax
from jax.experimental import pallas as pl
from jax.experimental.pallas import tpu as pltpu
from jax.sharding import PartitionSpec as P

HEADS = 8
HALF = HEADS // 2
SPAN = 3
NEG = -1e30
LOG2E = 1.4426950408889634
MIB = 1024 * 1024


def vmem():
    return pl.BlockSpec(memory_space=pltpu.VMEM)


def smem():
    return pl.BlockSpec(memory_space=pltpu.SMEM)


def anywhere():
    return pl.BlockSpec(memory_space=pl.ANY)


def limit(mib):
    return pltpu.CompilerParams(vmem_limit_bytes=mib * MIB)


PLACES = ((3, 1), (4, -1), (5, -3), (1, 5), (6, -5), (2, 3), (7, -7), (0, 7))


def asking(me, kind):
    return me if kind == 0 else me + 1 - 2 * (me % 2)


def key_block(me, number):
    half = me % 2
    return me - half - SPAN + PLACES[number][0] + PLACES[number][1] * half


def prepare_kernel(number, where_ref, *refs):
    sources, (own, swap, held, turned, sems) = refs[:number], refs[number:]
    part = held.shape[2] // 2
    loads = [
        pltpu.make_async_copy(ref, held.at[i], sems.at[i]) for i, ref in enumerate(sources)
    ]
    for load in loads:
        load.start()
    half = where_ref[0] % 2
    mine = pl.multiple_of(half * part, 16)
    other = pl.multiple_of((1 - half) * part, 16)
    for i in range(number):
        loads[i].wait()
        turned[i] = held[i].T
        own[i * part : (i + 1) * part, :] = turned[i, pl.ds(mine, part), :]
        swap[i * part : (i + 1) * part, :] = turned[i, pl.ds(other, part), :]


def prepare(where, *arrays):
    number = len(arrays)
    rows, features = arrays[0].shape
    out = jax.ShapeDtypeStruct((number * features // 2, rows), arrays[0].dtype)
    return pl.pallas_call(
        functools.partial(prepare_kernel, number),
        out_shape=[out] * 2,
        in_specs=[smem()] + [anywhere()] * number,
        out_specs=[vmem()] * 2,
        scratch_shapes=[
            pltpu.VMEM((number, rows, features), arrays[0].dtype),
            pltpu.VMEM((number, features, rows), arrays[0].dtype),
            pltpu.SemaphoreType.DMA((number,)),
        ],
        compiler_params=limit(53),
    )(where, *arrays)


def survey_kernel(where_ref, mask_ref, segs_ref, seg_out, need_out):
    seg_out[...] = segs_ref[...].astype(jnp.float32)
    me = where_ref[0]
    nblocks = mask_ref.shape[0]
    bits = jnp.int32(0)
    for kind in range(2):
        asker = asking(me, kind)
        for number in range(len(PLACES)):
            block = key_block(me, number)
            inside = (block >= 0) & (block < nblocks) & (jnp.abs(block - asker) <= SPAN)
            allowed = mask_ref[asker, jnp.clip(block, 0, nblocks - 1)] > 0
            bits += (inside & allowed).astype(jnp.int32) << (kind * len(PLACES) + number)
    need_out[...] = jnp.full(need_out.shape, bits, jnp.int32)


def survey(where, mask, segs):
    return pl.pallas_call(
        survey_kernel,
        out_shape=[
            jax.ShapeDtypeStruct(segs.shape, jnp.float32),
            jax.ShapeDtypeStruct((8, 128), jnp.int32),
        ],
        in_specs=[smem()] * 2 + [vmem()],
        out_specs=[vmem()] * 2,
        compiler_params=limit(16),
    )(where, mask, segs)


def attention_kernel(kinds, numbers, rows_of, follows, ends, where_ref, need_ref, seg_ref, *refs):
    queries, refs = refs[: len(kinds)], refs[len(kinds) :]
    arrays = max(array for array, _ in rows_of) + 1
    blocks, refs = refs[:arrays], refs[arrays:]
    if follows:
        (accum_b, peak_b), refs = refs[:2], refs[2:]
    if ends:
        out_ref, query_s, key_s, value_s, chosen_s = refs
    else:
        accum_ref, peak_ref, query_s, key_s, value_s, chosen_s = refs
    part, rows = queries[0].shape
    hdim = part // HALF
    wide = value_s.shape[2]
    nblocks = seg_ref.shape[1] // rows
    factor = LOG2E / (hdim**0.5)
    me = where_ref[0]
    column = [key_block(me, b) for b in numbers]
    asker = [asking(me, kind) for kind in kinds]
    bits = jnp.max(need_ref[...])
    need = [[(bits >> (kind * len(PLACES) + b)) & 1 for b in numbers] for kind in kinds]

    def segment(block):
        start = pl.multiple_of(jnp.clip(block, 0, nblocks - 1) * rows, 128)
        return seg_ref[:, pl.ds(start, rows)]

    for b in range(len(numbers)):
        wanted = need[0][b]
        for n in range(1, len(kinds)):
            wanted = wanted + need[n][b]

        @pl.when(wanted > 0)
        def _(b=b):
            array, first = rows_of[b]
            key_s[b] = blocks[array][first : first + part, :]
            for h in range(HALF):
                start = first + part + h * hdim
                value_s[b, h, :hdim, :] = blocks[array][start : start + hdim, :]
                value_s[b, h, hdim:, :] = jnp.ones((wide - hdim, rows), jnp.bfloat16)

    for n in range(len(kinds)):
        size = 0
        for b in range(len(numbers)):
            chosen_s[size] = b
            size = size + need[n][b]
        for h in range(HALF):
            query_s[h] = queries[n][h * hdim : (h + 1) * hdim, :].T
        query_seg = jnp.broadcast_to(segment(asker[n]), (128, rows)).T
        query_seg = jnp.concatenate([query_seg] * (rows // 128), axis=1)

        def finish(h, peak, accum, n=n):
            if ends:
                turned = accum.T
                lines = slice(h * hdim, (h + 1) * hdim)
                out_ref[lines, :] = (turned[:hdim] / turned[hdim : hdim + 1]).astype(out_ref.dtype)
            else:
                accum_ref[n, h] = accum
                peak_ref[n, h] = peak

        if follows:

            @pl.when(size == 0)
            def _():
                for h in range(HALF):
                    finish(h, peak_b[0, h], accum_b[0, h])

        for fixed in range(1, len(numbers) + 1):

            @pl.when(size == fixed)
            def _():
                picked = [chosen_s[b] for b in range(fixed)]
                key_segs = [
                    segment(sum(jnp.where(b == i, column[i], 0) for i in range(len(numbers))))
                    for b in picked
                ]

                def one_head(h):
                    lines = slice(h * hdim, (h + 1) * hdim)
                    query = query_s[h]
                    scores = []
                    for b, key_seg in zip(picked, key_segs):
                        score = jnp.dot(
                            query, key_s[b, lines, :], preferred_element_type=jnp.float32
                        )
                        scores.append(jnp.where(query_seg == key_seg, score, NEG))
                    peak = functools.reduce(jnp.maximum, scores)
                    peak = jnp.max(peak, axis=1, keepdims=True)
                    peak = jnp.broadcast_to(peak, (rows, wide))
                    accum = jnp.zeros((rows, wide), jnp.float32)
                    if follows:
                        old = peak_b[0, h]
                        peak = jnp.maximum(peak, old)
                        accum = accum_b[0, h] * jnp.exp2((old - peak) * factor)
                    spread = jnp.concatenate([peak] * (rows // wide), axis=1)
                    for b, score in zip(picked, scores):
                        weights = jnp.exp2((score - spread) * factor).astype(jnp.bfloat16)
                        accum += lax.dot_general(
                            weights,
                            value_s[b, h],
                            (((1,), (1,)), ((), ())),
                            preferred_element_type=jnp.float32,
                        )
                    finish(h, peak, accum)

                for h in range(HALF):
                    one_head(h)


def attention(where, need, segs, queries, kinds, blocks, numbers, before, ends):
    part, rows = queries[0].shape
    hdim = part // HALF
    wide = 128
    follows = before is not None
    rows_of = [
        (array, first)
        for array, block in enumerate(blocks)
        for first in range(0, block.shape[0], 2 * part)
    ]
    if ends:
        out = jax.ShapeDtypeStruct((part, rows), jnp.bfloat16)
    else:
        out = [jax.ShapeDtypeStruct((len(kinds), HALF, rows, wide), jnp.float32)] * 2
    return pl.pallas_call(
        functools.partial(attention_kernel, kinds, numbers, rows_of, follows, ends),
        out_shape=out,
        in_specs=[smem()] + [vmem()] * (2 + len(kinds) + len(blocks) + 2 * follows),
        out_specs=vmem() if ends else [vmem()] * 2,
        scratch_shapes=[
            pltpu.VMEM((HALF, rows, hdim), jnp.bfloat16),
            pltpu.VMEM((len(numbers), part, rows), jnp.bfloat16),
            pltpu.VMEM((len(numbers), HALF, wide, rows), jnp.bfloat16),
            pltpu.SMEM((len(numbers) + 1,), jnp.int32),
        ],
        compiler_params=limit(16),
        cost_estimate=pl.CostEstimate(flops=1000, bytes_accessed=1000, transcendentals=0),
    )(where, need, segs, *queries, *blocks, *(before or ()))


def stack_kernel(*refs):
    *parts, out_ref = refs
    first = 0
    for ref in parts:
        out_ref[first : first + ref.shape[0], :] = ref[...]
        first += ref.shape[0]


def stack(*parts):
    lines = sum(part.shape[0] for part in parts)
    return pl.pallas_call(
        stack_kernel,
        out_shape=jax.ShapeDtypeStruct((lines, parts[0].shape[1]), parts[0].dtype),
        in_specs=[vmem()] * len(parts),
        out_specs=vmem(),
        compiler_params=limit(16),
    )(*parts)


def half_of(where_ref, weight_ref, part, own):
    half = where_ref[0] % 2 if own else 1 - where_ref[0] % 2
    return weight_ref[pl.ds(pl.multiple_of(half * part, 16), part), :]


def begin_kernel(
    pair_rows, pieces, where_ref, owners_ref, offsets_ref, own_ref, weight_ref, tokens_ref,
    hidden_ref, meta_ref,
):
    rows = tokens_ref.shape[0]
    mrows = rows // 4
    owner = owners_ref[...]
    if pieces > 1:
        owner = owner ^ where_ref[0]
    owner = jnp.broadcast_to(owner.astype(jnp.float32), (mrows, mrows))
    earlier = lax.broadcasted_iota(jnp.int32, (mrows, mrows), 0)
    later = lax.broadcasted_iota(jnp.int32, (mrows, mrows), 1)
    column = jnp.sum(jnp.where(earlier == later, owner, 0.0), axis=1, keepdims=True)
    ahead = jnp.where((owner == column) & (earlier < later), 1.0, 0.0)
    slot = owner[:1] * pair_rows + jnp.sum(ahead, axis=0, keepdims=True)
    line = lax.broadcasted_iota(jnp.int32, (16, mrows), 0)
    meta = jnp.where(line == 0, slot, jnp.where(line == 1, offsets_ref[...].astype(jnp.float32), 0.0))
    row = lax.broadcasted_iota(jnp.int32, (mrows, rows), 0)
    patch = lax.broadcasted_iota(jnp.int32, (mrows, rows), 1)
    spread = jnp.where(patch // 4 == row, 1.0, 0.0).astype(jnp.bfloat16)
    meta_ref[...] = jnp.dot(
        meta.astype(jnp.bfloat16), spread, preferred_element_type=jnp.float32
    )
    hidden_ref[...] = tokens_ref[...].astype(jnp.float32) + lax.dot_general(
        own_ref[...],
        half_of(where_ref, weight_ref, own_ref.shape[0], True),
        (((0,), (0,)), ((), ())),
        preferred_element_type=jnp.float32,
    )


def begin(where, owners, offsets, own, out_weight, tokens, pieces, pair_rows):
    return pl.pallas_call(
        functools.partial(begin_kernel, pair_rows, pieces),
        out_shape=[
            jax.ShapeDtypeStruct(tokens.shape, jnp.float32),
            jax.ShapeDtypeStruct((16, tokens.shape[0]), jnp.float32),
        ],
        in_specs=[smem()] + [vmem()] * 5,
        out_specs=[vmem()] * 2,
        compiler_params=limit(24),
    )(where, owners, offsets, own, out_weight, tokens)


def project_kernel(order, where_ref, hidden_ref, meta_ref, other_ref, weight_ref, *outs):
    piece = outs[0].shape[0]
    slots = piece * len(outs)
    first = piece * order[0]
    rows, width = hidden_ref.shape
    capacity = rows // 2
    meta = meta_ref[...]
    hidden = hidden_ref[...] + lax.dot_general(
        other_ref[...],
        half_of(where_ref, weight_ref, other_ref.shape[0], False),
        (((0,), (0,)), ((), ())),
        preferred_element_type=jnp.float32,
    )
    hidden = hidden.astype(jnp.bfloat16)
    slot = first + lax.broadcasted_iota(jnp.int32, (slots, rows), 0).astype(jnp.float32)
    quarter = lax.broadcasted_iota(jnp.int32, (1, rows), 1) % 4
    for j in range(4):
        mine = jnp.where(quarter == j, meta[:1], -1.0) == slot
        if j == 0:
            offset = jnp.where(mine, meta[1:2] - capacity, 0.0)
            offset = capacity + jnp.sum(offset, axis=1, keepdims=True)
            offset = jnp.broadcast_to(offset, (slots, 128)).astype(jnp.bfloat16)
            for d, out in enumerate(outs):
                out[:, 4 * width :] = offset[d * piece : (d + 1) * piece]
        pick = jnp.where(mine, 1.0, 0.0).astype(jnp.bfloat16)
        picked = jnp.dot(pick, hidden, preferred_element_type=jnp.float32).astype(jnp.bfloat16)
        for d, out in enumerate(outs):
            out[:, j * width : (j + 1) * width] = picked[d * piece : (d + 1) * piece]


def project(where, hidden, meta, other, out_weight, order, rows):
    width = hidden.shape[1]
    return pl.pallas_call(
        functools.partial(project_kernel, order),
        out_shape=[jax.ShapeDtypeStruct((rows, 4 * width + 128), jnp.bfloat16)] * len(order),
        in_specs=[smem()] + [vmem()] * 4,
        out_specs=[vmem()] * len(order),
        compiler_params=limit(24),
    )(where, hidden, meta, other, out_weight)


def place_kernel(*refs):
    *arrived, out_hbm, held, sems = refs
    capacity, merged = out_hbm.shape
    step = merged // 4

    def columns_of(start, size):
        return jnp.concatenate([ref[:, start : start + size] for ref in arrived], axis=0)

    offset = columns_of(merged, 128).astype(jnp.float32)[:, :1]
    row = lax.broadcasted_iota(jnp.int32, (offset.shape[0], capacity), 1).astype(jnp.float32)
    pick = jnp.where(offset == row, 1.0, 0.0).astype(jnp.bfloat16)
    stores = []
    for j in range(4):
        held[j] = lax.dot_general(
            pick,
            columns_of(j * step, step),
            (((0,), (0,)), ((), ())),
            preferred_element_type=jnp.float32,
        ).astype(jnp.bfloat16)
        columns = out_hbm.at[:, pl.ds(j * step, step)]
        stores.append(pltpu.make_async_copy(held.at[j], columns, sems.at[j]))
        stores[j].start()
    for store in stores:
        store.wait()


def place(arrived, capacity, merged):
    return pl.pallas_call(
        place_kernel,
        out_shape=jax.ShapeDtypeStruct((capacity, merged), jnp.bfloat16),
        in_specs=[vmem()] * len(arrived),
        out_specs=anywhere(),
        scratch_shapes=[
            pltpu.VMEM((4, capacity, merged // 4), jnp.bfloat16),
            pltpu.SemaphoreType.DMA((4,)),
        ],
        compiler_params=limit(24),
    )(*arrived)


def per_device(segment_ids, block_mask, queries, keys, values, tokens, out_weight, owners, offsets):
    rows = queries.shape[0]
    width = tokens.shape[1]
    nblocks = lax.axis_size("blk")
    block_index = lax.axis_index("blk")
    mrows = rows // 4
    capacity = 2 * mrows
    pair_rows = max(2, 2 * mrows // nblocks)
    slots = nblocks * pair_rows
    assert slots <= 256

    def route(step):
        return [(i, i + step(i)) for i in range(nblocks) if 0 <= i + step(i) < nblocks]

    swap = functools.partial(
        lax.ppermute, axis_name="blk", perm=route(lambda i: 1 - 2 * (i % 2))
    )
    ahead = functools.partial(
        lax.ppermute, axis_name="blk", perm=route(lambda i: 2 if i % 2 else -2)
    )
    back = functools.partial(
        lax.ppermute, axis_name="blk", perm=route(lambda i: -2 if i % 2 else 2)
    )

    relay = functools.partial(
        lax.ppermute,
        axis_name="blk",
        perm=route(lambda i: -1 if i == 1 else 1 if i == nblocks - 2 else -2 if i % 2 else 2),
    )

    where = block_index[None].astype(jnp.int32)
    own_kv, swap_kv = prepare(where, keys, values)
    queries, own_kv, swap_kv = lax.optimization_barrier((queries, own_kv, swap_kv))
    own_q, swap_q = prepare(where, queries)
    segs, need = survey(where, block_mask, segment_ids[None, :])
    other_kv = swap(swap_kv)
    ahead_own = ahead(own_kv)
    back_own = back(own_kv)
    other_q = swap(swap_q)
    ready, back_own, other_q = lax.optimization_barrier((other_kv, back_own, other_q))
    back_other = relay(ready)
    ahead_both = ahead(stack(other_kv, ahead_own))
    near = (own_kv, other_kv, ahead_own, back_own)
    near_numbers = (0, 1, 2, 3)
    fixed = (where, need, segs)
    own = attention(*fixed, (own_q,), (0,), near, near_numbers, None, False)
    back_other, own = lax.optimization_barrier((back_other, own))
    back_far = relay(back_other)
    other = attention(
        *fixed, (other_q,), (1,), (*near, back_other), (*near_numbers, 5), None, False
    )
    other = attention(*fixed, (other_q,), (1,), (ahead_both,), (4, 6), other, True)
    other = swap(other)
    far = (ahead_both, back_other, back_far)
    own = attention(*fixed, (own_q,), (0,), far, (4, 6, 5, 7), own, True)

    order = tuple(range(nblocks)) if nblocks in (4, 8) else (0,)
    hidden, meta = begin(
        where, owners[None, :], offsets[None, :], own, out_weight, tokens, len(order), pair_rows
    )
    if len(order) > 1:
        middle = nblocks // 2
        far = project(where, hidden, meta, other, out_weight, order[middle:], pair_rows)
        *far, hidden = lax.optimization_barrier((*far, hidden))
        near = project(where, hidden, meta, other, out_weight, order[:middle], pair_rows)
        arrived = [*near, *far]

        def cross(d):
            arrived[d] = lax.ppermute(arrived[d], "blk", [(i, i ^ d) for i in range(nblocks)])

        for d in (*order[middle:], middle - 1):
            cross(d)
        arrived[1:middle] = lax.optimization_barrier(arrived[1:middle])
        for d in range(1, middle - 1):
            cross(d)
    else:
        (outgoing,) = project(where, hidden, meta, other, out_weight, order, slots)
        arrived = [lax.all_to_all(outgoing, "blk", split_axis=0, concat_axis=0, tiled=True)]
    return place(arrived, capacity, 4 * width)


def solution(mesh):
    placed = (
        P("rep"),
        P("rep", None),
        P(("rep", "blk"), None),
        P(("rep", "blk"), None),
        P(("rep", "blk"), None),
        P(("rep", "blk"), None),
        P(),
        P(("rep", "blk")),
        P(("rep", "blk")),
    )
    return jax.shard_map(
        per_device, mesh=mesh, in_specs=placed, out_specs=P(("rep", "blk"), None), check_vma=False
    )
```

```python
import functools

import jax
import jax.numpy as jnp
from jax import lax
from jax.experimental import pallas as pl
from jax.experimental.pallas import tpu as pltpu
from jax.sharding import PartitionSpec as P

HEADS = 8
HALF = HEADS // 2
SPAN = 3
NEG = -1e30
LOG2E = 1.4426950408889634
MIB = 1024 * 1024


def vmem():
    return pl.BlockSpec(memory_space=pltpu.VMEM)


def smem():
    return pl.BlockSpec(memory_space=pltpu.SMEM)


def anywhere():
    return pl.BlockSpec(memory_space=pl.ANY)


def limit(mib):
    return pltpu.CompilerParams(vmem_limit_bytes=mib * MIB)


PLACES = ((3, 1), (4, -1), (5, -3), (1, 5), (6, -5), (2, 3), (7, -7), (0, 7))


def asking(me, kind):
    return me if kind == 0 else me + 1 - 2 * (me % 2)


def key_block(me, number):
    half = me % 2
    return me - half - SPAN + PLACES[number][0] + PLACES[number][1] * half


def prepare_kernel(number, where_ref, *refs):
    sources, (own, swap, held, turned, sems) = refs[:number], refs[number:]
    part = held.shape[2] // 2
    loads = [
        pltpu.make_async_copy(ref, held.at[i], sems.at[i]) for i, ref in enumerate(sources)
    ]
    for load in loads:
        load.start()
    half = where_ref[0] % 2
    mine = pl.multiple_of(half * part, 16)
    other = pl.multiple_of((1 - half) * part, 16)
    for i in range(number):
        loads[i].wait()
        turned[i] = held[i].T
        own[i * part : (i + 1) * part, :] = turned[i, pl.ds(mine, part), :]
        swap[i * part : (i + 1) * part, :] = turned[i, pl.ds(other, part), :]


def prepare(where, *arrays):
    number = len(arrays)
    rows, features = arrays[0].shape
    out = jax.ShapeDtypeStruct((number * features // 2, rows), arrays[0].dtype)
    return pl.pallas_call(
        functools.partial(prepare_kernel, number),
        out_shape=[out] * 2,
        in_specs=[smem()] + [anywhere()] * number,
        out_specs=[vmem()] * 2,
        scratch_shapes=[
            pltpu.VMEM((number, rows, features), arrays[0].dtype),
            pltpu.VMEM((number, features, rows), arrays[0].dtype),
            pltpu.SemaphoreType.DMA((number,)),
        ],
        compiler_params=limit(53),
    )(where, *arrays)


def survey_kernel(where_ref, mask_ref, segs_ref, seg_out, need_out):
    seg_out[...] = segs_ref[...].astype(jnp.float32)
    me = where_ref[0]
    nblocks = mask_ref.shape[0]
    bits = jnp.int32(0)
    for kind in range(2):
        asker = asking(me, kind)
        for number in range(len(PLACES)):
            block = key_block(me, number)
            inside = (block >= 0) & (block < nblocks) & (jnp.abs(block - asker) <= SPAN)
            allowed = mask_ref[asker, jnp.clip(block, 0, nblocks - 1)] > 0
            bits += (inside & allowed).astype(jnp.int32) << (kind * len(PLACES) + number)
    need_out[...] = jnp.full(need_out.shape, bits, jnp.int32)


def survey(where, mask, segs):
    return pl.pallas_call(
        survey_kernel,
        out_shape=[
            jax.ShapeDtypeStruct(segs.shape, jnp.float32),
            jax.ShapeDtypeStruct((8, 128), jnp.int32),
        ],
        in_specs=[smem()] * 2 + [vmem()],
        out_specs=[vmem()] * 2,
        compiler_params=limit(16),
    )(where, mask, segs)


def attention_kernel(kinds, numbers, rows_of, follows, ends, where_ref, need_ref, seg_ref, *refs):
    queries, refs = refs[: len(kinds)], refs[len(kinds) :]
    arrays = max(array for array, _ in rows_of) + 1
    blocks, refs = refs[:arrays], refs[arrays:]
    if follows:
        (accum_b, peak_b), refs = refs[:2], refs[2:]
    if ends:
        out_ref, query_s, key_s, value_s, chosen_s = refs
    else:
        accum_ref, peak_ref, query_s, key_s, value_s, chosen_s = refs
    part, rows = queries[0].shape
    hdim = part // HALF
    wide = value_s.shape[2]
    nblocks = seg_ref.shape[1] // rows
    factor = LOG2E / (hdim**0.5)
    me = where_ref[0]
    column = [key_block(me, b) for b in numbers]
    asker = [asking(me, kind) for kind in kinds]
    bits = jnp.max(need_ref[...])
    need = [[(bits >> (kind * len(PLACES) + b)) & 1 for b in numbers] for kind in kinds]

    def segment(block):
        start = pl.multiple_of(jnp.clip(block, 0, nblocks - 1) * rows, 128)
        return seg_ref[:, pl.ds(start, rows)]

    for b in range(len(numbers)):
        wanted = need[0][b]
        for n in range(1, len(kinds)):
            wanted = wanted + need[n][b]

        @pl.when(wanted > 0)
        def _(b=b):
            array, first = rows_of[b]
            key_s[b] = blocks[array][first : first + part, :]
            for h in range(HALF):
                start = first + part + h * hdim
                value_s[b, h, :hdim, :] = blocks[array][start : start + hdim, :]
                value_s[b, h, hdim:, :] = jnp.ones((wide - hdim, rows), jnp.bfloat16)

    for n in range(len(kinds)):
        size = 0
        for b in range(len(numbers)):
            chosen_s[size] = b
            size = size + need[n][b]
        for h in range(HALF):
            query_s[h] = queries[n][h * hdim : (h + 1) * hdim, :].T
        query_seg = jnp.broadcast_to(segment(asker[n]), (128, rows)).T
        query_seg = jnp.concatenate([query_seg] * (rows // 128), axis=1)

        def finish(h, peak, accum, n=n):
            if ends:
                turned = accum.T
                lines = slice(h * hdim, (h + 1) * hdim)
                out_ref[lines, :] = (turned[:hdim] / turned[hdim : hdim + 1]).astype(out_ref.dtype)
            else:
                accum_ref[n, h] = accum
                peak_ref[n, h] = peak

        if follows:

            @pl.when(size == 0)
            def _():
                for h in range(HALF):
                    finish(h, peak_b[0, h], accum_b[0, h])

        for fixed in range(1, len(numbers) + 1):

            @pl.when(size == fixed)
            def _():
                picked = [chosen_s[b] for b in range(fixed)]
                key_segs = [
                    segment(sum(jnp.where(b == i, column[i], 0) for i in range(len(numbers))))
                    for b in picked
                ]

                def one_head(h):
                    lines = slice(h * hdim, (h + 1) * hdim)
                    query = query_s[h]
                    scores = []
                    for b, key_seg in zip(picked, key_segs):
                        score = jnp.dot(
                            query, key_s[b, lines, :], preferred_element_type=jnp.float32
                        )
                        scores.append(jnp.where(query_seg == key_seg, score, NEG))
                    peak = functools.reduce(jnp.maximum, scores)
                    peak = jnp.max(peak, axis=1, keepdims=True)
                    peak = jnp.broadcast_to(peak, (rows, wide))
                    accum = jnp.zeros((rows, wide), jnp.float32)
                    if follows:
                        old = peak_b[0, h]
                        peak = jnp.maximum(peak, old)
                        accum = accum_b[0, h] * jnp.exp2((old - peak) * factor)
                    spread = jnp.concatenate([peak] * (rows // wide), axis=1)
                    for b, score in zip(picked, scores):
                        weights = jnp.exp2((score - spread) * factor).astype(jnp.bfloat16)
                        accum += lax.dot_general(
                            weights,
                            value_s[b, h],
                            (((1,), (1,)), ((), ())),
                            preferred_element_type=jnp.float32,
                        )
                    finish(h, peak, accum)

                for h in range(HALF):
                    one_head(h)


def attention(where, need, segs, queries, kinds, blocks, numbers, before, ends):
    part, rows = queries[0].shape
    hdim = part // HALF
    wide = 128
    follows = before is not None
    rows_of = [
        (array, first)
        for array, block in enumerate(blocks)
        for first in range(0, block.shape[0], 2 * part)
    ]
    if ends:
        out = jax.ShapeDtypeStruct((part, rows), jnp.bfloat16)
    else:
        out = [jax.ShapeDtypeStruct((len(kinds), HALF, rows, wide), jnp.float32)] * 2
    return pl.pallas_call(
        functools.partial(attention_kernel, kinds, numbers, rows_of, follows, ends),
        out_shape=out,
        in_specs=[smem()] + [vmem()] * (2 + len(kinds) + len(blocks) + 2 * follows),
        out_specs=vmem() if ends else [vmem()] * 2,
        scratch_shapes=[
            pltpu.VMEM((HALF, rows, hdim), jnp.bfloat16),
            pltpu.VMEM((len(numbers), part, rows), jnp.bfloat16),
            pltpu.VMEM((len(numbers), HALF, wide, rows), jnp.bfloat16),
            pltpu.SMEM((len(numbers) + 1,), jnp.int32),
        ],
        compiler_params=limit(16),
        cost_estimate=pl.CostEstimate(flops=1000, bytes_accessed=1000, transcendentals=0),
    )(where, need, segs, *queries, *blocks, *(before or ()))


def stack_kernel(*refs):
    *parts, out_ref = refs
    first = 0
    for ref in parts:
        out_ref[first : first + ref.shape[0], :] = ref[...]
        first += ref.shape[0]


def stack(*parts):
    lines = sum(part.shape[0] for part in parts)
    return pl.pallas_call(
        stack_kernel,
        out_shape=jax.ShapeDtypeStruct((lines, parts[0].shape[1]), parts[0].dtype),
        in_specs=[vmem()] * len(parts),
        out_specs=vmem(),
        compiler_params=limit(16),
    )(*parts)


def half_of(where_ref, weight_ref, part, own):
    half = where_ref[0] % 2 if own else 1 - where_ref[0] % 2
    return weight_ref[pl.ds(pl.multiple_of(half * part, 16), part), :]


def begin_kernel(
    pair_rows, few, where_ref, owners_ref, offsets_ref, own_ref, weight_ref, tokens_ref,
    hidden_ref, meta_ref,
):
    rows = tokens_ref.shape[0]
    mrows = rows // 4
    owner = owners_ref[...]
    if few:
        owner = owner ^ where_ref[0]
    owner = jnp.broadcast_to(owner.astype(jnp.float32), (mrows, mrows))
    earlier = lax.broadcasted_iota(jnp.int32, (mrows, mrows), 0)
    later = lax.broadcasted_iota(jnp.int32, (mrows, mrows), 1)
    column = jnp.sum(jnp.where(earlier == later, owner, 0.0), axis=1, keepdims=True)
    ahead = jnp.where((owner == column) & (earlier < later), 1.0, 0.0)
    slot = owner[:1] * pair_rows + jnp.sum(ahead, axis=0, keepdims=True)
    line = lax.broadcasted_iota(jnp.int32, (16, mrows), 0)
    meta = jnp.where(line == 0, slot, jnp.where(line == 1, offsets_ref[...].astype(jnp.float32), 0.0))
    row = lax.broadcasted_iota(jnp.int32, (mrows, rows), 0)
    patch = lax.broadcasted_iota(jnp.int32, (mrows, rows), 1)
    spread = jnp.where(patch // 4 == row, 1.0, 0.0).astype(jnp.bfloat16)
    meta_ref[...] = jnp.dot(
        meta.astype(jnp.bfloat16), spread, preferred_element_type=jnp.float32
    )
    hidden_ref[...] = tokens_ref[...].astype(jnp.float32) + lax.dot_general(
        own_ref[...],
        half_of(where_ref, weight_ref, own_ref.shape[0], True),
        (((0,), (0,)), ((), ())),
        preferred_element_type=jnp.float32,
    )


def begin(where, owners, offsets, own, out_weight, tokens, few, pair_rows):
    return pl.pallas_call(
        functools.partial(begin_kernel, pair_rows, few),
        out_shape=[
            jax.ShapeDtypeStruct(tokens.shape, jnp.float32),
            jax.ShapeDtypeStruct((16, tokens.shape[0]), jnp.float32),
        ],
        in_specs=[smem()] + [vmem()] * 5,
        out_specs=[vmem()] * 2,
        compiler_params=limit(24),
    )(where, owners, offsets, own, out_weight, tokens)


def share(outs, columns, block):
    first = 0
    for out in outs:
        out[:, columns] = block[first : first + out.shape[0]]
        first += out.shape[0]


def project_kernel(where_ref, hidden_ref, meta_ref, other_ref, weight_ref, *outs):
    slots = sum(out.shape[0] for out in outs)
    rows, width = hidden_ref.shape
    capacity = rows // 2
    meta = meta_ref[...]
    hidden = hidden_ref[...] + lax.dot_general(
        other_ref[...],
        half_of(where_ref, weight_ref, other_ref.shape[0], False),
        (((0,), (0,)), ((), ())),
        preferred_element_type=jnp.float32,
    )
    hidden = hidden.astype(jnp.bfloat16)
    slot = lax.broadcasted_iota(jnp.int32, (slots, rows), 0).astype(jnp.float32)
    quarter = lax.broadcasted_iota(jnp.int32, (1, rows), 1) % 4
    for j in range(4):
        mine = jnp.where(quarter == j, meta[:1], -1.0) == slot
        if j == 0:
            offset = jnp.where(mine, meta[1:2] - capacity, 0.0)
            offset = capacity + jnp.sum(offset, axis=1, keepdims=True)
            offset = jnp.broadcast_to(offset, (slots, 128)).astype(jnp.bfloat16)
            share(outs, slice(4 * width, None), offset)
        pick = jnp.where(mine, 1.0, 0.0).astype(jnp.bfloat16)
        picked = jnp.dot(pick, hidden, preferred_element_type=jnp.float32).astype(jnp.bfloat16)
        share(outs, slice(j * width, (j + 1) * width), picked)


def project(where, hidden, meta, other, out_weight, sizes):
    width = hidden.shape[1]
    return pl.pallas_call(
        project_kernel,
        out_shape=[jax.ShapeDtypeStruct((rows, 4 * width + 128), jnp.bfloat16) for rows in sizes],
        in_specs=[smem()] + [vmem()] * 4,
        out_specs=[vmem()] * len(sizes),
        compiler_params=limit(24),
    )(where, hidden, meta, other, out_weight)


def join_kernel(rows, first_ref, second_ref, out_ref):
    out_ref[:rows, :] = first_ref[...]
    out_ref[rows:, :] = second_ref[rows:, :]


def join(first, second):
    return pl.pallas_call(
        functools.partial(join_kernel, first.shape[0]),
        out_shape=jax.ShapeDtypeStruct(second.shape, second.dtype),
        in_specs=[vmem()] * 2,
        out_specs=vmem(),
        compiler_params=limit(16),
    )(first, second)


def place_kernel(kept, *refs):
    *arrived, out_hbm, held, sems = refs
    capacity, merged = out_hbm.shape
    step = merged // 4

    def columns_of(start, size):
        return jnp.concatenate(
            [ref[:rows, start : start + size] for rows, ref in zip(kept, arrived)], axis=0
        )

    offset = columns_of(merged, 128).astype(jnp.float32)[:, :1]
    row = lax.broadcasted_iota(jnp.int32, (offset.shape[0], capacity), 1).astype(jnp.float32)
    pick = jnp.where(offset == row, 1.0, 0.0).astype(jnp.bfloat16)
    stores = []
    for j in range(4):
        held[j] = lax.dot_general(
            pick,
            columns_of(j * step, step),
            (((0,), (0,)), ((), ())),
            preferred_element_type=jnp.float32,
        ).astype(jnp.bfloat16)
        columns = out_hbm.at[:, pl.ds(j * step, step)]
        stores.append(pltpu.make_async_copy(held.at[j], columns, sems.at[j]))
        stores[j].start()
    for store in stores:
        store.wait()


def place(arrived, kept, capacity, merged):
    return pl.pallas_call(
        functools.partial(place_kernel, kept),
        out_shape=jax.ShapeDtypeStruct((capacity, merged), jnp.bfloat16),
        in_specs=[vmem()] * len(arrived),
        out_specs=anywhere(),
        scratch_shapes=[
            pltpu.VMEM((4, capacity, merged // 4), jnp.bfloat16),
            pltpu.SemaphoreType.DMA((4,)),
        ],
        compiler_params=limit(24),
    )(*arrived)


def per_device(segment_ids, block_mask, queries, keys, values, tokens, out_weight, owners, offsets):
    rows = queries.shape[0]
    width = tokens.shape[1]
    nblocks = lax.axis_size("blk")
    block_index = lax.axis_index("blk")
    mrows = rows // 4
    capacity = 2 * mrows
    pair_rows = max(2, 2 * mrows // nblocks)
    slots = nblocks * pair_rows
    assert slots <= 256

    def route(step):
        return [(i, i + step(i)) for i in range(nblocks) if 0 <= i + step(i) < nblocks]

    swap = functools.partial(
        lax.ppermute, axis_name="blk", perm=route(lambda i: 1 - 2 * (i % 2))
    )
    ahead = functools.partial(
        lax.ppermute, axis_name="blk", perm=route(lambda i: 2 if i % 2 else -2)
    )
    back = functools.partial(
        lax.ppermute, axis_name="blk", perm=route(lambda i: -2 if i % 2 else 2)
    )

    relay = functools.partial(
        lax.ppermute,
        axis_name="blk",
        perm=route(lambda i: -1 if i == 1 else 1 if i == nblocks - 2 else -2 if i % 2 else 2),
    )

    where = block_index[None].astype(jnp.int32)
    own_kv, swap_kv = prepare(where, keys, values)
    queries, own_kv, swap_kv = lax.optimization_barrier((queries, own_kv, swap_kv))
    own_q, swap_q = prepare(where, queries)
    segs, need = survey(where, block_mask, segment_ids[None, :])
    other_kv = swap(swap_kv)
    ahead_own = ahead(own_kv)
    back_own = back(own_kv)
    other_q = swap(swap_q)
    ready, back_own, other_q = lax.optimization_barrier((other_kv, back_own, other_q))
    back_other = relay(ready)
    ahead_both = ahead(stack(other_kv, ahead_own))
    near = (own_kv, other_kv, ahead_own, back_own)
    near_numbers = (0, 1, 2, 3)
    fixed = (where, need, segs)
    own = attention(*fixed, (own_q,), (0,), near, near_numbers, None, False)
    back_other, own = lax.optimization_barrier((back_other, own))
    back_far = relay(back_other)
    other = attention(
        *fixed, (other_q,), (1,), (*near, back_other), (*near_numbers, 5), None, False
    )
    other = attention(*fixed, (other_q,), (1,), (ahead_both,), (4, 6), other, True)
    other = swap(other)
    far = (ahead_both, back_other, back_far)
    own = attention(*fixed, (own_q,), (0,), far, (4, 6, 5, 7), own, True)

    few = nblocks == 8
    hidden, meta = begin(
        where, owners[None, :], offsets[None, :], own, out_weight, tokens, few, pair_rows
    )
    if few:
        def cross(block, d):
            return lax.ppermute(block, "blk", [(i, i ^ d) for i in range(nblocks)])

        own, one, two, *far = project(
            where, hidden, meta, other, out_weight, [pair_rows * n for n in (1, 1, 2, 1, 1, 1, 1)]
        )
        far = [cross(block, d) for d, block in zip(range(4, 8), far)]
        two = cross(two, 2)
        one = cross(join(one, two), 1)
        arrived = [own, one, two, *far]
        kept = [pair_rows * n for n in (1, 2, 1, 1, 1, 1, 1)]
    else:
        outgoing = project(where, hidden, meta, other, out_weight, [slots])
        arrived = [lax.all_to_all(outgoing[0], "blk", split_axis=0, concat_axis=0, tiled=True)]
        kept = [slots]
    return place(arrived, kept, capacity, 4 * width)


def solution(mesh):
    placed = (
        P("rep"),
        P("rep", None),
        P(("rep", "blk"), None),
        P(("rep", "blk"), None),
        P(("rep", "blk"), None),
        P(("rep", "blk"), None),
        P(),
        P(("rep", "blk")),
        P(("rep", "blk")),
    )
    return jax.shard_map(
        per_device, mesh=mesh, in_specs=placed, out_specs=P(("rep", "blk"), None), check_vma=False
    )
```

```python
import functools

import jax
import jax.numpy as jnp
from jax import lax
from jax.experimental import pallas as pl
from jax.experimental.pallas import tpu as pltpu
from jax.sharding import PartitionSpec as P

HEADS = 8
HALF = HEADS // 2
SPAN = 3
NEG = -1e30
LOG2E = 1.4426950408889634
MIB = 1024 * 1024


def vmem():
    return pl.BlockSpec(memory_space=pltpu.VMEM)


def smem():
    return pl.BlockSpec(memory_space=pltpu.SMEM)


def anywhere():
    return pl.BlockSpec(memory_space=pl.ANY)


def limit(mib):
    return pltpu.CompilerParams(vmem_limit_bytes=mib * MIB)


PLACES = ((3, 1), (4, -1), (5, -3), (1, 5), (6, -5), (2, 3), (7, -7), (0, 7))


def asking(me, kind):
    return me if kind == 0 else me + 1 - 2 * (me % 2)


def key_block(me, number):
    half = me % 2
    return me - half - SPAN + PLACES[number][0] + PLACES[number][1] * half


def prepare_kernel(number, where_ref, *refs):
    sources, (own, swap, held, turned, sems) = refs[:number], refs[number:]
    part = held.shape[2] // 2
    loads = [
        pltpu.make_async_copy(ref, held.at[i], sems.at[i]) for i, ref in enumerate(sources)
    ]
    for load in loads:
        load.start()
    half = where_ref[0] % 2
    mine = pl.multiple_of(half * part, 16)
    other = pl.multiple_of((1 - half) * part, 16)
    for i in range(number):
        loads[i].wait()
        turned[i] = held[i].T
        own[i * part : (i + 1) * part, :] = turned[i, pl.ds(mine, part), :]
        swap[i * part : (i + 1) * part, :] = turned[i, pl.ds(other, part), :]


def prepare(where, *arrays):
    number = len(arrays)
    rows, features = arrays[0].shape
    out = jax.ShapeDtypeStruct((number * features // 2, rows), arrays[0].dtype)
    return pl.pallas_call(
        functools.partial(prepare_kernel, number),
        out_shape=[out] * 2,
        in_specs=[smem()] + [anywhere()] * number,
        out_specs=[vmem()] * 2,
        scratch_shapes=[
            pltpu.VMEM((number, rows, features), arrays[0].dtype),
            pltpu.VMEM((number, features, rows), arrays[0].dtype),
            pltpu.SemaphoreType.DMA((number,)),
        ],
        compiler_params=limit(53),
    )(where, *arrays)


def survey_kernel(where_ref, mask_ref, segs_ref, seg_out, need_out):
    seg_out[...] = segs_ref[...].astype(jnp.float32)
    me = where_ref[0]
    nblocks = mask_ref.shape[0]
    bits = jnp.int32(0)
    for kind in range(2):
        asker = asking(me, kind)
        for number in range(len(PLACES)):
            block = key_block(me, number)
            inside = (block >= 0) & (block < nblocks) & (jnp.abs(block - asker) <= SPAN)
            allowed = mask_ref[asker, jnp.clip(block, 0, nblocks - 1)] > 0
            bits += (inside & allowed).astype(jnp.int32) << (kind * len(PLACES) + number)
    need_out[...] = jnp.full(need_out.shape, bits, jnp.int32)


def survey(where, mask, segs):
    return pl.pallas_call(
        survey_kernel,
        out_shape=[
            jax.ShapeDtypeStruct(segs.shape, jnp.float32),
            jax.ShapeDtypeStruct((8, 128), jnp.int32),
        ],
        in_specs=[smem()] * 2 + [vmem()],
        out_specs=[vmem()] * 2,
        compiler_params=limit(16),
    )(where, mask, segs)


def attention_kernel(kinds, numbers, rows_of, follows, ends, where_ref, need_ref, seg_ref, *refs):
    queries, refs = refs[: len(kinds)], refs[len(kinds) :]
    arrays = max(array for array, _ in rows_of) + 1
    blocks, refs = refs[:arrays], refs[arrays:]
    if follows:
        (accum_b, peak_b), refs = refs[:2], refs[2:]
    if ends:
        out_ref, query_s, key_s, value_s, chosen_s = refs
    else:
        accum_ref, peak_ref, query_s, key_s, value_s, chosen_s = refs
    part, rows = queries[0].shape
    hdim = part // HALF
    wide = value_s.shape[2]
    nblocks = seg_ref.shape[1] // rows
    factor = LOG2E / (hdim**0.5)
    me = where_ref[0]
    column = [key_block(me, b) for b in numbers]
    asker = [asking(me, kind) for kind in kinds]
    bits = jnp.max(need_ref[...])
    need = [[(bits >> (kind * len(PLACES) + b)) & 1 for b in numbers] for kind in kinds]

    def segment(block):
        start = pl.multiple_of(jnp.clip(block, 0, nblocks - 1) * rows, 128)
        return seg_ref[:, pl.ds(start, rows)]

    for b in range(len(numbers)):
        wanted = need[0][b]
        for n in range(1, len(kinds)):
            wanted = wanted + need[n][b]

        @pl.when(wanted > 0)
        def _(b=b):
            array, first = rows_of[b]
            key_s[b] = blocks[array][first : first + part, :]
            for h in range(HALF):
                start = first + part + h * hdim
                value_s[b, h, :hdim, :] = blocks[array][start : start + hdim, :]
                value_s[b, h, hdim:, :] = jnp.ones((wide - hdim, rows), jnp.bfloat16)

    for n in range(len(kinds)):
        size = 0
        for b in range(len(numbers)):
            chosen_s[size] = b
            size = size + need[n][b]
        for h in range(HALF):
            query_s[h] = queries[n][h * hdim : (h + 1) * hdim, :].T
        query_seg = jnp.broadcast_to(segment(asker[n]), (128, rows)).T
        query_seg = jnp.concatenate([query_seg] * (rows // 128), axis=1)

        def finish(h, peak, accum, n=n):
            if ends:
                turned = accum.T
                lines = slice(h * hdim, (h + 1) * hdim)
                out_ref[lines, :] = (turned[:hdim] / turned[hdim : hdim + 1]).astype(out_ref.dtype)
            else:
                accum_ref[n, h] = accum
                peak_ref[n, h] = peak

        if follows:

            @pl.when(size == 0)
            def _():
                for h in range(HALF):
                    finish(h, peak_b[0, h], accum_b[0, h])

        for fixed in range(1, len(numbers) + 1):

            @pl.when(size == fixed)
            def _():
                picked = [chosen_s[b] for b in range(fixed)]
                key_segs = [
                    segment(sum(jnp.where(b == i, column[i], 0) for i in range(len(numbers))))
                    for b in picked
                ]

                def one_head(h):
                    lines = slice(h * hdim, (h + 1) * hdim)
                    query = query_s[h]
                    scores = []
                    for b, key_seg in zip(picked, key_segs):
                        score = jnp.dot(
                            query, key_s[b, lines, :], preferred_element_type=jnp.float32
                        )
                        scores.append(jnp.where(query_seg == key_seg, score, NEG))
                    peak = functools.reduce(jnp.maximum, scores)
                    peak = jnp.max(peak, axis=1, keepdims=True)
                    peak = jnp.broadcast_to(peak, (rows, wide))
                    accum = jnp.zeros((rows, wide), jnp.float32)
                    if follows:
                        old = peak_b[0, h]
                        peak = jnp.maximum(peak, old)
                        accum = accum_b[0, h] * jnp.exp2((old - peak) * factor)
                    spread = jnp.concatenate([peak] * (rows // wide), axis=1)
                    for b, score in zip(picked, scores):
                        weights = jnp.exp2((score - spread) * factor).astype(jnp.bfloat16)
                        accum += lax.dot_general(
                            weights,
                            value_s[b, h],
                            (((1,), (1,)), ((), ())),
                            preferred_element_type=jnp.float32,
                        )
                    finish(h, peak, accum)

                for h in range(HALF):
                    one_head(h)


def attention(where, need, segs, queries, kinds, blocks, numbers, before, ends):
    part, rows = queries[0].shape
    hdim = part // HALF
    wide = 128
    follows = before is not None
    rows_of = [
        (array, first)
        for array, block in enumerate(blocks)
        for first in range(0, block.shape[0], 2 * part)
    ]
    if ends:
        out = jax.ShapeDtypeStruct((part, rows), jnp.bfloat16)
    else:
        out = [jax.ShapeDtypeStruct((len(kinds), HALF, rows, wide), jnp.float32)] * 2
    return pl.pallas_call(
        functools.partial(attention_kernel, kinds, numbers, rows_of, follows, ends),
        out_shape=out,
        in_specs=[smem()] + [vmem()] * (2 + len(kinds) + len(blocks) + 2 * follows),
        out_specs=vmem() if ends else [vmem()] * 2,
        scratch_shapes=[
            pltpu.VMEM((HALF, rows, hdim), jnp.bfloat16),
            pltpu.VMEM((len(numbers), part, rows), jnp.bfloat16),
            pltpu.VMEM((len(numbers), HALF, wide, rows), jnp.bfloat16),
            pltpu.SMEM((len(numbers) + 1,), jnp.int32),
        ],
        compiler_params=limit(16),
        cost_estimate=pl.CostEstimate(flops=1000, bytes_accessed=1000, transcendentals=0),
    )(where, need, segs, *queries, *blocks, *(before or ()))


def stack_kernel(*refs):
    *parts, out_ref = refs
    first = 0
    for ref in parts:
        out_ref[first : first + ref.shape[0], :] = ref[...]
        first += ref.shape[0]


def stack(*parts):
    lines = sum(part.shape[0] for part in parts)
    return pl.pallas_call(
        stack_kernel,
        out_shape=jax.ShapeDtypeStruct((lines, parts[0].shape[1]), parts[0].dtype),
        in_specs=[vmem()] * len(parts),
        out_specs=vmem(),
        compiler_params=limit(16),
    )(*parts)


def half_of(where_ref, weight_ref, part, own):
    half = where_ref[0] % 2 if own else 1 - where_ref[0] % 2
    return weight_ref[pl.ds(pl.multiple_of(half * part, 16), part), :]


def begin_kernel(
    pair_rows, pieces, where_ref, owners_ref, offsets_ref, own_ref, weight_ref, tokens_ref,
    hidden_ref, meta_ref,
):
    rows = tokens_ref.shape[0]
    mrows = rows // 4
    owner = owners_ref[...]
    if pieces > 1:
        owner = owner ^ where_ref[0]
    owner = jnp.broadcast_to(owner.astype(jnp.float32), (mrows, mrows))
    earlier = lax.broadcasted_iota(jnp.int32, (mrows, mrows), 0)
    later = lax.broadcasted_iota(jnp.int32, (mrows, mrows), 1)
    column = jnp.sum(jnp.where(earlier == later, owner, 0.0), axis=1, keepdims=True)
    ahead = jnp.where((owner == column) & (earlier < later), 1.0, 0.0)
    slot = owner[:1] * pair_rows + jnp.sum(ahead, axis=0, keepdims=True)
    line = lax.broadcasted_iota(jnp.int32, (16, mrows), 0)
    meta = jnp.where(line == 0, slot, jnp.where(line == 1, offsets_ref[...].astype(jnp.float32), 0.0))
    row = lax.broadcasted_iota(jnp.int32, (mrows, rows), 0)
    patch = lax.broadcasted_iota(jnp.int32, (mrows, rows), 1)
    spread = jnp.where(patch // 4 == row, 1.0, 0.0).astype(jnp.bfloat16)
    meta_ref[...] = jnp.dot(
        meta.astype(jnp.bfloat16), spread, preferred_element_type=jnp.float32
    )
    hidden_ref[...] = tokens_ref[...].astype(jnp.float32) + lax.dot_general(
        own_ref[...],
        half_of(where_ref, weight_ref, own_ref.shape[0], True),
        (((0,), (0,)), ((), ())),
        preferred_element_type=jnp.float32,
    )


def begin(where, owners, offsets, own, out_weight, tokens, pieces, pair_rows):
    return pl.pallas_call(
        functools.partial(begin_kernel, pair_rows, pieces),
        out_shape=[
            jax.ShapeDtypeStruct(tokens.shape, jnp.float32),
            jax.ShapeDtypeStruct((16, tokens.shape[0]), jnp.float32),
        ],
        in_specs=[smem()] + [vmem()] * 5,
        out_specs=[vmem()] * 2,
        compiler_params=limit(24),
    )(where, owners, offsets, own, out_weight, tokens)


def project_kernel(order, where_ref, hidden_ref, meta_ref, other_ref, weight_ref, *outs):
    piece = outs[0].shape[0]
    slots = piece * len(outs)
    rows, width = hidden_ref.shape
    capacity = rows // 2
    meta = meta_ref[...]
    hidden = hidden_ref[...] + lax.dot_general(
        other_ref[...],
        half_of(where_ref, weight_ref, other_ref.shape[0], False),
        (((0,), (0,)), ((), ())),
        preferred_element_type=jnp.float32,
    )
    hidden = hidden.astype(jnp.bfloat16)
    slot = lax.broadcasted_iota(jnp.int32, (slots, rows), 0).astype(jnp.float32)
    quarter = lax.broadcasted_iota(jnp.int32, (1, rows), 1) % 4
    for j in range(4):
        mine = jnp.where(quarter == j, meta[:1], -1.0) == slot
        if j == 0:
            offset = jnp.where(mine, meta[1:2] - capacity, 0.0)
            offset = capacity + jnp.sum(offset, axis=1, keepdims=True)
            offset = jnp.broadcast_to(offset, (slots, 128)).astype(jnp.bfloat16)
            for d, out in zip(order, outs):
                out[:, 4 * width :] = offset[d * piece : (d + 1) * piece]
        pick = jnp.where(mine, 1.0, 0.0).astype(jnp.bfloat16)
        picked = jnp.dot(pick, hidden, preferred_element_type=jnp.float32).astype(jnp.bfloat16)
        for d, out in zip(order, outs):
            out[:, j * width : (j + 1) * width] = picked[d * piece : (d + 1) * piece]


def project(where, hidden, meta, other, out_weight, order, slots):
    width = hidden.shape[1]
    pieces = len(order)
    return pl.pallas_call(
        functools.partial(project_kernel, order),
        out_shape=[jax.ShapeDtypeStruct((slots // pieces, 4 * width + 128), jnp.bfloat16)] * pieces,
        in_specs=[smem()] + [vmem()] * 4,
        out_specs=[vmem()] * pieces,
        compiler_params=limit(24),
    )(where, hidden, meta, other, out_weight)


def place_kernel(*refs):
    *arrived, out_hbm, held, sems = refs
    capacity, merged = out_hbm.shape
    step = merged // 4

    def columns_of(start, size):
        return jnp.concatenate([ref[:, start : start + size] for ref in arrived], axis=0)

    offset = columns_of(merged, 128).astype(jnp.float32)[:, :1]
    row = lax.broadcasted_iota(jnp.int32, (offset.shape[0], capacity), 1).astype(jnp.float32)
    pick = jnp.where(offset == row, 1.0, 0.0).astype(jnp.bfloat16)
    stores = []
    for j in range(4):
        held[j] = lax.dot_general(
            pick,
            columns_of(j * step, step),
            (((0,), (0,)), ((), ())),
            preferred_element_type=jnp.float32,
        ).astype(jnp.bfloat16)
        columns = out_hbm.at[:, pl.ds(j * step, step)]
        stores.append(pltpu.make_async_copy(held.at[j], columns, sems.at[j]))
        stores[j].start()
    for store in stores:
        store.wait()


def place(arrived, capacity, merged):
    return pl.pallas_call(
        place_kernel,
        out_shape=jax.ShapeDtypeStruct((capacity, merged), jnp.bfloat16),
        in_specs=[vmem()] * len(arrived),
        out_specs=anywhere(),
        scratch_shapes=[
            pltpu.VMEM((4, capacity, merged // 4), jnp.bfloat16),
            pltpu.SemaphoreType.DMA((4,)),
        ],
        compiler_params=limit(24),
    )(*arrived)


def per_device(segment_ids, block_mask, queries, keys, values, tokens, out_weight, owners, offsets):
    rows = queries.shape[0]
    width = tokens.shape[1]
    nblocks = lax.axis_size("blk")
    block_index = lax.axis_index("blk")
    mrows = rows // 4
    capacity = 2 * mrows
    pair_rows = max(2, 2 * mrows // nblocks)
    slots = nblocks * pair_rows
    assert slots <= 256

    def route(step):
        return [(i, i + step(i)) for i in range(nblocks) if 0 <= i + step(i) < nblocks]

    swap = functools.partial(
        lax.ppermute, axis_name="blk", perm=route(lambda i: 1 - 2 * (i % 2))
    )
    ahead = functools.partial(
        lax.ppermute, axis_name="blk", perm=route(lambda i: 2 if i % 2 else -2)
    )
    back = functools.partial(
        lax.ppermute, axis_name="blk", perm=route(lambda i: -2 if i % 2 else 2)
    )

    relay = functools.partial(
        lax.ppermute,
        axis_name="blk",
        perm=route(lambda i: -1 if i == 1 else 1 if i == nblocks - 2 else -2 if i % 2 else 2),
    )
    ahead_all = functools.partial(
        lax.ppermute,
        axis_name="blk",
        perm=route(lambda i: 1 if i == 0 else -1 if i == nblocks - 1 else 2 if i % 2 else -2),
    )

    where = block_index[None].astype(jnp.int32)
    own_kv, swap_kv = prepare(where, keys, values)
    queries, own_kv, swap_kv = lax.optimization_barrier((queries, own_kv, swap_kv))
    own_q, swap_q = prepare(where, queries)
    segs, need = survey(where, block_mask, segment_ids[None, :])
    other_kv = swap(swap_kv)
    ahead_own = ahead(own_kv)
    back_own = back(own_kv)
    other_q = swap(swap_q)
    ready, back_own, other_q = lax.optimization_barrier((other_kv, back_own, other_q))
    back_other = relay(ready)
    ahead_both = ahead_all(stack(other_kv, ahead_own))
    near = (own_kv, other_kv, ahead_own, back_own)
    near_numbers = (0, 1, 2, 3)
    fixed = (where, need, segs)
    own = attention(*fixed, (own_q,), (0,), near, near_numbers, None, False)
    back_other, own = lax.optimization_barrier((back_other, own))
    back_far = relay(back_other)
    other = attention(
        *fixed, (other_q,), (1,), (*near, back_other), (*near_numbers, 5), None, False
    )
    other = attention(*fixed, (other_q,), (1,), (ahead_both,), (4, 6), other, True)
    other = swap(other)
    far = (ahead_both, back_other, back_far)
    own = attention(*fixed, (own_q,), (0,), far, (4, 6, 5, 7), own, True)

    order = tuple(range(nblocks)) if nblocks in (4, 8) else (0,)
    hidden, meta = begin(
        where, owners[None, :], offsets[None, :], own, out_weight, tokens, len(order), pair_rows
    )
    outgoing = project(where, hidden, meta, other, out_weight, order, slots)
    if len(order) > 1:
        arrived = list(outgoing)

        def cross(d):
            arrived[d] = lax.ppermute(arrived[d], "blk", [(i, i ^ d) for i in range(nblocks)])

        short, *late = range(nblocks // 2 - 1, 0, -1)
        for d in (*range(nblocks // 2, nblocks), short):
            cross(d)
        group = lax.optimization_barrier([arrived[d] for d in (short, *late)])
        for d, block in zip((short, *late), group):
            arrived[d] = block
        for d in late:
            cross(d)
    else:
        arrived = [lax.all_to_all(outgoing[0], "blk", split_axis=0, concat_axis=0, tiled=True)]
    return place(arrived, capacity, 4 * width)


def solution(mesh):
    placed = (
        P("rep"),
        P("rep", None),
        P(("rep", "blk"), None),
        P(("rep", "blk"), None),
        P(("rep", "blk"), None),
        P(("rep", "blk"), None),
        P(),
        P(("rep", "blk")),
        P(("rep", "blk")),
    )
    return jax.shard_map(
        per_device, mesh=mesh, in_specs=placed, out_specs=P(("rep", "blk"), None), check_vma=False
    )
```

```python
import functools

import jax
import jax.numpy as jnp
from jax import lax
from jax.experimental import pallas as pl
from jax.experimental.pallas import tpu as pltpu
from jax.sharding import PartitionSpec as P

HEADS = 8
HALF = HEADS // 2
SPAN = 3
NEG = -1e30
LOG2E = 1.4426950408889634
MIB = 1024 * 1024


def vmem():
    return pl.BlockSpec(memory_space=pltpu.VMEM)


def smem():
    return pl.BlockSpec(memory_space=pltpu.SMEM)


def anywhere():
    return pl.BlockSpec(memory_space=pl.ANY)


def limit(mib):
    return pltpu.CompilerParams(vmem_limit_bytes=mib * MIB)


PLACES = ((3, 1), (4, -1), (5, -3), (1, 5), (6, -5), (2, 3), (7, -7), (0, 7))


def asking(me, kind):
    return me if kind == 0 else me + 1 - 2 * (me % 2)


def key_block(me, number):
    half = me % 2
    return me - half - SPAN + PLACES[number][0] + PLACES[number][1] * half


def prepare_kernel(number, where_ref, *refs):
    sources, (own, swap, held, turned, sems) = refs[:number], refs[number:]
    part = held.shape[2] // 2
    loads = [
        pltpu.make_async_copy(ref, held.at[i], sems.at[i]) for i, ref in enumerate(sources)
    ]
    for load in loads:
        load.start()
    half = where_ref[0] % 2
    mine = pl.multiple_of(half * part, 16)
    other = pl.multiple_of((1 - half) * part, 16)
    for i in range(number):
        loads[i].wait()
        turned[i] = held[i].T
        own[i * part : (i + 1) * part, :] = turned[i, pl.ds(mine, part), :]
        swap[i * part : (i + 1) * part, :] = turned[i, pl.ds(other, part), :]


def prepare(where, *arrays):
    number = len(arrays)
    rows, features = arrays[0].shape
    out = jax.ShapeDtypeStruct((number * features // 2, rows), arrays[0].dtype)
    return pl.pallas_call(
        functools.partial(prepare_kernel, number),
        out_shape=[out] * 2,
        in_specs=[smem()] + [anywhere()] * number,
        out_specs=[vmem()] * 2,
        scratch_shapes=[
            pltpu.VMEM((number, rows, features), arrays[0].dtype),
            pltpu.VMEM((number, features, rows), arrays[0].dtype),
            pltpu.SemaphoreType.DMA((number,)),
        ],
        compiler_params=limit(53),
    )(where, *arrays)


def survey_kernel(where_ref, mask_ref, segs_ref, seg_out, need_out):
    seg_out[...] = segs_ref[...].astype(jnp.float32)
    me = where_ref[0]
    nblocks = mask_ref.shape[0]
    bits = jnp.int32(0)
    for kind in range(2):
        asker = asking(me, kind)
        for number in range(len(PLACES)):
            block = key_block(me, number)
            inside = (block >= 0) & (block < nblocks) & (jnp.abs(block - asker) <= SPAN)
            allowed = mask_ref[asker, jnp.clip(block, 0, nblocks - 1)] > 0
            bits += (inside & allowed).astype(jnp.int32) << (kind * len(PLACES) + number)
    need_out[...] = jnp.full(need_out.shape, bits, jnp.int32)


def survey(where, mask, segs):
    return pl.pallas_call(
        survey_kernel,
        out_shape=[
            jax.ShapeDtypeStruct(segs.shape, jnp.float32),
            jax.ShapeDtypeStruct((8, 128), jnp.int32),
        ],
        in_specs=[smem()] * 2 + [vmem()],
        out_specs=[vmem()] * 2,
        compiler_params=limit(16),
    )(where, mask, segs)


def attention_kernel(kinds, numbers, rows_of, follows, ends, where_ref, need_ref, seg_ref, *refs):
    queries, refs = refs[: len(kinds)], refs[len(kinds) :]
    arrays = max(array for array, _ in rows_of) + 1
    blocks, refs = refs[:arrays], refs[arrays:]
    if follows:
        (accum_b, peak_b), refs = refs[:2], refs[2:]
    if ends:
        out_ref, query_s, key_s, value_s, chosen_s = refs
    else:
        accum_ref, peak_ref, query_s, key_s, value_s, chosen_s = refs
    part, rows = queries[0].shape
    hdim = part // HALF
    wide = value_s.shape[2]
    nblocks = seg_ref.shape[1] // rows
    factor = LOG2E / (hdim**0.5)
    me = where_ref[0]
    column = [key_block(me, b) for b in numbers]
    asker = [asking(me, kind) for kind in kinds]
    bits = jnp.max(need_ref[...])
    need = [[(bits >> (kind * len(PLACES) + b)) & 1 for b in numbers] for kind in kinds]

    def segment(block):
        start = pl.multiple_of(jnp.clip(block, 0, nblocks - 1) * rows, 128)
        return seg_ref[:, pl.ds(start, rows)]

    for b in range(len(numbers)):
        wanted = need[0][b]
        for n in range(1, len(kinds)):
            wanted = wanted + need[n][b]

        @pl.when(wanted > 0)
        def _(b=b):
            array, first = rows_of[b]
            key_s[b] = blocks[array][first : first + part, :]
            for h in range(HALF):
                start = first + part + h * hdim
                value_s[b, h, :hdim, :] = blocks[array][start : start + hdim, :]
                value_s[b, h, hdim:, :] = jnp.ones((wide - hdim, rows), jnp.bfloat16)

    for n in range(len(kinds)):
        size = 0
        for b in range(len(numbers)):
            chosen_s[size] = b
            size = size + need[n][b]
        for h in range(HALF):
            query_s[h] = queries[n][h * hdim : (h + 1) * hdim, :].T
        query_seg = jnp.broadcast_to(segment(asker[n]), (128, rows)).T
        query_seg = jnp.concatenate([query_seg] * (rows // 128), axis=1)

        def finish(h, peak, accum, n=n):
            if ends:
                turned = accum.T
                lines = slice(h * hdim, (h + 1) * hdim)
                out_ref[lines, :] = (turned[:hdim] / turned[hdim : hdim + 1]).astype(out_ref.dtype)
            else:
                accum_ref[n, h] = accum
                peak_ref[n, h] = peak

        if follows:

            @pl.when(size == 0)
            def _():
                for h in range(HALF):
                    finish(h, peak_b[0, h], accum_b[0, h])

        for fixed in range(1, len(numbers) + 1):

            @pl.when(size == fixed)
            def _():
                picked = [chosen_s[b] for b in range(fixed)]
                key_segs = [
                    segment(sum(jnp.where(b == i, column[i], 0) for i in range(len(numbers))))
                    for b in picked
                ]

                def one_head(h):
                    lines = slice(h * hdim, (h + 1) * hdim)
                    query = query_s[h]
                    scores = []
                    for b, key_seg in zip(picked, key_segs):
                        score = jnp.dot(
                            query, key_s[b, lines, :], preferred_element_type=jnp.float32
                        )
                        scores.append(jnp.where(query_seg == key_seg, score, NEG))
                    peak = functools.reduce(jnp.maximum, scores)
                    peak = jnp.max(peak, axis=1, keepdims=True)
                    peak = jnp.broadcast_to(peak, (rows, wide))
                    accum = jnp.zeros((rows, wide), jnp.float32)
                    if follows:
                        old = peak_b[0, h]
                        peak = jnp.maximum(peak, old)
                        accum = accum_b[0, h] * jnp.exp2((old - peak) * factor)
                    spread = jnp.concatenate([peak] * (rows // wide), axis=1)
                    for b, score in zip(picked, scores):
                        weights = jnp.exp2((score - spread) * factor).astype(jnp.bfloat16)
                        accum += lax.dot_general(
                            weights,
                            value_s[b, h],
                            (((1,), (1,)), ((), ())),
                            preferred_element_type=jnp.float32,
                        )
                    finish(h, peak, accum)

                for h in range(HALF):
                    one_head(h)


def attention(where, need, segs, queries, kinds, blocks, numbers, before, ends):
    part, rows = queries[0].shape
    hdim = part // HALF
    wide = 128
    follows = before is not None
    rows_of = [
        (array, first)
        for array, block in enumerate(blocks)
        for first in range(0, block.shape[0], 2 * part)
    ]
    if ends:
        out = jax.ShapeDtypeStruct((part, rows), jnp.bfloat16)
    else:
        out = [jax.ShapeDtypeStruct((len(kinds), HALF, rows, wide), jnp.float32)] * 2
    return pl.pallas_call(
        functools.partial(attention_kernel, kinds, numbers, rows_of, follows, ends),
        out_shape=out,
        in_specs=[smem()] + [vmem()] * (2 + len(kinds) + len(blocks) + 2 * follows),
        out_specs=vmem() if ends else [vmem()] * 2,
        scratch_shapes=[
            pltpu.VMEM((HALF, rows, hdim), jnp.bfloat16),
            pltpu.VMEM((len(numbers), part, rows), jnp.bfloat16),
            pltpu.VMEM((len(numbers), HALF, wide, rows), jnp.bfloat16),
            pltpu.SMEM((len(numbers) + 1,), jnp.int32),
        ],
        compiler_params=limit(16),
        cost_estimate=pl.CostEstimate(flops=1000, bytes_accessed=1000, transcendentals=0),
    )(where, need, segs, *queries, *blocks, *(before or ()))


def stack_kernel(*refs):
    *parts, out_ref = refs
    first = 0
    for ref in parts:
        out_ref[first : first + ref.shape[0], :] = ref[...]
        first += ref.shape[0]


def stack(*parts):
    lines = sum(part.shape[0] for part in parts)
    return pl.pallas_call(
        stack_kernel,
        out_shape=jax.ShapeDtypeStruct((lines, parts[0].shape[1]), parts[0].dtype),
        in_specs=[vmem()] * len(parts),
        out_specs=vmem(),
        compiler_params=limit(16),
    )(*parts)


def half_of(where_ref, weight_ref, part, own):
    half = where_ref[0] % 2 if own else 1 - where_ref[0] % 2
    return weight_ref[pl.ds(pl.multiple_of(half * part, 16), part), :]


def begin_kernel(
    pair_rows, pieces, where_ref, owners_ref, offsets_ref, own_ref, weight_ref, tokens_ref,
    hidden_ref, meta_ref,
):
    rows = tokens_ref.shape[0]
    mrows = rows // 4
    owner = owners_ref[...]
    if pieces > 1:
        owner = owner ^ where_ref[0]
    owner = jnp.broadcast_to(owner.astype(jnp.float32), (mrows, mrows))
    earlier = lax.broadcasted_iota(jnp.int32, (mrows, mrows), 0)
    later = lax.broadcasted_iota(jnp.int32, (mrows, mrows), 1)
    column = jnp.sum(jnp.where(earlier == later, owner, 0.0), axis=1, keepdims=True)
    ahead = jnp.where((owner == column) & (earlier < later), 1.0, 0.0)
    slot = owner[:1] * pair_rows + jnp.sum(ahead, axis=0, keepdims=True)
    line = lax.broadcasted_iota(jnp.int32, (16, mrows), 0)
    meta = jnp.where(line == 0, slot, jnp.where(line == 1, offsets_ref[...].astype(jnp.float32), 0.0))
    row = lax.broadcasted_iota(jnp.int32, (mrows, rows), 0)
    patch = lax.broadcasted_iota(jnp.int32, (mrows, rows), 1)
    spread = jnp.where(patch // 4 == row, 1.0, 0.0).astype(jnp.bfloat16)
    meta_ref[...] = jnp.dot(
        meta.astype(jnp.bfloat16), spread, preferred_element_type=jnp.float32
    )
    hidden_ref[...] = tokens_ref[...].astype(jnp.float32) + lax.dot_general(
        own_ref[...],
        half_of(where_ref, weight_ref, own_ref.shape[0], True),
        (((0,), (0,)), ((), ())),
        preferred_element_type=jnp.float32,
    )


def begin(where, owners, offsets, own, out_weight, tokens, pieces, pair_rows):
    return pl.pallas_call(
        functools.partial(begin_kernel, pair_rows, pieces),
        out_shape=[
            jax.ShapeDtypeStruct(tokens.shape, jnp.float32),
            jax.ShapeDtypeStruct((16, tokens.shape[0]), jnp.float32),
        ],
        in_specs=[smem()] + [vmem()] * 5,
        out_specs=[vmem()] * 2,
        compiler_params=limit(24),
    )(where, owners, offsets, own, out_weight, tokens)


def project_kernel(order, where_ref, hidden_ref, meta_ref, other_ref, weight_ref, *outs):
    piece = outs[0].shape[0]
    slots = piece * len(outs)
    rows, width = hidden_ref.shape
    capacity = rows // 2
    meta = meta_ref[...]
    hidden = hidden_ref[...] + lax.dot_general(
        other_ref[...],
        half_of(where_ref, weight_ref, other_ref.shape[0], False),
        (((0,), (0,)), ((), ())),
        preferred_element_type=jnp.float32,
    )
    hidden = hidden.astype(jnp.bfloat16)
    slot = lax.broadcasted_iota(jnp.int32, (slots, rows), 0).astype(jnp.float32)
    quarter = lax.broadcasted_iota(jnp.int32, (1, rows), 1) % 4
    for j in range(4):
        mine = jnp.where(quarter == j, meta[:1], -1.0) == slot
        if j == 0:
            offset = jnp.where(mine, meta[1:2] - capacity, 0.0)
            offset = capacity + jnp.sum(offset, axis=1, keepdims=True)
            offset = jnp.broadcast_to(offset, (slots, 128)).astype(jnp.bfloat16)
            for d, out in zip(order, outs):
                out[:, 4 * width :] = offset[d * piece : (d + 1) * piece]
        pick = jnp.where(mine, 1.0, 0.0).astype(jnp.bfloat16)
        picked = jnp.dot(pick, hidden, preferred_element_type=jnp.float32).astype(jnp.bfloat16)
        for d, out in zip(order, outs):
            out[:, j * width : (j + 1) * width] = picked[d * piece : (d + 1) * piece]


def project(where, hidden, meta, other, out_weight, order, slots):
    width = hidden.shape[1]
    pieces = len(order)
    return pl.pallas_call(
        functools.partial(project_kernel, order),
        out_shape=[jax.ShapeDtypeStruct((slots // pieces, 4 * width + 128), jnp.bfloat16)] * pieces,
        in_specs=[smem()] + [vmem()] * 4,
        out_specs=[vmem()] * pieces,
        compiler_params=limit(24),
    )(where, hidden, meta, other, out_weight)


def place_kernel(*refs):
    *arrived, out_hbm, held, sems = refs
    capacity, merged = out_hbm.shape
    step = merged // 4

    def columns_of(start, size):
        return jnp.concatenate([ref[:, start : start + size] for ref in arrived], axis=0)

    offset = columns_of(merged, 128).astype(jnp.float32)[:, :1]
    row = lax.broadcasted_iota(jnp.int32, (offset.shape[0], capacity), 1).astype(jnp.float32)
    pick = jnp.where(offset == row, 1.0, 0.0).astype(jnp.bfloat16)
    stores = []
    for j in range(4):
        held[j] = lax.dot_general(
            pick,
            columns_of(j * step, step),
            (((0,), (0,)), ((), ())),
            preferred_element_type=jnp.float32,
        ).astype(jnp.bfloat16)
        columns = out_hbm.at[:, pl.ds(j * step, step)]
        stores.append(pltpu.make_async_copy(held.at[j], columns, sems.at[j]))
        stores[j].start()
    for store in stores:
        store.wait()


def place(arrived, capacity, merged):
    return pl.pallas_call(
        place_kernel,
        out_shape=jax.ShapeDtypeStruct((capacity, merged), jnp.bfloat16),
        in_specs=[vmem()] * len(arrived),
        out_specs=anywhere(),
        scratch_shapes=[
            pltpu.VMEM((4, capacity, merged // 4), jnp.bfloat16),
            pltpu.SemaphoreType.DMA((4,)),
        ],
        compiler_params=limit(24),
    )(*arrived)


def per_device(segment_ids, block_mask, queries, keys, values, tokens, out_weight, owners, offsets):
    rows = queries.shape[0]
    width = tokens.shape[1]
    nblocks = lax.axis_size("blk")
    block_index = lax.axis_index("blk")
    mrows = rows // 4
    capacity = 2 * mrows
    pair_rows = max(2, 2 * mrows // nblocks)
    slots = nblocks * pair_rows
    assert slots <= 256

    def route(step):
        return [(i, i + step(i)) for i in range(nblocks) if 0 <= i + step(i) < nblocks]

    swap = functools.partial(
        lax.ppermute, axis_name="blk", perm=route(lambda i: 1 - 2 * (i % 2))
    )
    back = functools.partial(
        lax.ppermute, axis_name="blk", perm=route(lambda i: -2 if i % 2 else 2)
    )

    relay = functools.partial(
        lax.ppermute,
        axis_name="blk",
        perm=route(lambda i: -1 if i == 1 else 1 if i == nblocks - 2 else -2 if i % 2 else 2),
    )
    ahead = functools.partial(
        lax.ppermute,
        axis_name="blk",
        perm=route(lambda i: 1 if i == 0 else -1 if i == nblocks - 1 else 2 if i % 2 else -2),
    )

    where = block_index[None].astype(jnp.int32)
    own_kv, swap_kv = prepare(where, keys, values)
    queries, own_kv, swap_kv = lax.optimization_barrier((queries, own_kv, swap_kv))
    own_q, swap_q = prepare(where, queries)
    segs, need = survey(where, block_mask, segment_ids[None, :])
    other_kv = swap(swap_kv)
    ahead_own = ahead(own_kv)
    back_own = back(own_kv)
    other_q = swap(swap_q)
    ready, back_own, other_q = lax.optimization_barrier((other_kv, back_own, other_q))
    back_other = relay(ready)
    ahead_both = ahead(stack(other_kv, ahead_own))
    near = (own_kv, other_kv, ahead_own, back_own)
    near_numbers = (0, 1, 2, 3)
    fixed = (where, need, segs)
    own = attention(*fixed, (own_q,), (0,), near, near_numbers, None, False)
    back_other, own = lax.optimization_barrier((back_other, own))
    back_far = relay(back_other)
    other = attention(
        *fixed, (other_q,), (1,), (*near, back_other), (*near_numbers, 5), None, False
    )
    other = attention(*fixed, (other_q,), (1,), (ahead_both,), (4, 6), other, True)
    other = swap(other)
    far = (ahead_both, back_other, back_far)
    own = attention(*fixed, (own_q,), (0,), far, (4, 6, 5, 7), own, True)

    order = tuple(range(nblocks)) if nblocks in (4, 8) else (0,)
    hidden, meta = begin(
        where, owners[None, :], offsets[None, :], own, out_weight, tokens, len(order), pair_rows
    )
    outgoing = project(where, hidden, meta, other, out_weight, order, slots)
    if len(order) > 1:
        arrived = list(outgoing)

        def cross(d):
            arrived[d] = lax.ppermute(arrived[d], "blk", [(i, i ^ d) for i in range(nblocks)])

        short, *late = range(nblocks // 2 - 1, 0, -1)
        for d in (*range(nblocks // 2, nblocks), short):
            cross(d)
        group = lax.optimization_barrier([arrived[d] for d in (short, *late)])
        for d, block in zip((short, *late), group):
            arrived[d] = block
        for d in late:
            cross(d)
    else:
        arrived = [lax.all_to_all(outgoing[0], "blk", split_axis=0, concat_axis=0, tiled=True)]
    return place(arrived, capacity, 4 * width)


def solution(mesh):
    placed = (
        P("rep"),
        P("rep", None),
        P(("rep", "blk"), None),
        P(("rep", "blk"), None),
        P(("rep", "blk"), None),
        P(("rep", "blk"), None),
        P(),
        P(("rep", "blk")),
        P(("rep", "blk")),
    )
    return jax.shard_map(
        per_device, mesh=mesh, in_specs=placed, out_specs=P(("rep", "blk"), None), check_vma=False
    )
```

```python
import functools

import jax
import jax.numpy as jnp
from jax import lax
from jax.experimental import pallas as pl
from jax.experimental.pallas import tpu as pltpu
from jax.sharding import PartitionSpec as P

HEADS = 8
HALF = HEADS // 2
SPAN = 3
NEG = -1e30
LOG2E = 1.4426950408889634
MIB = 1024 * 1024


def vmem():
    return pl.BlockSpec(memory_space=pltpu.VMEM)


def smem():
    return pl.BlockSpec(memory_space=pltpu.SMEM)


def anywhere():
    return pl.BlockSpec(memory_space=pl.ANY)


def limit(mib):
    return pltpu.CompilerParams(vmem_limit_bytes=mib * MIB)


PLACES = ((3, 1), (4, -1), (5, -3), (1, 5), (6, -5), (2, 3), (7, -7), (0, 7))


def asking(me, kind):
    return me if kind == 0 else me + 1 - 2 * (me % 2)


def key_block(me, number):
    half = me % 2
    return me - half - SPAN + PLACES[number][0] + PLACES[number][1] * half


def prepare_kernel(number, where_ref, *refs):
    sources, (own, swap, held, turned, sems) = refs[:number], refs[number:]
    part = held.shape[2] // 2
    cut = held.shape[1] // 2
    loads = [
        [
            pltpu.make_async_copy(
                ref.at[pl.ds(k * cut, cut)], held.at[i, pl.ds(k * cut, cut)], sems.at[2 * i + k]
            )
            for k in range(2)
        ]
        for i, ref in enumerate(sources)
    ]
    for pair in loads:
        for load in pair:
            load.start()
    half = where_ref[0] % 2
    mine = pl.multiple_of(half * part, 16)
    other = pl.multiple_of((1 - half) * part, 16)
    for i in range(number):
        for k in range(2):
            loads[i][k].wait()
            piece = slice(k * cut, (k + 1) * cut)
            turned[i, :, piece] = held[i, piece, :].T
        own[i * part : (i + 1) * part, :] = turned[i, pl.ds(mine, part), :]
        swap[i * part : (i + 1) * part, :] = turned[i, pl.ds(other, part), :]


def prepare(where, *arrays):
    number = len(arrays)
    rows, features = arrays[0].shape
    out = jax.ShapeDtypeStruct((number * features // 2, rows), arrays[0].dtype)
    return pl.pallas_call(
        functools.partial(prepare_kernel, number),
        out_shape=[out] * 2,
        in_specs=[smem()] + [anywhere()] * number,
        out_specs=[vmem()] * 2,
        scratch_shapes=[
            pltpu.VMEM((number, rows, features), arrays[0].dtype),
            pltpu.VMEM((number, features, rows), arrays[0].dtype),
            pltpu.SemaphoreType.DMA((2 * number,)),
        ],
        compiler_params=limit(53),
    )(where, *arrays)


def survey_kernel(where_ref, mask_ref, segs_ref, seg_out, need_out):
    seg_out[...] = segs_ref[...].astype(jnp.float32)
    me = where_ref[0]
    nblocks = mask_ref.shape[0]
    bits = jnp.int32(0)
    for kind in range(2):
        asker = asking(me, kind)
        for number in range(len(PLACES)):
            block = key_block(me, number)
            inside = (block >= 0) & (block < nblocks) & (jnp.abs(block - asker) <= SPAN)
            allowed = mask_ref[asker, jnp.clip(block, 0, nblocks - 1)] > 0
            bits += (inside & allowed).astype(jnp.int32) << (kind * len(PLACES) + number)
    need_out[...] = jnp.full(need_out.shape, bits, jnp.int32)


def survey(where, mask, segs):
    return pl.pallas_call(
        survey_kernel,
        out_shape=[
            jax.ShapeDtypeStruct(segs.shape, jnp.float32),
            jax.ShapeDtypeStruct((8, 128), jnp.int32),
        ],
        in_specs=[smem()] * 2 + [vmem()],
        out_specs=[vmem()] * 2,
        compiler_params=limit(16),
    )(where, mask, segs)


def attention_kernel(kinds, numbers, rows_of, follows, ends, where_ref, need_ref, seg_ref, *refs):
    queries, refs = refs[: len(kinds)], refs[len(kinds) :]
    arrays = max(array for array, _ in rows_of) + 1
    blocks, refs = refs[:arrays], refs[arrays:]
    if follows:
        (accum_b, peak_b), refs = refs[:2], refs[2:]
    if ends:
        out_ref, query_s, key_s, value_s, chosen_s = refs
    else:
        accum_ref, peak_ref, query_s, key_s, value_s, chosen_s = refs
    part, rows = queries[0].shape
    hdim = part // HALF
    wide = value_s.shape[2]
    nblocks = seg_ref.shape[1] // rows
    factor = LOG2E / (hdim**0.5)
    me = where_ref[0]
    column = [key_block(me, b) for b in numbers]
    asker = [asking(me, kind) for kind in kinds]
    bits = jnp.max(need_ref[...])
    need = [[(bits >> (kind * len(PLACES) + b)) & 1 for b in numbers] for kind in kinds]

    def segment(block):
        start = pl.multiple_of(jnp.clip(block, 0, nblocks - 1) * rows, 128)
        return seg_ref[:, pl.ds(start, rows)]

    for b in range(len(numbers)):
        wanted = need[0][b]
        for n in range(1, len(kinds)):
            wanted = wanted + need[n][b]

        @pl.when(wanted > 0)
        def _(b=b):
            array, first = rows_of[b]
            key_s[b] = blocks[array][first : first + part, :]
            for h in range(HALF):
                start = first + part + h * hdim
                value_s[b, h, :hdim, :] = blocks[array][start : start + hdim, :]
                value_s[b, h, hdim:, :] = jnp.ones((wide - hdim, rows), jnp.bfloat16)

    for n in range(len(kinds)):
        size = 0
        for b in range(len(numbers)):
            chosen_s[size] = b
            size = size + need[n][b]
        for h in range(HALF):
            query_s[h] = queries[n][h * hdim : (h + 1) * hdim, :].T
        query_seg = jnp.broadcast_to(segment(asker[n]), (128, rows)).T
        query_seg = jnp.concatenate([query_seg] * (rows // 128), axis=1)

        def finish(h, peak, accum, n=n):
            if ends:
                turned = accum.T
                lines = slice(h * hdim, (h + 1) * hdim)
                out_ref[lines, :] = (turned[:hdim] / turned[hdim : hdim + 1]).astype(out_ref.dtype)
            else:
                accum_ref[n, h] = accum
                peak_ref[n, h] = peak

        if follows:

            @pl.when(size == 0)
            def _():
                for h in range(HALF):
                    finish(h, peak_b[0, h], accum_b[0, h])

        for fixed in range(1, len(numbers) + 1):

            @pl.when(size == fixed)
            def _():
                picked = [chosen_s[b] for b in range(fixed)]
                key_segs = [
                    segment(sum(jnp.where(b == i, column[i], 0) for i in range(len(numbers))))
                    for b in picked
                ]

                def one_head(h):
                    lines = slice(h * hdim, (h + 1) * hdim)
                    query = query_s[h]
                    scores = []
                    for b, key_seg in zip(picked, key_segs):
                        score = jnp.dot(
                            query, key_s[b, lines, :], preferred_element_type=jnp.float32
                        )
                        scores.append(jnp.where(query_seg == key_seg, score, NEG))
                    peak = functools.reduce(jnp.maximum, scores)
                    peak = jnp.max(peak, axis=1, keepdims=True)
                    peak = jnp.broadcast_to(peak, (rows, wide))
                    accum = jnp.zeros((rows, wide), jnp.float32)
                    if follows:
                        old = peak_b[0, h]
                        peak = jnp.maximum(peak, old)
                        accum = accum_b[0, h] * jnp.exp2((old - peak) * factor)
                    spread = jnp.concatenate([peak] * (rows // wide), axis=1)
                    for b, score in zip(picked, scores):
                        weights = jnp.exp2((score - spread) * factor).astype(jnp.bfloat16)
                        accum += lax.dot_general(
                            weights,
                            value_s[b, h],
                            (((1,), (1,)), ((), ())),
                            preferred_element_type=jnp.float32,
                        )
                    finish(h, peak, accum)

                for h in range(HALF):
                    one_head(h)


def attention(where, need, segs, queries, kinds, blocks, numbers, before, ends):
    part, rows = queries[0].shape
    hdim = part // HALF
    wide = 128
    follows = before is not None
    rows_of = [
        (array, first)
        for array, block in enumerate(blocks)
        for first in range(0, block.shape[0], 2 * part)
    ]
    if ends:
        out = jax.ShapeDtypeStruct((part, rows), jnp.bfloat16)
    else:
        out = [jax.ShapeDtypeStruct((len(kinds), HALF, rows, wide), jnp.float32)] * 2
    return pl.pallas_call(
        functools.partial(attention_kernel, kinds, numbers, rows_of, follows, ends),
        out_shape=out,
        in_specs=[smem()] + [vmem()] * (2 + len(kinds) + len(blocks) + 2 * follows),
        out_specs=vmem() if ends else [vmem()] * 2,
        scratch_shapes=[
            pltpu.VMEM((HALF, rows, hdim), jnp.bfloat16),
            pltpu.VMEM((len(numbers), part, rows), jnp.bfloat16),
            pltpu.VMEM((len(numbers), HALF, wide, rows), jnp.bfloat16),
            pltpu.SMEM((len(numbers) + 1,), jnp.int32),
        ],
        compiler_params=limit(16),
        cost_estimate=pl.CostEstimate(flops=1000, bytes_accessed=1000, transcendentals=0),
    )(where, need, segs, *queries, *blocks, *(before or ()))


def stack_kernel(*refs):
    *parts, out_ref = refs
    first = 0
    for ref in parts:
        out_ref[first : first + ref.shape[0], :] = ref[...]
        first += ref.shape[0]


def stack(*parts):
    lines = sum(part.shape[0] for part in parts)
    return pl.pallas_call(
        stack_kernel,
        out_shape=jax.ShapeDtypeStruct((lines, parts[0].shape[1]), parts[0].dtype),
        in_specs=[vmem()] * len(parts),
        out_specs=vmem(),
        compiler_params=limit(16),
    )(*parts)


def half_of(where_ref, weight_ref, part, own):
    half = where_ref[0] % 2 if own else 1 - where_ref[0] % 2
    return weight_ref[pl.ds(pl.multiple_of(half * part, 16), part), :]


def begin_kernel(
    pair_rows, pieces, where_ref, owners_ref, offsets_ref, own_ref, weight_ref, tokens_ref,
    hidden_ref, meta_ref,
):
    rows = tokens_ref.shape[0]
    mrows = rows // 4
    owner = owners_ref[...]
    if pieces > 1:
        owner = owner ^ where_ref[0]
    owner = jnp.broadcast_to(owner.astype(jnp.float32), (mrows, mrows))
    earlier = lax.broadcasted_iota(jnp.int32, (mrows, mrows), 0)
    later = lax.broadcasted_iota(jnp.int32, (mrows, mrows), 1)
    column = jnp.sum(jnp.where(earlier == later, owner, 0.0), axis=1, keepdims=True)
    ahead = jnp.where((owner == column) & (earlier < later), 1.0, 0.0)
    slot = owner[:1] * pair_rows + jnp.sum(ahead, axis=0, keepdims=True)
    line = lax.broadcasted_iota(jnp.int32, (16, mrows), 0)
    meta = jnp.where(line == 0, slot, jnp.where(line == 1, offsets_ref[...].astype(jnp.float32), 0.0))
    row = lax.broadcasted_iota(jnp.int32, (mrows, rows), 0)
    patch = lax.broadcasted_iota(jnp.int32, (mrows, rows), 1)
    spread = jnp.where(patch // 4 == row, 1.0, 0.0).astype(jnp.bfloat16)
    meta_ref[...] = jnp.dot(
        meta.astype(jnp.bfloat16), spread, preferred_element_type=jnp.float32
    )
    hidden_ref[...] = tokens_ref[...].astype(jnp.float32) + lax.dot_general(
        own_ref[...],
        half_of(where_ref, weight_ref, own_ref.shape[0], True),
        (((0,), (0,)), ((), ())),
        preferred_element_type=jnp.float32,
    )


def begin(where, owners, offsets, own, out_weight, tokens, pieces, pair_rows):
    return pl.pallas_call(
        functools.partial(begin_kernel, pair_rows, pieces),
        out_shape=[
            jax.ShapeDtypeStruct(tokens.shape, jnp.float32),
            jax.ShapeDtypeStruct((16, tokens.shape[0]), jnp.float32),
        ],
        in_specs=[smem()] + [vmem()] * 5,
        out_specs=[vmem()] * 2,
        compiler_params=limit(24),
    )(where, owners, offsets, own, out_weight, tokens)


def project_kernel(order, where_ref, hidden_ref, meta_ref, other_ref, weight_ref, *outs):
    piece = outs[0].shape[0]
    slots = piece * len(outs)
    rows, width = hidden_ref.shape
    capacity = rows // 2
    meta = meta_ref[...]
    hidden = hidden_ref[...] + lax.dot_general(
        other_ref[...],
        half_of(where_ref, weight_ref, other_ref.shape[0], False),
        (((0,), (0,)), ((), ())),
        preferred_element_type=jnp.float32,
    )
    hidden = hidden.astype(jnp.bfloat16)
    slot = lax.broadcasted_iota(jnp.int32, (slots, rows), 0).astype(jnp.float32)
    quarter = lax.broadcasted_iota(jnp.int32, (1, rows), 1) % 4
    for j in range(4):
        mine = jnp.where(quarter == j, meta[:1], -1.0) == slot
        if j == 0:
            offset = jnp.where(mine, meta[1:2] - capacity, 0.0)
            offset = capacity + jnp.sum(offset, axis=1, keepdims=True)
            offset = jnp.broadcast_to(offset, (slots, 128)).astype(jnp.bfloat16)
            for d, out in zip(order, outs):
                out[:, 4 * width :] = offset[d * piece : (d + 1) * piece]
        pick = jnp.where(mine, 1.0, 0.0).astype(jnp.bfloat16)
        picked = jnp.dot(pick, hidden, preferred_element_type=jnp.float32).astype(jnp.bfloat16)
        for d, out in zip(order, outs):
            out[:, j * width : (j + 1) * width] = picked[d * piece : (d + 1) * piece]


def project(where, hidden, meta, other, out_weight, order, slots):
    width = hidden.shape[1]
    pieces = len(order)
    return pl.pallas_call(
        functools.partial(project_kernel, order),
        out_shape=[jax.ShapeDtypeStruct((slots // pieces, 4 * width + 128), jnp.bfloat16)] * pieces,
        in_specs=[smem()] + [vmem()] * 4,
        out_specs=[vmem()] * pieces,
        compiler_params=limit(24),
    )(where, hidden, meta, other, out_weight)


def place_kernel(*refs):
    *arrived, out_hbm, held, sems = refs
    capacity, merged = out_hbm.shape
    step = merged // 8

    def columns_of(start, size):
        return jnp.concatenate([ref[:, start : start + size] for ref in arrived], axis=0)

    offset = columns_of(merged, 128).astype(jnp.float32)[:, :1]
    row = lax.broadcasted_iota(jnp.int32, (offset.shape[0], capacity), 1).astype(jnp.float32)
    pick = jnp.where(offset == row, 1.0, 0.0).astype(jnp.bfloat16)
    stores = []
    for j in range(8):
        held[j] = lax.dot_general(
            pick,
            columns_of(j * step, step),
            (((0,), (0,)), ((), ())),
            preferred_element_type=jnp.float32,
        ).astype(jnp.bfloat16)
        columns = out_hbm.at[:, pl.ds(j * step, step)]
        stores.append(pltpu.make_async_copy(held.at[j], columns, sems.at[j]))
        stores[j].start()
    for store in stores:
        store.wait()


def place(arrived, capacity, merged):
    return pl.pallas_call(
        place_kernel,
        out_shape=jax.ShapeDtypeStruct((capacity, merged), jnp.bfloat16),
        in_specs=[vmem()] * len(arrived),
        out_specs=anywhere(),
        scratch_shapes=[
            pltpu.VMEM((8, capacity, merged // 8), jnp.bfloat16),
            pltpu.SemaphoreType.DMA((8,)),
        ],
        compiler_params=limit(24),
    )(*arrived)


def per_device(segment_ids, block_mask, queries, keys, values, tokens, out_weight, owners, offsets):
    rows = queries.shape[0]
    width = tokens.shape[1]
    nblocks = lax.axis_size("blk")
    block_index = lax.axis_index("blk")
    mrows = rows // 4
    capacity = 2 * mrows
    pair_rows = max(2, 2 * mrows // nblocks)
    slots = nblocks * pair_rows
    assert slots <= 256

    def route(step):
        return [(i, i + step(i)) for i in range(nblocks) if 0 <= i + step(i) < nblocks]

    swap = functools.partial(
        lax.ppermute, axis_name="blk", perm=route(lambda i: 1 - 2 * (i % 2))
    )
    ahead = functools.partial(
        lax.ppermute, axis_name="blk", perm=route(lambda i: 2 if i % 2 else -2)
    )
    back = functools.partial(
        lax.ppermute, axis_name="blk", perm=route(lambda i: -2 if i % 2 else 2)
    )

    relay = functools.partial(
        lax.ppermute,
        axis_name="blk",
        perm=route(lambda i: -1 if i == 1 else 1 if i == nblocks - 2 else -2 if i % 2 else 2),
    )
    ahead_all = functools.partial(
        lax.ppermute,
        axis_name="blk",
        perm=route(lambda i: 1 if i == 0 else -1 if i == nblocks - 1 else 2 if i % 2 else -2),
    )

    where = block_index[None].astype(jnp.int32)
    own_kv, swap_kv = prepare(where, keys, values)
    queries, own_kv, swap_kv = lax.optimization_barrier((queries, own_kv, swap_kv))
    own_q, swap_q = prepare(where, queries)
    segs, need = survey(where, block_mask, segment_ids[None, :])
    other_kv = swap(swap_kv)
    ahead_own = ahead(own_kv)
    back_own = back(own_kv)
    other_q = swap(swap_q)
    ready, back_own, other_q = lax.optimization_barrier((other_kv, back_own, other_q))
    back_other = relay(ready)
    ahead_both = ahead_all(stack(other_kv, ahead_own))
    near = (own_kv, other_kv, ahead_own, back_own)
    near_numbers = (0, 1, 2, 3)
    fixed = (where, need, segs)
    own = attention(*fixed, (own_q,), (0,), near, near_numbers, None, False)
    back_other, own = lax.optimization_barrier((back_other, own))
    back_far = relay(back_other)
    other = attention(
        *fixed, (other_q,), (1,), (*near, back_other), (*near_numbers, 5), None, False
    )
    other = attention(*fixed, (other_q,), (1,), (ahead_both,), (4, 6), other, True)
    other = swap(other)
    far = (ahead_both, back_other, back_far)
    own = attention(*fixed, (own_q,), (0,), far, (4, 6, 5, 7), own, True)

    order = tuple(range(nblocks)) if nblocks in (4, 8) else (0,)
    hidden, meta = begin(
        where, owners[None, :], offsets[None, :], own, out_weight, tokens, len(order), pair_rows
    )
    outgoing = project(where, hidden, meta, other, out_weight, order, slots)
    if len(order) > 1:
        arrived = list(outgoing)

        def cross(d):
            arrived[d] = lax.ppermute(arrived[d], "blk", [(i, i ^ d) for i in range(nblocks)])

        short, *late = range(nblocks // 2 - 1, 0, -1)
        for d in (*range(nblocks // 2, nblocks), short):
            cross(d)
        group = lax.optimization_barrier([arrived[d] for d in (short, *late)])
        for d, block in zip((short, *late), group):
            arrived[d] = block
        for d in late:
            cross(d)
    else:
        arrived = [lax.all_to_all(outgoing[0], "blk", split_axis=0, concat_axis=0, tiled=True)]
    return place(arrived, capacity, 4 * width)


def solution(mesh):
    placed = (
        P("rep"),
        P("rep", None),
        P(("rep", "blk"), None),
        P(("rep", "blk"), None),
        P(("rep", "blk"), None),
        P(("rep", "blk"), None),
        P(),
        P(("rep", "blk")),
        P(("rep", "blk")),
    )
    return jax.shard_map(
        per_device, mesh=mesh, in_specs=placed, out_specs=P(("rep", "blk"), None), check_vma=False
    )
```

```python
import functools

import jax
import jax.numpy as jnp
from jax import lax
from jax.experimental import pallas as pl
from jax.experimental.pallas import tpu as pltpu
from jax.sharding import PartitionSpec as P

HEADS = 8
HALF = HEADS // 2
SPAN = 3
NEG = -1e30
LOG2E = 1.4426950408889634
MIB = 1024 * 1024


def vmem():
    return pl.BlockSpec(memory_space=pltpu.VMEM)


def smem():
    return pl.BlockSpec(memory_space=pltpu.SMEM)


def anywhere():
    return pl.BlockSpec(memory_space=pl.ANY)


def limit(mib):
    return pltpu.CompilerParams(vmem_limit_bytes=mib * MIB)


PLACES = ((3, 1), (4, -1), (5, -3), (1, 5), (6, -5), (2, 3), (7, -7), (0, 7))


def asking(me, kind):
    return me if kind == 0 else me + 1 - 2 * (me % 2)


def key_block(me, number):
    half = me % 2
    return me - half - SPAN + PLACES[number][0] + PLACES[number][1] * half


def prepare_kernel(number, where_ref, *refs):
    sources, (own, swap, held, turned, sems) = refs[:number], refs[number:]
    part = held.shape[2] // 2
    loads = [
        pltpu.make_async_copy(ref, held.at[i], sems.at[i]) for i, ref in enumerate(sources)
    ]
    for load in loads:
        load.start()
    half = where_ref[0] % 2
    mine = pl.multiple_of(half * part, 16)
    other = pl.multiple_of((1 - half) * part, 16)
    for i in range(number):
        loads[i].wait()
        turned[i] = held[i].T
        own[i * part : (i + 1) * part, :] = turned[i, pl.ds(mine, part), :]
        swap[i * part : (i + 1) * part, :] = turned[i, pl.ds(other, part), :]


def prepare(where, *arrays):
    number = len(arrays)
    rows, features = arrays[0].shape
    out = jax.ShapeDtypeStruct((number * features // 2, rows), arrays[0].dtype)
    return pl.pallas_call(
        functools.partial(prepare_kernel, number),
        out_shape=[out] * 2,
        in_specs=[smem()] + [anywhere()] * number,
        out_specs=[vmem()] * 2,
        scratch_shapes=[
            pltpu.VMEM((number, rows, features), arrays[0].dtype),
            pltpu.VMEM((number, features, rows), arrays[0].dtype),
            pltpu.SemaphoreType.DMA((number,)),
        ],
        compiler_params=limit(53),
    )(where, *arrays)


def survey_kernel(where_ref, mask_ref, segs_ref, seg_out, need_out):
    seg_out[...] = segs_ref[...].astype(jnp.float32)
    me = where_ref[0]
    nblocks = mask_ref.shape[0]
    bits = jnp.int32(0)
    for kind in range(2):
        asker = asking(me, kind)
        for number in range(len(PLACES)):
            block = key_block(me, number)
            inside = (block >= 0) & (block < nblocks) & (jnp.abs(block - asker) <= SPAN)
            allowed = mask_ref[asker, jnp.clip(block, 0, nblocks - 1)] > 0
            bits += (inside & allowed).astype(jnp.int32) << (kind * len(PLACES) + number)
    need_out[...] = jnp.full(need_out.shape, bits, jnp.int32)


def survey(where, mask, segs):
    return pl.pallas_call(
        survey_kernel,
        out_shape=[
            jax.ShapeDtypeStruct(segs.shape, jnp.float32),
            jax.ShapeDtypeStruct((8, 128), jnp.int32),
        ],
        in_specs=[smem()] * 2 + [vmem()],
        out_specs=[vmem()] * 2,
        compiler_params=limit(16),
    )(where, mask, segs)


def attention_kernel(kinds, numbers, rows_of, follows, ends, where_ref, need_ref, seg_ref, *refs):
    queries, refs = refs[: len(kinds)], refs[len(kinds) :]
    arrays = max(array for array, _ in rows_of) + 1
    blocks, refs = refs[:arrays], refs[arrays:]
    if follows:
        (accum_b, peak_b), refs = refs[:2], refs[2:]
    if ends:
        out_ref, query_s, key_s, value_s, chosen_s = refs
    else:
        accum_ref, peak_ref, query_s, key_s, value_s, chosen_s = refs
    part, rows = queries[0].shape
    hdim = part // HALF
    wide = value_s.shape[2]
    nblocks = seg_ref.shape[1] // rows
    factor = LOG2E / (hdim**0.5)
    me = where_ref[0]
    column = [key_block(me, b) for b in numbers]
    asker = [asking(me, kind) for kind in kinds]
    bits = jnp.max(need_ref[...])
    need = [[(bits >> (kind * len(PLACES) + b)) & 1 for b in numbers] for kind in kinds]

    def segment(block):
        start = pl.multiple_of(jnp.clip(block, 0, nblocks - 1) * rows, 128)
        return seg_ref[:, pl.ds(start, rows)]

    for b in range(len(numbers)):
        wanted = need[0][b]
        for n in range(1, len(kinds)):
            wanted = wanted + need[n][b]

        @pl.when(wanted > 0)
        def _(b=b):
            array, first = rows_of[b]
            key_s[b] = blocks[array][first : first + part, :]
            for h in range(HALF):
                start = first + part + h * hdim
                value_s[b, h, :hdim, :] = blocks[array][start : start + hdim, :]
                value_s[b, h, hdim:, :] = jnp.ones((wide - hdim, rows), jnp.bfloat16)

    for n in range(len(kinds)):
        size = 0
        for b in range(len(numbers)):
            chosen_s[size] = b
            size = size + need[n][b]
        for h in range(HALF):
            query_s[h] = queries[n][h * hdim : (h + 1) * hdim, :].T
        query_seg = jnp.broadcast_to(segment(asker[n]), (128, rows)).T
        query_seg = jnp.concatenate([query_seg] * (rows // 128), axis=1)

        def finish(h, peak, accum, n=n):
            if ends:
                turned = accum.T
                lines = slice(h * hdim, (h + 1) * hdim)
                out_ref[lines, :] = (turned[:hdim] / turned[hdim : hdim + 1]).astype(out_ref.dtype)
            else:
                accum_ref[n, h] = accum
                peak_ref[n, h] = peak

        if follows:

            @pl.when(size == 0)
            def _():
                for h in range(HALF):
                    finish(h, peak_b[0, h], accum_b[0, h])

        for fixed in range(1, len(numbers) + 1):

            @pl.when(size == fixed)
            def _():
                picked = [chosen_s[b] for b in range(fixed)]
                key_segs = [
                    segment(sum(jnp.where(b == i, column[i], 0) for i in range(len(numbers))))
                    for b in picked
                ]

                def one_head(h):
                    lines = slice(h * hdim, (h + 1) * hdim)
                    query = query_s[h]
                    scores = []
                    for b, key_seg in zip(picked, key_segs):
                        score = jnp.dot(
                            query, key_s[b, lines, :], preferred_element_type=jnp.float32
                        )
                        scores.append(jnp.where(query_seg == key_seg, score, NEG))
                    peak = functools.reduce(jnp.maximum, scores)
                    peak = jnp.max(peak, axis=1, keepdims=True)
                    peak = jnp.broadcast_to(peak, (rows, wide))
                    accum = jnp.zeros((rows, wide), jnp.float32)
                    if follows:
                        old = peak_b[0, h]
                        peak = jnp.maximum(peak, old)
                        accum = accum_b[0, h] * jnp.exp2((old - peak) * factor)
                    spread = jnp.concatenate([peak] * (rows // wide), axis=1)
                    for b, score in zip(picked, scores):
                        weights = jnp.exp2((score - spread) * factor).astype(jnp.bfloat16)
                        accum += lax.dot_general(
                            weights,
                            value_s[b, h],
                            (((1,), (1,)), ((), ())),
                            preferred_element_type=jnp.float32,
                        )
                    finish(h, peak, accum)

                for h in range(HALF):
                    one_head(h)


def attention(where, need, segs, queries, kinds, blocks, numbers, before, ends):
    part, rows = queries[0].shape
    hdim = part // HALF
    wide = 128
    follows = before is not None
    rows_of = [
        (array, first)
        for array, block in enumerate(blocks)
        for first in range(0, block.shape[0], 2 * part)
    ]
    if ends:
        out = jax.ShapeDtypeStruct((part, rows), jnp.bfloat16)
    else:
        out = [jax.ShapeDtypeStruct((len(kinds), HALF, rows, wide), jnp.float32)] * 2
    return pl.pallas_call(
        functools.partial(attention_kernel, kinds, numbers, rows_of, follows, ends),
        out_shape=out,
        in_specs=[smem()] + [vmem()] * (2 + len(kinds) + len(blocks) + 2 * follows),
        out_specs=vmem() if ends else [vmem()] * 2,
        scratch_shapes=[
            pltpu.VMEM((HALF, rows, hdim), jnp.bfloat16),
            pltpu.VMEM((len(numbers), part, rows), jnp.bfloat16),
            pltpu.VMEM((len(numbers), HALF, wide, rows), jnp.bfloat16),
            pltpu.SMEM((len(numbers) + 1,), jnp.int32),
        ],
        compiler_params=limit(16),
        cost_estimate=pl.CostEstimate(flops=1000, bytes_accessed=1000, transcendentals=0),
    )(where, need, segs, *queries, *blocks, *(before or ()))


def stack_kernel(*refs):
    *parts, out_ref = refs
    first = 0
    for ref in parts:
        out_ref[first : first + ref.shape[0], :] = ref[...]
        first += ref.shape[0]


def stack(*parts):
    lines = sum(part.shape[0] for part in parts)
    return pl.pallas_call(
        stack_kernel,
        out_shape=jax.ShapeDtypeStruct((lines, parts[0].shape[1]), parts[0].dtype),
        in_specs=[vmem()] * len(parts),
        out_specs=vmem(),
        compiler_params=limit(16),
    )(*parts)


def half_of(where_ref, weight_ref, part, own):
    half = where_ref[0] % 2 if own else 1 - where_ref[0] % 2
    return weight_ref[pl.ds(pl.multiple_of(half * part, 16), part), :]


def begin_kernel(
    pair_rows, pieces, where_ref, owners_ref, offsets_ref, own_ref, weight_ref, tokens_ref,
    hidden_ref, meta_ref,
):
    rows = tokens_ref.shape[0]
    mrows = rows // 4
    owner = owners_ref[...]
    if pieces > 1:
        owner = owner ^ where_ref[0]
    owner = jnp.broadcast_to(owner.astype(jnp.float32), (mrows, mrows))
    earlier = lax.broadcasted_iota(jnp.int32, (mrows, mrows), 0)
    later = lax.broadcasted_iota(jnp.int32, (mrows, mrows), 1)
    column = jnp.sum(jnp.where(earlier == later, owner, 0.0), axis=1, keepdims=True)
    ahead = jnp.where((owner == column) & (earlier < later), 1.0, 0.0)
    slot = owner[:1] * pair_rows + jnp.sum(ahead, axis=0, keepdims=True)
    line = lax.broadcasted_iota(jnp.int32, (16, mrows), 0)
    meta = jnp.where(line == 0, slot, jnp.where(line == 1, offsets_ref[...].astype(jnp.float32), 0.0))
    row = lax.broadcasted_iota(jnp.int32, (mrows, rows), 0)
    patch = lax.broadcasted_iota(jnp.int32, (mrows, rows), 1)
    spread = jnp.where(patch // 4 == row, 1.0, 0.0).astype(jnp.bfloat16)
    meta_ref[...] = jnp.dot(
        meta.astype(jnp.bfloat16), spread, preferred_element_type=jnp.float32
    )
    hidden_ref[...] = tokens_ref[...].astype(jnp.float32) + lax.dot_general(
        own_ref[...],
        half_of(where_ref, weight_ref, own_ref.shape[0], True),
        (((0,), (0,)), ((), ())),
        preferred_element_type=jnp.float32,
    )


def begin(where, owners, offsets, own, out_weight, tokens, pieces, pair_rows):
    return pl.pallas_call(
        functools.partial(begin_kernel, pair_rows, pieces),
        out_shape=[
            jax.ShapeDtypeStruct(tokens.shape, jnp.float32),
            jax.ShapeDtypeStruct((16, tokens.shape[0]), jnp.float32),
        ],
        in_specs=[smem()] + [vmem()] * 5,
        out_specs=[vmem()] * 2,
        compiler_params=limit(24),
    )(where, owners, offsets, own, out_weight, tokens)


def project_kernel(order, where_ref, hidden_ref, meta_ref, other_ref, weight_ref, *outs):
    piece = outs[0].shape[0]
    slots = piece * len(outs)
    rows, width = hidden_ref.shape
    capacity = rows // 2
    meta = meta_ref[...]
    hidden = hidden_ref[...] + lax.dot_general(
        other_ref[...],
        half_of(where_ref, weight_ref, other_ref.shape[0], False),
        (((0,), (0,)), ((), ())),
        preferred_element_type=jnp.float32,
    )
    hidden = hidden.astype(jnp.bfloat16)
    slot = lax.broadcasted_iota(jnp.int32, (slots, rows), 0).astype(jnp.float32)
    quarter = lax.broadcasted_iota(jnp.int32, (1, rows), 1) % 4
    for j in range(4):
        mine = jnp.where(quarter == j, meta[:1], -1.0) == slot
        if j == 0:
            offset = jnp.where(mine, meta[1:2] - capacity, 0.0)
            offset = capacity + jnp.sum(offset, axis=1, keepdims=True)
            offset = jnp.broadcast_to(offset, (slots, 128)).astype(jnp.bfloat16)
            for d, out in zip(order, outs):
                out[:, 4 * width :] = offset[d * piece : (d + 1) * piece]
        pick = jnp.where(mine, 1.0, 0.0).astype(jnp.bfloat16)
        picked = jnp.dot(pick, hidden, preferred_element_type=jnp.float32).astype(jnp.bfloat16)
        for d, out in zip(order, outs):
            out[:, j * width : (j + 1) * width] = picked[d * piece : (d + 1) * piece]


def project(where, hidden, meta, other, out_weight, order, slots):
    width = hidden.shape[1]
    pieces = len(order)
    return pl.pallas_call(
        functools.partial(project_kernel, order),
        out_shape=[jax.ShapeDtypeStruct((slots // pieces, 4 * width + 128), jnp.bfloat16)] * pieces,
        in_specs=[smem()] + [vmem()] * 4,
        out_specs=[vmem()] * pieces,
        compiler_params=limit(24),
    )(where, hidden, meta, other, out_weight)


def place_kernel(*refs):
    *arrived, out_hbm, held, sems = refs
    capacity, merged = out_hbm.shape
    step = merged // 4

    def columns_of(start, size):
        return jnp.concatenate([ref[:, start : start + size] for ref in arrived], axis=0)

    offset = columns_of(merged, 128).astype(jnp.float32)[:, :1]
    row = lax.broadcasted_iota(jnp.int32, (offset.shape[0], capacity), 1).astype(jnp.float32)
    pick = jnp.where(offset == row, 1.0, 0.0).astype(jnp.bfloat16)
    stores = []
    for j in range(4):
        held[j] = lax.dot_general(
            pick,
            columns_of(j * step, step),
            (((0,), (0,)), ((), ())),
            preferred_element_type=jnp.float32,
        ).astype(jnp.bfloat16)
        columns = out_hbm.at[:, pl.ds(j * step, step)]
        stores.append(pltpu.make_async_copy(held.at[j], columns, sems.at[j]))
        stores[j].start()
    for store in stores:
        store.wait()


def place(arrived, capacity, merged):
    return pl.pallas_call(
        place_kernel,
        out_shape=jax.ShapeDtypeStruct((capacity, merged), jnp.bfloat16),
        in_specs=[vmem()] * len(arrived),
        out_specs=anywhere(),
        scratch_shapes=[
            pltpu.VMEM((4, capacity, merged // 4), jnp.bfloat16),
            pltpu.SemaphoreType.DMA((4,)),
        ],
        compiler_params=limit(24),
    )(*arrived)


def per_device(segment_ids, block_mask, queries, keys, values, tokens, out_weight, owners, offsets):
    rows = queries.shape[0]
    width = tokens.shape[1]
    nblocks = lax.axis_size("blk")
    block_index = lax.axis_index("blk")
    mrows = rows // 4
    capacity = 2 * mrows
    pair_rows = max(2, 2 * mrows // nblocks)
    slots = nblocks * pair_rows
    assert slots <= 256

    def route(step):
        return [(i, i + step(i)) for i in range(nblocks) if 0 <= i + step(i) < nblocks]

    swap = functools.partial(
        lax.ppermute, axis_name="blk", perm=route(lambda i: 1 - 2 * (i % 2))
    )
    ahead = functools.partial(
        lax.ppermute, axis_name="blk", perm=route(lambda i: 2 if i % 2 else -2)
    )
    back = functools.partial(
        lax.ppermute, axis_name="blk", perm=route(lambda i: -2 if i % 2 else 2)
    )

    relay = functools.partial(
        lax.ppermute,
        axis_name="blk",
        perm=route(lambda i: -1 if i == 1 else 1 if i == nblocks - 2 else -2 if i % 2 else 2),
    )
    ahead_all = functools.partial(
        lax.ppermute,
        axis_name="blk",
        perm=route(lambda i: 1 if i == 0 else -1 if i == nblocks - 1 else 2 if i % 2 else -2),
    )

    where = block_index[None].astype(jnp.int32)
    own_kv, swap_kv = prepare(where, keys, values)
    queries, own_kv, swap_kv = lax.optimization_barrier((queries, own_kv, swap_kv))
    own_q, swap_q = prepare(where, queries)
    segs, need = survey(where, block_mask, segment_ids[None, :])
    other_kv = swap(swap_kv)
    ahead_own = ahead(own_kv)
    back_own = back(own_kv)
    other_q = swap(swap_q)
    ready, back_own, other_q = lax.optimization_barrier((other_kv, back_own, other_q))
    back_other = relay(ready)
    ahead_both = ahead_all(stack(other_kv, ahead_own))
    near = (own_kv, other_kv, ahead_own, back_own)
    near_numbers = (0, 1, 2, 3)
    fixed = (where, need, segs)
    own = attention(*fixed, (own_q,), (0,), near, near_numbers, None, False)
    back_other, own = lax.optimization_barrier((back_other, own))
    back_far = back(back_other)
    other = attention(
        *fixed, (other_q,), (1,), (*near, back_other), (*near_numbers, 5), None, False
    )
    other = attention(*fixed, (other_q,), (1,), (ahead_both,), (4, 6), other, True)
    other = swap(other)
    far = (ahead_both, back_other, back_far)
    own = attention(*fixed, (own_q,), (0,), far, (4, 6, 5, 7), own, True)

    order = tuple(range(nblocks)) if nblocks in (4, 8) else (0,)
    hidden, meta = begin(
        where, owners[None, :], offsets[None, :], own, out_weight, tokens, len(order), pair_rows
    )
    outgoing = project(where, hidden, meta, other, out_weight, order, slots)
    if len(order) > 1:
        arrived = list(outgoing)

        def cross(d):
            arrived[d] = lax.ppermute(arrived[d], "blk", [(i, i ^ d) for i in range(nblocks)])

        short, *late = range(nblocks // 2 - 1, 0, -1)
        for d in (*range(nblocks // 2, nblocks), short):
            cross(d)
        group = lax.optimization_barrier([arrived[d] for d in (short, *late)])
        for d, block in zip((short, *late), group):
            arrived[d] = block
        for d in late:
            cross(d)
    else:
        arrived = [lax.all_to_all(outgoing[0], "blk", split_axis=0, concat_axis=0, tiled=True)]
    return place(arrived, capacity, 4 * width)


def solution(mesh):
    placed = (
        P("rep"),
        P("rep", None),
        P(("rep", "blk"), None),
        P(("rep", "blk"), None),
        P(("rep", "blk"), None),
        P(("rep", "blk"), None),
        P(),
        P(("rep", "blk")),
        P(("rep", "blk")),
    )
    return jax.shard_map(
        per_device, mesh=mesh, in_specs=placed, out_specs=P(("rep", "blk"), None), check_vma=False
    )
```
